128 devices in a mesh: tile: 8 (over y_hi, x), step: 16 (over z, y_lo, core).
Axes of the slice: x: 4, y: 4 (y_hi: 2, y_lo: 2; y = y_hi * 2 + y_lo), z: 4, core: 2. Of those that a mesh axis runs over, the one named last changes fastest.
Arguments:
- features: bfloat16 [64, 256, 256], P('tile', 'step'), may hold values from -6 to 6
- encoder_weight: bfloat16 [9, 256, 512], replicated, may hold values from -0.125 to 0.125
- latent_weight: bfloat16 [512, 32], replicated, may hold values from -0.25 to 0.25
- timesteps: int32 [16], P('step'), may hold values from 0 to 999
- noise_field: bfloat16 [16, 64, 8192], P('step', 'tile'), may hold values from -6 to 6
- time_table: bfloat16 [1000, 384], replicated, may hold values from -6 to 6
- input_weight: bfloat16 [32, 384], replicated, may hold values from -1 to 1
- middle_weight: bfloat16 [9, 384, 384], replicated, may hold values from -0.099609375 to 0.099609375
- output_weight: bfloat16 [384, 32], replicated, may hold values from -0.3125 to 0.3125
Outputs:
- feature_grad: float32 [64, 256, 256], P('tile', 'step')
- middle_grad: float32 [384, 9, 384], P(('tile', 'step'))
The draws below stay inside these ranges and needn't reach their ends.
All inputs are finite; a program needn't handle non-finite values.
Results may differ from the reference program's by a relative error of at most 0.02.
Values may be sent and summed in bfloat16 or wider, within the bound.
A program may use at most 128 MiB of HBM per device.

```python
import math
import jax
import jax.numpy as jnp
from jax import lax

FEAT = 256
HID = 512
LAT = 32
UNET = 384
TSTEPS = 1000
SAMPLES = 16
ROWS = 64
COLS = 256


def with_ends(array, stream_key, smallest, high):
    longest = array.shape.index(max(array.shape))
    spots = []
    for shift in (0, 1):
        where = [jax.random.randint(jax.random.fold_in(stream_key, axis), (), 0, length) for axis, length in enumerate(array.shape)]
        where[longest] = (where[longest] + shift) % array.shape[longest]
        spots.append(tuple(where))
    return array.at[spots[0]].set(smallest).at[spots[1]].set(high)


def block_scale(key, extent, cuts, smallest, largest):
    gain, own = 1.0, jax.random.fold_in(key, 6)
    for position, shards_of in cuts:
        steps = jnp.exp(jax.random.uniform(jax.random.fold_in(own, position), (shards_of,), jnp.float32, smallest / len(cuts), largest / len(cuts)))
        gain = gain * jnp.repeat(steps, extent[position] // shards_of).reshape([-1 if axis == position else 1 for axis in range(len(extent))])
    return gain


def gaussian(stream_key, dims, scale, reach, split=(), kind=jnp.bfloat16):
    entries = scale * jax.random.normal(stream_key, dims, jnp.float32)
    if split:
        entries = entries * block_scale(stream_key, dims, split, -0.22, 0.18)
    return jnp.clip(entries, -reach, reach).astype(kind)


def setup_inputs(seed: int = 0) -> dict:
    keys = jax.random.split(jax.random.key(seed), 10)
    features = gaussian(keys[0], (ROWS, COLS, FEAT), 1.0, 6.0, ((0, 8), (1, 16)))
    encoder_weight = gaussian(keys[1], (9, FEAT, HID), (9 * FEAT) ** -0.5, 0.125)
    latent_weight = gaussian(keys[2], (HID, LAT), HID ** -0.5, 0.25)
    timesteps = with_ends(jax.random.randint(keys[3], (SAMPLES,), 0, TSTEPS), jax.random.fold_in(keys[3], 1), 0, TSTEPS - 1).astype(jnp.int32)
    noise_field = gaussian(keys[4], (SAMPLES, ROWS, COLS * LAT), 1.0, 6.0, ((0, 16), (1, 8)))
    time_table = gaussian(keys[5], (TSTEPS, UNET), 1.0, 6.0)
    input_weight = jnp.clip(jax.random.uniform(keys[6], (LAT, UNET), jnp.float32, -1.0, 1.0), -1.0, 1.0).astype(jnp.bfloat16)
    middle_weight = jnp.clip(jax.random.uniform(keys[7], (9, UNET, UNET), jnp.float32, -0.099609375, 0.099609375), -0.099609375, 0.099609375).astype(jnp.bfloat16)
    output_weight = gaussian(keys[8], (UNET, LAT), UNET ** -0.5, 0.3125)
    return {"features": features, "encoder_weight": encoder_weight, "latent_weight": latent_weight, "timesteps": timesteps, "noise_field": noise_field, "time_table": time_table, "input_weight": input_weight, "middle_weight": middle_weight, "output_weight": output_weight}


def silu_slope(values):
    sigma = jax.nn.sigmoid(values)
    return sigma * (1.0 + values * (1.0 - sigma))

def conv_taps(padded, tile_height, tile_width, weights, backward):
    accum = None
    for tap_index in range(9):
        row_shift, col_shift = divmod(tap_index, 3)
        if backward:
            window = padded[2 - row_shift:2 - row_shift + tile_height, 2 - col_shift:2 - col_shift + tile_width]
            window = window.reshape(tile_height * tile_width, window.shape[2])
            partial_sum = lax.dot_general(window, weights[tap_index], (((1,), (1,)), ((), ())), preferred_element_type=jnp.float32)
        else:
            window = padded[row_shift:row_shift + tile_height, col_shift:col_shift + tile_width]
            window = window.reshape(tile_height * tile_width, window.shape[2])
            partial_sum = jnp.dot(window, weights[tap_index], preferred_element_type=jnp.float32)
        accum = partial_sum if accum is None else accum + partial_sum
    return accum

def reference(features, encoder_weight, latent_weight, timesteps, noise_field, time_table, input_weight, middle_weight, output_weight):
    padded = jnp.pad(features, ((1, 1), (1, 1), (0, 0)))
    pre_hidden = conv_taps(padded, ROWS, COLS, encoder_weight, False)
    hidden = jax.nn.silu(pre_hidden).astype(jnp.bfloat16)
    latent = jnp.dot(hidden, latent_weight, preferred_element_type=jnp.float32).astype(jnp.bfloat16)
    inv_root = 1.0 / math.sqrt(SAMPLES)
    positions = jnp.arange(TSTEPS, dtype=jnp.int32)
    grad_middle = jnp.zeros((UNET, 9, UNET), jnp.float32)
    latent_back = jnp.zeros((ROWS * COLS, LAT), jnp.float32)
    for sample in range(SAMPLES):
        chosen = timesteps[sample]
        theta = ((chosen.astype(jnp.float32) + 1.0) / TSTEPS + 0.008) / 1.008 * (math.pi / 2.0)
        cosine = jnp.cos(theta)
        sine = jnp.sin(theta)
        noise_rows = noise_field[sample].reshape(ROWS * COLS, LAT).astype(jnp.float32)
        noisy = (cosine * latent.astype(jnp.float32) + sine * noise_rows).astype(jnp.bfloat16)
        onehot = (positions == chosen).astype(jnp.bfloat16)[None, :]
        embedding = jnp.dot(onehot, time_table, preferred_element_type=jnp.float32)
        pre_input = jnp.dot(noisy, input_weight, preferred_element_type=jnp.float32) + embedding
        inner = jax.nn.silu(pre_input).astype(jnp.bfloat16)
        inner_pad = jnp.pad(inner.reshape(ROWS, COLS, UNET), ((1, 1), (1, 1), (0, 0)))
        pre_middle = conv_taps(inner_pad, ROWS, COLS, middle_weight, False)
        mixed = (inner.astype(jnp.float32) + jax.nn.silu(pre_middle)).astype(jnp.bfloat16)
        prediction = jnp.dot(mixed, output_weight, preferred_element_type=jnp.float32)
        error = ((prediction - noise_rows) * inv_root).astype(jnp.bfloat16)
        back_mixed = lax.dot_general(error, output_weight, (((1,), (1,)), ((), ())), preferred_element_type=jnp.float32)
        back_middle = (back_mixed * silu_slope(pre_middle)).astype(jnp.bfloat16)
        tap_terms = []
        for tap_index in range(9):
            row_shift, col_shift = divmod(tap_index, 3)
            window = inner_pad[row_shift:row_shift + ROWS, col_shift:col_shift + COLS].reshape(ROWS * COLS, UNET)
            tap_terms.append(lax.dot_general(window, back_middle, (((0,), (0,)), ((), ())), preferred_element_type=jnp.float32))
        grad_middle = grad_middle + jnp.stack(tap_terms, axis=1)
        back_pad = jnp.pad(back_middle.reshape(ROWS, COLS, UNET), ((1, 1), (1, 1), (0, 0)))
        through = back_mixed + conv_taps(back_pad, ROWS, COLS, middle_weight, True)
        back_input = (through * silu_slope(pre_input)).astype(jnp.bfloat16)
        back_noisy = lax.dot_general(back_input, input_weight, (((1,), (1,)), ((), ())), preferred_element_type=jnp.float32)
        latent_back = latent_back + cosine * back_noisy
    middle_grad = grad_middle * (1.0 / math.sqrt(ROWS * COLS))
    latent_round = latent_back.astype(jnp.bfloat16)
    hidden_pull = lax.dot_general(latent_round, latent_weight, (((1,), (1,)), ((), ())), preferred_element_type=jnp.float32)
    hidden_back = (hidden_pull * silu_slope(pre_hidden)).astype(jnp.bfloat16).reshape(ROWS, COLS, HID)
    padded_back = jnp.pad(hidden_back, ((1, 1), (1, 1), (0, 0)))
    feature_grad = conv_taps(padded_back, ROWS, COLS, encoder_weight, True).reshape(ROWS, COLS, FEAT)
    return (feature_grad, middle_grad)
```

```python
import math

import jax
import jax.numpy as jnp
from jax import lax
from jax.experimental import pallas as pl
from jax.experimental.pallas import tpu as pltpu
from jax.sharding import PartitionSpec as P

F32 = jnp.float32
BF16 = jnp.bfloat16
MESH = pl.DeviceIdType.MESH

FEAT, HID, LAT, UNET = 256, 512, 32, 384
TILES, STEPS = 8, 16
AROUND = ((-1, -1), (-1, 0), (-1, 1), (0, -1), (0, 1), (1, -1), (1, 0), (1, 1))


def sigmoid(values):
    return 0.5 * jnp.tanh(0.5 * values) + 0.5


def slope_of(values, sigma):
    return sigma * (1.0 + values * (1.0 - sigma))


def dot(left, right):
    return jnp.dot(left, right, preferred_element_type=F32)


def dot_nt(left, right):
    return lax.dot_general(left, right, (((1,), (1,)), ((), ())), preferred_element_type=F32)


def lane_tiles(value):
    return [value[:, 128 * i : 128 * i + 128] for i in range(value.shape[1] // 128)]


def shift_down(block):
    last = pltpu.roll(block[48:64], 1, 0)
    rows = lax.broadcasted_iota(jnp.int32, last.shape, 0)
    return jnp.concatenate([jnp.where(rows == 0, 0.0, last), block[0:48]], axis=0)


def shift_up(block):
    first = pltpu.roll(block[0:16], 15, 0)
    rows = lax.broadcasted_iota(jnp.int32, first.shape, 0)
    return jnp.concatenate([block[16:64], jnp.where(rows == 15, 0.0, first)], axis=0)


def kernel(
    time_ref,
    feat_hbm,
    enc_hbm,
    latw_hbm,
    noise_hbm,
    table_hbm,
    inw_hbm,
    midw_hbm,
    outw_hbm,
    fgrad_ref,
    mgrad_ref,
    feat,
    enc,
    latw,
    noise,
    table,
    inw,
    midw,
    outw,
    in_sem,
    enc_t,
    mid_t,
    latw4,
    latw4_t,
    inw4,
    inw4_t,
    outw4,
    outw4_t,
    embed,
    edge,
    edge_in,
    rows_in,
    grid,
    blocks_even,
    blocks_odd,
    pre_hidden,
    lat_tile,
    lat_pack,
    lat_send,
    lat_recv,
    lat_flat,
    noise_rows,
    noise_edge,
    noise_edge_in,
    inner_ext,
    inner_slope,
    inner_t,
    back_mixed,
    back_ext,
    back_part,
    part_send,
    part_recv,
    round_pack,
    round_send,
    round_recv,
    round_grid,
    hidden_even,
    hidden_odd,
    out_grid,
    grad,
    s1_send,
    s1_recv,
    sum1,
    s2_send,
    s2_recv,
    sum2,
    s3_send,
    s3_recv,
    feat_ss,
    feat_rs,
    noise_ss,
    noise_rs,
    lat_ss,
    lat_rs,
    halo_ss,
    halo_rs,
    part_ss,
    part_rs,
    round_ss,
    round_rs,
    s1_ss,
    s1_rs,
    s2_ss,
    s2_rs,
    s3_ss,
    s3_rs,
):
    t = lax.axis_index("tile")
    s = lax.axis_index("step")
    y_hi, x = t // 4, t % 4
    z, y_lo, core = s // 4, (s // 2) % 2, s % 2
    y = y_hi * 2 + y_lo

    def remote(src, dst, ss, rs, tile, step):
        return pltpu.make_async_remote_copy(
            src_ref=src, dst_ref=dst, send_sem=ss, recv_sem=rs, device_id=(tile, step), device_id_type=MESH
        )

    def near(offsets):
        return (t + offsets[0] + TILES) % TILES, (s + offsets[1] + STEPS) % STEPS

    loads = [
        pltpu.make_async_copy(src, dst, in_sem.at[i])
        for i, (src, dst) in enumerate(
            (
                (feat_hbm, feat),
                (noise_hbm, noise),
                (enc_hbm, enc),
                (latw_hbm, latw),
                (inw_hbm, inw),
                (outw_hbm, outw),
                (table_hbm, table),
                (midw_hbm, midw),
            )
        )
    ]
    for load in loads:
        load.start()
    l_feat, l_noise, l_enc, l_latw, l_inw, l_outw, l_table, l_midw = loads

    barrier = pltpu.get_barrier_semaphore()

    def greet_step(k, _):
        pl.semaphore_signal(barrier, inc=1, device_id=(t, (s + k) % STEPS), device_id_type=MESH)
        return 0

    def greet_tile(k, _):
        pl.semaphore_signal(barrier, inc=1, device_id=((t + k) % TILES, s), device_id_type=MESH)
        return 0

    lax.fori_loop(1, STEPS, greet_step, 0)
    lax.fori_loop(1, TILES, greet_tile, 0)
    for offsets in AROUND:
        if offsets[0] and offsets[1]:
            pl.semaphore_signal(barrier, inc=1, device_id=near(offsets), device_id_type=MESH)

    l_feat.wait()
    grid[...] = jnp.zeros_like(grid)
    for r in range(8):
        for i, part in enumerate(lane_tiles(feat[r].astype(F32))):
            grid[i, (r + 2) * 32 + 8 : (r + 2) * 32 + 24, :] = part
    for side, first in ((0, 8), (1, 22)):
        for i in range(2):
            pair = [grid[i, pl.ds(64 + first + col, 8, stride=32), :] for col in (0, 1)]
            edge[side, :, 128 * i : 128 * i + 128] = jnp.concatenate(pair, axis=0).astype(BF16)

    pl.semaphore_wait(barrier, STEPS - 1 + TILES - 1 + 4)

    feat_copies = []
    for d, offsets in enumerate(AROUND):
        tile, step = near(offsets)
        if offsets[0] == 0:
            side = 0 if offsets[1] < 0 else 1
            src, dst = edge.at[side], edge_in.at[side]
        else:
            slot = d if d < 3 else d - 2
            src, dst = feat.at[pl.ds(0 if offsets[0] < 0 else 6, 2)], rows_in.at[slot]
        copy = remote(src, dst, feat_ss.at[d], feat_rs.at[d], tile, step)
        copy.start()
        feat_copies.append(copy)

    l_noise.wait()
    for q in range(64):
        piece = noise[0, :, 128 * q : 128 * q + 128].astype(F32)
        noise_rows[pl.ds(64 + (q % 4) * 16 + q // 4, 8, stride=64), :] = piece
    noise_edge[0] = noise_rows[64:128, :].astype(BF16)
    noise_edge[1] = noise_rows[512:576, :].astype(BF16)
    noise_copies = []
    for side, offset in ((0, -1), (1, 1)):
        tile, step = near((offset, 0))
        copy = remote(noise_edge.at[side], noise_edge_in.at[side], noise_ss.at[side], noise_rs.at[side], tile, step)
        copy.start()
        noise_copies.append(copy)

    def spread(j):
        row = lax.broadcasted_iota(jnp.int32, (LAT, 128), 0)
        lane = lax.broadcasted_iota(jnp.int32, (LAT, 128), 1)
        return (lane == row + LAT * j).astype(F32).astype(BF16)

    def spread_t(j):
        row = lax.broadcasted_iota(jnp.int32, (128, LAT), 0)
        lane = lax.broadcasted_iota(jnp.int32, (128, LAT), 1)
        return (row == lane + LAT * j).astype(F32).astype(BF16)

    l_latw.wait()
    for j in range(4):
        latw4[HID * j : HID * j + HID, :] = dot(latw[...], spread(j)).astype(BF16)
        latw4_t[:, HID * j : HID * j + HID] = dot_nt(spread_t(j), latw[...]).astype(BF16)
    l_inw.wait()
    inw4[...] = jnp.zeros_like(inw4)
    for j in range(4):
        inw4[LAT * j : LAT * j + LAT, UNET * j : UNET * j + UNET] = inw[...]
    for j in range(4):
        part = inw4[:, UNET * j : UNET * j + UNET].astype(F32)
        inw4_t[UNET * j : UNET * j + UNET, :] = jnp.transpose(part).astype(BF16)
    l_outw.wait()
    for j in range(4):
        outw4[UNET * j : UNET * j + UNET, :] = dot(outw[...], spread(j)).astype(BF16)
        outw4_t[:, UNET * j : UNET * j + UNET] = dot_nt(spread_t(j), outw[...]).astype(BF16)

    chosen = time_ref[0]
    angle = ((jnp.full((8, 128), chosen, jnp.int32).astype(F32) + 1.0) / 1000.0 + 0.008) / 1.008 * (math.pi / 2.0)
    cosine = jnp.cos(angle)[0:1, :]
    sine = jnp.sin(angle)[0:1, :]
    l_table.wait()
    onehot = (lax.broadcasted_iota(jnp.int32, (16, table.shape[0]), 1) == chosen).astype(F32).astype(BF16)
    embed[...] = dot(onehot, table[...])[0:8]

    l_enc.wait()

    for d, copy in enumerate(feat_copies):
        copy.wait()
    for d, offsets in enumerate(AROUND):
        dt, ds = offsets
        valid = jnp.bool_(True)
        if dt:
            valid = (t < TILES - 1) if dt < 0 else (t > 0)
        if ds:
            beside = (s < STEPS - 1) if ds < 0 else (s > 0)
            valid = jnp.logical_and(valid, beside) if dt else beside
        if dt == 0:
            side = 0 if ds < 0 else 1
            taken = jnp.where(valid, edge_in[side].astype(F32), 0.0)
            first = 24 if ds < 0 else 6
            for i, part in enumerate(lane_tiles(taken)):
                for col in (0, 1):
                    grid[i, pl.ds(64 + first + col, 8, stride=32), :] = part[8 * col : 8 * col + 8]
        else:
            slot = d if d < 3 else d - 2
            for r in range(2):
                taken = jnp.where(valid, rows_in[slot, r].astype(F32), 0.0)
                row = (10 + r if dt < 0 else r) * 32
                for i, part in enumerate(lane_tiles(taken)):
                    if ds == 0:
                        grid[i, row + 8 : row + 24, :] = part
                    elif ds < 0:
                        grid[i, row + 24 : row + 32, :] = part[0:8]
                    else:
                        grid[i, row : row + 8, :] = part[8:16]

    def put_blocks(even, odd, index, value):
        even[index] = value.astype(BF16)
        odd[index] = value[8:].astype(BF16)

    for j in range(4):
        value = jnp.concatenate([grid[i, pl.ds(j, 96, stride=4), :] for i in range(2)], axis=1)
        put_blocks(blocks_even, blocks_odd, 1 + j, value)
        if j == 0:
            put_blocks(blocks_even, blocks_odd, 5, pltpu.roll(value, 95, 0))
        if j == 3:
            put_blocks(blocks_even, blocks_odd, 0, pltpu.roll(value, 1, 0))
    pieces = []
    for a in range(3):
        for b in range(3):
            if a == 1:
                window = blocks_odd[b : b + 4, 0:80, :]
            else:
                window = blocks_even[b : b + 4, 8 * a : 8 * a + 80, :]
            pieces.append(window.reshape(320, FEAT))
    pre = dot(jnp.concatenate(pieces, axis=1), enc[...].reshape(9 * FEAT, HID))
    pre_hidden[...] = pre
    hidden = (pre * sigmoid(pre)).astype(BF16)
    hidden = jnp.concatenate([hidden[80 * j : 80 * j + 80] for j in range(4)], axis=1)
    lat_tile[...] = dot(hidden, latw4[...])
    lat_pack[...] = jnp.zeros_like(lat_pack)
    for q in range(4):
        lat_pack[pl.ds(q, 10, stride=4), :] = lat_tile[pl.ds(2 + q, 10, stride=8), :]
    lat_send[...] = lat_pack[...].astype(BF16)

    def lat_copy(k):
        return remote(lat_send, lat_recv.at[k - 1], lat_ss.at[k - 1], lat_rs.at[k - 1], t, (s + k) % STEPS)

    def lat_start(k, _):
        lat_copy(k).start()
        return 0

    lax.fori_loop(1, STEPS, lat_start, 0)

    l_midw.wait()

    def flip_mid(k, _):
        mid_t[k] = jnp.transpose(midw[k])
        return 0

    lax.fori_loop(0, 9, flip_mid, 0)

    def flip_enc(k, _):
        enc_t[k] = jnp.transpose(enc[k])
        return 0

    lax.fori_loop(0, 9, flip_enc, 0)

    for side in (0, 1):
        noise_copies[side].wait()
    noise_rows[576:640, :] = noise_edge_in[0].astype(F32)
    noise_rows[0:64, :] = noise_edge_in[1].astype(F32)

    lat_flat[pl.ds(pl.multiple_of(s * 48, 16), 48), :] = lat_pack[...].astype(BF16).astype(F32)

    def lat_take(k, _):
        lat_copy(k).wait()
        source = (s - k + STEPS) % STEPS
        lat_flat[pl.ds(pl.multiple_of(source * 48, 16), 48), :] = lat_recv[k - 1].astype(F32)
        return 0

    lax.fori_loop(1, STEPS, lat_take, 0)

    def input_rows(r, _):
        latent = jnp.concatenate([lat_flat[pl.ds(r * 4 + q, 16, stride=48), :] for q in range(4)], axis=0)
        noisy = (cosine * latent + sine * noise_rows[pl.ds(pl.multiple_of(r * 64, 64), 64), :]).astype(BF16)
        shown = jnp.logical_and(jnp.logical_or(r > 0, t > 0), jnp.logical_or(r < 9, t < TILES - 1))
        gate = jnp.where(shown, 1.0, 0.0)
        for j in range(4):
            pre = dot(noisy, inw4[:, UNET * j : UNET * j + UNET]) + embed[0:1, :]
            sigma = sigmoid(pre)
            inner = pre * sigma * gate
            inner_slope[r, 64 * j : 64 * j + 64, :] = slope_of(pre, sigma)
            inner_ext[r, 64 + 64 * j : 128 + 64 * j, :] = inner.astype(BF16)
            if j == 0:
                inner_ext[r, 320:384, :] = shift_up(inner).astype(BF16)
            if j == 3:
                inner_ext[r, 0:64, :] = shift_down(inner).astype(BF16)
        for b in range(3):
            flipped = jnp.transpose(inner_ext[r, 64 * b : 64 * b + 256, :])
            inner_t[UNET * b : UNET * b + UNET, pl.ds(pl.multiple_of(r * 256, 256), 256)] = flipped
        return 0

    lax.fori_loop(0, 10, input_rows, 0)

    def by_class(value):
        rows = value.shape[0] // 256
        return jnp.concatenate(
            [
                jnp.concatenate([value[256 * r + 64 * j : 256 * r + 64 * j + 64] for j in range(4)], axis=1)
                for r in range(rows)
            ],
            axis=0,
        )

    def by_position(value):
        rows = value.shape[0] // 64
        return jnp.concatenate(
            [value[64 * r : 64 * r + 64, UNET * j : UNET * j + UNET] for r in range(rows) for j in range(4)], axis=0
        )

    def forward_rows(i, _):
        r = 2 * i
        windows = [
            inner_ext[pl.ds(r + a, 2), 64 * b : 64 * b + 256, :].reshape(512, UNET)
            for a in range(3)
            for b in range(3)
        ]
        pre = dot(jnp.concatenate(windows, axis=1), midw[...].reshape(9 * UNET, UNET))
        sigma = sigmoid(pre)
        mixed = (windows[4].astype(F32) + pre * sigma).astype(BF16)
        prediction = dot(by_class(mixed), outw4[...])
        own_noise = noise_rows[pl.ds(pl.multiple_of(64 + r * 64, 64), 128), :]
        error = ((prediction - own_noise) * (1.0 / math.sqrt(STEPS))).astype(BF16)
        pulled = by_position(dot(error, outw4_t[...]))
        back_mixed[pl.ds(pl.multiple_of(r * 256, 256), 512), :] = pulled
        back = pulled * slope_of(pre, sigma)
        for row in range(2):
            own = back[256 * row : 256 * row + 256]
            back_ext[r + 1 + row, 64:320, :] = own.astype(BF16)
            back_ext[r + 1 + row, 320:384, :] = shift_up(own[0:64]).astype(BF16)
            back_ext[r + 1 + row, 0:64, :] = shift_down(own[192:256]).astype(BF16)
        return 0

    lax.fori_loop(0, 4, forward_rows, 0)

    halo_copies = []
    for side, offset in ((0, -1), (1, 1)):
        tile, step = near((offset, 0))
        src, dst = (1, 9) if side == 0 else (8, 0)
        copy = remote(back_ext.at[src], back_ext.at[dst], halo_ss.at[side], halo_rs.at[side], tile, step)
        copy.start()
        halo_copies.append(copy)

    def s1_copy(a):
        return remote(s1_send.at[a], s1_recv.at[a], s1_ss.at[a], s1_rs.at[a], t, s + 1 - 2 * core)

    def s1_start(a):
        def pack(n, _):
            first = (n // 3) * UNET + n % 3 + 3 * (1 - core)
            block = jnp.concatenate([grad[a * 3 + i, pl.ds(first, 64, stride=6), :] for i in range(3)], axis=1)
            s1_send[a, pl.ds(pl.multiple_of(n * 64, 64), 64), :] = block.astype(BF16)
            return 0

        lax.fori_loop(0, 9, pack, 0)
        s1_copy(a).start()

    def axis_peer(a, k):
        if a == 0:
            there = (z + k) % 4
            return there, t, there * 4 + s % 4
        if a == 1:
            there = (x + k) % 4
            return there, y_hi * 4 + there, s
        there = (y + k) % 4
        return there, (there // 2) * 4 + x, z * 4 + (there % 2) * 2 + core

    def plane_rows(a, n, there):
        base = n * 64
        parts = []
        for i in range(3):
            if a == 0:
                half = [sum1[a * 3 + i, pl.ds(base + 2 * there + low, 8, stride=8), :] for low in (0, 1)]
                parts.append(jnp.concatenate(half, axis=0))
            elif a == 1:
                half = [
                    sum1[a * 3 + i, pl.ds(pl.multiple_of(base + high * 32 + there * 8, 8), 8), :] for high in (0, 1)
                ]
                parts.append(jnp.concatenate(half, axis=0))
            else:
                first = base + (there // 2) * 32 + there % 2
                parts.append(sum1[a * 3 + i, pl.ds(first, 16, stride=2), :])
        return jnp.concatenate(parts, axis=1)

    def s2_copy(a, k):
        _, tile, step = axis_peer(a, k)
        index = a * 3 + k - 1
        return remote(s2_send.at[index], s2_recv.at[index], s2_ss.at[index], s2_rs.at[index], tile, step)

    def s2_start(a):
        s1_copy(a).wait()

        def add(n, _):
            first = (n // 3) * UNET + n % 3 + 3 * core
            rows = pl.ds(pl.multiple_of(n * 64, 64), 64)
            got = s1_recv[a, rows, :].astype(F32)
            for i in range(3):
                own = grad[a * 3 + i, pl.ds(first, 64, stride=6), :]
                sum1[a * 3 + i, rows, :] = own + got[:, 128 * i : 128 * i + 128]
            return 0

        lax.fori_loop(0, 9, add, 0)
        for k in range(1, 4):
            there = axis_peer(a, k)[0]

            def pack(n, _, there=there, k=k):
                rows = pl.ds(pl.multiple_of(n * 16, 16), 16)
                s2_send[a * 3 + k - 1, rows, :] = plane_rows(a, n, there).astype(BF16)
                return 0

            lax.fori_loop(0, 9, pack, 0)
            s2_copy(a, k).start()

    def plane_peer(a, k):
        if a == 0:
            mine = y_lo * 8 + t
            there = (mine + k) % 16
            return mine, there, there % 8, z * 4 + (there // 8) * 2 + core
        if a == 1:
            mine = y_hi * 8 + s // 2
            there = (mine + k) % 16
            return mine, there, (there // 8) * 4 + x, (there % 8) * 2 + core
        mine = x * 4 + z
        there = (mine + k) % 16
        return mine, there, y_hi * 4 + there // 4, (there % 4) * 4 + s % 4

    def s3_copy(a, k):
        _, _, tile, step = plane_peer(a, k)
        index = a * 15 + k - 1
        return remote(s3_send.at[index], s3_recv.at[index], s3_ss.at[index], s3_rs.at[index], tile, step)

    def s3_start(a):
        for k in range(1, 4):
            s2_copy(a, k).wait()
        mine = axis_peer(a, 0)[0]

        def add(n, _):
            rows = pl.ds(pl.multiple_of(n * 16, 16), 16)
            total = plane_rows(a, n, mine)
            for k in range(3):
                total = total + s2_recv[a * 3 + k, rows, :].astype(F32)
            for i, part in enumerate(lane_tiles(total)):
                sum2[a * 3 + i, rows, :] = part
            return 0

        lax.fori_loop(0, 9, add, 0)

        def send(k, _):
            there = plane_peer(a, k)[1]
            block = jnp.concatenate([sum2[a * 3 + i, pl.ds(there, 16, stride=16), :] for i in range(3)], axis=1)
            s3_send[a * 15 + k - 1] = block.astype(BF16)
            s3_copy(a, k).start()
            return 0

        lax.fori_loop(1, 16, send, 0)

    def finish(a):
        mine = plane_peer(a, 0)[0]
        own = jnp.concatenate([sum2[a * 3 + i, pl.ds(mine, 16, stride=16), :] for i in range(3)], axis=1)

        def add(k, total):
            s3_copy(a, k).wait()
            return total + s3_recv[a * 15 + k - 1].astype(F32)

        total = lax.fori_loop(1, 16, add, own) * (1.0 / math.sqrt(64 * 256))
        for b in range(3):
            for i in range(3):
                mgrad_ref[i, 3 * a + b : 3 * a + b + 1, :] = total[3 * b + i : 3 * b + i + 1]

    sum2[...] = jnp.zeros_like(sum2)
    for a in range(3):
        result = dot(inner_t[:, 256 * a : 256 * a + 2048], back_ext[1:9, 64:320, :].reshape(2048, UNET))
        for i, part in enumerate(lane_tiles(result)):
            grad[a * 3 + i] = part
        s1_start(a)
        if a:
            s2_start(a - 1)

    for side in (0, 1):
        halo_copies[side].wait()

    @pl.when(t == 0)
    def _():
        back_ext[0] = jnp.zeros_like(back_ext[0])

    @pl.when(t == TILES - 1)
    def _():
        back_ext[9] = jnp.zeros_like(back_ext[9])

    def backward_rows(i, _):
        r = 2 * i
        windows = [
            back_ext[pl.ds(r + 2 - a, 2), 64 * (2 - b) : 64 * (2 - b) + 256, :].reshape(512, UNET)
            for a in range(3)
            for b in range(3)
        ]
        through = dot(jnp.concatenate(windows, axis=1), mid_t[...].reshape(9 * UNET, UNET))
        through = through + back_mixed[pl.ds(pl.multiple_of(r * 256, 256), 512), :]
        back = (through * inner_slope[pl.ds(r + 1, 2)].reshape(512, UNET)).astype(BF16)
        back_part[pl.ds(pl.multiple_of(r * 64, 64), 128), :] = cosine * dot(by_class(back), inw4_t[...])
        return 0

    lax.fori_loop(0, 2, backward_rows, 0)
    s2_start(2)
    lax.fori_loop(2, 4, backward_rows, 0)

    def part_copy(k):
        return remote(
            part_send.at[k - 1], part_recv.at[k - 1], part_ss.at[k - 1], part_rs.at[k - 1], t, (s + k) % STEPS
        )

    def part_start(k, _):
        part_send[k - 1] = back_part[pl.ds((s + k) % STEPS, 32, stride=16), :].astype(BF16)
        part_copy(k).start()
        return 0

    lax.fori_loop(1, STEPS, part_start, 0)

    for a in range(3):
        s3_start(a)

    def part_add(k, total):
        part_copy(k).wait()
        return total + part_recv[k - 1].astype(F32)

    latent_round = lax.fori_loop(1, STEPS, part_add, back_part[pl.ds(s, 32, stride=16), :])
    round_send[...] = latent_round.astype(BF16)
    round_copies = []
    for d, offsets in enumerate(AROUND):
        tile, step = near(offsets)
        copy = remote(round_send, round_recv.at[d], round_ss.at[d], round_rs.at[d], tile, step)
        copy.start()
        round_copies.append(copy)

    round_grid[...] = jnp.zeros_like(round_grid)
    round_pack[...] = round_send[...].astype(F32)
    for q in range(4):
        round_grid[pl.ds(10 + q, 8, stride=8), :] = round_pack[pl.ds(q, 8, stride=4), :]
    for d, (dt, ds) in enumerate(AROUND):
        round_copies[d].wait()
        valid = jnp.bool_(True)
        if dt:
            valid = (t < TILES - 1) if dt < 0 else (t > 0)
        if ds:
            beside = (s < STEPS - 1) if ds < 0 else (s > 0)
            valid = jnp.logical_and(valid, beside) if dt else beside
        round_pack[...] = jnp.where(valid, round_recv[d].astype(F32), 0.0)
        if dt == 0:
            q, place = (0, 6) if ds < 0 else (3, 1)
            round_grid[pl.ds(8 + place, 8, stride=8), :] = round_pack[pl.ds(q, 8, stride=4), :]
        else:
            source, row = (0, 72) if dt < 0 else (28, 0)
            if ds == 0:
                round_grid[row + 2 : row + 6, :] = round_pack[source : source + 4, :]
            else:
                q, place = (0, 6) if ds < 0 else (3, 1)
                round_grid[row + place : row + place + 1, :] = round_pack[source + q : source + q + 1, :]
    pulled = dot(round_grid[...].astype(BF16), latw4_t[...])
    for j in range(4):
        pre = pre_hidden[80 * j : 80 * j + 80, :]
        value = pulled[:, HID * j : HID * j + HID] * slope_of(pre, sigmoid(pre))
        put_blocks(hidden_even, hidden_odd, 1 + j, value)
        if j == 0:
            put_blocks(hidden_even, hidden_odd, 5, pltpu.roll(value, 79, 0))
        if j == 3:
            put_blocks(hidden_even, hidden_odd, 0, pltpu.roll(value, 1, 0))
    pieces = []
    for a in range(3):
        for b in range(3):
            if a == 1:
                window = hidden_odd[2 - b : 6 - b, 0:64, :]
            else:
                window = hidden_even[2 - b : 6 - b, 8 * (2 - a) : 8 * (2 - a) + 64, :]
            pieces.append(window.reshape(256, HID))
    result = dot(jnp.concatenate(pieces, axis=1), enc_t[...].reshape(9 * HID, FEAT))
    for j in range(4):
        for i, part in enumerate(lane_tiles(result[64 * j : 64 * j + 64])):
            out_grid[i, pl.ds(j, 64, stride=4), :] = part
    for r in range(8):
        for i in range(2):
            fgrad_ref[r, :, 128 * i : 128 * i + 128] = out_grid[i, r * 32 + 8 : r * 32 + 24, :]

    for a in range(3):
        finish(a)


def per_device(
    features,
    encoder_weight,
    latent_weight,
    timesteps,
    noise_field,
    time_table,
    input_weight,
    middle_weight,
    output_weight,
):
    hbm = pl.BlockSpec(memory_space=pl.ANY)
    vmem = pl.BlockSpec(memory_space=pltpu.VMEM)
    dma = pltpu.SemaphoreType.DMA
    operands = (
        features,
        encoder_weight,
        latent_weight,
        noise_field,
        time_table,
        input_weight,
        middle_weight,
        output_weight,
    )
    scratch = [
        pltpu.VMEM((8, 16, FEAT), BF16),
        pltpu.VMEM((9, FEAT, HID), BF16),
        pltpu.VMEM((HID, LAT), BF16),
        pltpu.VMEM(noise_field.shape, BF16),
        pltpu.VMEM(time_table.shape, BF16),
        pltpu.VMEM((LAT, UNET), BF16),
        pltpu.VMEM((9, UNET, UNET), BF16),
        pltpu.VMEM((UNET, LAT), BF16),
        dma((8,)),
        pltpu.VMEM((9, HID, FEAT), BF16),
        pltpu.VMEM((9, UNET, UNET), BF16),
        pltpu.VMEM((4 * HID, 128), BF16),
        pltpu.VMEM((128, 4 * HID), BF16),
        pltpu.VMEM((128, 4 * UNET), BF16),
        pltpu.VMEM((4 * UNET, 128), BF16),
        pltpu.VMEM((4 * UNET, 128), BF16),
        pltpu.VMEM((128, 4 * UNET), BF16),
        pltpu.VMEM((8, UNET), F32),
        pltpu.VMEM((2, 16, FEAT), BF16),
        pltpu.VMEM((2, 16, FEAT), BF16),
        pltpu.VMEM((6, 2, 16, FEAT), BF16),
        pltpu.VMEM((2, 12 * 32, 128), F32),
        pltpu.VMEM((6, 96, FEAT), BF16),
        pltpu.VMEM((6, 88, FEAT), BF16),
        pltpu.VMEM((320, HID), F32),
        pltpu.VMEM((80, 128), F32),
        pltpu.VMEM((48, 128), F32),
        pltpu.VMEM((48, 128), BF16),
        pltpu.VMEM((15, 48, 128), BF16),
        pltpu.VMEM((16 * 48, 128), F32),
        pltpu.VMEM((640, 128), F32),
        pltpu.VMEM((2, 64, 128), BF16),
        pltpu.VMEM((2, 64, 128), BF16),
        pltpu.VMEM((10, 384, UNET), BF16),
        pltpu.VMEM((10, 256, UNET), F32),
        pltpu.VMEM((3 * UNET, 2560), BF16),
        pltpu.VMEM((2048, UNET), F32),
        pltpu.VMEM((10, 384, UNET), BF16),
        pltpu.VMEM((512, 128), F32),
        pltpu.VMEM((15, 32, 128), BF16),
        pltpu.VMEM((15, 32, 128), BF16),
        pltpu.VMEM((32, 128), F32),
        pltpu.VMEM((32, 128), BF16),
        pltpu.VMEM((8, 32, 128), BF16),
        pltpu.VMEM((80, 128), F32),
        pltpu.VMEM((6, 80, HID), BF16),
        pltpu.VMEM((6, 72, HID), BF16),
        pltpu.VMEM((2, 256, 128), F32),
        pltpu.VMEM((9, 3 * UNET, 128), F32),
        pltpu.VMEM((3, 576, UNET), BF16),
        pltpu.VMEM((3, 576, UNET), BF16),
        pltpu.VMEM((9, 576, 128), F32),
        pltpu.VMEM((9, 144, UNET), BF16),
        pltpu.VMEM((9, 144, UNET), BF16),
        pltpu.VMEM((9, 256, 128), F32),
        pltpu.VMEM((45, 16, UNET), BF16),
        pltpu.VMEM((45, 16, UNET), BF16),
        dma((8,)),
        dma((8,)),
        dma((2,)),
        dma((2,)),
        dma((15,)),
        dma((15,)),
        dma((2,)),
        dma((2,)),
        dma((15,)),
        dma((15,)),
        dma((8,)),
        dma((8,)),
        dma((3,)),
        dma((3,)),
        dma((9,)),
        dma((9,)),
        dma((45,)),
        dma((45,)),
    ]
    return pl.pallas_call(
        kernel,
        out_shape=(
            jax.ShapeDtypeStruct((8, 16, FEAT), F32),
            jax.ShapeDtypeStruct((3, 9, UNET), F32),
        ),
        in_specs=[pl.BlockSpec(memory_space=pltpu.SMEM)] + [hbm] * 8,
        out_specs=(vmem, vmem),
        scratch_shapes=scratch,
        compiler_params=pltpu.CompilerParams(
            collective_id=0, has_side_effects=True, vmem_limit_bytes=60 * 1024 * 1024
        ),
        cost_estimate=pl.CostEstimate(flops=18_000_000_000, bytes_accessed=8_000_000, transcendentals=3_000_000),
    )(timesteps, *operands)


def solution(mesh):
    in_specs = (
        P("tile", "step", None),
        P(),
        P(),
        P("step"),
        P("step", "tile", None),
        P(),
        P(),
        P(),
        P(),
    )
    out_specs = (P("tile", "step", None), P(("tile", "step"), None, None))
    return jax.shard_map(per_device, mesh=mesh, in_specs=in_specs, out_specs=out_specs, check_vma=False)
```

```python
import math

import jax
import jax.numpy as jnp
from jax import lax
from jax.experimental import pallas as pl
from jax.experimental.pallas import tpu as pltpu
from jax.sharding import PartitionSpec as P

F32 = jnp.float32
BF16 = jnp.bfloat16
MESH = pl.DeviceIdType.MESH

FEAT, HID, LAT, UNET = 256, 512, 32, 384
TILES, STEPS = 8, 16
AROUND = ((-1, -1), (-1, 0), (-1, 1), (0, -1), (0, 1), (1, -1), (1, 0), (1, 1))


def sigmoid(values):
    return 0.5 * jnp.tanh(0.5 * values) + 0.5


def slope_of(values, sigma):
    return sigma * (1.0 + values * (1.0 - sigma))


def dot(left, right):
    return jnp.dot(left, right, preferred_element_type=F32)


def dot_nt(left, right):
    return lax.dot_general(left, right, (((1,), (1,)), ((), ())), preferred_element_type=F32)


def lane_tiles(value):
    return [value[:, 128 * i : 128 * i + 128] for i in range(value.shape[1] // 128)]


def shift_down(block):
    last = pltpu.roll(block[48:64], 1, 0)
    rows = lax.broadcasted_iota(jnp.int32, last.shape, 0)
    return jnp.concatenate([jnp.where(rows == 0, 0.0, last), block[0:48]], axis=0)


def shift_up(block):
    first = pltpu.roll(block[0:16], 15, 0)
    rows = lax.broadcasted_iota(jnp.int32, first.shape, 0)
    return jnp.concatenate([block[16:64], jnp.where(rows == 15, 0.0, first)], axis=0)


def kernel(
    time_ref,
    feat_hbm,
    enc_hbm,
    latw_hbm,
    noise_hbm,
    table_hbm,
    inw_hbm,
    midw_hbm,
    outw_hbm,
    fgrad_ref,
    mgrad_ref,
    feat,
    enc,
    latw,
    noise,
    table,
    inw,
    midw,
    outw,
    in_sem,
    latw4_t,
    inw4,
    outw4_t,
    embed,
    edge,
    edge_in,
    rows_in,
    grid,
    blocks_even,
    blocks_odd,
    pre_hidden,
    lat_tile,
    lat_pack,
    lat_send,
    lat_recv,
    lat_flat,
    noise_rows,
    noise_edge,
    noise_edge_in,
    inner_ext,
    inner_slope,
    inner_t,
    inner_tm,
    pre_middle,
    back_mixed,
    back_ext,
    back_part,
    part_send,
    part_recv,
    round_pack,
    round_send,
    round_recv,
    round_grid,
    hidden_even,
    hidden_odd,
    out_grid,
    grad,
    s1_send,
    s1_recv,
    sum1,
    s2_send,
    s2_recv,
    sum2,
    s3_send,
    s3_recv,
    feat_ss,
    feat_rs,
    noise_ss,
    noise_rs,
    lat_ss,
    lat_rs,
    halo_ss,
    halo_rs,
    part_ss,
    part_rs,
    round_ss,
    round_rs,
    s1_ss,
    s1_rs,
    s2_ss,
    s2_rs,
    s3_ss,
    s3_rs,
):
    t = lax.axis_index("tile")
    s = lax.axis_index("step")
    y_hi, x = t // 4, t % 4
    z, y_lo, core = s // 4, (s // 2) % 2, s % 2
    y = y_hi * 2 + y_lo

    def remote(src, dst, ss, rs, tile, step):
        return pltpu.make_async_remote_copy(
            src_ref=src, dst_ref=dst, send_sem=ss, recv_sem=rs, device_id=(tile, step), device_id_type=MESH
        )

    def near(offsets):
        return (t + offsets[0] + TILES) % TILES, (s + offsets[1] + STEPS) % STEPS

    loads = [
        pltpu.make_async_copy(src, dst, in_sem.at[i])
        for i, (src, dst) in enumerate(
            (
                (feat_hbm, feat),
                (noise_hbm, noise),
                (enc_hbm, enc),
                (latw_hbm, latw),
                (inw_hbm, inw),
                (outw_hbm, outw),
                (table_hbm, table),
                (midw_hbm, midw),
            )
        )
    ]
    for load in loads:
        load.start()
    l_feat, l_noise, l_enc, l_latw, l_inw, l_outw, l_table, l_midw = loads

    barrier = pltpu.get_barrier_semaphore()

    def greet_step(k, _):
        pl.semaphore_signal(barrier, inc=1, device_id=(t, (s + k) % STEPS), device_id_type=MESH)
        return 0

    def greet_tile(k, _):
        pl.semaphore_signal(barrier, inc=1, device_id=((t + k) % TILES, s), device_id_type=MESH)
        return 0

    lax.fori_loop(1, STEPS, greet_step, 0)
    lax.fori_loop(1, TILES, greet_tile, 0)
    for offsets in AROUND:
        if offsets[0] and offsets[1]:
            pl.semaphore_signal(barrier, inc=1, device_id=near(offsets), device_id_type=MESH)

    l_feat.wait()
    grid[...] = jnp.zeros_like(grid)
    for r in range(8):
        for i, part in enumerate(lane_tiles(feat[r].astype(F32))):
            grid[i, (r + 2) * 32 + 8 : (r + 2) * 32 + 24, :] = part
    for side, first in ((0, 8), (1, 22)):
        for i in range(2):
            pair = [grid[i, pl.ds(64 + first + col, 8, stride=32), :] for col in (0, 1)]
            edge[side, :, 128 * i : 128 * i + 128] = jnp.concatenate(pair, axis=0).astype(BF16)

    pl.semaphore_wait(barrier, STEPS - 1 + TILES - 1 + 4)

    feat_copies = []
    for d, offsets in enumerate(AROUND):
        tile, step = near(offsets)
        if offsets[0] == 0:
            side = 0 if offsets[1] < 0 else 1
            src, dst = edge.at[side], edge_in.at[side]
        else:
            slot = d if d < 3 else d - 2
            src, dst = feat.at[pl.ds(0 if offsets[0] < 0 else 6, 2)], rows_in.at[slot]
        copy = remote(src, dst, feat_ss.at[d], feat_rs.at[d], tile, step)
        copy.start()
        feat_copies.append(copy)

    l_noise.wait()
    for q in range(64):
        piece = noise[0, :, 128 * q : 128 * q + 128].astype(F32)
        noise_rows[pl.ds(64 + (q % 4) * 16 + q // 4, 8, stride=64), :] = piece
    noise_edge[0] = noise_rows[64:128, :].astype(BF16)
    noise_edge[1] = noise_rows[512:576, :].astype(BF16)
    noise_copies = []
    for side, offset in ((0, -1), (1, 1)):
        tile, step = near((offset, 0))
        copy = remote(noise_edge.at[side], noise_edge_in.at[side], noise_ss.at[side], noise_rs.at[side], tile, step)
        copy.start()
        noise_copies.append(copy)

    for load, weight, wide in ((l_latw, latw, latw4_t), (l_inw, inw, inw4), (l_outw, outw, outw4_t)):
        load.wait()
        columns = weight.shape[1]
        wide[...] = jnp.zeros_like(wide)
        for j in range(4):
            wide[LAT * j : LAT * j + LAT, columns * j : columns * j + columns] = weight[...]

    chosen = time_ref[0]
    angle = ((jnp.full((8, 128), chosen, jnp.int32).astype(F32) + 1.0) / 1000.0 + 0.008) / 1.008 * (math.pi / 2.0)
    cosine = jnp.cos(angle)[0:1, :]
    sine = jnp.sin(angle)[0:1, :]
    l_table.wait()
    onehot = (lax.broadcasted_iota(jnp.int32, (16, table.shape[0]), 1) == chosen).astype(F32).astype(BF16)
    embed[...] = dot(onehot, table[...])[0:8]

    l_enc.wait()

    for d, copy in enumerate(feat_copies):
        copy.wait()
    for d, offsets in enumerate(AROUND):
        dt, ds = offsets
        valid = jnp.bool_(True)
        if dt:
            valid = (t < TILES - 1) if dt < 0 else (t > 0)
        if ds:
            beside = (s < STEPS - 1) if ds < 0 else (s > 0)
            valid = jnp.logical_and(valid, beside) if dt else beside
        if dt == 0:
            side = 0 if ds < 0 else 1
            taken = jnp.where(valid, edge_in[side].astype(F32), 0.0)
            first = 24 if ds < 0 else 6
            for i, part in enumerate(lane_tiles(taken)):
                for col in (0, 1):
                    grid[i, pl.ds(64 + first + col, 8, stride=32), :] = part[8 * col : 8 * col + 8]
        else:
            slot = d if d < 3 else d - 2
            for r in range(2):
                taken = jnp.where(valid, rows_in[slot, r].astype(F32), 0.0)
                row = (10 + r if dt < 0 else r) * 32
                for i, part in enumerate(lane_tiles(taken)):
                    if ds == 0:
                        grid[i, row + 8 : row + 24, :] = part
                    elif ds < 0:
                        grid[i, row + 24 : row + 32, :] = part[0:8]
                    else:
                        grid[i, row : row + 8, :] = part[8:16]

    def put_blocks(even, odd, index, value):
        even[index] = value.astype(BF16)
        odd[index] = value[8:].astype(BF16)

    for j in range(4):
        value = jnp.concatenate([grid[i, pl.ds(j, 96, stride=4), :] for i in range(2)], axis=1)
        put_blocks(blocks_even, blocks_odd, 1 + j, value)
        if j == 0:
            put_blocks(blocks_even, blocks_odd, 5, pltpu.roll(value, 95, 0))
        if j == 3:
            put_blocks(blocks_even, blocks_odd, 0, pltpu.roll(value, 1, 0))
    pieces = []
    for a in range(3):
        for b in range(3):
            if a == 1:
                window = blocks_odd[b : b + 4, 0:80, :]
            else:
                window = blocks_even[b : b + 4, 8 * a : 8 * a + 80, :]
            pieces.append(window.reshape(320, FEAT))
    pre = dot(jnp.concatenate(pieces, axis=1), enc[...].reshape(9 * FEAT, HID))
    pre_hidden[...] = pre
    hidden = (pre * sigmoid(pre)).astype(BF16)
    hidden = jnp.concatenate([hidden[80 * j : 80 * j + 80] for j in range(4)], axis=1)
    lat_tile[...] = dot_nt(hidden, latw4_t[...])
    lat_pack[...] = jnp.zeros_like(lat_pack)
    for q in range(4):
        lat_pack[pl.ds(q, 10, stride=4), :] = lat_tile[pl.ds(2 + q, 10, stride=8), :]
    lat_send[...] = lat_pack[...].astype(BF16)

    def lat_copy(k):
        return remote(lat_send, lat_recv.at[k - 1], lat_ss.at[k - 1], lat_rs.at[k - 1], t, (s + k) % STEPS)

    def lat_start(k, _):
        lat_copy(k).start()
        return 0

    lax.fori_loop(1, STEPS, lat_start, 0)

    l_midw.wait()
    for side in (0, 1):
        noise_copies[side].wait()
    noise_rows[576:640, :] = noise_edge_in[0].astype(F32)
    noise_rows[0:64, :] = noise_edge_in[1].astype(F32)

    lat_flat[pl.ds(pl.multiple_of(s * 48, 16), 48), :] = lat_pack[...].astype(BF16).astype(F32)

    def lat_take(k, _):
        lat_copy(k).wait()
        source = (s - k + STEPS) % STEPS
        lat_flat[pl.ds(pl.multiple_of(source * 48, 16), 48), :] = lat_recv[k - 1].astype(F32)
        return 0

    lax.fori_loop(1, STEPS, lat_take, 0)

    def input_rows(pair):
        first = 2 * pair
        latent = [lat_flat[pl.ds((first + r) * 4 + q, 16, stride=48), :] for r in range(2) for q in range(4)]
        noisy = cosine * jnp.concatenate(latent, axis=0) + sine * noise_rows[64 * first : 64 * first + 128, :]
        noisy = noisy.astype(BF16)
        for j in range(4):
            pre = dot(noisy, inw4[:, UNET * j : UNET * j + UNET]) + embed[0:1, :]
            sigma = sigmoid(pre)
            inner = pre * sigma
            slope = slope_of(pre, sigma)
            for r in range(2):
                row = first + r
                own = inner[64 * r : 64 * r + 64]
                if row == 0:
                    own = own * jnp.where(t > 0, 1.0, 0.0)
                if row == 9:
                    own = own * jnp.where(t < TILES - 1, 1.0, 0.0)
                inner_ext[row, 64 + 64 * j : 128 + 64 * j, :] = own.astype(BF16)
                if j == 0:
                    inner_ext[row, 320:384, :] = shift_up(own).astype(BF16)
                if j == 3:
                    inner_ext[row, 0:64, :] = shift_down(own).astype(BF16)
                if 0 < row < 9:
                    inner_slope[row - 1, 64 * j : 64 * j + 64, :] = slope[64 * r : 64 * r + 64]

    def flip_rows(pair):
        for row in (2 * pair, 2 * pair + 1):
            flipped = jnp.transpose(inner_ext[row])
            inner_t[row] = flipped
            inner_tm[row] = flipped[:, 64:320]

    def by_class(value):
        rows = value.shape[0] // 256
        return jnp.concatenate(
            [
                jnp.concatenate([value[256 * r + 64 * j : 256 * r + 64 * j + 64] for j in range(4)], axis=1)
                for r in range(rows)
            ],
            axis=0,
        )

    def by_position(value):
        rows = value.shape[0] // 64
        return jnp.concatenate(
            [value[64 * r : 64 * r + 64, UNET * j : UNET * j + UNET] for r in range(rows) for j in range(4)], axis=0
        )

    def forward_conv(i):
        windows = [
            inner_ext[2 * i + a : 2 * i + a + 2, 64 * b : 64 * b + 256, :].reshape(512, UNET)
            for a in range(3)
            for b in range(3)
        ]
        pre_middle[i % 2] = dot(jnp.concatenate(windows, axis=1), midw[...].reshape(9 * UNET, UNET))

    def forward_after(i):
        r = 2 * i
        pre = pre_middle[i % 2]
        sigma = sigmoid(pre)
        own = inner_ext[r + 1 : r + 3, 64:320, :].reshape(512, UNET)
        mixed = (own.astype(F32) + pre * sigma).astype(BF16)
        prediction = dot_nt(by_class(mixed), outw4_t[...])
        own_noise = noise_rows[64 + r * 64 : 192 + r * 64, :]
        error = ((prediction - own_noise) * (1.0 / math.sqrt(STEPS))).astype(BF16)
        pulled = by_position(dot(error, outw4_t[...]))
        back_mixed[256 * r : 256 * r + 512, :] = pulled
        back = pulled * slope_of(pre, sigma)
        for row in range(2):
            own = back[256 * row : 256 * row + 256]
            back_ext[r + 1 + row, 64:320, :] = own.astype(BF16)
            back_ext[r + 1 + row, 320:384, :] = shift_up(own[0:64]).astype(BF16)
            back_ext[r + 1 + row, 0:64, :] = shift_down(own[192:256]).astype(BF16)

    input_rows(0)
    input_rows(1)
    for i in range(4):
        forward_conv(i)
        if i < 3:
            input_rows(i + 2)
        flip_rows(i)
        if i:
            forward_after(i - 1)
    flip_rows(4)
    forward_after(3)

    halo_copies = []
    for side, offset in ((0, -1), (1, 1)):
        tile, step = near((offset, 0))
        src, dst = (1, 9) if side == 0 else (8, 0)
        copy = remote(back_ext.at[src], back_ext.at[dst], halo_ss.at[side], halo_rs.at[side], tile, step)
        copy.start()
        halo_copies.append(copy)

    def s1_copy(a):
        return remote(s1_send.at[a], s1_recv.at[a], s1_ss.at[a], s1_rs.at[a], t, s + 1 - 2 * core)

    def s1_start(a):
        for n in range(9):
            first = (n // 3) * UNET + n % 3 + 3 * (1 - core)
            block = jnp.concatenate([grad[a * 3 + i, pl.ds(first, 64, stride=6), :] for i in range(3)], axis=1)
            s1_send[a, 64 * n : 64 * n + 64, :] = block.astype(BF16)
        s1_copy(a).start()

    def axis_peer(a, k):
        if a == 0:
            there = (z + k) % 4
            return there, t, there * 4 + s % 4
        if a == 1:
            there = (x + k) % 4
            return there, y_hi * 4 + there, s
        there = (y + k) % 4
        return there, (there // 2) * 4 + x, z * 4 + (there % 2) * 2 + core

    def plane_rows(a, n, there):
        base = n * 64
        parts = []
        for i in range(3):
            if a == 0:
                half = [sum1[a * 3 + i, pl.ds(base + 2 * there + low, 8, stride=8), :] for low in (0, 1)]
                parts.append(jnp.concatenate(half, axis=0))
            elif a == 1:
                half = [
                    sum1[a * 3 + i, pl.ds(base + high * 32 + pl.multiple_of(there * 8, 8), 8), :] for high in (0, 1)
                ]
                parts.append(jnp.concatenate(half, axis=0))
            else:
                first = base + (there // 2) * 32 + there % 2
                parts.append(sum1[a * 3 + i, pl.ds(first, 16, stride=2), :])
        return jnp.concatenate(parts, axis=1)

    def s2_copy(a, k):
        _, tile, step = axis_peer(a, k)
        index = a * 3 + k - 1
        return remote(s2_send.at[index], s2_recv.at[index], s2_ss.at[index], s2_rs.at[index], tile, step)

    def s2_start(a):
        s1_copy(a).wait()

        for n in range(9):
            first = (n // 3) * UNET + n % 3 + 3 * core
            got = s1_recv[a, 64 * n : 64 * n + 64, :].astype(F32)
            for i in range(3):
                own = grad[a * 3 + i, pl.ds(first, 64, stride=6), :]
                sum1[a * 3 + i, 64 * n : 64 * n + 64, :] = own + got[:, 128 * i : 128 * i + 128]
        for k in (2, 1, 3):
            there = axis_peer(a, k)[0]
            for n in range(9):
                s2_send[a * 3 + k - 1, 16 * n : 16 * n + 16, :] = plane_rows(a, n, there).astype(BF16)
            s2_copy(a, k).start()

    def plane_peer(a, k):
        if a == 0:
            mine = y_lo * 8 + t
            there = (mine + k) % 16
            return mine, there, there % 8, z * 4 + (there // 8) * 2 + core
        if a == 1:
            mine = y_hi * 8 + s // 2
            there = (mine + k) % 16
            return mine, there, (there // 8) * 4 + x, (there % 8) * 2 + core
        mine = x * 4 + z
        there = (mine + k) % 16
        return mine, there, y_hi * 4 + there // 4, (there % 4) * 4 + s % 4

    def s3_copy(a, k):
        _, _, tile, step = plane_peer(a, k)
        index = a * 15 + k - 1
        return remote(s3_send.at[index], s3_recv.at[index], s3_ss.at[index], s3_rs.at[index], tile, step)

    def s3_start(a):
        for k in range(1, 4):
            s2_copy(a, k).wait()
        mine = axis_peer(a, 0)[0]

        for n in range(9):
            total = plane_rows(a, n, mine)
            for k in range(3):
                total = total + s2_recv[a * 3 + k, 16 * n : 16 * n + 16, :].astype(F32)
            for i, part in enumerate(lane_tiles(total)):
                sum2[a * 3 + i, 16 * n : 16 * n + 16, :] = part

        def send(k, _):
            there = plane_peer(a, k)[1]
            block = jnp.concatenate([sum2[a * 3 + i, pl.ds(there, 16, stride=16), :] for i in range(3)], axis=1)
            s3_send[a * 15 + k - 1] = block.astype(BF16)
            s3_copy(a, k).start()
            return 0

        lax.fori_loop(1, 16, send, 0)

    def finish(a):
        mine = plane_peer(a, 0)[0]
        own = jnp.concatenate([sum2[a * 3 + i, pl.ds(mine, 16, stride=16), :] for i in range(3)], axis=1)

        def add(k, total):
            s3_copy(a, k).wait()
            return total + s3_recv[a * 15 + k - 1].astype(F32)

        total = lax.fori_loop(1, 16, add, own) * (1.0 / math.sqrt(64 * 256))
        for b in range(3):
            mgrad_ref[3 * a + b] = total[3 * b : 3 * b + 3]

    sum2[...] = jnp.zeros_like(sum2)
    for a in range(3):
        taps = [
            jnp.concatenate([inner_t[r + a, :, 0:256] for r in range(8)], axis=1),
            jnp.concatenate([inner_tm[r + a] for r in range(8)], axis=1),
            jnp.concatenate([inner_t[r + a, :, 128:384] for r in range(8)], axis=1),
        ]
        result = dot(jnp.concatenate(taps, axis=0), back_ext[1:9, 64:320, :].reshape(2048, UNET))
        for i, part in enumerate(lane_tiles(result)):
            grad[a * 3 + i] = part
        s1_start(a)
        if a:
            s2_start(a - 1)

    for side in (0, 1):
        halo_copies[side].wait()

    @pl.when(t == 0)
    def _():
        back_ext[0] = jnp.zeros_like(back_ext[0])

    @pl.when(t == TILES - 1)
    def _():
        back_ext[9] = jnp.zeros_like(back_ext[9])

    def backward_rows(i):
        r = 2 * i
        windows = [
            back_ext[r + 2 - a : r + 4 - a, 64 * (2 - b) : 64 * (2 - b) + 256, :].reshape(512, UNET)
            for a in range(3)
            for b in range(3)
        ]
        weights = jnp.concatenate([midw[k] for k in range(9)], axis=1)
        through = dot_nt(jnp.concatenate(windows, axis=1), weights) + back_mixed[256 * r : 256 * r + 512, :]
        back = (through * inner_slope[r : r + 2].reshape(512, UNET)).astype(BF16)
        back_part[64 * r : 64 * r + 128, :] = cosine * dot_nt(by_class(back), inw4[...])

    backward_rows(0)
    s2_start(2)
    backward_rows(1)
    backward_rows(2)
    s3_start(0)
    backward_rows(3)

    def part_copy(k):
        return remote(
            part_send.at[k - 1], part_recv.at[k - 1], part_ss.at[k - 1], part_rs.at[k - 1], t, (s + k) % STEPS
        )

    def part_start(k, _):
        part_send[k - 1] = back_part[pl.ds((s + k) % STEPS, 32, stride=16), :].astype(BF16)
        part_copy(k).start()
        return 0

    lax.fori_loop(1, STEPS, part_start, 0)

    s3_start(1)

    def part_add(k, total):
        part_copy(k).wait()
        return total + part_recv[k - 1].astype(F32)

    latent_round = lax.fori_loop(1, STEPS, part_add, back_part[pl.ds(s, 32, stride=16), :])
    round_send[...] = latent_round.astype(BF16)
    round_copies = []
    for d, offsets in enumerate(AROUND):
        tile, step = near(offsets)
        copy = remote(round_send, round_recv.at[d], round_ss.at[d], round_rs.at[d], tile, step)
        copy.start()
        round_copies.append(copy)

    s3_start(2)

    round_grid[...] = jnp.zeros_like(round_grid)
    round_pack[...] = round_send[...].astype(F32)
    for q in range(4):
        round_grid[pl.ds(10 + q, 8, stride=8), :] = round_pack[pl.ds(q, 8, stride=4), :]
    for d, (dt, ds) in enumerate(AROUND):
        round_copies[d].wait()
        valid = jnp.bool_(True)
        if dt:
            valid = (t < TILES - 1) if dt < 0 else (t > 0)
        if ds:
            beside = (s < STEPS - 1) if ds < 0 else (s > 0)
            valid = jnp.logical_and(valid, beside) if dt else beside
        round_pack[...] = jnp.where(valid, round_recv[d].astype(F32), 0.0)
        if dt == 0:
            q, place = (0, 6) if ds < 0 else (3, 1)
            round_grid[pl.ds(8 + place, 8, stride=8), :] = round_pack[pl.ds(q, 8, stride=4), :]
        else:
            source, row = (0, 72) if dt < 0 else (28, 0)
            if ds == 0:
                round_grid[row + 2 : row + 6, :] = round_pack[source : source + 4, :]
            else:
                q, place = (0, 6) if ds < 0 else (3, 1)
                round_grid[row + place : row + place + 1, :] = round_pack[source + q : source + q + 1, :]
    pulled = dot(round_grid[...].astype(BF16), latw4_t[...])
    for j in range(4):
        pre = pre_hidden[80 * j : 80 * j + 80, :]
        value = pulled[:, HID * j : HID * j + HID] * slope_of(pre, sigmoid(pre))
        put_blocks(hidden_even, hidden_odd, 1 + j, value)
        if j == 0:
            put_blocks(hidden_even, hidden_odd, 5, pltpu.roll(value, 79, 0))
        if j == 3:
            put_blocks(hidden_even, hidden_odd, 0, pltpu.roll(value, 1, 0))
    pieces = []
    for a in range(3):
        for b in range(3):
            if a == 1:
                window = hidden_odd[2 - b : 6 - b, 0:64, :]
            else:
                window = hidden_even[2 - b : 6 - b, 8 * (2 - a) : 8 * (2 - a) + 64, :]
            pieces.append(window.reshape(256, HID))
    result = dot_nt(jnp.concatenate(pieces, axis=1), jnp.concatenate([enc[k] for k in range(9)], axis=1))
    for j in range(4):
        for i, part in enumerate(lane_tiles(result[64 * j : 64 * j + 64])):
            out_grid[i, pl.ds(j, 64, stride=4), :] = part
    for r in range(8):
        for i in range(2):
            fgrad_ref[r, :, 128 * i : 128 * i + 128] = out_grid[i, r * 32 + 8 : r * 32 + 24, :]

    for a in range(3):
        finish(a)


def hand_over(fgrad_ref, mgrad_ref, fgrad_out, mgrad_out, sem):
    first = pltpu.make_async_copy(fgrad_ref, fgrad_out, sem.at[0])
    second = pltpu.make_async_copy(mgrad_ref, mgrad_out, sem.at[1])
    first.start()
    second.start()
    first.wait()
    second.wait()


def per_device(
    features,
    encoder_weight,
    latent_weight,
    timesteps,
    noise_field,
    time_table,
    input_weight,
    middle_weight,
    output_weight,
):
    hbm = pl.BlockSpec(memory_space=pl.ANY)
    vmem = pl.BlockSpec(memory_space=pltpu.VMEM)
    dma = pltpu.SemaphoreType.DMA
    operands = (
        features,
        encoder_weight,
        latent_weight.T,
        noise_field,
        time_table,
        input_weight,
        middle_weight,
        output_weight.T,
    )
    scratch = [
        pltpu.VMEM((8, 16, FEAT), BF16),
        pltpu.VMEM((9, FEAT, HID), BF16),
        pltpu.VMEM((LAT, HID), BF16),
        pltpu.VMEM(noise_field.shape, BF16),
        pltpu.VMEM(time_table.shape, BF16),
        pltpu.VMEM((LAT, UNET), BF16),
        pltpu.VMEM((9, UNET, UNET), BF16),
        pltpu.VMEM((LAT, UNET), BF16),
        dma((8,)),
        pltpu.VMEM((128, 4 * HID), BF16),
        pltpu.VMEM((128, 4 * UNET), BF16),
        pltpu.VMEM((128, 4 * UNET), BF16),
        pltpu.VMEM((8, UNET), F32),
        pltpu.VMEM((2, 16, FEAT), BF16),
        pltpu.VMEM((2, 16, FEAT), BF16),
        pltpu.VMEM((6, 2, 16, FEAT), BF16),
        pltpu.VMEM((2, 12 * 32, 128), F32),
        pltpu.VMEM((6, 96, FEAT), BF16),
        pltpu.VMEM((6, 88, FEAT), BF16),
        pltpu.VMEM((320, HID), F32),
        pltpu.VMEM((80, 128), F32),
        pltpu.VMEM((48, 128), F32),
        pltpu.VMEM((48, 128), BF16),
        pltpu.VMEM((15, 48, 128), BF16),
        pltpu.VMEM((16 * 48, 128), F32),
        pltpu.VMEM((640, 128), F32),
        pltpu.VMEM((2, 64, 128), BF16),
        pltpu.VMEM((2, 64, 128), BF16),
        pltpu.VMEM((10, 384, UNET), BF16),
        pltpu.VMEM((8, 256, UNET), F32),
        pltpu.VMEM((10, UNET, 384), BF16),
        pltpu.VMEM((10, UNET, 256), BF16),
        pltpu.VMEM((2, 512, UNET), F32),
        pltpu.VMEM((2048, UNET), F32),
        pltpu.VMEM((10, 384, UNET), BF16),
        pltpu.VMEM((512, 128), F32),
        pltpu.VMEM((15, 32, 128), BF16),
        pltpu.VMEM((15, 32, 128), BF16),
        pltpu.VMEM((32, 128), F32),
        pltpu.VMEM((32, 128), BF16),
        pltpu.VMEM((8, 32, 128), BF16),
        pltpu.VMEM((80, 128), F32),
        pltpu.VMEM((6, 80, HID), BF16),
        pltpu.VMEM((6, 72, HID), BF16),
        pltpu.VMEM((2, 256, 128), F32),
        pltpu.VMEM((9, 3 * UNET, 128), F32),
        pltpu.VMEM((3, 576, UNET), BF16),
        pltpu.VMEM((3, 576, UNET), BF16),
        pltpu.VMEM((9, 576, 128), F32),
        pltpu.VMEM((9, 144, UNET), BF16),
        pltpu.VMEM((9, 144, UNET), BF16),
        pltpu.VMEM((9, 256, 128), F32),
        pltpu.VMEM((45, 16, UNET), BF16),
        pltpu.VMEM((45, 16, UNET), BF16),
        dma((8,)),
        dma((8,)),
        dma((2,)),
        dma((2,)),
        dma((15,)),
        dma((15,)),
        dma((2,)),
        dma((2,)),
        dma((15,)),
        dma((15,)),
        dma((8,)),
        dma((8,)),
        dma((3,)),
        dma((3,)),
        dma((9,)),
        dma((9,)),
        dma((45,)),
        dma((45,)),
    ]
    shapes = (
        jax.ShapeDtypeStruct((8, 16, FEAT), F32),
        jax.ShapeDtypeStruct((9, 3, UNET), F32),
    )
    results = pl.pallas_call(
        kernel,
        out_shape=shapes,
        in_specs=[pl.BlockSpec(memory_space=pltpu.SMEM)] + [hbm] * 8,
        out_specs=(vmem, vmem),
        scratch_shapes=scratch,
        compiler_params=pltpu.CompilerParams(
            collective_id=0, has_side_effects=True, vmem_limit_bytes=60 * 1024 * 1024
        ),
        cost_estimate=pl.CostEstimate(flops=18_000_000_000, bytes_accessed=8_000_000, transcendentals=3_000_000),
    )(timesteps, *operands)
    feature_grad, middle_grad = pl.pallas_call(
        hand_over,
        out_shape=shapes,
        in_specs=[hbm, hbm],
        out_specs=(hbm, hbm),
        scratch_shapes=[dma((2,))],
    )(*results)
    return feature_grad, jnp.transpose(middle_grad, (1, 0, 2))


def solution(mesh):
    in_specs = (
        P("tile", "step", None),
        P(),
        P(),
        P("step"),
        P("step", "tile", None),
        P(),
        P(),
        P(),
        P(),
    )
    out_specs = (P("tile", "step", None), P(("tile", "step"), None, None))
    return jax.shard_map(per_device, mesh=mesh, in_specs=in_specs, out_specs=out_specs, check_vma=False)
```

```python
import math

import jax
import jax.numpy as jnp
from jax import lax
from jax.experimental import pallas as pl
from jax.experimental.pallas import tpu as pltpu
from jax.sharding import PartitionSpec as P

F32 = jnp.float32
BF16 = jnp.bfloat16
MESH = pl.DeviceIdType.MESH

FEAT, HID, LAT, UNET = 256, 512, 32, 384
TILES, STEPS = 8, 16
AROUND = ((-1, -1), (-1, 0), (-1, 1), (0, -1), (0, 1), (1, -1), (1, 0), (1, 1))


def sigmoid(values):
    return 0.5 * jnp.tanh(0.5 * values) + 0.5


def slope_of(values, sigma):
    return sigma * (1.0 + values * (1.0 - sigma))


def dot(left, right):
    return jnp.dot(left, right, preferred_element_type=F32)


def lane_tiles(value):
    return [value[:, 128 * i : 128 * i + 128] for i in range(value.shape[1] // 128)]


def shift_down(block):
    last = pltpu.roll(block[48:64], 1, 0)
    rows = lax.broadcasted_iota(jnp.int32, last.shape, 0)
    return jnp.concatenate([jnp.where(rows == 0, 0.0, last), block[0:48]], axis=0)


def shift_up(block):
    first = pltpu.roll(block[0:16], 15, 0)
    rows = lax.broadcasted_iota(jnp.int32, first.shape, 0)
    return jnp.concatenate([block[16:64], jnp.where(rows == 15, 0.0, first)], axis=0)


def kernel(
    time_ref,
    feat_hbm,
    enc_hbm,
    latw_hbm,
    noise_hbm,
    table_hbm,
    inw_hbm,
    midw_hbm,
    outw_hbm,
    fgrad_ref,
    mgrad_ref,
    feat,
    enc,
    latw,
    noise,
    table,
    inw,
    midw,
    outw,
    in_sem,
    enc_t,
    mid_t,
    latw4,
    latw4_t,
    inw4,
    inw4_t,
    outw4,
    outw4_t,
    embed,
    edge,
    edge_in,
    rows_in,
    grid,
    blocks_even,
    blocks_odd,
    pre_hidden,
    lat_tile,
    lat_pack,
    lat_send,
    lat_recv,
    lat_flat,
    noise_rows,
    noise_edge,
    noise_edge_in,
    inner_ext,
    inner_slope,
    inner_t,
    inner_tm,
    pre_middle,
    back_mixed,
    back_ext,
    back_part,
    part_send,
    part_recv,
    round_pack,
    round_send,
    round_recv,
    round_grid,
    hidden_even,
    hidden_odd,
    out_grid,
    grad,
    s1_send,
    s1_recv,
    sum1,
    s2_send,
    s2_recv,
    sum2,
    s3_send,
    s3_recv,
    feat_ss,
    feat_rs,
    noise_ss,
    noise_rs,
    lat_ss,
    lat_rs,
    halo_ss,
    halo_rs,
    part_ss,
    part_rs,
    round_ss,
    round_rs,
    s1_ss,
    s1_rs,
    s2_ss,
    s2_rs,
    s3_ss,
    s3_rs,
):
    t = lax.axis_index("tile")
    s = lax.axis_index("step")
    y_hi, x = t // 4, t % 4
    z, y_lo, core = s // 4, (s // 2) % 2, s % 2
    y = y_hi * 2 + y_lo

    def remote(src, dst, ss, rs, tile, step):
        return pltpu.make_async_remote_copy(
            src_ref=src, dst_ref=dst, send_sem=ss, recv_sem=rs, device_id=(tile, step), device_id_type=MESH
        )

    def near(offsets):
        return (t + offsets[0] + TILES) % TILES, (s + offsets[1] + STEPS) % STEPS

    loads = [
        pltpu.make_async_copy(src, dst, in_sem.at[i])
        for i, (src, dst) in enumerate(
            (
                (feat_hbm, feat),
                (noise_hbm, noise),
                (enc_hbm, enc),
                (latw_hbm, latw),
                (inw_hbm, inw),
                (outw_hbm, outw),
                (table_hbm, table),
                (midw_hbm, midw),
            )
        )
    ]
    for load in loads:
        load.start()
    l_feat, l_noise, l_enc, l_latw, l_inw, l_outw, l_table, l_midw = loads

    barrier = pltpu.get_barrier_semaphore()

    def greet_step(k, _):
        pl.semaphore_signal(barrier, inc=1, device_id=(t, (s + k) % STEPS), device_id_type=MESH)
        return 0

    def greet_tile(k, _):
        pl.semaphore_signal(barrier, inc=1, device_id=((t + k) % TILES, s), device_id_type=MESH)
        return 0

    lax.fori_loop(1, STEPS, greet_step, 0)
    lax.fori_loop(1, TILES, greet_tile, 0)
    for offsets in AROUND:
        if offsets[0] and offsets[1]:
            pl.semaphore_signal(barrier, inc=1, device_id=near(offsets), device_id_type=MESH)

    l_feat.wait()
    grid[...] = jnp.zeros_like(grid)
    for r in range(8):
        for i, part in enumerate(lane_tiles(feat[r].astype(F32))):
            grid[i, (r + 2) * 32 + 8 : (r + 2) * 32 + 24, :] = part
    for side, first in ((0, 8), (1, 22)):
        for i in range(2):
            pair = [grid[i, pl.ds(64 + first + col, 8, stride=32), :] for col in (0, 1)]
            edge[side, :, 128 * i : 128 * i + 128] = jnp.concatenate(pair, axis=0).astype(BF16)

    pl.semaphore_wait(barrier, STEPS - 1 + TILES - 1 + 4)

    feat_copies = []
    for d, offsets in enumerate(AROUND):
        tile, step = near(offsets)
        if offsets[0] == 0:
            side = 0 if offsets[1] < 0 else 1
            src, dst = edge.at[side], edge_in.at[side]
        else:
            slot = d if d < 3 else d - 2
            src, dst = feat.at[pl.ds(0 if offsets[0] < 0 else 6, 2)], rows_in.at[slot]
        copy = remote(src, dst, feat_ss.at[d], feat_rs.at[d], tile, step)
        copy.start()
        feat_copies.append(copy)

    l_noise.wait()
    for q in range(64):
        piece = noise[0, :, 128 * q : 128 * q + 128].astype(F32)
        noise_rows[pl.ds(64 + (q % 4) * 16 + q // 4, 8, stride=64), :] = piece
    noise_edge[0] = noise_rows[64:128, :].astype(BF16)
    noise_edge[1] = noise_rows[512:576, :].astype(BF16)
    noise_copies = []
    for side, offset in ((0, -1), (1, 1)):
        tile, step = near((offset, 0))
        copy = remote(noise_edge.at[side], noise_edge_in.at[side], noise_ss.at[side], noise_rs.at[side], tile, step)
        copy.start()
        noise_copies.append(copy)

    for load, weight, wide, flipped in (
        (l_latw, latw, latw4_t, latw4),
        (l_inw, inw, inw4, inw4_t),
        (l_outw, outw, outw4_t, outw4),
    ):
        load.wait()
        columns = weight.shape[1]
        wide[...] = jnp.zeros_like(wide)
        for j in range(4):
            wide[LAT * j : LAT * j + LAT, columns * j : columns * j + columns] = weight[...]
        flipped[...] = jnp.transpose(wide[...])

    chosen = time_ref[0]
    angle = ((jnp.full((8, 128), chosen, jnp.int32).astype(F32) + 1.0) / 1000.0 + 0.008) / 1.008 * (math.pi / 2.0)
    cosine = jnp.cos(angle)[0:1, :]
    sine = jnp.sin(angle)[0:1, :]
    l_table.wait()
    onehot = (lax.broadcasted_iota(jnp.int32, (16, table.shape[0]), 1) == chosen).astype(F32).astype(BF16)
    embed[...] = dot(onehot, table[...])[0:8]

    l_enc.wait()

    for d, copy in enumerate(feat_copies):
        copy.wait()
    for d, offsets in enumerate(AROUND):
        dt, ds = offsets
        valid = jnp.bool_(True)
        if dt:
            valid = (t < TILES - 1) if dt < 0 else (t > 0)
        if ds:
            beside = (s < STEPS - 1) if ds < 0 else (s > 0)
            valid = jnp.logical_and(valid, beside) if dt else beside
        if dt == 0:
            side = 0 if ds < 0 else 1
            taken = jnp.where(valid, edge_in[side].astype(F32), 0.0)
            first = 24 if ds < 0 else 6
            for i, part in enumerate(lane_tiles(taken)):
                for col in (0, 1):
                    grid[i, pl.ds(64 + first + col, 8, stride=32), :] = part[8 * col : 8 * col + 8]
        else:
            slot = d if d < 3 else d - 2
            for r in range(2):
                taken = jnp.where(valid, rows_in[slot, r].astype(F32), 0.0)
                row = (10 + r if dt < 0 else r) * 32
                for i, part in enumerate(lane_tiles(taken)):
                    if ds == 0:
                        grid[i, row + 8 : row + 24, :] = part
                    elif ds < 0:
                        grid[i, row + 24 : row + 32, :] = part[0:8]
                    else:
                        grid[i, row : row + 8, :] = part[8:16]

    def put_blocks(even, odd, index, value):
        even[index] = value.astype(BF16)
        odd[index] = value[8:].astype(BF16)

    for j in range(4):
        value = jnp.concatenate([grid[i, pl.ds(j, 96, stride=4), :] for i in range(2)], axis=1)
        put_blocks(blocks_even, blocks_odd, 1 + j, value)
        if j == 0:
            put_blocks(blocks_even, blocks_odd, 5, pltpu.roll(value, 95, 0))
        if j == 3:
            put_blocks(blocks_even, blocks_odd, 0, pltpu.roll(value, 1, 0))
    pieces = []
    for a in range(3):
        for b in range(3):
            if a == 1:
                window = blocks_odd[b : b + 4, 0:80, :]
            else:
                window = blocks_even[b : b + 4, 8 * a : 8 * a + 80, :]
            pieces.append(window.reshape(320, FEAT))
    pre = dot(jnp.concatenate(pieces, axis=1), enc[...].reshape(9 * FEAT, HID))
    pre_hidden[...] = pre
    hidden = (pre * sigmoid(pre)).astype(BF16)
    hidden = jnp.concatenate([hidden[80 * j : 80 * j + 80] for j in range(4)], axis=1)
    lat_tile[...] = dot(hidden, latw4[...])
    lat_pack[...] = jnp.zeros_like(lat_pack)
    for q in range(4):
        lat_pack[pl.ds(q, 10, stride=4), :] = lat_tile[pl.ds(2 + q, 10, stride=8), :]
    lat_send[...] = lat_pack[...].astype(BF16)

    def lat_copy(k):
        return remote(lat_send, lat_recv.at[k - 1], lat_ss.at[k - 1], lat_rs.at[k - 1], t, (s + k) % STEPS)

    def lat_start(k, _):
        lat_copy(k).start()
        return 0

    lax.fori_loop(1, STEPS, lat_start, 0)

    l_midw.wait()

    def flip_mid(k, _):
        mid_t[k] = jnp.transpose(midw[k])
        return 0

    lax.fori_loop(0, 9, flip_mid, 0)
    for side in (0, 1):
        noise_copies[side].wait()
    noise_rows[576:640, :] = noise_edge_in[0].astype(F32)
    noise_rows[0:64, :] = noise_edge_in[1].astype(F32)

    lat_flat[pl.ds(pl.multiple_of(s * 48, 16), 48), :] = lat_pack[...].astype(BF16).astype(F32)

    def lat_take(k, _):
        lat_copy(k).wait()
        source = (s - k + STEPS) % STEPS
        lat_flat[pl.ds(pl.multiple_of(source * 48, 16), 48), :] = lat_recv[k - 1].astype(F32)
        return 0

    lax.fori_loop(1, STEPS, lat_take, 0)

    def input_rows(pair):
        first = 2 * pair
        latent = [lat_flat[pl.ds((first + r) * 4 + q, 16, stride=48), :] for r in range(2) for q in range(4)]
        noisy = cosine * jnp.concatenate(latent, axis=0) + sine * noise_rows[64 * first : 64 * first + 128, :]
        noisy = noisy.astype(BF16)
        for j in range(4):
            pre = dot(noisy, inw4[:, UNET * j : UNET * j + UNET]) + embed[0:1, :]
            sigma = sigmoid(pre)
            inner = pre * sigma
            slope = slope_of(pre, sigma)
            for r in range(2):
                row = first + r
                own = inner[64 * r : 64 * r + 64]
                if row == 0:
                    own = own * jnp.where(t > 0, 1.0, 0.0)
                if row == 9:
                    own = own * jnp.where(t < TILES - 1, 1.0, 0.0)
                inner_ext[row, 64 + 64 * j : 128 + 64 * j, :] = own.astype(BF16)
                if j == 0:
                    inner_ext[row, 320:384, :] = shift_up(own).astype(BF16)
                if j == 3:
                    inner_ext[row, 0:64, :] = shift_down(own).astype(BF16)
                if 0 < row < 9:
                    inner_slope[row - 1, 64 * j : 64 * j + 64, :] = slope[64 * r : 64 * r + 64]

    def flip_rows(pair):
        for row in (2 * pair, 2 * pair + 1):
            flipped = jnp.transpose(inner_ext[row])
            inner_t[row] = flipped
            inner_tm[row] = flipped[:, 64:320]

    def by_class(value):
        rows = value.shape[0] // 256
        return jnp.concatenate(
            [
                jnp.concatenate([value[256 * r + 64 * j : 256 * r + 64 * j + 64] for j in range(4)], axis=1)
                for r in range(rows)
            ],
            axis=0,
        )

    def by_position(value):
        rows = value.shape[0] // 64
        return jnp.concatenate(
            [value[64 * r : 64 * r + 64, UNET * j : UNET * j + UNET] for r in range(rows) for j in range(4)], axis=0
        )

    def forward_conv(i):
        windows = [
            inner_ext[2 * i + a : 2 * i + a + 2, 64 * b : 64 * b + 256, :].reshape(512, UNET)
            for a in range(3)
            for b in range(3)
        ]
        pre_middle[i % 2] = dot(jnp.concatenate(windows, axis=1), midw[...].reshape(9 * UNET, UNET))

    def forward_after(i):
        r = 2 * i
        pre = pre_middle[i % 2]
        sigma = sigmoid(pre)
        own = inner_ext[r + 1 : r + 3, 64:320, :].reshape(512, UNET)
        mixed = (own.astype(F32) + pre * sigma).astype(BF16)
        prediction = dot(by_class(mixed), outw4[...])
        own_noise = noise_rows[64 + r * 64 : 192 + r * 64, :]
        error = ((prediction - own_noise) * (1.0 / math.sqrt(STEPS))).astype(BF16)
        pulled = by_position(dot(error, outw4_t[...]))
        back_mixed[256 * r : 256 * r + 512, :] = pulled
        back = pulled * slope_of(pre, sigma)
        for row in range(2):
            own = back[256 * row : 256 * row + 256]
            back_ext[r + 1 + row, 64:320, :] = own.astype(BF16)
            back_ext[r + 1 + row, 320:384, :] = shift_up(own[0:64]).astype(BF16)
            back_ext[r + 1 + row, 0:64, :] = shift_down(own[192:256]).astype(BF16)

    input_rows(0)
    input_rows(1)
    for i in range(4):
        forward_conv(i)
        if i < 3:
            input_rows(i + 2)
        flip_rows(i)
        if i:
            forward_after(i - 1)
    flip_rows(4)
    forward_after(3)

    halo_copies = []
    for side, offset in ((0, -1), (1, 1)):
        tile, step = near((offset, 0))
        src, dst = (1, 9) if side == 0 else (8, 0)
        src, dst = back_ext.at[src, pl.ds(64, 256)], back_ext.at[dst, pl.ds(64, 256)]
        copy = remote(src, dst, halo_ss.at[side], halo_rs.at[side], tile, step)
        copy.start()
        halo_copies.append(copy)

    def s1_copy(a):
        return remote(s1_send.at[a], s1_recv.at[a], s1_ss.at[a], s1_rs.at[a], t, s + 1 - 2 * core)

    def s1_start(a):
        for n in range(9):
            first = (n // 3) * UNET + n % 3 + 3 * (1 - core)
            block = jnp.concatenate([grad[a * 3 + i, pl.ds(first, 64, stride=6), :] for i in range(3)], axis=1)
            s1_send[a, 64 * n : 64 * n + 64, :] = block.astype(BF16)
        s1_copy(a).start()

    def axis_peer(a, k):
        if a == 0:
            there = (z + k) % 4
            return there, t, there * 4 + s % 4
        if a == 1:
            there = (x + k) % 4
            return there, y_hi * 4 + there, s
        there = (y + k) % 4
        return there, (there // 2) * 4 + x, z * 4 + (there % 2) * 2 + core

    def plane_rows(a, n, there):
        base = n * 64
        parts = []
        for i in range(3):
            if a == 0:
                half = [sum1[a * 3 + i, pl.ds(base + 2 * there + low, 8, stride=8), :] for low in (0, 1)]
                parts.append(jnp.concatenate(half, axis=0))
            elif a == 1:
                half = [
                    sum1[a * 3 + i, pl.ds(base + high * 32 + pl.multiple_of(there * 8, 8), 8), :] for high in (0, 1)
                ]
                parts.append(jnp.concatenate(half, axis=0))
            else:
                first = base + (there // 2) * 32 + there % 2
                parts.append(sum1[a * 3 + i, pl.ds(first, 16, stride=2), :])
        return jnp.concatenate(parts, axis=1)

    def s2_copy(a, k):
        _, tile, step = axis_peer(a, k)
        index = a * 3 + k - 1
        return remote(s2_send.at[index], s2_recv.at[index], s2_ss.at[index], s2_rs.at[index], tile, step)

    def s2_start(a):
        s1_copy(a).wait()

        for n in range(9):
            first = (n // 3) * UNET + n % 3 + 3 * core
            got = s1_recv[a, 64 * n : 64 * n + 64, :].astype(F32)
            for i in range(3):
                own = grad[a * 3 + i, pl.ds(first, 64, stride=6), :]
                sum1[a * 3 + i, 64 * n : 64 * n + 64, :] = own + got[:, 128 * i : 128 * i + 128]
        for k in (2, 1, 3):
            there = axis_peer(a, k)[0]
            for n in range(9):
                s2_send[a * 3 + k - 1, 16 * n : 16 * n + 16, :] = plane_rows(a, n, there).astype(BF16)
            s2_copy(a, k).start()

    def plane_peer(a, k):
        if a == 0:
            mine = y_lo * 8 + t
            there = (mine + k) % 16
            return mine, there, there % 8, z * 4 + (there // 8) * 2 + core
        if a == 1:
            mine = y_hi * 8 + s // 2
            there = (mine + k) % 16
            return mine, there, (there // 8) * 4 + x, (there % 8) * 2 + core
        mine = x * 4 + z
        there = (mine + k) % 16
        return mine, there, y_hi * 4 + there // 4, (there % 4) * 4 + s % 4

    def s3_copy(a, k):
        _, _, tile, step = plane_peer(a, k)
        index = a * 15 + k - 1
        return remote(s3_send.at[index], s3_recv.at[index], s3_ss.at[index], s3_rs.at[index], tile, step)

    def s3_start(a):
        for k in range(1, 4):
            s2_copy(a, k).wait()
        mine = axis_peer(a, 0)[0]

        for n in range(9):
            total = plane_rows(a, n, mine)
            for k in range(3):
                total = total + s2_recv[a * 3 + k, 16 * n : 16 * n + 16, :].astype(F32)
            for i, part in enumerate(lane_tiles(total)):
                sum2[a * 3 + i, 16 * n : 16 * n + 16, :] = part

        def send(k, _):
            there = plane_peer(a, k)[1]
            block = jnp.concatenate([sum2[a * 3 + i, pl.ds(there, 16, stride=16), :] for i in range(3)], axis=1)
            s3_send[a * 15 + k - 1] = block.astype(BF16)
            s3_copy(a, k).start()
            return 0

        lax.fori_loop(1, 16, send, 0)

    def finish(a):
        mine = plane_peer(a, 0)[0]
        own = jnp.concatenate([sum2[a * 3 + i, pl.ds(mine, 16, stride=16), :] for i in range(3)], axis=1)

        def add(k, total):
            s3_copy(a, k).wait()
            return total + s3_recv[a * 15 + k - 1].astype(F32)

        total = lax.fori_loop(1, 16, add, own) * (1.0 / math.sqrt(64 * 256))
        for b in range(3):
            mgrad_ref[3 * a + b] = total[3 * b : 3 * b + 3]

    sum2[...] = jnp.zeros_like(sum2)
    for a in range(3):
        taps = [
            jnp.concatenate([inner_t[r + a, :, 0:256] for r in range(8)], axis=1),
            jnp.concatenate([inner_tm[r + a] for r in range(8)], axis=1),
            jnp.concatenate([inner_t[r + a, :, 128:384] for r in range(8)], axis=1),
        ]
        result = dot(jnp.concatenate(taps, axis=0), back_ext[1:9, 64:320, :].reshape(2048, UNET))
        for i, part in enumerate(lane_tiles(result)):
            grad[a * 3 + i] = part
        for k in range(3 * a, 3 * a + 3):
            enc_t[k] = jnp.transpose(enc[k])
        s1_start(a)
        if a:
            s2_start(a - 1)

    for row, copy in ((9, halo_copies[0]), (0, halo_copies[1])):
        copy.wait()
        back_ext[row, 320:384, :] = shift_up(back_ext[row, 64:128, :].astype(F32)).astype(BF16)
        back_ext[row, 0:64, :] = shift_down(back_ext[row, 256:320, :].astype(F32)).astype(BF16)

    @pl.when(t == 0)
    def _():
        back_ext[0] = jnp.zeros_like(back_ext[0])

    @pl.when(t == TILES - 1)
    def _():
        back_ext[9] = jnp.zeros_like(back_ext[9])

    def backward_rows(i):
        r = 2 * i
        windows = [
            back_ext[r + 2 - a : r + 4 - a, 64 * (2 - b) : 64 * (2 - b) + 256, :].reshape(512, UNET)
            for a in range(3)
            for b in range(3)
        ]
        through = dot(jnp.concatenate(windows, axis=1), mid_t[...].reshape(9 * UNET, UNET))
        through = through + back_mixed[256 * r : 256 * r + 512, :]
        back = (through * inner_slope[r : r + 2].reshape(512, UNET)).astype(BF16)
        back_part[64 * r : 64 * r + 128, :] = cosine * dot(by_class(back), inw4_t[...])

    backward_rows(0)
    s2_start(2)
    backward_rows(1)
    backward_rows(2)
    s3_start(0)
    backward_rows(3)

    def part_copy(k):
        return remote(
            part_send.at[k - 1], part_recv.at[k - 1], part_ss.at[k - 1], part_rs.at[k - 1], t, (s + k) % STEPS
        )

    def part_start(k, _):
        part_send[k - 1] = back_part[pl.ds((s + k) % STEPS, 32, stride=16), :].astype(BF16)
        part_copy(k).start()
        return 0

    lax.fori_loop(1, STEPS, part_start, 0)

    s3_start(1)

    def part_add(k, total):
        part_copy(k).wait()
        return total + part_recv[k - 1].astype(F32)

    latent_round = lax.fori_loop(1, STEPS, part_add, back_part[pl.ds(s, 32, stride=16), :])
    round_send[...] = latent_round.astype(BF16)
    round_copies = []
    for d, offsets in enumerate(AROUND):
        tile, step = near(offsets)
        copy = remote(round_send, round_recv.at[d], round_ss.at[d], round_rs.at[d], tile, step)
        copy.start()
        round_copies.append(copy)

    s3_start(2)

    round_grid[...] = jnp.zeros_like(round_grid)
    round_pack[...] = round_send[...].astype(F32)
    for q in range(4):
        round_grid[pl.ds(10 + q, 8, stride=8), :] = round_pack[pl.ds(q, 8, stride=4), :]
    for d, (dt, ds) in enumerate(AROUND):
        round_copies[d].wait()
        valid = jnp.bool_(True)
        if dt:
            valid = (t < TILES - 1) if dt < 0 else (t > 0)
        if ds:
            beside = (s < STEPS - 1) if ds < 0 else (s > 0)
            valid = jnp.logical_and(valid, beside) if dt else beside
        round_pack[...] = jnp.where(valid, round_recv[d].astype(F32), 0.0)
        if dt == 0:
            q, place = (0, 6) if ds < 0 else (3, 1)
            round_grid[pl.ds(8 + place, 8, stride=8), :] = round_pack[pl.ds(q, 8, stride=4), :]
        else:
            source, row = (0, 72) if dt < 0 else (28, 0)
            if ds == 0:
                round_grid[row + 2 : row + 6, :] = round_pack[source : source + 4, :]
            else:
                q, place = (0, 6) if ds < 0 else (3, 1)
                round_grid[row + place : row + place + 1, :] = round_pack[source + q : source + q + 1, :]
    pulled = dot(round_grid[...].astype(BF16), latw4_t[...])
    for j in range(4):
        pre = pre_hidden[80 * j : 80 * j + 80, :]
        value = pulled[:, HID * j : HID * j + HID] * slope_of(pre, sigmoid(pre))
        put_blocks(hidden_even, hidden_odd, 1 + j, value)
        if j == 0:
            put_blocks(hidden_even, hidden_odd, 5, pltpu.roll(value, 79, 0))
        if j == 3:
            put_blocks(hidden_even, hidden_odd, 0, pltpu.roll(value, 1, 0))
    pieces = []
    for a in range(3):
        for b in range(3):
            if a == 1:
                window = hidden_odd[2 - b : 6 - b, 0:64, :]
            else:
                window = hidden_even[2 - b : 6 - b, 8 * (2 - a) : 8 * (2 - a) + 64, :]
            pieces.append(window.reshape(256, HID))
    result = dot(jnp.concatenate(pieces, axis=1), enc_t[...].reshape(9 * HID, FEAT))
    for j in range(4):
        for i, part in enumerate(lane_tiles(result[64 * j : 64 * j + 64])):
            out_grid[i, pl.ds(j, 64, stride=4), :] = part
    for r in range(8):
        for i in range(2):
            fgrad_ref[r, :, 128 * i : 128 * i + 128] = out_grid[i, r * 32 + 8 : r * 32 + 24, :]

    for a in range(3):
        finish(a)


def hand_over(fgrad_ref, mgrad_ref, fgrad_out, mgrad_out):
    fgrad_out[...] = fgrad_ref[...]
    mgrad_out[...] = mgrad_ref[...]


def per_device(
    features,
    encoder_weight,
    latent_weight,
    timesteps,
    noise_field,
    time_table,
    input_weight,
    middle_weight,
    output_weight,
):
    hbm = pl.BlockSpec(memory_space=pl.ANY)
    vmem = pl.BlockSpec(memory_space=pltpu.VMEM)
    dma = pltpu.SemaphoreType.DMA
    operands = (
        features,
        encoder_weight,
        latent_weight.T,
        noise_field,
        time_table,
        input_weight,
        middle_weight,
        output_weight.T,
    )
    scratch = [
        pltpu.VMEM((8, 16, FEAT), BF16),
        pltpu.VMEM((9, FEAT, HID), BF16),
        pltpu.VMEM((LAT, HID), BF16),
        pltpu.VMEM(noise_field.shape, BF16),
        pltpu.VMEM(time_table.shape, BF16),
        pltpu.VMEM((LAT, UNET), BF16),
        pltpu.VMEM((9, UNET, UNET), BF16),
        pltpu.VMEM((LAT, UNET), BF16),
        dma((8,)),
        pltpu.VMEM((9, HID, FEAT), BF16),
        pltpu.VMEM((9, UNET, UNET), BF16),
        pltpu.VMEM((4 * HID, 128), BF16),
        pltpu.VMEM((128, 4 * HID), BF16),
        pltpu.VMEM((128, 4 * UNET), BF16),
        pltpu.VMEM((4 * UNET, 128), BF16),
        pltpu.VMEM((4 * UNET, 128), BF16),
        pltpu.VMEM((128, 4 * UNET), BF16),
        pltpu.VMEM((8, UNET), F32),
        pltpu.VMEM((2, 16, FEAT), BF16),
        pltpu.VMEM((2, 16, FEAT), BF16),
        pltpu.VMEM((6, 2, 16, FEAT), BF16),
        pltpu.VMEM((2, 12 * 32, 128), F32),
        pltpu.VMEM((6, 96, FEAT), BF16),
        pltpu.VMEM((6, 88, FEAT), BF16),
        pltpu.VMEM((320, HID), F32),
        pltpu.VMEM((80, 128), F32),
        pltpu.VMEM((48, 128), F32),
        pltpu.VMEM((48, 128), BF16),
        pltpu.VMEM((15, 48, 128), BF16),
        pltpu.VMEM((16 * 48, 128), F32),
        pltpu.VMEM((640, 128), F32),
        pltpu.VMEM((2, 64, 128), BF16),
        pltpu.VMEM((2, 64, 128), BF16),
        pltpu.VMEM((10, 384, UNET), BF16),
        pltpu.VMEM((8, 256, UNET), F32),
        pltpu.VMEM((10, UNET, 384), BF16),
        pltpu.VMEM((10, UNET, 256), BF16),
        pltpu.VMEM((2, 512, UNET), F32),
        pltpu.VMEM((2048, UNET), F32),
        pltpu.VMEM((10, 384, UNET), BF16),
        pltpu.VMEM((512, 128), F32),
        pltpu.VMEM((15, 32, 128), BF16),
        pltpu.VMEM((15, 32, 128), BF16),
        pltpu.VMEM((32, 128), F32),
        pltpu.VMEM((32, 128), BF16),
        pltpu.VMEM((8, 32, 128), BF16),
        pltpu.VMEM((80, 128), F32),
        pltpu.VMEM((6, 80, HID), BF16),
        pltpu.VMEM((6, 72, HID), BF16),
        pltpu.VMEM((2, 256, 128), F32),
        pltpu.VMEM((9, 3 * UNET, 128), F32),
        pltpu.VMEM((3, 576, UNET), BF16),
        pltpu.VMEM((3, 576, UNET), BF16),
        pltpu.VMEM((9, 576, 128), F32),
        pltpu.VMEM((9, 144, UNET), BF16),
        pltpu.VMEM((9, 144, UNET), BF16),
        pltpu.VMEM((9, 256, 128), F32),
        pltpu.VMEM((45, 16, UNET), BF16),
        pltpu.VMEM((45, 16, UNET), BF16),
        dma((8,)),
        dma((8,)),
        dma((2,)),
        dma((2,)),
        dma((15,)),
        dma((15,)),
        dma((2,)),
        dma((2,)),
        dma((15,)),
        dma((15,)),
        dma((8,)),
        dma((8,)),
        dma((3,)),
        dma((3,)),
        dma((9,)),
        dma((9,)),
        dma((45,)),
        dma((45,)),
    ]
    shapes = (
        jax.ShapeDtypeStruct((8, 16, FEAT), F32),
        jax.ShapeDtypeStruct((9, 3, UNET), F32),
    )
    results = pl.pallas_call(
        kernel,
        out_shape=shapes,
        in_specs=[pl.BlockSpec(memory_space=pltpu.SMEM)] + [hbm] * 8,
        out_specs=(vmem, vmem),
        scratch_shapes=scratch,
        compiler_params=pltpu.CompilerParams(
            collective_id=0, has_side_effects=True, vmem_limit_bytes=60 * 1024 * 1024
        ),
        cost_estimate=pl.CostEstimate(flops=18_000_000_000, bytes_accessed=8_000_000, transcendentals=3_000_000),
    )(timesteps, *operands)
    feature_grad, middle_grad = pl.pallas_call(
        hand_over,
        out_shape=shapes,
        in_specs=[vmem, vmem],
        out_specs=(vmem, vmem),
    )(*results)
    return feature_grad, jnp.transpose(middle_grad, (1, 0, 2))


def solution(mesh):
    in_specs = (
        P("tile", "step", None),
        P(),
        P(),
        P("step"),
        P("step", "tile", None),
        P(),
        P(),
        P(),
        P(),
    )
    out_specs = (P("tile", "step", None), P(("tile", "step"), None, None))
    return jax.shard_map(per_device, mesh=mesh, in_specs=in_specs, out_specs=out_specs, check_vma=False)
```

```python
import math

import jax
import jax.numpy as jnp
from jax import lax
from jax.experimental import pallas as pl
from jax.experimental.pallas import tpu as pltpu
from jax.sharding import PartitionSpec as P

F32 = jnp.float32
BF16 = jnp.bfloat16
MESH = pl.DeviceIdType.MESH

FEAT, HID, LAT, UNET = 256, 512, 32, 384
TILES, STEPS = 8, 16
AROUND = ((-1, -1), (-1, 0), (-1, 1), (0, -1), (0, 1), (1, -1), (1, 0), (1, 1))


def sigmoid(values):
    return 0.5 * jnp.tanh(0.5 * values) + 0.5


def slope_of(values, sigma):
    return sigma * (1.0 + values * (1.0 - sigma))


def dot(left, right):
    return jnp.dot(left, right, preferred_element_type=F32)


def lane_tiles(value):
    return [value[:, 128 * i : 128 * i + 128] for i in range(value.shape[1] // 128)]


def shift_down(block):
    last = pltpu.roll(block[48:64], 1, 0)
    rows = lax.broadcasted_iota(jnp.int32, last.shape, 0)
    return jnp.concatenate([jnp.where(rows == 0, 0.0, last), block[0:48]], axis=0)


def shift_up(block):
    first = pltpu.roll(block[0:16], 15, 0)
    rows = lax.broadcasted_iota(jnp.int32, first.shape, 0)
    return jnp.concatenate([block[16:64], jnp.where(rows == 15, 0.0, first)], axis=0)


def kernel(
    time_ref,
    feat_hbm,
    enc_hbm,
    latw_hbm,
    noise_hbm,
    table_hbm,
    inw_hbm,
    midw_hbm,
    outw_hbm,
    fgrad_ref,
    mgrad_ref,
    feat,
    enc,
    latw,
    noise,
    table,
    inw,
    midw,
    outw,
    in_sem,
    enc_t,
    mid_t,
    latw4,
    latw4_t,
    inw4,
    inw4_t,
    outw4,
    outw4_t,
    embed,
    edge,
    edge_in,
    rows_in,
    grid,
    blocks_even,
    blocks_odd,
    pre_hidden,
    lat_tile,
    lat_pack,
    lat_send,
    lat_recv,
    lat_flat,
    noise_rows,
    noise_edge,
    noise_edge_in,
    inner_ext,
    inner_slope,
    inner_t,
    inner_tm,
    pre_middle,
    back_mixed,
    back_ext,
    back_part,
    part_send,
    part_recv,
    round_pack,
    round_send,
    round_recv,
    round_grid,
    hidden_even,
    hidden_odd,
    out_grid,
    grad,
    s1_send,
    s1_recv,
    sum1,
    s2_send,
    s2_recv,
    sum2,
    s3_send,
    s3_recv,
    feat_ss,
    feat_rs,
    noise_ss,
    noise_rs,
    lat_ss,
    lat_rs,
    halo_ss,
    halo_rs,
    part_ss,
    part_rs,
    round_ss,
    round_rs,
    s1_ss,
    s1_rs,
    s2_ss,
    s2_rs,
    s3_ss,
    s3_rs,
):
    t = lax.axis_index("tile")
    s = lax.axis_index("step")
    y_hi, x = t // 4, t % 4
    z, y_lo, core = s // 4, (s // 2) % 2, s % 2
    y = y_hi * 2 + y_lo

    def remote(src, dst, ss, rs, tile, step):
        return pltpu.make_async_remote_copy(
            src_ref=src, dst_ref=dst, send_sem=ss, recv_sem=rs, device_id=(tile, step), device_id_type=MESH
        )

    def near(offsets):
        return (t + offsets[0] + TILES) % TILES, (s + offsets[1] + STEPS) % STEPS

    loads = [
        pltpu.make_async_copy(src, dst, in_sem.at[i])
        for i, (src, dst) in enumerate(
            (
                (feat_hbm, feat),
                (noise_hbm, noise),
                (enc_hbm, enc),
                (latw_hbm, latw),
                (inw_hbm, inw),
                (outw_hbm, outw),
                (table_hbm, table),
                (midw_hbm, midw),
            )
        )
    ]
    for load in loads:
        load.start()
    l_feat, l_noise, l_enc, l_latw, l_inw, l_outw, l_table, l_midw = loads

    barrier = pltpu.get_barrier_semaphore()

    def greet_step(k, _):
        pl.semaphore_signal(barrier, inc=1, device_id=(t, (s + k) % STEPS), device_id_type=MESH)
        return 0

    def greet_tile(k, _):
        pl.semaphore_signal(barrier, inc=1, device_id=((t + k) % TILES, s), device_id_type=MESH)
        return 0

    lax.fori_loop(1, STEPS, greet_step, 0)
    lax.fori_loop(1, TILES, greet_tile, 0)
    for offsets in AROUND:
        if offsets[0] and offsets[1]:
            pl.semaphore_signal(barrier, inc=1, device_id=near(offsets), device_id_type=MESH)

    l_feat.wait()
    grid[...] = jnp.zeros_like(grid)
    for r in range(8):
        for i, part in enumerate(lane_tiles(feat[r].astype(F32))):
            grid[i, (r + 2) * 32 + 8 : (r + 2) * 32 + 24, :] = part
    for side, first in ((0, 8), (1, 22)):
        for i in range(2):
            pair = [grid[i, pl.ds(64 + first + col, 8, stride=32), :] for col in (0, 1)]
            edge[side, :, 128 * i : 128 * i + 128] = jnp.concatenate(pair, axis=0).astype(BF16)

    pl.semaphore_wait(barrier, STEPS - 1 + TILES - 1 + 4)

    feat_copies = []
    for d, offsets in enumerate(AROUND):
        tile, step = near(offsets)
        if offsets[0] == 0:
            side = 0 if offsets[1] < 0 else 1
            src, dst = edge.at[side], edge_in.at[side]
        else:
            slot = d if d < 3 else d - 2
            src, dst = feat.at[pl.ds(0 if offsets[0] < 0 else 6, 2)], rows_in.at[slot]
        copy = remote(src, dst, feat_ss.at[d], feat_rs.at[d], tile, step)
        copy.start()
        feat_copies.append(copy)

    l_noise.wait()
    for q in range(64):
        piece = noise[0, :, 128 * q : 128 * q + 128].astype(F32)
        noise_rows[pl.ds(64 + (q % 4) * 16 + q // 4, 8, stride=64), :] = piece
    noise_edge[0] = noise_rows[64:128, :].astype(BF16)
    noise_edge[1] = noise_rows[512:576, :].astype(BF16)
    noise_copies = []
    for side, offset in ((0, -1), (1, 1)):
        tile, step = near((offset, 0))
        copy = remote(noise_edge.at[side], noise_edge_in.at[side], noise_ss.at[side], noise_rs.at[side], tile, step)
        copy.start()
        noise_copies.append(copy)

    for load, weight, wide, flipped in (
        (l_latw, latw, latw4_t, latw4),
        (l_inw, inw, inw4, inw4_t),
        (l_outw, outw, outw4_t, outw4),
    ):
        load.wait()
        columns = weight.shape[1]
        wide[...] = jnp.zeros_like(wide)
        for j in range(4):
            wide[LAT * j : LAT * j + LAT, columns * j : columns * j + columns] = weight[...]
        flipped[...] = jnp.transpose(wide[...])

    chosen = time_ref[0]
    angle = ((jnp.full((8, 128), chosen, jnp.int32).astype(F32) + 1.0) / 1000.0 + 0.008) / 1.008 * (math.pi / 2.0)
    cosine = jnp.cos(angle)[0:1, :]
    sine = jnp.sin(angle)[0:1, :]
    l_table.wait()
    onehot = (lax.broadcasted_iota(jnp.int32, (16, table.shape[0]), 1) == chosen).astype(F32).astype(BF16)
    embed[...] = dot(onehot, table[...])[0:8]

    l_enc.wait()

    for d, copy in enumerate(feat_copies):
        copy.wait()
    for d, offsets in enumerate(AROUND):
        dt, ds = offsets
        valid = jnp.bool_(True)
        if dt:
            valid = (t < TILES - 1) if dt < 0 else (t > 0)
        if ds:
            beside = (s < STEPS - 1) if ds < 0 else (s > 0)
            valid = jnp.logical_and(valid, beside) if dt else beside
        if dt == 0:
            side = 0 if ds < 0 else 1
            taken = jnp.where(valid, edge_in[side].astype(F32), 0.0)
            first = 24 if ds < 0 else 6
            for i, part in enumerate(lane_tiles(taken)):
                for col in (0, 1):
                    grid[i, pl.ds(64 + first + col, 8, stride=32), :] = part[8 * col : 8 * col + 8]
        else:
            slot = d if d < 3 else d - 2
            for r in range(2):
                taken = jnp.where(valid, rows_in[slot, r].astype(F32), 0.0)
                row = (10 + r if dt < 0 else r) * 32
                for i, part in enumerate(lane_tiles(taken)):
                    if ds == 0:
                        grid[i, row + 8 : row + 24, :] = part
                    elif ds < 0:
                        grid[i, row + 24 : row + 32, :] = part[0:8]
                    else:
                        grid[i, row : row + 8, :] = part[8:16]

    def put_blocks(even, odd, index, value):
        even[index] = value.astype(BF16)
        odd[index] = value[8:].astype(BF16)

    for j in range(4):
        value = jnp.concatenate([grid[i, pl.ds(j, 96, stride=4), :] for i in range(2)], axis=1)
        put_blocks(blocks_even, blocks_odd, 1 + j, value)
        if j == 0:
            put_blocks(blocks_even, blocks_odd, 5, pltpu.roll(value, 95, 0))
        if j == 3:
            put_blocks(blocks_even, blocks_odd, 0, pltpu.roll(value, 1, 0))
    pieces = []
    for a in range(3):
        for b in range(3):
            if a == 1:
                window = blocks_odd[b : b + 4, 0:80, :]
            else:
                window = blocks_even[b : b + 4, 8 * a : 8 * a + 80, :]
            pieces.append(window.reshape(320, FEAT))
    pre = dot(jnp.concatenate(pieces, axis=1), enc[...].reshape(9 * FEAT, HID))
    pre_hidden[...] = pre
    hidden = (pre * sigmoid(pre)).astype(BF16)
    hidden = jnp.concatenate([hidden[80 * j : 80 * j + 80] for j in range(4)], axis=1)
    lat_tile[...] = dot(hidden, latw4[...])
    lat_pack[...] = jnp.zeros_like(lat_pack)
    for q in range(4):
        lat_pack[pl.ds(q, 10, stride=4), :] = lat_tile[pl.ds(2 + q, 10, stride=8), :]
    lat_send[...] = lat_pack[...].astype(BF16)

    def lat_copy(k):
        return remote(lat_send, lat_recv.at[k - 1], lat_ss.at[k - 1], lat_rs.at[k - 1], t, (s + k) % STEPS)

    def lat_start(k, _):
        lat_copy(k).start()
        return 0

    lax.fori_loop(1, STEPS, lat_start, 0)

    l_midw.wait()

    def flip_mid(k, _):
        mid_t[k] = jnp.transpose(midw[k])
        return 0

    lax.fori_loop(0, 9, flip_mid, 0)
    for side in (0, 1):
        noise_copies[side].wait()
    noise_rows[576:640, :] = noise_edge_in[0].astype(F32)
    noise_rows[0:64, :] = noise_edge_in[1].astype(F32)

    lat_flat[pl.ds(pl.multiple_of(s * 48, 16), 48), :] = lat_pack[...].astype(BF16).astype(F32)

    def lat_take(k, _):
        lat_copy(k).wait()
        source = (s - k + STEPS) % STEPS
        lat_flat[pl.ds(pl.multiple_of(source * 48, 16), 48), :] = lat_recv[k - 1].astype(F32)
        return 0

    lax.fori_loop(1, STEPS, lat_take, 0)

    def input_rows(pair, _):
        first = 2 * pair
        latent = [lat_flat[pl.ds((first + r) * 4 + q, 16, stride=48), :] for r in range(2) for q in range(4)]
        noisy = sine * noise_rows[pl.ds(pl.multiple_of(64 * first, 128), 128), :]
        noisy = (cosine * jnp.concatenate(latent, axis=0) + noisy).astype(BF16)
        gates = [
            jnp.where(jnp.logical_or(pair > 0, t > 0), 1.0, 0.0),
            jnp.where(jnp.logical_or(pair < 4, t < TILES - 1), 1.0, 0.0),
        ]
        for j in range(4):
            pre = dot(noisy, inw4[:, UNET * j : UNET * j + UNET]) + embed[0:1, :]
            sigma = sigmoid(pre)
            inner = pre * sigma
            slope = slope_of(pre, sigma)
            for r in range(2):
                own = inner[64 * r : 64 * r + 64] * gates[r]
                inner_ext[first + r, 64 + 64 * j : 128 + 64 * j, :] = own.astype(BF16)
                if j == 0:
                    inner_ext[first + r, 320:384, :] = shift_up(own).astype(BF16)
                if j == 3:
                    inner_ext[first + r, 0:64, :] = shift_down(own).astype(BF16)
                inner_slope[first + r, 64 * j : 64 * j + 64, :] = slope[64 * r : 64 * r + 64]
        return 0

    lax.fori_loop(0, 5, input_rows, 0)

    def flip_rows(pair):
        for r in range(2):
            row = 2 * pair + r
            flipped = jnp.transpose(inner_ext[row])
            inner_t[row] = flipped
            inner_tm[row] = flipped[:, 64:320]

    def by_class(value):
        rows = value.shape[0] // 256
        return jnp.concatenate(
            [
                jnp.concatenate([value[256 * r + 64 * j : 256 * r + 64 * j + 64] for j in range(4)], axis=1)
                for r in range(rows)
            ],
            axis=0,
        )

    def by_position(value):
        rows = value.shape[0] // 64
        return jnp.concatenate(
            [value[64 * r : 64 * r + 64, UNET * j : UNET * j + UNET] for r in range(rows) for j in range(4)], axis=0
        )

    def forward_conv(i):
        windows = [
            inner_ext[pl.ds(2 * i + a, 2), 64 * b : 64 * b + 256, :].reshape(512, UNET)
            for a in range(3)
            for b in range(3)
        ]
        pre_middle[...] = dot(jnp.concatenate(windows, axis=1), midw[...].reshape(9 * UNET, UNET))

    def forward_after(i):
        r = 2 * i
        pre = pre_middle[...]
        sigma = sigmoid(pre)
        own = inner_ext[pl.ds(r + 1, 2), 64:320, :].reshape(512, UNET)
        mixed = (own.astype(F32) + pre * sigma).astype(BF16)
        prediction = dot(by_class(mixed), outw4[...])
        own_noise = noise_rows[pl.ds(pl.multiple_of(64 + r * 64, 64), 128), :]
        error = ((prediction - own_noise) * (1.0 / math.sqrt(STEPS))).astype(BF16)
        pulled = by_position(dot(error, outw4_t[...]))
        back_mixed[pl.ds(pl.multiple_of(256 * r, 512), 512), :] = pulled
        back = pulled * slope_of(pre, sigma)
        for row in range(2):
            own = back[256 * row : 256 * row + 256]
            back_ext[r + 1 + row, 64:320, :] = own.astype(BF16)
            back_ext[r + 1 + row, 320:384, :] = shift_up(own[0:64]).astype(BF16)
            back_ext[r + 1 + row, 0:64, :] = shift_down(own[192:256]).astype(BF16)

    def forward_rows(i, _):
        forward_after((i + 3) % 4)
        forward_conv(i)
        flip_rows(i)
        return 0

    pre_middle[...] = jnp.zeros_like(pre_middle)
    lax.fori_loop(0, 4, forward_rows, 0)
    flip_rows(4)
    forward_after(3)

    halo_copies = []
    for side, offset in ((0, -1), (1, 1)):
        tile, step = near((offset, 0))
        src, dst = (1, 9) if side == 0 else (8, 0)
        src, dst = back_ext.at[src, pl.ds(64, 256)], back_ext.at[dst, pl.ds(64, 256)]
        copy = remote(src, dst, halo_ss.at[side], halo_rs.at[side], tile, step)
        copy.start()
        halo_copies.append(copy)

    def s1_copy(a):
        return remote(s1_send.at[a], s1_recv.at[a], s1_ss.at[a], s1_rs.at[a], t, s + 1 - 2 * core)

    def s1_start(a):
        for n in range(9):
            first = (n // 3) * UNET + n % 3 + 3 * (1 - core)
            block = jnp.concatenate([grad[a * 3 + i, pl.ds(first, 64, stride=6), :] for i in range(3)], axis=1)
            s1_send[a, 64 * n : 64 * n + 64, :] = block.astype(BF16)
        s1_copy(a).start()

    def axis_peer(a, k):
        if a == 0:
            there = (z + k) % 4
            return there, t, there * 4 + s % 4
        if a == 1:
            there = (x + k) % 4
            return there, y_hi * 4 + there, s
        there = (y + k) % 4
        return there, (there // 2) * 4 + x, z * 4 + (there % 2) * 2 + core

    def plane_rows(a, n, there):
        base = n * 64
        parts = []
        for i in range(3):
            if a == 0:
                half = [sum1[a * 3 + i, pl.ds(base + 2 * there + low, 8, stride=8), :] for low in (0, 1)]
                parts.append(jnp.concatenate(half, axis=0))
            elif a == 1:
                half = [
                    sum1[a * 3 + i, pl.ds(pl.multiple_of(base + high * 32 + there * 8, 8), 8), :] for high in (0, 1)
                ]
                parts.append(jnp.concatenate(half, axis=0))
            else:
                first = base + (there // 2) * 32 + there % 2
                parts.append(sum1[a * 3 + i, pl.ds(first, 16, stride=2), :])
        return jnp.concatenate(parts, axis=1)

    def s2_copy(a, k):
        _, tile, step = axis_peer(a, k)
        index = a * 3 + k - 1
        return remote(s2_send.at[index], s2_recv.at[index], s2_ss.at[index], s2_rs.at[index], tile, step)

    def s2_start(a):
        s1_copy(a).wait()

        def add(n, _):
            first = (n // 3) * UNET + n % 3 + 3 * core
            rows = pl.ds(pl.multiple_of(64 * n, 64), 64)
            got = s1_recv[a, rows, :].astype(F32)
            for i in range(3):
                own = grad[a * 3 + i, pl.ds(first, 64, stride=6), :]
                sum1[a * 3 + i, rows, :] = own + got[:, 128 * i : 128 * i + 128]
            return 0

        lax.fori_loop(0, 9, add, 0)

        def pack(n, _):
            for k in (1, 2, 3):
                rows = pl.ds(pl.multiple_of(16 * n, 16), 16)
                s2_send[a * 3 + k - 1, rows, :] = plane_rows(a, n, axis_peer(a, k)[0]).astype(BF16)
            return 0

        lax.fori_loop(0, 9, pack, 0)
        for k in (2, 1, 3):
            s2_copy(a, k).start()

    def plane_peer(a, k):
        if a == 0:
            mine = y_lo * 8 + t
            there = (mine + k) % 16
            return mine, there, there % 8, z * 4 + (there // 8) * 2 + core
        if a == 1:
            mine = y_hi * 8 + s // 2
            there = (mine + k) % 16
            return mine, there, (there // 8) * 4 + x, (there % 8) * 2 + core
        mine = x * 4 + z
        there = (mine + k) % 16
        return mine, there, y_hi * 4 + there // 4, (there % 4) * 4 + s % 4

    def s3_copy(a, k):
        _, _, tile, step = plane_peer(a, k)
        index = a * 15 + k - 1
        return remote(s3_send.at[index], s3_recv.at[index], s3_ss.at[index], s3_rs.at[index], tile, step)

    def s3_start(a):
        for k in range(1, 4):
            s2_copy(a, k).wait()
        mine = axis_peer(a, 0)[0]

        def add(n, _):
            rows = pl.ds(pl.multiple_of(16 * n, 16), 16)
            total = plane_rows(a, n, mine)
            for k in range(3):
                total = total + s2_recv[a * 3 + k, rows, :].astype(F32)
            for i, part in enumerate(lane_tiles(total)):
                sum2[a * 3 + i, rows, :] = part
            return 0

        lax.fori_loop(0, 9, add, 0)

        def send(k, _):
            there = plane_peer(a, k)[1]
            block = jnp.concatenate([sum2[a * 3 + i, pl.ds(there, 16, stride=16), :] for i in range(3)], axis=1)
            s3_send[a * 15 + k - 1] = block.astype(BF16)
            s3_copy(a, k).start()
            return 0

        lax.fori_loop(1, 16, send, 0)

    def finish(a):
        mine = plane_peer(a, 0)[0]
        own = jnp.concatenate([sum2[a * 3 + i, pl.ds(mine, 16, stride=16), :] for i in range(3)], axis=1)

        def add(k, total):
            s3_copy(a, k).wait()
            return total + s3_recv[a * 15 + k - 1].astype(F32)

        total = lax.fori_loop(1, 16, add, own) * (1.0 / math.sqrt(64 * 256))
        for b in range(3):
            mgrad_ref[3 * a + b] = total[3 * b : 3 * b + 3]

    sum2[...] = jnp.zeros_like(sum2)
    def weight_rows(a, _):
        taps = [
            jnp.concatenate([inner_t[r + a, :, 0:256] for r in range(8)], axis=1),
            jnp.concatenate([inner_tm[r + a] for r in range(8)], axis=1),
            jnp.concatenate([inner_t[r + a, :, 128:384] for r in range(8)], axis=1),
        ]
        result = dot(jnp.concatenate(taps, axis=0), back_ext[1:9, 64:320, :].reshape(2048, UNET))
        for i, part in enumerate(lane_tiles(result)):
            grad[a * 3 + i] = part
        for k in range(3):
            enc_t[3 * a + k] = jnp.transpose(enc[3 * a + k])
        s1_start(a)

        @pl.when(a == 1)
        def _():
            s2_start(0)

        @pl.when(a == 2)
        def _():
            s2_start(1)

        return 0

    lax.fori_loop(0, 3, weight_rows, 0)

    for row, copy in ((9, halo_copies[0]), (0, halo_copies[1])):
        copy.wait()
        back_ext[row, 320:384, :] = shift_up(back_ext[row, 64:128, :].astype(F32)).astype(BF16)
        back_ext[row, 0:64, :] = shift_down(back_ext[row, 256:320, :].astype(F32)).astype(BF16)

    @pl.when(t == 0)
    def _():
        back_ext[0] = jnp.zeros_like(back_ext[0])

    @pl.when(t == TILES - 1)
    def _():
        back_ext[9] = jnp.zeros_like(back_ext[9])

    def backward_after(i):
        r = 2 * i
        through = pre_middle[...] + back_mixed[pl.ds(pl.multiple_of(256 * r, 512), 512), :]
        back = (through * inner_slope[pl.ds(r + 1, 2)].reshape(512, UNET)).astype(BF16)
        back_part[pl.ds(pl.multiple_of(64 * r, 128), 128), :] = cosine * dot(by_class(back), inw4_t[...])

    def backward_rows(i, _):
        backward_after((i + 3) % 4)
        windows = [
            back_ext[pl.ds(2 * i + 2 - a, 2), 64 * (2 - b) : 64 * (2 - b) + 256, :].reshape(512, UNET)
            for a in range(3)
            for b in range(3)
        ]
        pre_middle[...] = dot(jnp.concatenate(windows, axis=1), mid_t[...].reshape(9 * UNET, UNET))

        @pl.when(i == 0)
        def _():
            s2_start(2)

        @pl.when(i == 2)
        def _():
            s3_start(0)

        return 0

    lax.fori_loop(0, 4, backward_rows, 0)
    backward_after(3)

    def part_copy(k):
        return remote(
            part_send.at[k - 1], part_recv.at[k - 1], part_ss.at[k - 1], part_rs.at[k - 1], t, (s + k) % STEPS
        )

    def part_start(k, _):
        part_send[k - 1] = back_part[pl.ds((s + k) % STEPS, 32, stride=16), :].astype(BF16)
        part_copy(k).start()
        return 0

    lax.fori_loop(1, STEPS, part_start, 0)

    s3_start(1)

    def part_add(k, total):
        part_copy(k).wait()
        return total + part_recv[k - 1].astype(F32)

    latent_round = lax.fori_loop(1, STEPS, part_add, back_part[pl.ds(s, 32, stride=16), :])
    round_send[...] = latent_round.astype(BF16)
    round_copies = []
    for d, offsets in enumerate(AROUND):
        tile, step = near(offsets)
        copy = remote(round_send, round_recv.at[d], round_ss.at[d], round_rs.at[d], tile, step)
        copy.start()
        round_copies.append(copy)

    s3_start(2)

    round_grid[...] = jnp.zeros_like(round_grid)
    round_pack[...] = round_send[...].astype(F32)
    for q in range(4):
        round_grid[pl.ds(10 + q, 8, stride=8), :] = round_pack[pl.ds(q, 8, stride=4), :]
    for d, (dt, ds) in enumerate(AROUND):
        round_copies[d].wait()
        valid = jnp.bool_(True)
        if dt:
            valid = (t < TILES - 1) if dt < 0 else (t > 0)
        if ds:
            beside = (s < STEPS - 1) if ds < 0 else (s > 0)
            valid = jnp.logical_and(valid, beside) if dt else beside
        round_pack[...] = jnp.where(valid, round_recv[d].astype(F32), 0.0)
        if dt == 0:
            q, place = (0, 6) if ds < 0 else (3, 1)
            round_grid[pl.ds(8 + place, 8, stride=8), :] = round_pack[pl.ds(q, 8, stride=4), :]
        else:
            source, row = (0, 72) if dt < 0 else (28, 0)
            if ds == 0:
                round_grid[row + 2 : row + 6, :] = round_pack[source : source + 4, :]
            else:
                q, place = (0, 6) if ds < 0 else (3, 1)
                round_grid[row + place : row + place + 1, :] = round_pack[source + q : source + q + 1, :]
    pulled = dot(round_grid[...].astype(BF16), latw4_t[...])
    for j in range(4):
        pre = pre_hidden[80 * j : 80 * j + 80, :]
        value = pulled[:, HID * j : HID * j + HID] * slope_of(pre, sigmoid(pre))
        put_blocks(hidden_even, hidden_odd, 1 + j, value)
        if j == 0:
            put_blocks(hidden_even, hidden_odd, 5, pltpu.roll(value, 79, 0))
        if j == 3:
            put_blocks(hidden_even, hidden_odd, 0, pltpu.roll(value, 1, 0))
    pieces = []
    for a in range(3):
        for b in range(3):
            if a == 1:
                window = hidden_odd[2 - b : 6 - b, 0:64, :]
            else:
                window = hidden_even[2 - b : 6 - b, 8 * (2 - a) : 8 * (2 - a) + 64, :]
            pieces.append(window.reshape(256, HID))
    result = dot(jnp.concatenate(pieces, axis=1), enc_t[...].reshape(9 * HID, FEAT))
    for j in range(4):
        for i, part in enumerate(lane_tiles(result[64 * j : 64 * j + 64])):
            out_grid[i, pl.ds(j, 64, stride=4), :] = part
    for r in range(8):
        for i in range(2):
            fgrad_ref[r, :, 128 * i : 128 * i + 128] = out_grid[i, r * 32 + 8 : r * 32 + 24, :]

    for a in range(3):
        finish(a)


def hand_over(fgrad_ref, mgrad_ref, fgrad_out, mgrad_out):
    fgrad_out[...] = fgrad_ref[...]
    mgrad_out[...] = mgrad_ref[...]


def per_device(
    features,
    encoder_weight,
    latent_weight,
    timesteps,
    noise_field,
    time_table,
    input_weight,
    middle_weight,
    output_weight,
):
    hbm = pl.BlockSpec(memory_space=pl.ANY)
    vmem = pl.BlockSpec(memory_space=pltpu.VMEM)
    dma = pltpu.SemaphoreType.DMA
    operands = (
        features,
        encoder_weight,
        latent_weight.T,
        noise_field,
        time_table,
        input_weight,
        middle_weight,
        output_weight.T,
    )
    scratch = [
        pltpu.VMEM((8, 16, FEAT), BF16),
        pltpu.VMEM((9, FEAT, HID), BF16),
        pltpu.VMEM((LAT, HID), BF16),
        pltpu.VMEM(noise_field.shape, BF16),
        pltpu.VMEM(time_table.shape, BF16),
        pltpu.VMEM((LAT, UNET), BF16),
        pltpu.VMEM((9, UNET, UNET), BF16),
        pltpu.VMEM((LAT, UNET), BF16),
        dma((8,)),
        pltpu.VMEM((9, HID, FEAT), BF16),
        pltpu.VMEM((9, UNET, UNET), BF16),
        pltpu.VMEM((4 * HID, 128), BF16),
        pltpu.VMEM((128, 4 * HID), BF16),
        pltpu.VMEM((128, 4 * UNET), BF16),
        pltpu.VMEM((4 * UNET, 128), BF16),
        pltpu.VMEM((4 * UNET, 128), BF16),
        pltpu.VMEM((128, 4 * UNET), BF16),
        pltpu.VMEM((8, UNET), F32),
        pltpu.VMEM((2, 16, FEAT), BF16),
        pltpu.VMEM((2, 16, FEAT), BF16),
        pltpu.VMEM((6, 2, 16, FEAT), BF16),
        pltpu.VMEM((2, 12 * 32, 128), F32),
        pltpu.VMEM((6, 96, FEAT), BF16),
        pltpu.VMEM((6, 88, FEAT), BF16),
        pltpu.VMEM((320, HID), F32),
        pltpu.VMEM((80, 128), F32),
        pltpu.VMEM((48, 128), F32),
        pltpu.VMEM((48, 128), BF16),
        pltpu.VMEM((15, 48, 128), BF16),
        pltpu.VMEM((16 * 48, 128), F32),
        pltpu.VMEM((640, 128), F32),
        pltpu.VMEM((2, 64, 128), BF16),
        pltpu.VMEM((2, 64, 128), BF16),
        pltpu.VMEM((10, 384, UNET), BF16),
        pltpu.VMEM((10, 256, UNET), F32),
        pltpu.VMEM((10, UNET, 384), BF16),
        pltpu.VMEM((10, UNET, 256), BF16),
        pltpu.VMEM((512, UNET), F32),
        pltpu.VMEM((2048, UNET), F32),
        pltpu.VMEM((10, 384, UNET), BF16),
        pltpu.VMEM((512, 128), F32),
        pltpu.VMEM((15, 32, 128), BF16),
        pltpu.VMEM((15, 32, 128), BF16),
        pltpu.VMEM((32, 128), F32),
        pltpu.VMEM((32, 128), BF16),
        pltpu.VMEM((8, 32, 128), BF16),
        pltpu.VMEM((80, 128), F32),
        pltpu.VMEM((6, 80, HID), BF16),
        pltpu.VMEM((6, 72, HID), BF16),
        pltpu.VMEM((2, 256, 128), F32),
        pltpu.VMEM((9, 3 * UNET, 128), F32),
        pltpu.VMEM((3, 576, UNET), BF16),
        pltpu.VMEM((3, 576, UNET), BF16),
        pltpu.VMEM((9, 576, 128), F32),
        pltpu.VMEM((9, 144, UNET), BF16),
        pltpu.VMEM((9, 144, UNET), BF16),
        pltpu.VMEM((9, 256, 128), F32),
        pltpu.VMEM((45, 16, UNET), BF16),
        pltpu.VMEM((45, 16, UNET), BF16),
        dma((8,)),
        dma((8,)),
        dma((2,)),
        dma((2,)),
        dma((15,)),
        dma((15,)),
        dma((2,)),
        dma((2,)),
        dma((15,)),
        dma((15,)),
        dma((8,)),
        dma((8,)),
        dma((3,)),
        dma((3,)),
        dma((9,)),
        dma((9,)),
        dma((45,)),
        dma((45,)),
    ]
    shapes = (
        jax.ShapeDtypeStruct((8, 16, FEAT), F32),
        jax.ShapeDtypeStruct((9, 3, UNET), F32),
    )
    results = pl.pallas_call(
        kernel,
        out_shape=shapes,
        in_specs=[pl.BlockSpec(memory_space=pltpu.SMEM)] + [hbm] * 8,
        out_specs=(vmem, vmem),
        scratch_shapes=scratch,
        compiler_params=pltpu.CompilerParams(
            collective_id=0, has_side_effects=True, vmem_limit_bytes=60 * 1024 * 1024
        ),
        cost_estimate=pl.CostEstimate(flops=18_000_000_000, bytes_accessed=8_000_000, transcendentals=3_000_000),
    )(timesteps, *operands)
    feature_grad, middle_grad = pl.pallas_call(
        hand_over,
        out_shape=shapes,
        in_specs=[vmem, vmem],
        out_specs=(vmem, vmem),
    )(*results)
    return feature_grad, jnp.transpose(middle_grad, (1, 0, 2))


def solution(mesh):
    in_specs = (
        P("tile", "step", None),
        P(),
        P(),
        P("step"),
        P("step", "tile", None),
        P(),
        P(),
        P(),
        P(),
    )
    out_specs = (P("tile", "step", None), P(("tile", "step"), None, None))
    return jax.shard_map(per_device, mesh=mesh, in_specs=in_specs, out_specs=out_specs, check_vma=False)
```

```python
import math

import jax
import jax.numpy as jnp
from jax import lax
from jax.experimental import pallas as pl
from jax.experimental.pallas import tpu as pltpu
from jax.sharding import PartitionSpec as P

F32 = jnp.float32
BF16 = jnp.bfloat16
MESH = pl.DeviceIdType.MESH

FEAT, HID, LAT, UNET = 256, 512, 32, 384
TILES, STEPS = 8, 16
AROUND = ((-1, -1), (-1, 0), (-1, 1), (0, -1), (0, 1), (1, -1), (1, 0), (1, 1))


def sigmoid(values):
    return 0.5 * jnp.tanh(0.5 * values) + 0.5


def slope_of(values, sigma):
    return sigma * (1.0 + values * (1.0 - sigma))


def dot(left, right):
    return jnp.dot(left, right, preferred_element_type=F32)


def lane_tiles(value):
    return [value[:, 128 * i : 128 * i + 128] for i in range(value.shape[1] // 128)]


def shift_down(block):
    last = pltpu.roll(block[48:64], 1, 0)
    rows = lax.broadcasted_iota(jnp.int32, last.shape, 0)
    return jnp.concatenate([jnp.where(rows == 0, 0.0, last), block[0:48]], axis=0)


def shift_up(block):
    first = pltpu.roll(block[0:16], 15, 0)
    rows = lax.broadcasted_iota(jnp.int32, first.shape, 0)
    return jnp.concatenate([block[16:64], jnp.where(rows == 15, 0.0, first)], axis=0)


def kernel(
    time_ref,
    feat_hbm,
    enc_hbm,
    latw_hbm,
    noise_hbm,
    table_hbm,
    inw_hbm,
    midw_hbm,
    outw_hbm,
    fgrad_ref,
    mgrad_ref,
    feat,
    enc,
    latw,
    noise,
    table,
    inw,
    midw,
    outw,
    in_sem,
    enc_t,
    mid_t,
    latw4,
    latw4_t,
    inw4,
    inw4_t,
    outw4,
    outw4_t,
    embed,
    edge,
    edge_in,
    rows_in,
    grid,
    blocks_even,
    blocks_odd,
    pre_hidden,
    lat_tile,
    lat_pack,
    lat_send,
    lat_recv,
    lat_flat,
    noise_rows,
    noise_edge,
    noise_edge_in,
    inner_ext,
    inner_slope,
    inner_t,
    inner_tm,
    pre_middle,
    back_mixed,
    back_ext,
    back_part,
    part_send,
    part_recv,
    round_pack,
    round_send,
    round_recv,
    round_grid,
    hidden_even,
    hidden_odd,
    out_grid,
    grad,
    s1_send,
    s1_recv,
    sum1,
    s2_send,
    s2_recv,
    sum2,
    s3_send,
    s3_recv,
    sum3,
    s4_send,
    s4_recv,
    feat_ss,
    feat_rs,
    noise_ss,
    noise_rs,
    lat_ss,
    lat_rs,
    halo_ss,
    halo_rs,
    part_ss,
    part_rs,
    round_ss,
    round_rs,
    s1_ss,
    s1_rs,
    s2_ss,
    s2_rs,
    s3_ss,
    s3_rs,
    s4_ss,
    s4_rs,
):
    t = lax.axis_index("tile")
    s = lax.axis_index("step")
    y_hi, x = t // 4, t % 4
    z, y_lo, core = s // 4, (s // 2) % 2, s % 2
    y = y_hi * 2 + y_lo

    def remote(src, dst, ss, rs, tile, step):
        return pltpu.make_async_remote_copy(
            src_ref=src, dst_ref=dst, send_sem=ss, recv_sem=rs, device_id=(tile, step), device_id_type=MESH
        )

    def near(offsets):
        return (t + offsets[0] + TILES) % TILES, (s + offsets[1] + STEPS) % STEPS

    loads = [
        pltpu.make_async_copy(src, dst, in_sem.at[i])
        for i, (src, dst) in enumerate(
            (
                (feat_hbm, feat),
                (noise_hbm, noise),
                (enc_hbm, enc),
                (latw_hbm, latw),
                (inw_hbm, inw),
                (outw_hbm, outw),
                (table_hbm, table),
                (midw_hbm, midw),
            )
        )
    ]
    for load in loads:
        load.start()
    l_feat, l_noise, l_enc, l_latw, l_inw, l_outw, l_table, l_midw = loads

    barrier = pltpu.get_barrier_semaphore()

    for k in range(1, STEPS):
        pl.semaphore_signal(barrier, inc=1, device_id=(t, (s + k) % STEPS), device_id_type=MESH)
    for k in range(1, TILES):
        pl.semaphore_signal(barrier, inc=1, device_id=((t + k) % TILES, s), device_id_type=MESH)
    for offsets in AROUND:
        if offsets[0] and offsets[1]:
            pl.semaphore_signal(barrier, inc=1, device_id=near(offsets), device_id_type=MESH)

    l_feat.wait()
    grid[...] = jnp.zeros_like(grid)
    for r in range(8):
        for i, part in enumerate(lane_tiles(feat[r].astype(F32))):
            grid[i, (r + 2) * 32 + 8 : (r + 2) * 32 + 24, :] = part
    for side, first in ((0, 8), (1, 22)):
        for i in range(2):
            pair = [grid[i, pl.ds(64 + first + col, 8, stride=32), :] for col in (0, 1)]
            edge[side, :, 128 * i : 128 * i + 128] = jnp.concatenate(pair, axis=0).astype(BF16)

    pl.semaphore_wait(barrier, STEPS - 1 + TILES - 1 + 4)

    feat_copies = []
    for d, offsets in enumerate(AROUND):
        tile, step = near(offsets)
        if offsets[0] == 0:
            side = 0 if offsets[1] < 0 else 1
            src, dst = edge.at[side], edge_in.at[side]
        else:
            slot = d if d < 3 else d - 2
            src, dst = feat.at[pl.ds(0 if offsets[0] < 0 else 6, 2)], rows_in.at[slot]
        copy = remote(src, dst, feat_ss.at[d], feat_rs.at[d], tile, step)
        copy.start()
        feat_copies.append(copy)

    l_noise.wait()
    for q in range(64):
        piece = noise[0, :, 128 * q : 128 * q + 128].astype(F32)
        noise_rows[pl.ds(64 + (q % 4) * 16 + q // 4, 8, stride=64), :] = piece
    noise_edge[0] = noise_rows[64:128, :].astype(BF16)
    noise_edge[1] = noise_rows[512:576, :].astype(BF16)
    noise_copies = []
    for side, offset in ((0, -1), (1, 1)):
        tile, step = near((offset, 0))
        copy = remote(noise_edge.at[side], noise_edge_in.at[side], noise_ss.at[side], noise_rs.at[side], tile, step)
        copy.start()
        noise_copies.append(copy)

    for load, weight, wide, flipped in (
        (l_latw, latw, latw4_t, latw4),
        (l_inw, inw, inw4, inw4_t),
        (l_outw, outw, outw4_t, outw4),
    ):
        load.wait()
        columns = weight.shape[1]
        wide[...] = jnp.zeros_like(wide)
        for j in range(4):
            wide[LAT * j : LAT * j + LAT, columns * j : columns * j + columns] = weight[...]
        if flipped is latw4:
            flipped[...] = jnp.transpose(wide[...])

    l_enc.wait()

    for d, copy in enumerate(feat_copies):
        copy.wait()
    for d, offsets in enumerate(AROUND):
        dt, ds = offsets
        valid = jnp.bool_(True)
        if dt:
            valid = (t < TILES - 1) if dt < 0 else (t > 0)
        if ds:
            beside = (s < STEPS - 1) if ds < 0 else (s > 0)
            valid = jnp.logical_and(valid, beside) if dt else beside
        if dt == 0:
            side = 0 if ds < 0 else 1
            taken = jnp.where(valid, edge_in[side].astype(F32), 0.0)
            first = 24 if ds < 0 else 6
            for i, part in enumerate(lane_tiles(taken)):
                for col in (0, 1):
                    grid[i, pl.ds(64 + first + col, 8, stride=32), :] = part[8 * col : 8 * col + 8]
        else:
            slot = d if d < 3 else d - 2
            for r in range(2):
                taken = jnp.where(valid, rows_in[slot, r].astype(F32), 0.0)
                row = (10 + r if dt < 0 else r) * 32
                for i, part in enumerate(lane_tiles(taken)):
                    if ds == 0:
                        grid[i, row + 8 : row + 24, :] = part
                    elif ds < 0:
                        grid[i, row + 24 : row + 32, :] = part[0:8]
                    else:
                        grid[i, row : row + 8, :] = part[8:16]

    def put_blocks(even, odd, index, value):
        even[index] = value.astype(BF16)
        odd[index] = value[8:].astype(BF16)

    for j in range(4):
        value = jnp.concatenate([grid[i, pl.ds(j, 96, stride=4), :] for i in range(2)], axis=1)
        put_blocks(blocks_even, blocks_odd, 1 + j, value)
        if j == 0:
            put_blocks(blocks_even, blocks_odd, 5, pltpu.roll(value, 95, 0))
        if j == 3:
            put_blocks(blocks_even, blocks_odd, 0, pltpu.roll(value, 1, 0))
    pieces = []
    for a in range(3):
        for b in range(3):
            if a == 1:
                window = blocks_odd[b : b + 4, 0:80, :]
            else:
                window = blocks_even[b : b + 4, 8 * a : 8 * a + 80, :]
            pieces.append(window.reshape(320, FEAT))
    pre = dot(jnp.concatenate(pieces, axis=1), enc[...].reshape(9 * FEAT, HID))
    pre_hidden[...] = pre
    hidden = (pre * sigmoid(pre)).astype(BF16)
    hidden = jnp.concatenate([hidden[80 * j : 80 * j + 80] for j in range(4)], axis=1)
    lat_tile[...] = dot(hidden, latw4[...])
    lat_pack[...] = jnp.zeros_like(lat_pack)
    for q in range(4):
        lat_pack[pl.ds(q, 10, stride=4), :] = lat_tile[pl.ds(2 + q, 10, stride=8), :]
    lat_send[...] = lat_pack[...].astype(BF16)

    def lat_copy(k):
        return remote(lat_send, lat_recv.at[k - 1], lat_ss.at[k - 1], lat_rs.at[k - 1], t, (s + k) % STEPS)

    for k in range(1, STEPS):
        lat_copy(k).start()

    inw4_t[...] = jnp.transpose(inw4[...])
    outw4[...] = jnp.transpose(outw4_t[...])
    chosen = time_ref[0]
    angle = ((jnp.full((8, 128), chosen, jnp.int32).astype(F32) + 1.0) / 1000.0 + 0.008) / 1.008 * (math.pi / 2.0)
    cosine = jnp.cos(angle)[0:1, :]
    sine = jnp.sin(angle)[0:1, :]
    l_table.wait()
    onehot = (lax.broadcasted_iota(jnp.int32, (16, table.shape[0]), 1) == chosen).astype(F32).astype(BF16)
    embed[...] = dot(onehot, table[...])[0:8]

    l_midw.wait()
    for side in (0, 1):
        noise_copies[side].wait()
    noise_rows[576:640, :] = noise_edge_in[0].astype(F32)
    noise_rows[0:64, :] = noise_edge_in[1].astype(F32)

    lat_flat[pl.ds(pl.multiple_of(s * 48, 16), 48), :] = lat_pack[...].astype(BF16).astype(F32)

    for k in range(1, STEPS):
        lat_copy(k).wait()
    for k in range(1, STEPS):
        source = (s - k + STEPS) % STEPS
        lat_flat[pl.ds(pl.multiple_of(source * 48, 16), 48), :] = lat_recv[k - 1].astype(F32)

    def input_rows(pair):
        first = 2 * pair
        latent = [lat_flat[pl.ds((first + r) * 4 + q, 16, stride=48), :] for r in range(2) for q in range(4)]
        noisy = cosine * jnp.concatenate(latent, axis=0) + sine * noise_rows[64 * first : 64 * first + 128, :]
        noisy = noisy.astype(BF16)
        for j in range(4):
            pre = dot(noisy, inw4[:, UNET * j : UNET * j + UNET]) + embed[0:1, :]
            sigma = sigmoid(pre)
            inner = pre * sigma
            slope = slope_of(pre, sigma)
            for r in range(2):
                row = first + r
                own = inner[64 * r : 64 * r + 64]
                if row == 0:
                    own = own * jnp.where(t > 0, 1.0, 0.0)
                if row == 9:
                    own = own * jnp.where(t < TILES - 1, 1.0, 0.0)
                inner_ext[row, 64 + 64 * j : 128 + 64 * j, :] = own.astype(BF16)
                if j == 0:
                    inner_ext[row, 320:384, :] = shift_up(own).astype(BF16)
                if j == 3:
                    inner_ext[row, 0:64, :] = shift_down(own).astype(BF16)
                if 0 < row < 9:
                    inner_slope[row - 1, 64 * j : 64 * j + 64, :] = slope[64 * r : 64 * r + 64]

    def flip_rows(pair):
        for row in (2 * pair, 2 * pair + 1):
            flipped = jnp.transpose(inner_ext[row])
            inner_t[row] = flipped
            inner_tm[row] = flipped[:, 64:320]

    def by_class(value):
        rows = value.shape[0] // 256
        return jnp.concatenate(
            [
                jnp.concatenate([value[256 * r + 64 * j : 256 * r + 64 * j + 64] for j in range(4)], axis=1)
                for r in range(rows)
            ],
            axis=0,
        )

    def by_position(value):
        rows = value.shape[0] // 64
        return jnp.concatenate(
            [value[64 * r : 64 * r + 64, UNET * j : UNET * j + UNET] for r in range(rows) for j in range(4)], axis=0
        )

    def forward_conv(i):
        windows = [
            inner_ext[2 * i + a : 2 * i + a + 2, 64 * b : 64 * b + 256, :].reshape(512, UNET)
            for a in range(3)
            for b in range(3)
        ]
        pre_middle[i % 2] = dot(jnp.concatenate(windows, axis=1), midw[...].reshape(9 * UNET, UNET))

    def forward_after(i):
        r = 2 * i
        pre = pre_middle[i % 2]
        sigma = sigmoid(pre)
        own = inner_ext[r + 1 : r + 3, 64:320, :].reshape(512, UNET)
        mixed = (own.astype(F32) + pre * sigma).astype(BF16)
        prediction = dot(by_class(mixed), outw4[...])
        own_noise = noise_rows[64 + r * 64 : 192 + r * 64, :]
        error = ((prediction - own_noise) * (1.0 / math.sqrt(STEPS))).astype(BF16)
        pulled = by_position(dot(error, outw4_t[...]))
        back_mixed[256 * r : 256 * r + 512, :] = pulled
        back = pulled * slope_of(pre, sigma)
        for row in range(2):
            own = back[256 * row : 256 * row + 256]
            back_ext[r + 1 + row, 64:320, :] = own.astype(BF16)
            back_ext[r + 1 + row, 320:384, :] = shift_up(own[0:64]).astype(BF16)
            back_ext[r + 1 + row, 0:64, :] = shift_down(own[192:256]).astype(BF16)

    halo_copies = []

    def halo_start(side):
        tile, step = near((2 * side - 1, 0))
        src, dst = ((1, 9), (8, 0))[side]
        src, dst = back_ext.at[src, pl.ds(64, 256)], back_ext.at[dst, pl.ds(64, 256)]
        copy = remote(src, dst, halo_ss.at[side], halo_rs.at[side], tile, step)
        copy.start()
        halo_copies.append(copy)

    input_rows(0)
    input_rows(1)
    for i in range(4):
        forward_conv(i)
        if i < 3:
            input_rows(i + 2)
        flip_rows(i)
        if i:
            forward_after(i - 1)
        if i == 1:
            halo_start(0)
    flip_rows(4)
    forward_after(3)
    halo_start(1)

    def s1_copy(a):
        return remote(s1_send.at[a], s1_recv.at[a], s1_ss.at[a], s1_rs.at[a], t, s + 1 - 2 * core)

    def s1_pack(a):
        for n in range(9):
            first = (n // 3) * UNET + n % 3 + 3 * (1 - core)
            block = jnp.concatenate([grad[a * 3 + i, pl.ds(first, 64, stride=6), :] for i in range(3)], axis=1)
            s1_send[a, 64 * n : 64 * n + 64, :] = block.astype(BF16)

    def s1_add(a):
        for n in range(9):
            first = (n // 3) * UNET + n % 3 + 3 * core
            got = s1_recv[a, 64 * n : 64 * n + 64, :].astype(F32)
            for i in range(3):
                own = grad[a * 3 + i, pl.ds(first, 64, stride=6), :]
                sum1[a * 3 + i, 64 * n : 64 * n + 64, :] = own + got[:, 128 * i : 128 * i + 128]

    def axis_peer(axis, k):
        if axis == "z":
            there = (z + k) % 4
            return there, t, there * 4 + s % 4
        if axis == "x":
            there = (x + k) % 4
            return there, y_hi * 4 + there, s
        there = (y + k) % 4
        return there, (there // 2) * 4 + x, z * 4 + (there % 2) * 2 + core

    first_axis, second_axis, third_axis = ("z", "x", "y"), ("x", "z", "z"), ("y", "y", "x")

    def plane_rows(a, b, c, there):
        base = (3 * b + c) * 64
        parts = []
        for i in range(3):
            ref = sum1.at[a * 3 + i]
            if b == 0:
                parts.append(
                    jnp.concatenate([ref[pl.ds(base + 2 * there + low, 8, stride=8), :] for low in (0, 1)], axis=0)
                )
            elif b == 1:
                rows = [pl.ds(pl.multiple_of(base + high * 32 + there * 8, 8), 8) for high in (0, 1)]
                parts.append(jnp.concatenate([ref[row, :] for row in rows], axis=0))
            else:
                parts.append(ref[pl.ds(base + (there // 2) * 32 + there % 2, 16, stride=2), :])
        return jnp.concatenate(parts, axis=1)

    def s2_copy(a, b, k):
        _, tile, step = axis_peer(first_axis[b], k)
        index = (a * 3 + b) * 3 + k - 1
        return remote(s2_send.at[index], s2_recv.at[index], s2_ss.at[index], s2_rs.at[index], tile, step)

    def s2_pack(a):
        for b in range(3):
            for k in range(1, 4):
                there = axis_peer(first_axis[b], k)[0]
                for c in range(3):
                    block = plane_rows(a, b, c, there).astype(BF16)
                    s2_send[(a * 3 + b) * 3 + k - 1, 16 * c : 16 * c + 16, :] = block

    def s2_start(a):
        for k in (2, 1, 3):
            for b in range(3):
                s2_copy(a, b, k).start()

    def s2_wait(a):
        for b in range(3):
            for k in range(1, 4):
                s2_copy(a, b, k).wait()

    def s2_add(a):
        for b in range(3):
            mine = axis_peer(first_axis[b], 0)[0]
            for c in range(3):
                total = plane_rows(a, b, c, mine)
                for k in range(3):
                    total = total + s2_recv[(a * 3 + b) * 3 + k, 16 * c : 16 * c + 16, :].astype(F32)
                row = 16 * (3 * a + c)
                for i, part in enumerate(lane_tiles(total)):
                    sum2[b * 3 + i, row : row + 16, :] = part

    def line_rows(b, there):
        parts = []
        for i in range(3):
            ref = sum2.at[b * 3 + i]
            if b == 1:
                parts.append(
                    jnp.concatenate([ref[pl.ds(2 * there + low, 24, stride=8), :] for low in (0, 1)], axis=0)
                )
            else:
                parts.append(ref[pl.ds(there, 48, stride=4), :])
        return jnp.concatenate(parts, axis=1)

    def s3_copy(b, k):
        _, tile, step = axis_peer(second_axis[b], k)
        index = b * 3 + k - 1
        return remote(s3_send.at[index], s3_recv.at[index], s3_ss.at[index], s3_rs.at[index], tile, step)

    def s3_start():
        for b in range(3):
            for k in range(1, 4):
                s3_send[b * 3 + k - 1] = line_rows(b, axis_peer(second_axis[b], k)[0]).astype(BF16)
        for b in range(3):
            for k in range(1, 4):
                s3_copy(b, k).start()

    def point_rows(b, there):
        if b == 0:
            rows = pl.ds((there % 2) * 2 + there // 2, 16, stride=4)
        elif b == 1:
            rows = pl.ds((there % 2) * 24 + there // 2, 16, stride=2)
        else:
            rows = pl.ds(there, 16, stride=4)
        return jnp.concatenate([sum3[b * 3 + i, rows, :] for i in range(3)], axis=1)

    def s4_copy(b, k):
        _, tile, step = axis_peer(third_axis[b], k)
        index = b * 3 + k - 1
        return remote(s4_send.at[index], s4_recv.at[index], s4_ss.at[index], s4_rs.at[index], tile, step)

    def s4_start():
        for b in range(3):
            for k in range(1, 4):
                s3_copy(b, k).wait()
        for b in range(3):
            total = line_rows(b, axis_peer(second_axis[b], 0)[0])
            for k in range(3):
                total = total + s3_recv[b * 3 + k].astype(F32)
            for i, part in enumerate(lane_tiles(total)):
                sum3[b * 3 + i, 0:48, :] = part
        for b in range(3):
            for k in range(1, 4):
                s4_send[b * 3 + k - 1] = point_rows(b, axis_peer(third_axis[b], k)[0]).astype(BF16)
        for b in range(3):
            for k in range(1, 4):
                s4_copy(b, k).start()

    def finish():
        for b in range(3):
            for k in range(1, 4):
                s4_copy(b, k).wait()
        for b in range(3):
            total = point_rows(b, axis_peer(third_axis[b], 0)[0])
            for k in range(3):
                total = total + s4_recv[b * 3 + k].astype(F32)
            total = total * (1.0 / math.sqrt(64 * 256))
            for a in range(3):
                mgrad_ref[3 * a + b] = total[3 * a : 3 * a + 3]

    def weight_product(a):
        taps = [
            jnp.concatenate([inner_t[r + a, :, 0:256] for r in range(8)], axis=1),
            jnp.concatenate([inner_tm[r + a] for r in range(8)], axis=1),
            jnp.concatenate([inner_t[r + a, :, 128:384] for r in range(8)], axis=1),
        ]
        result = dot(jnp.concatenate(taps, axis=0), back_ext[1:9, 64:320, :].reshape(2048, UNET))
        for i, part in enumerate(lane_tiles(result)):
            grad[a * 3 + i] = part

    sum2[...] = jnp.zeros_like(sum2)
    sum3[...] = jnp.zeros_like(sum3)
    for a in range(3):
        weight_product(a)
        for k in range(3 * a, 3 * a + 3):
            mid_t[k] = jnp.transpose(midw[k])
        if a:
            s1_pack(a - 1)
            s1_copy(a - 1).start()

    for row, copy in ((9, halo_copies[0]), (0, halo_copies[1])):
        copy.wait()
        back_ext[row, 320:384, :] = shift_up(back_ext[row, 64:128, :].astype(F32)).astype(BF16)
        back_ext[row, 0:64, :] = shift_down(back_ext[row, 256:320, :].astype(F32)).astype(BF16)

    @pl.when(t == 0)
    def _():
        back_ext[0] = jnp.zeros_like(back_ext[0])

    @pl.when(t == TILES - 1)
    def _():
        back_ext[9] = jnp.zeros_like(back_ext[9])

    def backward_conv(i):
        r = 2 * i
        windows = [
            back_ext[r + 2 - a : r + 4 - a, 64 * (2 - b) : 64 * (2 - b) + 256, :].reshape(512, UNET)
            for a in range(3)
            for b in range(3)
        ]
        pre_middle[i % 2] = dot(jnp.concatenate(windows, axis=1), mid_t[...].reshape(9 * UNET, UNET))

    def backward_after(i):
        r = 2 * i
        through = pre_middle[i % 2] + back_mixed[256 * r : 256 * r + 512, :]
        back = (through * inner_slope[r : r + 2].reshape(512, UNET)).astype(BF16)
        back_part[64 * r : 64 * r + 128, :] = cosine * dot(by_class(back), inw4_t[...])

    def flip_enc(first, last):
        for k in range(first, last):
            enc_t[k] = jnp.transpose(enc[k])

    s1_copy(0).wait()
    backward_conv(0)
    s1_pack(2)
    s1_add(0)
    s2_pack(0)
    flip_enc(0, 3)
    s1_copy(2).start()
    s2_start(0)

    s1_copy(1).wait()
    backward_conv(1)
    backward_after(0)
    s1_add(1)
    s2_pack(1)
    flip_enc(3, 6)
    s2_start(1)

    s1_copy(2).wait()
    backward_conv(2)
    backward_after(1)
    s1_add(2)
    s2_pack(2)
    flip_enc(6, 9)
    s2_start(2)

    s2_wait(0)
    backward_conv(3)
    backward_after(2)
    s2_add(0)
    backward_after(3)

    def part_copy(k):
        return remote(
            part_send.at[k - 1], part_recv.at[k - 1], part_ss.at[k - 1], part_rs.at[k - 1], t, (s + k) % STEPS
        )

    for k in range(1, STEPS):
        part_send[k - 1] = back_part[pl.ds((s + k) % STEPS, 32, stride=16), :].astype(BF16)
    for k in range(1, STEPS):
        part_copy(k).start()

    for a in (1, 2):
        s2_wait(a)
        s2_add(a)
    s3_start()

    for k in range(1, STEPS):
        part_copy(k).wait()
    latent_round = back_part[pl.ds(s, 32, stride=16), :]
    for k in range(1, STEPS):
        latent_round = latent_round + part_recv[k - 1].astype(F32)
    round_send[...] = latent_round.astype(BF16)
    round_copies = []
    for d, offsets in enumerate(AROUND):
        tile, step = near(offsets)
        copy = remote(round_send, round_recv.at[d], round_ss.at[d], round_rs.at[d], tile, step)
        copy.start()
        round_copies.append(copy)

    s4_start()

    round_grid[...] = jnp.zeros_like(round_grid)
    round_pack[...] = round_send[...].astype(F32)
    for q in range(4):
        round_grid[pl.ds(10 + q, 8, stride=8), :] = round_pack[pl.ds(q, 8, stride=4), :]
    for d, (dt, ds) in enumerate(AROUND):
        round_copies[d].wait()
        valid = jnp.bool_(True)
        if dt:
            valid = (t < TILES - 1) if dt < 0 else (t > 0)
        if ds:
            beside = (s < STEPS - 1) if ds < 0 else (s > 0)
            valid = jnp.logical_and(valid, beside) if dt else beside
        round_pack[...] = jnp.where(valid, round_recv[d].astype(F32), 0.0)
        if dt == 0:
            q, place = (0, 6) if ds < 0 else (3, 1)
            round_grid[pl.ds(8 + place, 8, stride=8), :] = round_pack[pl.ds(q, 8, stride=4), :]
        else:
            source, row = (0, 72) if dt < 0 else (28, 0)
            if ds == 0:
                round_grid[row + 2 : row + 6, :] = round_pack[source : source + 4, :]
            else:
                q, place = (0, 6) if ds < 0 else (3, 1)
                round_grid[row + place : row + place + 1, :] = round_pack[source + q : source + q + 1, :]
    pulled = dot(round_grid[...].astype(BF16), latw4_t[...])
    for j in range(4):
        pre = pre_hidden[80 * j : 80 * j + 80, :]
        value = pulled[:, HID * j : HID * j + HID] * slope_of(pre, sigmoid(pre))
        put_blocks(hidden_even, hidden_odd, 1 + j, value)
        if j == 0:
            put_blocks(hidden_even, hidden_odd, 5, pltpu.roll(value, 79, 0))
        if j == 3:
            put_blocks(hidden_even, hidden_odd, 0, pltpu.roll(value, 1, 0))
    pieces = []
    for a in range(3):
        for b in range(3):
            if a == 1:
                window = hidden_odd[2 - b : 6 - b, 0:64, :]
            else:
                window = hidden_even[2 - b : 6 - b, 8 * (2 - a) : 8 * (2 - a) + 64, :]
            pieces.append(window.reshape(256, HID))
    result = dot(jnp.concatenate(pieces, axis=1), enc_t[...].reshape(9 * HID, FEAT))
    for j in range(4):
        for i, part in enumerate(lane_tiles(result[64 * j : 64 * j + 64])):
            out_grid[i, pl.ds(j, 64, stride=4), :] = part
    for r in range(8):
        for i in range(2):
            fgrad_ref[r, :, 128 * i : 128 * i + 128] = out_grid[i, r * 32 + 8 : r * 32 + 24, :]

    finish()


def hand_over(fgrad_ref, mgrad_ref, fgrad_out, mgrad_out):
    fgrad_out[...] = fgrad_ref[...]
    mgrad_out[...] = mgrad_ref[...]


def per_device(
    features,
    encoder_weight,
    latent_weight,
    timesteps,
    noise_field,
    time_table,
    input_weight,
    middle_weight,
    output_weight,
):
    hbm = pl.BlockSpec(memory_space=pl.ANY)
    vmem = pl.BlockSpec(memory_space=pltpu.VMEM)
    dma = pltpu.SemaphoreType.DMA
    operands = (
        features,
        encoder_weight,
        latent_weight.T,
        noise_field,
        time_table,
        input_weight,
        middle_weight,
        output_weight.T,
    )
    scratch = [
        pltpu.VMEM((8, 16, FEAT), BF16),
        pltpu.VMEM((9, FEAT, HID), BF16),
        pltpu.VMEM((LAT, HID), BF16),
        pltpu.VMEM(noise_field.shape, BF16),
        pltpu.VMEM(time_table.shape, BF16),
        pltpu.VMEM((LAT, UNET), BF16),
        pltpu.VMEM((9, UNET, UNET), BF16),
        pltpu.VMEM((LAT, UNET), BF16),
        dma((8,)),
        pltpu.VMEM((9, HID, FEAT), BF16),
        pltpu.VMEM((9, UNET, UNET), BF16),
        pltpu.VMEM((4 * HID, 128), BF16),
        pltpu.VMEM((128, 4 * HID), BF16),
        pltpu.VMEM((128, 4 * UNET), BF16),
        pltpu.VMEM((4 * UNET, 128), BF16),
        pltpu.VMEM((4 * UNET, 128), BF16),
        pltpu.VMEM((128, 4 * UNET), BF16),
        pltpu.VMEM((8, UNET), F32),
        pltpu.VMEM((2, 16, FEAT), BF16),
        pltpu.VMEM((2, 16, FEAT), BF16),
        pltpu.VMEM((6, 2, 16, FEAT), BF16),
        pltpu.VMEM((2, 12 * 32, 128), F32),
        pltpu.VMEM((6, 96, FEAT), BF16),
        pltpu.VMEM((6, 88, FEAT), BF16),
        pltpu.VMEM((320, HID), F32),
        pltpu.VMEM((80, 128), F32),
        pltpu.VMEM((48, 128), F32),
        pltpu.VMEM((48, 128), BF16),
        pltpu.VMEM((15, 48, 128), BF16),
        pltpu.VMEM((16 * 48, 128), F32),
        pltpu.VMEM((640, 128), F32),
        pltpu.VMEM((2, 64, 128), BF16),
        pltpu.VMEM((2, 64, 128), BF16),
        pltpu.VMEM((10, 384, UNET), BF16),
        pltpu.VMEM((8, 256, UNET), F32),
        pltpu.VMEM((10, UNET, 384), BF16),
        pltpu.VMEM((10, UNET, 256), BF16),
        pltpu.VMEM((2, 512, UNET), F32),
        pltpu.VMEM((2048, UNET), F32),
        pltpu.VMEM((10, 384, UNET), BF16),
        pltpu.VMEM((512, 128), F32),
        pltpu.VMEM((15, 32, 128), BF16),
        pltpu.VMEM((15, 32, 128), BF16),
        pltpu.VMEM((32, 128), F32),
        pltpu.VMEM((32, 128), BF16),
        pltpu.VMEM((8, 32, 128), BF16),
        pltpu.VMEM((80, 128), F32),
        pltpu.VMEM((6, 80, HID), BF16),
        pltpu.VMEM((6, 72, HID), BF16),
        pltpu.VMEM((2, 256, 128), F32),
        pltpu.VMEM((9, 3 * UNET, 128), F32),
        pltpu.VMEM((3, 576, UNET), BF16),
        pltpu.VMEM((3, 576, UNET), BF16),
        pltpu.VMEM((9, 576, 128), F32),
        pltpu.VMEM((27, 48, UNET), BF16),
        pltpu.VMEM((27, 48, UNET), BF16),
        pltpu.VMEM((9, 256, 128), F32),
        pltpu.VMEM((9, 48, UNET), BF16),
        pltpu.VMEM((9, 48, UNET), BF16),
        pltpu.VMEM((9, 64, 128), F32),
        pltpu.VMEM((9, 16, UNET), BF16),
        pltpu.VMEM((9, 16, UNET), BF16),
        dma((8,)),
        dma((8,)),
        dma((2,)),
        dma((2,)),
        dma((15,)),
        dma((15,)),
        dma((2,)),
        dma((2,)),
        dma((15,)),
        dma((15,)),
        dma((8,)),
        dma((8,)),
        dma((3,)),
        dma((3,)),
        dma((27,)),
        dma((27,)),
        dma((9,)),
        dma((9,)),
        dma((9,)),
        dma((9,)),
    ]
    shapes = (
        jax.ShapeDtypeStruct((8, 16, FEAT), F32),
        jax.ShapeDtypeStruct((9, 3, UNET), F32),
    )
    results = pl.pallas_call(
        kernel,
        out_shape=shapes,
        in_specs=[pl.BlockSpec(memory_space=pltpu.SMEM)] + [hbm] * 8,
        out_specs=(vmem, vmem),
        scratch_shapes=scratch,
        compiler_params=pltpu.CompilerParams(
            collective_id=0, has_side_effects=True, vmem_limit_bytes=60 * 1024 * 1024
        ),
        cost_estimate=pl.CostEstimate(flops=18_000_000_000, bytes_accessed=8_000_000, transcendentals=3_000_000),
    )(timesteps, *operands)
    feature_grad, middle_grad = pl.pallas_call(
        hand_over,
        out_shape=shapes,
        in_specs=[vmem, vmem],
        out_specs=(vmem, vmem),
    )(*results)
    return feature_grad, jnp.transpose(middle_grad, (1, 0, 2))


def solution(mesh):
    in_specs = (
        P("tile", "step", None),
        P(),
        P(),
        P("step"),
        P("step", "tile", None),
        P(),
        P(),
        P(),
        P(),
    )
    out_specs = (P("tile", "step", None), P(("tile", "step"), None, None))
    return jax.shard_map(per_device, mesh=mesh, in_specs=in_specs, out_specs=out_specs, check_vma=False)
```

```python
import math

import jax
import jax.numpy as jnp
from jax import lax
from jax.experimental import pallas as pl
from jax.experimental.pallas import tpu as pltpu
from jax.sharding import PartitionSpec as P

F32 = jnp.float32
BF16 = jnp.bfloat16
MESH = pl.DeviceIdType.MESH

FEAT, HID, LAT, UNET = 256, 512, 32, 384
TILES, STEPS = 8, 16
AROUND = ((-1, -1), (-1, 0), (-1, 1), (0, -1), (0, 1), (1, -1), (1, 0), (1, 1))


def sigmoid(values):
    return 0.5 * jnp.tanh(0.5 * values) + 0.5


def slope_of(values, sigma):
    return sigma * (1.0 + values * (1.0 - sigma))


def dot(left, right):
    return jnp.dot(left, right, preferred_element_type=F32)


def lane_tiles(value):
    return [value[:, 128 * i : 128 * i + 128] for i in range(value.shape[1] // 128)]


def shift_down(block):
    last = pltpu.roll(block[48:64], 1, 0)
    rows = lax.broadcasted_iota(jnp.int32, last.shape, 0)
    return jnp.concatenate([jnp.where(rows == 0, 0.0, last), block[0:48]], axis=0)


def shift_up(block):
    first = pltpu.roll(block[0:16], 15, 0)
    rows = lax.broadcasted_iota(jnp.int32, first.shape, 0)
    return jnp.concatenate([block[16:64], jnp.where(rows == 15, 0.0, first)], axis=0)


def kernel(
    time_ref,
    feat_hbm,
    enc_hbm,
    latw_hbm,
    noise_hbm,
    table_hbm,
    inw_hbm,
    midw_hbm,
    outw_hbm,
    fgrad_ref,
    mgrad_ref,
    feat,
    enc,
    latw,
    noise,
    table,
    inw,
    midw,
    outw,
    in_sem,
    enc_t,
    mid_t,
    latw4,
    latw4_t,
    inw4,
    inw4_t,
    outw4,
    outw4_t,
    embed,
    edge,
    edge_in,
    rows_in,
    grid,
    blocks_even,
    blocks_odd,
    pre_hidden,
    lat_tile,
    lat_pack,
    lat_send,
    lat_recv,
    lat_flat,
    noise_rows,
    noise_edge,
    noise_edge_in,
    inner_ext,
    inner_slope,
    inner_t,
    inner_tm,
    pre_middle,
    back_mixed,
    back_ext,
    back_part,
    part_send,
    part_recv,
    round_pack,
    round_send,
    round_recv,
    round_grid,
    hidden_even,
    hidden_odd,
    out_grid,
    grad,
    s1_send,
    s1_recv,
    sum1,
    s2_send,
    s2_recv,
    sum2,
    s3_send,
    s3_recv,
    sum3,
    s4_send,
    s4_recv,
    feat_ss,
    feat_rs,
    noise_ss,
    noise_rs,
    lat_ss,
    lat_rs,
    halo_ss,
    halo_rs,
    part_ss,
    part_rs,
    round_ss,
    round_rs,
    s1_ss,
    s1_rs,
    s2_ss,
    s2_rs,
    s3_ss,
    s3_rs,
    s4_ss,
    s4_rs,
):
    t = lax.axis_index("tile")
    s = lax.axis_index("step")
    y_hi, x = t // 4, t % 4
    z, y_lo, core = s // 4, (s // 2) % 2, s % 2
    y = y_hi * 2 + y_lo

    def remote(src, dst, ss, rs, tile, step):
        return pltpu.make_async_remote_copy(
            src_ref=src, dst_ref=dst, send_sem=ss, recv_sem=rs, device_id=(tile, step), device_id_type=MESH
        )

    def near(offsets):
        return (t + offsets[0] + TILES) % TILES, (s + offsets[1] + STEPS) % STEPS

    loads = [
        pltpu.make_async_copy(src, dst, in_sem.at[i])
        for i, (src, dst) in enumerate(
            (
                (feat_hbm, feat),
                (noise_hbm, noise),
                (enc_hbm, enc),
                (latw_hbm, latw),
                (inw_hbm, inw),
                (outw_hbm, outw),
                (table_hbm, table),
                (midw_hbm, midw),
            )
        )
    ]
    for load in loads:
        load.start()
    l_feat, l_noise, l_enc, l_latw, l_inw, l_outw, l_table, l_midw = loads

    barrier = pltpu.get_barrier_semaphore()

    for k in range(1, STEPS):
        pl.semaphore_signal(barrier, inc=1, device_id=(t, (s + k) % STEPS), device_id_type=MESH)
    for k in range(1, TILES):
        pl.semaphore_signal(barrier, inc=1, device_id=((t + k) % TILES, s), device_id_type=MESH)
    for offsets in AROUND:
        if offsets[0] and offsets[1]:
            pl.semaphore_signal(barrier, inc=1, device_id=near(offsets), device_id_type=MESH)

    l_feat.wait()
    grid[...] = jnp.zeros_like(grid)
    for r in range(8):
        for i, part in enumerate(lane_tiles(feat[r].astype(F32))):
            grid[i, (r + 2) * 32 + 8 : (r + 2) * 32 + 24, :] = part
    for side, first in ((0, 8), (1, 22)):
        for i in range(2):
            pair = [grid[i, pl.ds(64 + first + col, 8, stride=32), :] for col in (0, 1)]
            edge[side, :, 128 * i : 128 * i + 128] = jnp.concatenate(pair, axis=0).astype(BF16)

    pl.semaphore_wait(barrier, STEPS - 1 + TILES - 1 + 4)

    feat_copies = []
    for d, offsets in enumerate(AROUND):
        tile, step = near(offsets)
        if offsets[0] == 0:
            side = 0 if offsets[1] < 0 else 1
            src, dst = edge.at[side], edge_in.at[side]
        else:
            slot = d if d < 3 else d - 2
            src, dst = feat.at[pl.ds(0 if offsets[0] < 0 else 6, 2)], rows_in.at[slot]
        copy = remote(src, dst, feat_ss.at[d], feat_rs.at[d], tile, step)
        copy.start()
        feat_copies.append(copy)

    l_noise.wait()
    for q in range(64):
        piece = noise[0, :, 128 * q : 128 * q + 128].astype(F32)
        noise_rows[pl.ds(64 + (q % 4) * 16 + q // 4, 8, stride=64), :] = piece
    noise_edge[0] = noise_rows[64:128, :].astype(BF16)
    noise_edge[1] = noise_rows[512:576, :].astype(BF16)
    noise_copies = []
    for side, offset in ((0, -1), (1, 1)):
        tile, step = near((offset, 0))
        copy = remote(noise_edge.at[side], noise_edge_in.at[side], noise_ss.at[side], noise_rs.at[side], tile, step)
        copy.start()
        noise_copies.append(copy)

    for load, weight, wide, flipped in (
        (l_latw, latw, latw4_t, latw4),
        (l_inw, inw, inw4, inw4_t),
        (l_outw, outw, outw4_t, outw4),
    ):
        load.wait()
        columns = weight.shape[1]
        wide[...] = jnp.zeros_like(wide)
        for j in range(4):
            wide[LAT * j : LAT * j + LAT, columns * j : columns * j + columns] = weight[...]
        if flipped is latw4:
            flipped[...] = jnp.transpose(wide[...])

    l_enc.wait()

    for d, copy in enumerate(feat_copies):
        copy.wait()
    for d, offsets in enumerate(AROUND):
        dt, ds = offsets
        valid = jnp.bool_(True)
        if dt:
            valid = (t < TILES - 1) if dt < 0 else (t > 0)
        if ds:
            beside = (s < STEPS - 1) if ds < 0 else (s > 0)
            valid = jnp.logical_and(valid, beside) if dt else beside
        if dt == 0:
            side = 0 if ds < 0 else 1
            taken = jnp.where(valid, edge_in[side].astype(F32), 0.0)
            first = 24 if ds < 0 else 6
            for i, part in enumerate(lane_tiles(taken)):
                for col in (0, 1):
                    grid[i, pl.ds(64 + first + col, 8, stride=32), :] = part[8 * col : 8 * col + 8]
        else:
            slot = d if d < 3 else d - 2
            for r in range(2):
                taken = jnp.where(valid, rows_in[slot, r].astype(F32), 0.0)
                row = (10 + r if dt < 0 else r) * 32
                for i, part in enumerate(lane_tiles(taken)):
                    if ds == 0:
                        grid[i, row + 8 : row + 24, :] = part
                    elif ds < 0:
                        grid[i, row + 24 : row + 32, :] = part[0:8]
                    else:
                        grid[i, row : row + 8, :] = part[8:16]

    def put_blocks(even, odd, index, value):
        even[index] = value.astype(BF16)
        odd[index] = value[8:].astype(BF16)

    for j in range(4):
        value = jnp.concatenate([grid[i, pl.ds(j, 96, stride=4), :] for i in range(2)], axis=1)
        put_blocks(blocks_even, blocks_odd, 1 + j, value)
        if j == 0:
            put_blocks(blocks_even, blocks_odd, 5, pltpu.roll(value, 95, 0))
        if j == 3:
            put_blocks(blocks_even, blocks_odd, 0, pltpu.roll(value, 1, 0))
    pieces = []
    for a in range(3):
        for b in range(3):
            if a == 1:
                window = blocks_odd[b : b + 4, 0:80, :]
            else:
                window = blocks_even[b : b + 4, 8 * a : 8 * a + 80, :]
            pieces.append(window.reshape(320, FEAT))
    pre = dot(jnp.concatenate(pieces, axis=1), enc[...].reshape(9 * FEAT, HID))
    pre_hidden[...] = pre
    hidden = (pre * sigmoid(pre)).astype(BF16)
    hidden = jnp.concatenate([hidden[80 * j : 80 * j + 80] for j in range(4)], axis=1)
    lat_tile[...] = dot(hidden, latw4[...])
    lat_pack[...] = jnp.zeros_like(lat_pack)
    for q in range(4):
        lat_pack[pl.ds(q, 10, stride=4), :] = lat_tile[pl.ds(2 + q, 10, stride=8), :]
    lat_send[...] = lat_pack[...].astype(BF16)

    def lat_copy(k):
        return remote(lat_send, lat_recv.at[k - 1], lat_ss.at[k - 1], lat_rs.at[k - 1], t, (s + k) % STEPS)

    for k in range(1, STEPS):
        lat_copy(k).start()

    inw4_t[...] = jnp.transpose(inw4[...])
    outw4[...] = jnp.transpose(outw4_t[...])
    chosen = time_ref[0]
    angle = ((jnp.full((8, 128), chosen, jnp.int32).astype(F32) + 1.0) / 1000.0 + 0.008) / 1.008 * (math.pi / 2.0)
    cosine = jnp.cos(angle)[0:1, :]
    sine = jnp.sin(angle)[0:1, :]
    l_table.wait()
    onehot = (lax.broadcasted_iota(jnp.int32, (16, table.shape[0]), 1) == chosen).astype(F32).astype(BF16)
    embed[...] = dot(onehot, table[...])[0:8]

    l_midw.wait()
    for side in (0, 1):
        noise_copies[side].wait()
    noise_rows[576:640, :] = noise_edge_in[0].astype(F32)
    noise_rows[0:64, :] = noise_edge_in[1].astype(F32)

    lat_flat[pl.ds(pl.multiple_of(s * 48, 16), 48), :] = lat_pack[...].astype(BF16).astype(F32)

    for k in range(1, STEPS):
        lat_copy(k).wait()
    for k in range(1, STEPS):
        source = (s - k + STEPS) % STEPS
        lat_flat[pl.ds(pl.multiple_of(source * 48, 16), 48), :] = lat_recv[k - 1].astype(F32)

    def input_rows(first, count):
        latent = [lat_flat[pl.ds((first + r) * 4 + q, 16, stride=48), :] for r in range(count) for q in range(4)]
        noisy = sine * noise_rows[64 * first : 64 * (first + count), :]
        noisy = (cosine * jnp.concatenate(latent, axis=0) + noisy).astype(BF16)
        for j in range(4):
            pre = dot(noisy, inw4[:, UNET * j : UNET * j + UNET]) + embed[0:1, :]
            sigma = sigmoid(pre)
            inner = pre * sigma
            slope = slope_of(pre, sigma)
            for r in range(count):
                row = first + r
                own = inner[64 * r : 64 * r + 64]
                if row == 0:
                    own = own * jnp.where(t > 0, 1.0, 0.0)
                if row == 9:
                    own = own * jnp.where(t < TILES - 1, 1.0, 0.0)
                inner_ext[row, 64 + 64 * j : 128 + 64 * j, :] = own.astype(BF16)
                if j == 0:
                    inner_ext[row, 320:384, :] = shift_up(own).astype(BF16)
                if j == 3:
                    inner_ext[row, 0:64, :] = shift_down(own).astype(BF16)
                if 0 < row < 9:
                    inner_slope[row - 1, 64 * j : 64 * j + 64, :] = slope[64 * r : 64 * r + 64]

    def flip_rows(first, last):
        for row in range(first, last):
            flipped = jnp.transpose(inner_ext[row])
            inner_t[row] = flipped
            inner_tm[row] = flipped[:, 64:320]

    def by_class(value):
        rows = value.shape[0] // 256
        return jnp.concatenate(
            [
                jnp.concatenate([value[256 * r + 64 * j : 256 * r + 64 * j + 64] for j in range(4)], axis=1)
                for r in range(rows)
            ],
            axis=0,
        )

    def by_position(value):
        rows = value.shape[0] // 64
        return jnp.concatenate(
            [value[64 * r : 64 * r + 64, UNET * j : UNET * j + UNET] for r in range(rows) for j in range(4)], axis=0
        )

    def forward_conv(i):
        windows = [
            inner_ext[4 * i + a : 4 * i + a + 4, 64 * b : 64 * b + 256, :].reshape(1024, UNET)
            for a in range(3)
            for b in range(3)
        ]
        pre_middle[i] = dot(jnp.concatenate(windows, axis=1), midw[...].reshape(9 * UNET, UNET))

    def forward_after(i):
        r = 4 * i
        pre = pre_middle[i]
        sigma = sigmoid(pre)
        own = inner_ext[r + 1 : r + 5, 64:320, :].reshape(1024, UNET)
        mixed = (own.astype(F32) + pre * sigma).astype(BF16)
        prediction = dot(by_class(mixed), outw4[...])
        own_noise = noise_rows[64 + r * 64 : 320 + r * 64, :]
        error = ((prediction - own_noise) * (1.0 / math.sqrt(STEPS))).astype(BF16)
        pulled = by_position(dot(error, outw4_t[...]))
        back_mixed[256 * r : 256 * r + 1024, :] = pulled
        back = pulled * slope_of(pre, sigma)
        for row in range(4):
            own = back[256 * row : 256 * row + 256]
            back_ext[r + 1 + row, 64:320, :] = own.astype(BF16)
            back_ext[r + 1 + row, 320:384, :] = shift_up(own[0:64]).astype(BF16)
            back_ext[r + 1 + row, 0:64, :] = shift_down(own[192:256]).astype(BF16)

    halo_copies = []

    def halo_start(side):
        tile, step = near((2 * side - 1, 0))
        src, dst = ((1, 9), (8, 0))[side]
        src, dst = back_ext.at[src, pl.ds(64, 256)], back_ext.at[dst, pl.ds(64, 256)]
        copy = remote(src, dst, halo_ss.at[side], halo_rs.at[side], tile, step)
        copy.start()
        halo_copies.append(copy)

    input_rows(0, 6)
    forward_conv(0)
    input_rows(6, 4)
    flip_rows(0, 5)
    forward_conv(1)
    forward_after(0)
    flip_rows(5, 10)
    halo_start(0)
    forward_after(1)
    halo_start(1)

    def s1_copy(a):
        return remote(s1_send.at[a], s1_recv.at[a], s1_ss.at[a], s1_rs.at[a], t, s + 1 - 2 * core)

    def s1_pack(a):
        for n in range(9):
            first = (n // 3) * UNET + n % 3 + 3 * (1 - core)
            block = jnp.concatenate([grad[a * 3 + i, pl.ds(first, 64, stride=6), :] for i in range(3)], axis=1)
            s1_send[a, 64 * n : 64 * n + 64, :] = block.astype(BF16)

    def s1_add(a):
        for n in range(9):
            first = (n // 3) * UNET + n % 3 + 3 * core
            got = s1_recv[a, 64 * n : 64 * n + 64, :].astype(F32)
            for i in range(3):
                own = grad[a * 3 + i, pl.ds(first, 64, stride=6), :]
                sum1[a * 3 + i, 64 * n : 64 * n + 64, :] = own + got[:, 128 * i : 128 * i + 128]

    def axis_peer(axis, k):
        if axis == "z":
            there = (z + k) % 4
            return there, t, there * 4 + s % 4
        if axis == "x":
            there = (x + k) % 4
            return there, y_hi * 4 + there, s
        there = (y + k) % 4
        return there, (there // 2) * 4 + x, z * 4 + (there % 2) * 2 + core

    first_axis, second_axis, third_axis = ("z", "x", "y"), ("x", "z", "z"), ("y", "y", "x")

    def plane_rows(a, b, c, there):
        base = (3 * b + c) * 64
        parts = []
        for i in range(3):
            ref = sum1.at[a * 3 + i]
            if b == 0:
                parts.append(
                    jnp.concatenate([ref[pl.ds(base + 2 * there + low, 8, stride=8), :] for low in (0, 1)], axis=0)
                )
            elif b == 1:
                rows = [pl.ds(pl.multiple_of(base + high * 32 + there * 8, 8), 8) for high in (0, 1)]
                parts.append(jnp.concatenate([ref[row, :] for row in rows], axis=0))
            else:
                parts.append(ref[pl.ds(base + (there // 2) * 32 + there % 2, 16, stride=2), :])
        return jnp.concatenate(parts, axis=1)

    def s2_copy(a, b, k):
        _, tile, step = axis_peer(first_axis[b], k)
        index = (a * 3 + b) * 3 + k - 1
        return remote(s2_send.at[index], s2_recv.at[index], s2_ss.at[index], s2_rs.at[index], tile, step)

    def s2_pack(a):
        for b in range(3):
            for k in range(1, 4):
                there = axis_peer(first_axis[b], k)[0]
                for c in range(3):
                    block = plane_rows(a, b, c, there).astype(BF16)
                    s2_send[(a * 3 + b) * 3 + k - 1, 16 * c : 16 * c + 16, :] = block

    def s2_start(a):
        for k in (2, 1, 3):
            for b in range(3):
                s2_copy(a, b, k).start()

    def s2_wait(a):
        for b in range(3):
            for k in range(1, 4):
                s2_copy(a, b, k).wait()

    def s2_add(a):
        for b in range(3):
            mine = axis_peer(first_axis[b], 0)[0]
            for c in range(3):
                total = plane_rows(a, b, c, mine)
                for k in range(3):
                    total = total + s2_recv[(a * 3 + b) * 3 + k, 16 * c : 16 * c + 16, :].astype(F32)
                row = 16 * (3 * a + c)
                for i, part in enumerate(lane_tiles(total)):
                    sum2[b * 3 + i, row : row + 16, :] = part

    def line_rows(b, there):
        parts = []
        for i in range(3):
            ref = sum2.at[b * 3 + i]
            if b == 1:
                parts.append(
                    jnp.concatenate([ref[pl.ds(2 * there + low, 24, stride=8), :] for low in (0, 1)], axis=0)
                )
            else:
                parts.append(ref[pl.ds(there, 48, stride=4), :])
        return jnp.concatenate(parts, axis=1)

    def s3_copy(b, k):
        _, tile, step = axis_peer(second_axis[b], k)
        index = b * 3 + k - 1
        return remote(s3_send.at[index], s3_recv.at[index], s3_ss.at[index], s3_rs.at[index], tile, step)

    def s3_start():
        for b in range(3):
            for k in range(1, 4):
                s3_send[b * 3 + k - 1] = line_rows(b, axis_peer(second_axis[b], k)[0]).astype(BF16)
        for b in range(3):
            for k in range(1, 4):
                s3_copy(b, k).start()

    def point_rows(b, there):
        if b == 0:
            rows = pl.ds((there % 2) * 2 + there // 2, 16, stride=4)
        elif b == 1:
            rows = pl.ds((there % 2) * 24 + there // 2, 16, stride=2)
        else:
            rows = pl.ds(there, 16, stride=4)
        return jnp.concatenate([sum3[b * 3 + i, rows, :] for i in range(3)], axis=1)

    def s4_copy(b, k):
        _, tile, step = axis_peer(third_axis[b], k)
        index = b * 3 + k - 1
        return remote(s4_send.at[index], s4_recv.at[index], s4_ss.at[index], s4_rs.at[index], tile, step)

    def s4_start():
        for b in range(3):
            for k in range(1, 4):
                s3_copy(b, k).wait()
        for b in range(3):
            total = line_rows(b, axis_peer(second_axis[b], 0)[0])
            for k in range(3):
                total = total + s3_recv[b * 3 + k].astype(F32)
            for i, part in enumerate(lane_tiles(total)):
                sum3[b * 3 + i, 0:48, :] = part
        for b in range(3):
            for k in range(1, 4):
                s4_send[b * 3 + k - 1] = point_rows(b, axis_peer(third_axis[b], k)[0]).astype(BF16)
        for b in range(3):
            for k in range(1, 4):
                s4_copy(b, k).start()

    def finish():
        for b in range(3):
            for k in range(1, 4):
                s4_copy(b, k).wait()
        for b in range(3):
            total = point_rows(b, axis_peer(third_axis[b], 0)[0])
            for k in range(3):
                total = total + s4_recv[b * 3 + k].astype(F32)
            total = total * (1.0 / math.sqrt(64 * 256))
            for a in range(3):
                mgrad_ref[3 * a + b] = total[3 * a : 3 * a + 3]

    def weight_product(a):
        taps = [
            jnp.concatenate([inner_t[r + a, :, 0:256] for r in range(8)], axis=1),
            jnp.concatenate([inner_tm[r + a] for r in range(8)], axis=1),
            jnp.concatenate([inner_t[r + a, :, 128:384] for r in range(8)], axis=1),
        ]
        result = dot(jnp.concatenate(taps, axis=0), back_ext[1:9, 64:320, :].reshape(2048, UNET))
        for i, part in enumerate(lane_tiles(result)):
            grad[a * 3 + i] = part

    sum2[...] = jnp.zeros_like(sum2)
    sum3[...] = jnp.zeros_like(sum3)
    for a in range(3):
        weight_product(a)
        for k in range(3 * a, 3 * a + 3):
            mid_t[k] = jnp.transpose(midw[k])
        if a == 2:
            s1_add(0)
            s2_pack(0)
            s2_start(0)
        s1_pack(a)
        s1_copy(a).start()
        if a == 1:
            s1_copy(0).wait()

    for row, copy in ((9, halo_copies[0]), (0, halo_copies[1])):
        copy.wait()
        back_ext[row, 320:384, :] = shift_up(back_ext[row, 64:128, :].astype(F32)).astype(BF16)
        back_ext[row, 0:64, :] = shift_down(back_ext[row, 256:320, :].astype(F32)).astype(BF16)

    @pl.when(t == 0)
    def _():
        back_ext[0] = jnp.zeros_like(back_ext[0])

    @pl.when(t == TILES - 1)
    def _():
        back_ext[9] = jnp.zeros_like(back_ext[9])

    def backward_conv(i):
        r = 4 * i
        windows = [
            back_ext[r + 2 - a : r + 6 - a, 64 * (2 - b) : 64 * (2 - b) + 256, :].reshape(1024, UNET)
            for a in range(3)
            for b in range(3)
        ]
        pre_middle[i] = dot(jnp.concatenate(windows, axis=1), mid_t[...].reshape(9 * UNET, UNET))

    def backward_after(i):
        r = 4 * i
        through = pre_middle[i] + back_mixed[256 * r : 256 * r + 1024, :]
        back = (through * inner_slope[r : r + 4].reshape(1024, UNET)).astype(BF16)
        back_part[64 * r : 64 * r + 256, :] = cosine * dot(by_class(back), inw4_t[...])

    def flip_enc(first, last):
        for k in range(first, last):
            enc_t[k] = jnp.transpose(enc[k])

    s1_copy(1).wait()
    backward_conv(0)
    s1_add(1)
    s2_pack(1)
    flip_enc(0, 5)
    s2_start(1)

    s1_copy(2).wait()
    backward_conv(1)
    backward_after(0)
    s1_add(2)
    s2_pack(2)
    flip_enc(5, 9)
    s2_start(2)
    backward_after(1)

    def part_copy(k):
        return remote(
            part_send.at[k - 1], part_recv.at[k - 1], part_ss.at[k - 1], part_rs.at[k - 1], t, (s + k) % STEPS
        )

    for k in range(1, STEPS):
        part_send[k - 1] = back_part[pl.ds((s + k) % STEPS, 32, stride=16), :].astype(BF16)
    for k in range(1, STEPS):
        part_copy(k).start()

    for a in range(3):
        s2_wait(a)
        s2_add(a)
    s3_start()

    for k in range(1, STEPS):
        part_copy(k).wait()
    latent_round = back_part[pl.ds(s, 32, stride=16), :]
    for k in range(1, STEPS):
        latent_round = latent_round + part_recv[k - 1].astype(F32)
    round_send[...] = latent_round.astype(BF16)
    round_copies = []
    for d, offsets in enumerate(AROUND):
        tile, step = near(offsets)
        copy = remote(round_send, round_recv.at[d], round_ss.at[d], round_rs.at[d], tile, step)
        copy.start()
        round_copies.append(copy)

    s4_start()

    round_grid[...] = jnp.zeros_like(round_grid)
    round_pack[...] = round_send[...].astype(F32)
    for q in range(4):
        round_grid[pl.ds(10 + q, 8, stride=8), :] = round_pack[pl.ds(q, 8, stride=4), :]
    for d, (dt, ds) in enumerate(AROUND):
        round_copies[d].wait()
        valid = jnp.bool_(True)
        if dt:
            valid = (t < TILES - 1) if dt < 0 else (t > 0)
        if ds:
            beside = (s < STEPS - 1) if ds < 0 else (s > 0)
            valid = jnp.logical_and(valid, beside) if dt else beside
        round_pack[...] = jnp.where(valid, round_recv[d].astype(F32), 0.0)
        if dt == 0:
            q, place = (0, 6) if ds < 0 else (3, 1)
            round_grid[pl.ds(8 + place, 8, stride=8), :] = round_pack[pl.ds(q, 8, stride=4), :]
        else:
            source, row = (0, 72) if dt < 0 else (28, 0)
            if ds == 0:
                round_grid[row + 2 : row + 6, :] = round_pack[source : source + 4, :]
            else:
                q, place = (0, 6) if ds < 0 else (3, 1)
                round_grid[row + place : row + place + 1, :] = round_pack[source + q : source + q + 1, :]
    pulled = dot(round_grid[...].astype(BF16), latw4_t[...])
    for j in range(4):
        pre = pre_hidden[80 * j : 80 * j + 80, :]
        value = pulled[:, HID * j : HID * j + HID] * slope_of(pre, sigmoid(pre))
        put_blocks(hidden_even, hidden_odd, 1 + j, value)
        if j == 0:
            put_blocks(hidden_even, hidden_odd, 5, pltpu.roll(value, 79, 0))
        if j == 3:
            put_blocks(hidden_even, hidden_odd, 0, pltpu.roll(value, 1, 0))
    pieces = []
    for a in range(3):
        for b in range(3):
            if a == 1:
                window = hidden_odd[2 - b : 6 - b, 0:64, :]
            else:
                window = hidden_even[2 - b : 6 - b, 8 * (2 - a) : 8 * (2 - a) + 64, :]
            pieces.append(window.reshape(256, HID))
    result = dot(jnp.concatenate(pieces, axis=1), enc_t[...].reshape(9 * HID, FEAT))
    for j in range(4):
        for i, part in enumerate(lane_tiles(result[64 * j : 64 * j + 64])):
            out_grid[i, pl.ds(j, 64, stride=4), :] = part
    for r in range(8):
        for i in range(2):
            fgrad_ref[r, :, 128 * i : 128 * i + 128] = out_grid[i, r * 32 + 8 : r * 32 + 24, :]

    finish()


def hand_over(fgrad_ref, mgrad_ref, fgrad_out, mgrad_out):
    fgrad_out[...] = fgrad_ref[...]
    mgrad_out[...] = mgrad_ref[...]


def per_device(
    features,
    encoder_weight,
    latent_weight,
    timesteps,
    noise_field,
    time_table,
    input_weight,
    middle_weight,
    output_weight,
):
    hbm = pl.BlockSpec(memory_space=pl.ANY)
    vmem = pl.BlockSpec(memory_space=pltpu.VMEM)
    dma = pltpu.SemaphoreType.DMA
    operands = (
        features,
        encoder_weight,
        latent_weight.T,
        noise_field,
        time_table,
        input_weight,
        middle_weight,
        output_weight.T,
    )
    scratch = [
        pltpu.VMEM((8, 16, FEAT), BF16),
        pltpu.VMEM((9, FEAT, HID), BF16),
        pltpu.VMEM((LAT, HID), BF16),
        pltpu.VMEM(noise_field.shape, BF16),
        pltpu.VMEM(time_table.shape, BF16),
        pltpu.VMEM((LAT, UNET), BF16),
        pltpu.VMEM((9, UNET, UNET), BF16),
        pltpu.VMEM((LAT, UNET), BF16),
        dma((8,)),
        pltpu.VMEM((9, HID, FEAT), BF16),
        pltpu.VMEM((9, UNET, UNET), BF16),
        pltpu.VMEM((4 * HID, 128), BF16),
        pltpu.VMEM((128, 4 * HID), BF16),
        pltpu.VMEM((128, 4 * UNET), BF16),
        pltpu.VMEM((4 * UNET, 128), BF16),
        pltpu.VMEM((4 * UNET, 128), BF16),
        pltpu.VMEM((128, 4 * UNET), BF16),
        pltpu.VMEM((8, UNET), F32),
        pltpu.VMEM((2, 16, FEAT), BF16),
        pltpu.VMEM((2, 16, FEAT), BF16),
        pltpu.VMEM((6, 2, 16, FEAT), BF16),
        pltpu.VMEM((2, 12 * 32, 128), F32),
        pltpu.VMEM((6, 96, FEAT), BF16),
        pltpu.VMEM((6, 88, FEAT), BF16),
        pltpu.VMEM((320, HID), F32),
        pltpu.VMEM((80, 128), F32),
        pltpu.VMEM((48, 128), F32),
        pltpu.VMEM((48, 128), BF16),
        pltpu.VMEM((15, 48, 128), BF16),
        pltpu.VMEM((16 * 48, 128), F32),
        pltpu.VMEM((640, 128), F32),
        pltpu.VMEM((2, 64, 128), BF16),
        pltpu.VMEM((2, 64, 128), BF16),
        pltpu.VMEM((10, 384, UNET), BF16),
        pltpu.VMEM((8, 256, UNET), F32),
        pltpu.VMEM((10, UNET, 384), BF16),
        pltpu.VMEM((10, UNET, 256), BF16),
        pltpu.VMEM((2, 1024, UNET), F32),
        pltpu.VMEM((2048, UNET), F32),
        pltpu.VMEM((10, 384, UNET), BF16),
        pltpu.VMEM((512, 128), F32),
        pltpu.VMEM((15, 32, 128), BF16),
        pltpu.VMEM((15, 32, 128), BF16),
        pltpu.VMEM((32, 128), F32),
        pltpu.VMEM((32, 128), BF16),
        pltpu.VMEM((8, 32, 128), BF16),
        pltpu.VMEM((80, 128), F32),
        pltpu.VMEM((6, 80, HID), BF16),
        pltpu.VMEM((6, 72, HID), BF16),
        pltpu.VMEM((2, 256, 128), F32),
        pltpu.VMEM((9, 3 * UNET, 128), F32),
        pltpu.VMEM((3, 576, UNET), BF16),
        pltpu.VMEM((3, 576, UNET), BF16),
        pltpu.VMEM((9, 576, 128), F32),
        pltpu.VMEM((27, 48, UNET), BF16),
        pltpu.VMEM((27, 48, UNET), BF16),
        pltpu.VMEM((9, 256, 128), F32),
        pltpu.VMEM((9, 48, UNET), BF16),
        pltpu.VMEM((9, 48, UNET), BF16),
        pltpu.VMEM((9, 64, 128), F32),
        pltpu.VMEM((9, 16, UNET), BF16),
        pltpu.VMEM((9, 16, UNET), BF16),
        dma((8,)),
        dma((8,)),
        dma((2,)),
        dma((2,)),
        dma((15,)),
        dma((15,)),
        dma((2,)),
        dma((2,)),
        dma((15,)),
        dma((15,)),
        dma((8,)),
        dma((8,)),
        dma((3,)),
        dma((3,)),
        dma((27,)),
        dma((27,)),
        dma((9,)),
        dma((9,)),
        dma((9,)),
        dma((9,)),
    ]
    shapes = (
        jax.ShapeDtypeStruct((8, 16, FEAT), F32),
        jax.ShapeDtypeStruct((9, 3, UNET), F32),
    )
    results = pl.pallas_call(
        kernel,
        out_shape=shapes,
        in_specs=[pl.BlockSpec(memory_space=pltpu.SMEM)] + [hbm] * 8,
        out_specs=(vmem, vmem),
        scratch_shapes=scratch,
        compiler_params=pltpu.CompilerParams(
            collective_id=0, has_side_effects=True, vmem_limit_bytes=60 * 1024 * 1024
        ),
        cost_estimate=pl.CostEstimate(flops=18_000_000_000, bytes_accessed=8_000_000, transcendentals=3_000_000),
    )(timesteps, *operands)
    feature_grad, middle_grad = pl.pallas_call(
        hand_over,
        out_shape=shapes,
        in_specs=[vmem, vmem],
        out_specs=(vmem, vmem),
    )(*results)
    return feature_grad, jnp.transpose(middle_grad, (1, 0, 2))


def solution(mesh):
    in_specs = (
        P("tile", "step", None),
        P(),
        P(),
        P("step"),
        P("step", "tile", None),
        P(),
        P(),
        P(),
        P(),
    )
    out_specs = (P("tile", "step", None), P(("tile", "step"), None, None))
    return jax.shard_map(per_device, mesh=mesh, in_specs=in_specs, out_specs=out_specs, check_vma=False)
```

```python
import math

import jax
import jax.numpy as jnp
from jax import lax
from jax.experimental import pallas as pl
from jax.experimental.pallas import tpu as pltpu
from jax.sharding import PartitionSpec as P

F32 = jnp.float32
BF16 = jnp.bfloat16
MESH = pl.DeviceIdType.MESH

FEAT, HID, LAT, UNET = 256, 512, 32, 384
TILES, STEPS = 8, 16
AROUND = ((-1, -1), (-1, 0), (-1, 1), (0, -1), (0, 1), (1, -1), (1, 0), (1, 1))


def sigmoid(values):
    return 0.5 * jnp.tanh(0.5 * values) + 0.5


def slope_of(values, sigma):
    return sigma * (1.0 + values * (1.0 - sigma))


def dot(left, right):
    return jnp.dot(left, right, preferred_element_type=F32)


def lane_tiles(value):
    return [value[:, 128 * i : 128 * i + 128] for i in range(value.shape[1] // 128)]


def shift_down(block):
    last = pltpu.roll(block[48:64], 1, 0)
    rows = lax.broadcasted_iota(jnp.int32, last.shape, 0)
    return jnp.concatenate([jnp.where(rows == 0, 0.0, last), block[0:48]], axis=0)


def shift_up(block):
    first = pltpu.roll(block[0:16], 15, 0)
    rows = lax.broadcasted_iota(jnp.int32, first.shape, 0)
    return jnp.concatenate([block[16:64], jnp.where(rows == 15, 0.0, first)], axis=0)


def kernel(
    time_ref,
    feat_hbm,
    enc_hbm,
    latw_hbm,
    noise_hbm,
    table_hbm,
    inw_hbm,
    midw_hbm,
    outw_hbm,
    fgrad_ref,
    mgrad_ref,
    feat,
    enc,
    latw,
    noise,
    table,
    inw,
    midw,
    outw,
    in_sem,
    enc_t,
    mid_t,
    latw4,
    latw4_t,
    inw4,
    inw4_t,
    outw4,
    outw4_t,
    embed,
    edge,
    edge_in,
    rows_in,
    grid,
    blocks_even,
    blocks_odd,
    pre_hidden,
    lat_tile,
    lat_pack,
    lat_send,
    lat_recv,
    lat_flat,
    noise_rows,
    noise_edge,
    noise_edge_in,
    inner_ext,
    inner_slope,
    inner_t,
    inner_tm,
    pre_middle,
    back_mixed,
    back_ext,
    back_part,
    part_send,
    part_recv,
    rim_send,
    rim_recv,
    part_sum,
    round_grid,
    hidden_even,
    hidden_odd,
    out_grid,
    grad,
    s1_send,
    s1_recv,
    sum1,
    s2_send,
    s2_recv,
    sum2,
    s3_send,
    s3_recv,
    sum3,
    s4_send,
    s4_recv,
    feat_ss,
    feat_rs,
    noise_ss,
    noise_rs,
    lat_ss,
    lat_rs,
    halo_ss,
    halo_rs,
    part_ss,
    part_rs,
    rim_ss,
    rim_rs,
    s1_ss,
    s1_rs,
    s2_ss,
    s2_rs,
    s3_ss,
    s3_rs,
    s4_ss,
    s4_rs,
):
    t = lax.axis_index("tile")
    s = lax.axis_index("step")
    y_hi, x = t // 4, t % 4
    z, y_lo, core = s // 4, (s // 2) % 2, s % 2
    y = y_hi * 2 + y_lo

    def remote(src, dst, ss, rs, tile, step):
        return pltpu.make_async_remote_copy(
            src_ref=src, dst_ref=dst, send_sem=ss, recv_sem=rs, device_id=(tile, step), device_id_type=MESH
        )

    def near(offsets):
        return (t + offsets[0] + TILES) % TILES, (s + offsets[1] + STEPS) % STEPS

    loads = [
        pltpu.make_async_copy(src, dst, in_sem.at[i])
        for i, (src, dst) in enumerate(
            (
                (feat_hbm, feat),
                (noise_hbm, noise),
                (enc_hbm, enc),
                (latw_hbm, latw),
                (inw_hbm, inw),
                (outw_hbm, outw),
                (table_hbm, table),
                (midw_hbm, midw),
            )
        )
    ]
    for load in loads:
        load.start()
    l_feat, l_noise, l_enc, l_latw, l_inw, l_outw, l_table, l_midw = loads

    barrier = pltpu.get_barrier_semaphore()

    for k in range(1, STEPS):
        pl.semaphore_signal(barrier, inc=1, device_id=(t, (s + k) % STEPS), device_id_type=MESH)
    for k in range(1, TILES):
        pl.semaphore_signal(barrier, inc=1, device_id=((t + k) % TILES, s), device_id_type=MESH)
    for offsets in AROUND:
        if offsets[0] and offsets[1]:
            pl.semaphore_signal(barrier, inc=1, device_id=near(offsets), device_id_type=MESH)

    l_feat.wait()
    grid[...] = jnp.zeros_like(grid)
    for r in range(8):
        for i, part in enumerate(lane_tiles(feat[r].astype(F32))):
            grid[i, (r + 2) * 32 + 8 : (r + 2) * 32 + 24, :] = part
    for side, first in ((0, 8), (1, 22)):
        for i in range(2):
            pair = [grid[i, pl.ds(64 + first + col, 8, stride=32), :] for col in (0, 1)]
            edge[side, :, 128 * i : 128 * i + 128] = jnp.concatenate(pair, axis=0).astype(BF16)

    pl.semaphore_wait(barrier, STEPS - 1 + TILES - 1 + 4)

    feat_copies = []
    for d, offsets in enumerate(AROUND):
        tile, step = near(offsets)
        if offsets[0] == 0:
            side = 0 if offsets[1] < 0 else 1
            src, dst = edge.at[side], edge_in.at[side]
        else:
            slot = d if d < 3 else d - 2
            src, dst = feat.at[pl.ds(0 if offsets[0] < 0 else 6, 2)], rows_in.at[slot]
        copy = remote(src, dst, feat_ss.at[d], feat_rs.at[d], tile, step)
        copy.start()
        feat_copies.append(copy)

    l_noise.wait()
    for q in range(64):
        piece = noise[0, :, 128 * q : 128 * q + 128].astype(F32)
        noise_rows[pl.ds(64 + (q % 4) * 16 + q // 4, 8, stride=64), :] = piece
    noise_edge[0] = noise_rows[64:128, :].astype(BF16)
    noise_edge[1] = noise_rows[512:576, :].astype(BF16)
    noise_copies = []
    for side, offset in ((0, -1), (1, 1)):
        tile, step = near((offset, 0))
        copy = remote(noise_edge.at[side], noise_edge_in.at[side], noise_ss.at[side], noise_rs.at[side], tile, step)
        copy.start()
        noise_copies.append(copy)

    for load, weight, wide, flipped in (
        (l_latw, latw, latw4_t, latw4),
        (l_inw, inw, inw4, inw4_t),
        (l_outw, outw, outw4_t, outw4),
    ):
        load.wait()
        columns = weight.shape[1]
        wide[...] = jnp.zeros_like(wide)
        for j in range(4):
            wide[LAT * j : LAT * j + LAT, columns * j : columns * j + columns] = weight[...]
        if flipped is latw4:
            flipped[...] = jnp.transpose(wide[...])

    l_enc.wait()

    for d, copy in enumerate(feat_copies):
        copy.wait()
    for d, offsets in enumerate(AROUND):
        dt, ds = offsets
        valid = jnp.bool_(True)
        if dt:
            valid = (t < TILES - 1) if dt < 0 else (t > 0)
        if ds:
            beside = (s < STEPS - 1) if ds < 0 else (s > 0)
            valid = jnp.logical_and(valid, beside) if dt else beside
        if dt == 0:
            side = 0 if ds < 0 else 1
            taken = jnp.where(valid, edge_in[side].astype(F32), 0.0)
            first = 24 if ds < 0 else 6
            for i, part in enumerate(lane_tiles(taken)):
                for col in (0, 1):
                    grid[i, pl.ds(64 + first + col, 8, stride=32), :] = part[8 * col : 8 * col + 8]
        else:
            slot = d if d < 3 else d - 2
            for r in range(2):
                taken = jnp.where(valid, rows_in[slot, r].astype(F32), 0.0)
                row = (10 + r if dt < 0 else r) * 32
                for i, part in enumerate(lane_tiles(taken)):
                    if ds == 0:
                        grid[i, row + 8 : row + 24, :] = part
                    elif ds < 0:
                        grid[i, row + 24 : row + 32, :] = part[0:8]
                    else:
                        grid[i, row : row + 8, :] = part[8:16]

    def put_blocks(even, odd, index, value):
        even[index] = value.astype(BF16)
        odd[index] = value[8:].astype(BF16)

    for j in range(4):
        value = jnp.concatenate([grid[i, pl.ds(j, 96, stride=4), :] for i in range(2)], axis=1)
        put_blocks(blocks_even, blocks_odd, 1 + j, value)
        if j == 0:
            put_blocks(blocks_even, blocks_odd, 5, pltpu.roll(value, 95, 0))
        if j == 3:
            put_blocks(blocks_even, blocks_odd, 0, pltpu.roll(value, 1, 0))
    pieces = []
    for a in range(3):
        for b in range(3):
            if a == 1:
                window = blocks_odd[b : b + 4, 0:80, :]
            else:
                window = blocks_even[b : b + 4, 8 * a : 8 * a + 80, :]
            pieces.append(window.reshape(320, FEAT))
    pre = dot(jnp.concatenate(pieces, axis=1), enc[...].reshape(9 * FEAT, HID))
    pre_hidden[...] = pre
    hidden = (pre * sigmoid(pre)).astype(BF16)
    hidden = jnp.concatenate([hidden[80 * j : 80 * j + 80] for j in range(4)], axis=1)
    lat_tile[...] = dot(hidden, latw4[...])
    lat_pack[...] = jnp.zeros_like(lat_pack)
    for q in range(4):
        lat_pack[pl.ds(q, 10, stride=4), :] = lat_tile[pl.ds(2 + q, 10, stride=8), :]
    lat_send[...] = lat_pack[...].astype(BF16)

    def lat_copy(k):
        return remote(lat_send, lat_recv.at[k - 1], lat_ss.at[k - 1], lat_rs.at[k - 1], t, (s + k) % STEPS)

    for k in range(1, STEPS):
        lat_copy(k).start()

    inw4_t[...] = jnp.transpose(inw4[...])
    outw4[...] = jnp.transpose(outw4_t[...])
    chosen = time_ref[0]
    angle = ((jnp.full((8, 128), chosen, jnp.int32).astype(F32) + 1.0) / 1000.0 + 0.008) / 1.008 * (math.pi / 2.0)
    cosine = jnp.cos(angle)[0:1, :]
    sine = jnp.sin(angle)[0:1, :]
    l_table.wait()
    onehot = (lax.broadcasted_iota(jnp.int32, (16, table.shape[0]), 1) == chosen).astype(F32).astype(BF16)
    embed[...] = dot(onehot, table[...])[0:8]

    l_midw.wait()
    for side in (0, 1):
        noise_copies[side].wait()
    noise_rows[576:640, :] = noise_edge_in[0].astype(F32)
    noise_rows[0:64, :] = noise_edge_in[1].astype(F32)

    lat_flat[pl.ds(pl.multiple_of(s * 48, 16), 48), :] = lat_pack[...].astype(BF16).astype(F32)

    for k in range(1, STEPS):
        lat_copy(k).wait()
    for k in range(1, STEPS):
        source = (s - k + STEPS) % STEPS
        lat_flat[pl.ds(pl.multiple_of(source * 48, 16), 48), :] = lat_recv[k - 1].astype(F32)

    def input_rows(pair):
        first = 2 * pair
        latent = [lat_flat[pl.ds((first + r) * 4 + q, 16, stride=48), :] for r in range(2) for q in range(4)]
        noisy = cosine * jnp.concatenate(latent, axis=0) + sine * noise_rows[64 * first : 64 * first + 128, :]
        noisy = noisy.astype(BF16)
        for j in range(4):
            pre = dot(noisy, inw4[:, UNET * j : UNET * j + UNET]) + embed[0:1, :]
            sigma = sigmoid(pre)
            inner = pre * sigma
            slope = slope_of(pre, sigma)
            for r in range(2):
                row = first + r
                own = inner[64 * r : 64 * r + 64]
                if row == 0:
                    own = own * jnp.where(t > 0, 1.0, 0.0)
                if row == 9:
                    own = own * jnp.where(t < TILES - 1, 1.0, 0.0)
                inner_ext[row, 64 + 64 * j : 128 + 64 * j, :] = own.astype(BF16)
                if j == 0:
                    inner_ext[row, 320:384, :] = shift_up(own).astype(BF16)
                if j == 3:
                    inner_ext[row, 0:64, :] = shift_down(own).astype(BF16)
                if 0 < row < 9:
                    inner_slope[row - 1, 64 * j : 64 * j + 64, :] = slope[64 * r : 64 * r + 64]

    def flip_rows(pair):
        for row in (2 * pair, 2 * pair + 1):
            flipped = jnp.transpose(inner_ext[row])
            inner_t[row] = flipped
            inner_tm[row] = flipped[:, 64:320]

    def by_class(value):
        rows = value.shape[0] // 256
        return jnp.concatenate(
            [
                jnp.concatenate([value[256 * r + 64 * j : 256 * r + 64 * j + 64] for j in range(4)], axis=1)
                for r in range(rows)
            ],
            axis=0,
        )

    def by_position(value):
        rows = value.shape[0] // 64
        return jnp.concatenate(
            [value[64 * r : 64 * r + 64, UNET * j : UNET * j + UNET] for r in range(rows) for j in range(4)], axis=0
        )

    def forward_conv(i):
        windows = [
            inner_ext[2 * i + a : 2 * i + a + 2, 64 * b : 64 * b + 256, :].reshape(512, UNET)
            for a in range(3)
            for b in range(3)
        ]
        pre_middle[i % 2] = dot(jnp.concatenate(windows, axis=1), midw[...].reshape(9 * UNET, UNET))

    def forward_after(i):
        r = 2 * i
        pre = pre_middle[i % 2]
        sigma = sigmoid(pre)
        own = inner_ext[r + 1 : r + 3, 64:320, :].reshape(512, UNET)
        mixed = (own.astype(F32) + pre * sigma).astype(BF16)
        prediction = dot(by_class(mixed), outw4[...])
        own_noise = noise_rows[64 + r * 64 : 192 + r * 64, :]
        error = ((prediction - own_noise) * (1.0 / math.sqrt(STEPS))).astype(BF16)
        pulled = by_position(dot(error, outw4_t[...]))
        back_mixed[256 * r : 256 * r + 512, :] = pulled
        back = pulled * slope_of(pre, sigma)
        for row in range(2):
            own = back[256 * row : 256 * row + 256]
            back_ext[r + 1 + row, 64:320, :] = own.astype(BF16)
            back_ext[r + 1 + row, 320:384, :] = shift_up(own[0:64]).astype(BF16)
            back_ext[r + 1 + row, 0:64, :] = shift_down(own[192:256]).astype(BF16)

    halo_copies = []

    def halo_start(side):
        tile, step = near((2 * side - 1, 0))
        src, dst = ((1, 9), (8, 0))[side]
        src, dst = back_ext.at[src, pl.ds(64, 256)], back_ext.at[dst, pl.ds(64, 256)]
        copy = remote(src, dst, halo_ss.at[side], halo_rs.at[side], tile, step)
        copy.start()
        halo_copies.append(copy)

    input_rows(0)
    input_rows(1)
    for i in range(4):
        forward_conv(i)
        if i < 3:
            input_rows(i + 2)
        flip_rows(i)
        if i:
            forward_after(i - 1)
        if i == 1:
            halo_start(0)
    flip_rows(4)
    forward_after(3)
    halo_start(1)

    def s1_copy(a):
        return remote(s1_send.at[a], s1_recv.at[a], s1_ss.at[a], s1_rs.at[a], t, s + 1 - 2 * core)

    def s1_pack(a):
        for n in range(9):
            first = (n // 3) * UNET + n % 3 + 3 * (1 - core)
            block = jnp.concatenate([grad[a * 3 + i, pl.ds(first, 64, stride=6), :] for i in range(3)], axis=1)
            s1_send[a, 64 * n : 64 * n + 64, :] = block.astype(BF16)

    def s1_add(a):
        for n in range(9):
            first = (n // 3) * UNET + n % 3 + 3 * core
            got = s1_recv[a, 64 * n : 64 * n + 64, :].astype(F32)
            for i in range(3):
                own = grad[a * 3 + i, pl.ds(first, 64, stride=6), :]
                sum1[a * 3 + i, 64 * n : 64 * n + 64, :] = own + got[:, 128 * i : 128 * i + 128]

    def axis_peer(axis, k):
        if axis == "z":
            there = (z + k) % 4
            return there, t, there * 4 + s % 4
        if axis == "x":
            there = (x + k) % 4
            return there, y_hi * 4 + there, s
        there = (y + k) % 4
        return there, (there // 2) * 4 + x, z * 4 + (there % 2) * 2 + core

    first_axis, second_axis, third_axis = ("z", "x", "y"), ("x", "z", "z"), ("y", "y", "x")

    def plane_rows(a, b, c, there):
        base = (3 * b + c) * 64
        parts = []
        for i in range(3):
            ref = sum1.at[a * 3 + i]
            if b == 0:
                parts.append(
                    jnp.concatenate([ref[pl.ds(base + 2 * there + low, 8, stride=8), :] for low in (0, 1)], axis=0)
                )
            elif b == 1:
                rows = [pl.ds(pl.multiple_of(base + high * 32 + there * 8, 8), 8) for high in (0, 1)]
                parts.append(jnp.concatenate([ref[row, :] for row in rows], axis=0))
            else:
                parts.append(ref[pl.ds(base + (there // 2) * 32 + there % 2, 16, stride=2), :])
        return jnp.concatenate(parts, axis=1)

    def s2_copy(a, b, k):
        _, tile, step = axis_peer(first_axis[b], k)
        index = (a * 3 + b) * 3 + k - 1
        return remote(s2_send.at[index], s2_recv.at[index], s2_ss.at[index], s2_rs.at[index], tile, step)

    def s2_pack(a):
        for b in range(3):
            for k in range(1, 4):
                there = axis_peer(first_axis[b], k)[0]
                for c in range(3):
                    block = plane_rows(a, b, c, there).astype(BF16)
                    s2_send[(a * 3 + b) * 3 + k - 1, 16 * c : 16 * c + 16, :] = block

    def s2_start(a):
        for k in (2, 1, 3):
            for b in range(3):
                s2_copy(a, b, k).start()

    def s2_wait(a):
        for b in range(3):
            for k in range(1, 4):
                s2_copy(a, b, k).wait()

    def s2_add(a):
        for b in range(3):
            mine = axis_peer(first_axis[b], 0)[0]
            for c in range(3):
                total = plane_rows(a, b, c, mine)
                for k in range(3):
                    total = total + s2_recv[(a * 3 + b) * 3 + k, 16 * c : 16 * c + 16, :].astype(F32)
                row = 16 * (3 * a + c)
                for i, part in enumerate(lane_tiles(total)):
                    sum2[b * 3 + i, row : row + 16, :] = part

    def line_rows(b, there):
        parts = []
        for i in range(3):
            ref = sum2.at[b * 3 + i]
            if b == 1:
                parts.append(
                    jnp.concatenate([ref[pl.ds(2 * there + low, 24, stride=8), :] for low in (0, 1)], axis=0)
                )
            else:
                parts.append(ref[pl.ds(there, 48, stride=4), :])
        return jnp.concatenate(parts, axis=1)

    def s3_copy(b, k):
        _, tile, step = axis_peer(second_axis[b], k)
        index = b * 3 + k - 1
        return remote(s3_send.at[index], s3_recv.at[index], s3_ss.at[index], s3_rs.at[index], tile, step)

    def s3_start():
        for b in range(3):
            for k in range(1, 4):
                s3_send[b * 3 + k - 1] = line_rows(b, axis_peer(second_axis[b], k)[0]).astype(BF16)
        for b in range(3):
            for k in range(1, 4):
                s3_copy(b, k).start()

    def point_rows(b, there):
        if b == 0:
            rows = pl.ds((there % 2) * 2 + there // 2, 16, stride=4)
        elif b == 1:
            rows = pl.ds((there % 2) * 24 + there // 2, 16, stride=2)
        else:
            rows = pl.ds(there, 16, stride=4)
        return jnp.concatenate([sum3[b * 3 + i, rows, :] for i in range(3)], axis=1)

    def s4_copy(b, k):
        _, tile, step = axis_peer(third_axis[b], k)
        index = b * 3 + k - 1
        return remote(s4_send.at[index], s4_recv.at[index], s4_ss.at[index], s4_rs.at[index], tile, step)

    def s4_start():
        for b in range(3):
            for k in range(1, 4):
                s3_copy(b, k).wait()
        for b in range(3):
            total = line_rows(b, axis_peer(second_axis[b], 0)[0])
            for k in range(3):
                total = total + s3_recv[b * 3 + k].astype(F32)
            for i, part in enumerate(lane_tiles(total)):
                sum3[b * 3 + i, 0:48, :] = part
        for b in range(3):
            for k in range(1, 4):
                s4_send[b * 3 + k - 1] = point_rows(b, axis_peer(third_axis[b], k)[0]).astype(BF16)
        for b in range(3):
            for k in range(1, 4):
                s4_copy(b, k).start()

    def finish():
        for b in range(3):
            for k in range(1, 4):
                s4_copy(b, k).wait()
        for b in range(3):
            total = point_rows(b, axis_peer(third_axis[b], 0)[0])
            for k in range(3):
                total = total + s4_recv[b * 3 + k].astype(F32)
            total = total * (1.0 / math.sqrt(64 * 256))
            for a in range(3):
                mgrad_ref[3 * a + b] = total[3 * a : 3 * a + 3]

    def weight_product(a):
        taps = [
            jnp.concatenate([inner_t[r + a, :, 0:256] for r in range(8)], axis=1),
            jnp.concatenate([inner_tm[r + a] for r in range(8)], axis=1),
            jnp.concatenate([inner_t[r + a, :, 128:384] for r in range(8)], axis=1),
        ]
        result = dot(jnp.concatenate(taps, axis=0), back_ext[1:9, 64:320, :].reshape(2048, UNET))
        for i, part in enumerate(lane_tiles(result)):
            grad[a * 3 + i] = part

    sum2[...] = jnp.zeros_like(sum2)
    sum3[...] = jnp.zeros_like(sum3)
    for a in range(3):
        weight_product(a)
        for k in range(3 * a, 3 * a + 3):
            mid_t[k] = jnp.transpose(midw[k])
        if a == 2:
            s1_add(0)
            s2_pack(0)
            s2_start(0)
        s1_pack(a)
        s1_copy(a).start()
        if a == 1:
            s1_copy(0).wait()

    for row, copy in ((9, halo_copies[0]), (0, halo_copies[1])):
        copy.wait()
        back_ext[row, 320:384, :] = shift_up(back_ext[row, 64:128, :].astype(F32)).astype(BF16)
        back_ext[row, 0:64, :] = shift_down(back_ext[row, 256:320, :].astype(F32)).astype(BF16)

    @pl.when(t == 0)
    def _():
        back_ext[0] = jnp.zeros_like(back_ext[0])

    @pl.when(t == TILES - 1)
    def _():
        back_ext[9] = jnp.zeros_like(back_ext[9])

    def backward_conv(i):
        r = 2 * i
        windows = [
            back_ext[r + 2 - a : r + 4 - a, 64 * (2 - b) : 64 * (2 - b) + 256, :].reshape(512, UNET)
            for a in range(3)
            for b in range(3)
        ]
        pre_middle[i % 2] = dot(jnp.concatenate(windows, axis=1), mid_t[...].reshape(9 * UNET, UNET))

    def backward_after(i):
        r = 2 * i
        through = pre_middle[i % 2] + back_mixed[256 * r : 256 * r + 512, :]
        back = (through * inner_slope[r : r + 2].reshape(512, UNET)).astype(BF16)
        back_part[64 * r + 64 : 64 * r + 192, :] = cosine * dot(by_class(back), inw4_t[...])

    def flip_enc(first, last):
        for k in range(first, last):
            enc_t[k] = jnp.transpose(enc[k])

    back_part[640:1024, :] = jnp.zeros((384, 128), F32)
    s1_copy(1).wait()
    backward_conv(0)
    s1_add(1)
    s2_pack(1)
    flip_enc(0, 3)
    s2_start(1)

    s1_copy(2).wait()
    backward_conv(3)
    backward_after(0)
    s1_add(2)
    s2_pack(2)
    flip_enc(3, 6)
    s2_start(2)

    backward_after(3)
    rim_copies = []
    for side, row in ((0, 1), (1, 8)):
        rim_send[side] = back_part[64 * row : 64 * row + 64, :].astype(BF16)
        tile, step = near((2 * side - 1, 0))
        copy = remote(rim_send.at[side], rim_recv.at[side], rim_ss.at[side], rim_rs.at[side], tile, step)
        copy.start()
        rim_copies.append(copy)

    backward_conv(1)
    flip_enc(6, 9)
    backward_conv(2)
    backward_after(1)
    backward_after(2)

    for copy in rim_copies:
        copy.wait()
    back_part[576:640, :] = jnp.where(t < TILES - 1, rim_recv[0].astype(F32), 0.0)
    back_part[0:64, :] = jnp.where(t > 0, rim_recv[1].astype(F32), 0.0)

    lane = lax.broadcasted_iota(jnp.int32, (16, 128), 1)

    def part_of(step):
        beside = jnp.where(
            lane < 64, back_part[pl.ds(step + 1, 16, stride=64), :], back_part[pl.ds(step + 47, 16, stride=64), :]
        )
        return jnp.concatenate([back_part[pl.ds(step, 40, stride=16), :], beside], axis=0)

    def part_copy(k):
        return remote(
            part_send.at[k - 1], part_recv.at[k - 1], part_ss.at[k - 1], part_rs.at[k - 1], t, (s + k) % STEPS
        )

    part_blank = jnp.zeros((8, 128), F32)
    for k in range(1, STEPS):
        block = jnp.concatenate([part_of((s + k) % STEPS), part_blank], axis=0)
        part_send[k - 1] = block.astype(BF16)
    for k in range(1, STEPS):
        part_copy(k).start()

    for a in range(3):
        s2_wait(a)
        s2_add(a)
    s3_start()

    for k in range(1, STEPS):
        part_copy(k).wait()
    total = part_of(s)
    for k in range(1, STEPS):
        total = total + part_recv[k - 1].astype(F32)[0:56]
    part_sum[0:56, :] = total

    s4_start()

    round_grid[...] = jnp.zeros_like(round_grid)
    for q in range(4):
        round_grid[pl.ds(2 + q, 10, stride=8), :] = part_sum[pl.ds(q, 10, stride=4), :]
    beside = part_sum[40:50, :]
    lane = lax.broadcasted_iota(jnp.int32, (10, 128), 1)
    left = jnp.logical_and(s > 0, lane >= 3 * LAT)
    right = jnp.logical_and(s < STEPS - 1, lane < LAT)
    round_grid[pl.ds(1, 10, stride=8), :] = jnp.where(left, beside, 0.0)
    round_grid[pl.ds(6, 10, stride=8), :] = jnp.where(right, beside, 0.0)

    @pl.when(t == 0)
    def _():
        round_grid[0:8, :] = jnp.zeros((8, 128), F32)

    @pl.when(t == TILES - 1)
    def _():
        round_grid[72:80, :] = jnp.zeros((8, 128), F32)

    pulled = dot(round_grid[...].astype(BF16), latw4_t[...])
    for j in range(4):
        pre = pre_hidden[80 * j : 80 * j + 80, :]
        value = pulled[:, HID * j : HID * j + HID] * slope_of(pre, sigmoid(pre))
        put_blocks(hidden_even, hidden_odd, 1 + j, value)
        if j == 0:
            put_blocks(hidden_even, hidden_odd, 5, pltpu.roll(value, 79, 0))
        if j == 3:
            put_blocks(hidden_even, hidden_odd, 0, pltpu.roll(value, 1, 0))
    pieces = []
    for a in range(3):
        for b in range(3):
            if a == 1:
                window = hidden_odd[2 - b : 6 - b, 0:64, :]
            else:
                window = hidden_even[2 - b : 6 - b, 8 * (2 - a) : 8 * (2 - a) + 64, :]
            pieces.append(window.reshape(256, HID))
    result = dot(jnp.concatenate(pieces, axis=1), enc_t[...].reshape(9 * HID, FEAT))
    for j in range(4):
        for i, part in enumerate(lane_tiles(result[64 * j : 64 * j + 64])):
            out_grid[i, pl.ds(j, 64, stride=4), :] = part
    for r in range(8):
        for i in range(2):
            fgrad_ref[r, :, 128 * i : 128 * i + 128] = out_grid[i, r * 32 + 8 : r * 32 + 24, :]

    finish()


def hand_over(fgrad_ref, mgrad_ref, fgrad_out, mgrad_out):
    fgrad_out[...] = fgrad_ref[...]
    mgrad_out[...] = mgrad_ref[...]


def per_device(
    features,
    encoder_weight,
    latent_weight,
    timesteps,
    noise_field,
    time_table,
    input_weight,
    middle_weight,
    output_weight,
):
    hbm = pl.BlockSpec(memory_space=pl.ANY)
    vmem = pl.BlockSpec(memory_space=pltpu.VMEM)
    dma = pltpu.SemaphoreType.DMA
    operands = (
        features,
        encoder_weight,
        latent_weight.T,
        noise_field,
        time_table,
        input_weight,
        middle_weight,
        output_weight.T,
    )
    scratch = [
        pltpu.VMEM((8, 16, FEAT), BF16),
        pltpu.VMEM((9, FEAT, HID), BF16),
        pltpu.VMEM((LAT, HID), BF16),
        pltpu.VMEM(noise_field.shape, BF16),
        pltpu.VMEM(time_table.shape, BF16),
        pltpu.VMEM((LAT, UNET), BF16),
        pltpu.VMEM((9, UNET, UNET), BF16),
        pltpu.VMEM((LAT, UNET), BF16),
        dma((8,)),
        pltpu.VMEM((9, HID, FEAT), BF16),
        pltpu.VMEM((9, UNET, UNET), BF16),
        pltpu.VMEM((4 * HID, 128), BF16),
        pltpu.VMEM((128, 4 * HID), BF16),
        pltpu.VMEM((128, 4 * UNET), BF16),
        pltpu.VMEM((4 * UNET, 128), BF16),
        pltpu.VMEM((4 * UNET, 128), BF16),
        pltpu.VMEM((128, 4 * UNET), BF16),
        pltpu.VMEM((8, UNET), F32),
        pltpu.VMEM((2, 16, FEAT), BF16),
        pltpu.VMEM((2, 16, FEAT), BF16),
        pltpu.VMEM((6, 2, 16, FEAT), BF16),
        pltpu.VMEM((2, 12 * 32, 128), F32),
        pltpu.VMEM((6, 96, FEAT), BF16),
        pltpu.VMEM((6, 88, FEAT), BF16),
        pltpu.VMEM((320, HID), F32),
        pltpu.VMEM((80, 128), F32),
        pltpu.VMEM((48, 128), F32),
        pltpu.VMEM((48, 128), BF16),
        pltpu.VMEM((15, 48, 128), BF16),
        pltpu.VMEM((16 * 48, 128), F32),
        pltpu.VMEM((640, 128), F32),
        pltpu.VMEM((2, 64, 128), BF16),
        pltpu.VMEM((2, 64, 128), BF16),
        pltpu.VMEM((10, 384, UNET), BF16),
        pltpu.VMEM((8, 256, UNET), F32),
        pltpu.VMEM((10, UNET, 384), BF16),
        pltpu.VMEM((10, UNET, 256), BF16),
        pltpu.VMEM((2, 512, UNET), F32),
        pltpu.VMEM((2048, UNET), F32),
        pltpu.VMEM((10, 384, UNET), BF16),
        pltpu.VMEM((1024, 128), F32),
        pltpu.VMEM((15, 64, 128), BF16),
        pltpu.VMEM((15, 64, 128), BF16),
        pltpu.VMEM((2, 64, 128), BF16),
        pltpu.VMEM((2, 64, 128), BF16),
        pltpu.VMEM((64, 128), F32),
        pltpu.VMEM((80, 128), F32),
        pltpu.VMEM((6, 80, HID), BF16),
        pltpu.VMEM((6, 72, HID), BF16),
        pltpu.VMEM((2, 256, 128), F32),
        pltpu.VMEM((9, 3 * UNET, 128), F32),
        pltpu.VMEM((3, 576, UNET), BF16),
        pltpu.VMEM((3, 576, UNET), BF16),
        pltpu.VMEM((9, 576, 128), F32),
        pltpu.VMEM((27, 48, UNET), BF16),
        pltpu.VMEM((27, 48, UNET), BF16),
        pltpu.VMEM((9, 256, 128), F32),
        pltpu.VMEM((9, 48, UNET), BF16),
        pltpu.VMEM((9, 48, UNET), BF16),
        pltpu.VMEM((9, 64, 128), F32),
        pltpu.VMEM((9, 16, UNET), BF16),
        pltpu.VMEM((9, 16, UNET), BF16),
        dma((8,)),
        dma((8,)),
        dma((2,)),
        dma((2,)),
        dma((15,)),
        dma((15,)),
        dma((2,)),
        dma((2,)),
        dma((15,)),
        dma((15,)),
        dma((2,)),
        dma((2,)),
        dma((3,)),
        dma((3,)),
        dma((27,)),
        dma((27,)),
        dma((9,)),
        dma((9,)),
        dma((9,)),
        dma((9,)),
    ]
    shapes = (
        jax.ShapeDtypeStruct((8, 16, FEAT), F32),
        jax.ShapeDtypeStruct((9, 3, UNET), F32),
    )
    results = pl.pallas_call(
        kernel,
        out_shape=shapes,
        in_specs=[pl.BlockSpec(memory_space=pltpu.SMEM)] + [hbm] * 8,
        out_specs=(vmem, vmem),
        scratch_shapes=scratch,
        compiler_params=pltpu.CompilerParams(
            collective_id=0, has_side_effects=True, vmem_limit_bytes=60 * 1024 * 1024
        ),
        cost_estimate=pl.CostEstimate(flops=18_000_000_000, bytes_accessed=8_000_000, transcendentals=3_000_000),
    )(timesteps, *operands)
    feature_grad, middle_grad = pl.pallas_call(
        hand_over,
        out_shape=shapes,
        in_specs=[vmem, vmem],
        out_specs=(vmem, vmem),
    )(*results)
    return feature_grad, jnp.transpose(middle_grad, (1, 0, 2))


def solution(mesh):
    in_specs = (
        P("tile", "step", None),
        P(),
        P(),
        P("step"),
        P("step", "tile", None),
        P(),
        P(),
        P(),
        P(),
    )
    out_specs = (P("tile", "step", None), P(("tile", "step"), None, None))
    return jax.shard_map(per_device, mesh=mesh, in_specs=in_specs, out_specs=out_specs, check_vma=False)
```

```python
import math

import jax
import jax.numpy as jnp
from jax import lax
from jax.experimental import pallas as pl
from jax.experimental.pallas import tpu as pltpu
from jax.sharding import PartitionSpec as P

F32 = jnp.float32
BF16 = jnp.bfloat16
MESH = pl.DeviceIdType.MESH

FEAT, HID, LAT, UNET = 256, 512, 32, 384
TILES, STEPS = 8, 16
AROUND = ((-1, -1), (-1, 0), (-1, 1), (0, -1), (0, 1), (1, -1), (1, 0), (1, 1))


def sigmoid(values):
    return 0.5 * jnp.tanh(0.5 * values) + 0.5


def slope_of(values, sigma):
    return sigma * (1.0 + values * (1.0 - sigma))


def dot(left, right):
    return jnp.dot(left, right, preferred_element_type=F32)


def lane_tiles(value):
    return [value[:, 128 * i : 128 * i + 128] for i in range(value.shape[1] // 128)]


def shift_down(block):
    last = pltpu.roll(block[48:64], 1, 0)
    rows = lax.broadcasted_iota(jnp.int32, last.shape, 0)
    return jnp.concatenate([jnp.where(rows == 0, 0.0, last), block[0:48]], axis=0)


def shift_up(block):
    first = pltpu.roll(block[0:16], 15, 0)
    rows = lax.broadcasted_iota(jnp.int32, first.shape, 0)
    return jnp.concatenate([block[16:64], jnp.where(rows == 15, 0.0, first)], axis=0)


def kernel(
    time_ref,
    feat_hbm,
    enc_hbm,
    latw_hbm,
    noise_hbm,
    table_hbm,
    inw_hbm,
    midw_hbm,
    outw_hbm,
    fgrad_ref,
    mgrad_ref,
    feat,
    enc,
    latw,
    noise,
    table,
    inw,
    midw,
    outw,
    in_sem,
    enc_t,
    mid_t,
    latw4,
    latw4_t,
    inw4,
    inw4_t,
    outw4,
    outw4_t,
    embed,
    edge,
    edge_in,
    rows_in,
    grid,
    blocks_even,
    blocks_odd,
    pre_hidden,
    lat_tile,
    lat_pack,
    lat_send,
    lat_recv,
    lat_flat,
    noise_rows,
    noise_edge,
    noise_edge_in,
    inner_ext,
    inner_slope,
    inner_t,
    inner_tm,
    pre_middle,
    back_mixed,
    back_ext,
    back_part,
    part_send,
    part_recv,
    rim_send,
    rim_recv,
    part_sum,
    round_grid,
    hidden_even,
    hidden_odd,
    out_grid,
    grad,
    s1_send,
    s1_recv,
    sum1,
    s2_send,
    s2_recv,
    sum2,
    s3_send,
    s3_recv,
    sum3,
    s4_send,
    s4_recv,
    feat_ss,
    feat_rs,
    noise_ss,
    noise_rs,
    lat_ss,
    lat_rs,
    halo_ss,
    halo_rs,
    part_ss,
    part_rs,
    rim_ss,
    rim_rs,
    s1_ss,
    s1_rs,
    s2_ss,
    s2_rs,
    s3_ss,
    s3_rs,
    s4_ss,
    s4_rs,
):
    t = lax.axis_index("tile")
    s = lax.axis_index("step")
    y_hi, x = t // 4, t % 4
    z, y_lo, core = s // 4, (s // 2) % 2, s % 2
    y = y_hi * 2 + y_lo

    def remote(src, dst, ss, rs, tile, step):
        return pltpu.make_async_remote_copy(
            src_ref=src, dst_ref=dst, send_sem=ss, recv_sem=rs, device_id=(tile, step), device_id_type=MESH
        )

    def near(offsets):
        return (t + offsets[0] + TILES) % TILES, (s + offsets[1] + STEPS) % STEPS

    small = ((feat_hbm, feat), (noise_hbm, noise), (latw_hbm, latw), (inw_hbm, inw), (outw_hbm, outw), (table_hbm, table))
    large = [
        (src.at[pl.ds(3 * i, 3)], dst.at[pl.ds(3 * i, 3)]) for src, dst in ((enc_hbm, enc), (midw_hbm, midw)) for i in range(3)
    ]
    loads = [
        pltpu.make_async_copy(src, dst, in_sem.at[i]) for i, (src, dst) in enumerate((*small[:2], *large, *small[2:]))
    ]
    for load in loads:
        load.start()
    l_feat, l_noise = loads[:2]
    l_enc, l_midw = loads[2:5], loads[5:8]
    l_latw, l_inw, l_outw, l_table = loads[8:]

    barrier = pltpu.get_barrier_semaphore()

    for k in range(1, STEPS):
        pl.semaphore_signal(barrier, inc=1, device_id=(t, (s + k) % STEPS), device_id_type=MESH)
    for k in range(1, TILES):
        pl.semaphore_signal(barrier, inc=1, device_id=((t + k) % TILES, s), device_id_type=MESH)
    for offsets in AROUND:
        if offsets[0] and offsets[1]:
            pl.semaphore_signal(barrier, inc=1, device_id=near(offsets), device_id_type=MESH)

    l_feat.wait()
    grid[...] = jnp.zeros_like(grid)
    for r in range(8):
        for i, part in enumerate(lane_tiles(feat[r].astype(F32))):
            grid[i, (r + 2) * 32 + 8 : (r + 2) * 32 + 24, :] = part
    for side, first in ((0, 8), (1, 22)):
        for i in range(2):
            pair = [grid[i, pl.ds(64 + first + col, 8, stride=32), :] for col in (0, 1)]
            edge[side, :, 128 * i : 128 * i + 128] = jnp.concatenate(pair, axis=0).astype(BF16)

    pl.semaphore_wait(barrier, STEPS - 1 + TILES - 1 + 4)

    feat_copies = []
    for d, offsets in enumerate(AROUND):
        tile, step = near(offsets)
        if offsets[0] == 0:
            side = 0 if offsets[1] < 0 else 1
            src, dst = edge.at[side], edge_in.at[side]
        else:
            slot = d if d < 3 else d - 2
            src, dst = feat.at[pl.ds(0 if offsets[0] < 0 else 6, 2)], rows_in.at[slot]
        copy = remote(src, dst, feat_ss.at[d], feat_rs.at[d], tile, step)
        copy.start()
        feat_copies.append(copy)

    l_noise.wait()
    for q in range(64):
        piece = noise[0, :, 128 * q : 128 * q + 128].astype(F32)
        noise_rows[pl.ds(64 + (q % 4) * 16 + q // 4, 8, stride=64), :] = piece
    noise_edge[0] = noise_rows[64:128, :].astype(BF16)
    noise_edge[1] = noise_rows[512:576, :].astype(BF16)
    noise_copies = []
    for side, offset in ((0, -1), (1, 1)):
        tile, step = near((offset, 0))
        copy = remote(noise_edge.at[side], noise_edge_in.at[side], noise_ss.at[side], noise_rs.at[side], tile, step)
        copy.start()
        noise_copies.append(copy)

    for load, weight, wide, flipped in (
        (l_latw, latw, latw4_t, latw4),
        (l_inw, inw, inw4, inw4_t),
        (l_outw, outw, outw4_t, outw4),
    ):
        load.wait()
        columns = weight.shape[1]
        wide[...] = jnp.zeros_like(wide)
        for j in range(4):
            wide[LAT * j : LAT * j + LAT, columns * j : columns * j + columns] = weight[...]
        if flipped is latw4:
            flipped[...] = jnp.transpose(wide[...])

    for load in l_enc:
        load.wait()

    for d, copy in enumerate(feat_copies):
        copy.wait()
    for d, offsets in enumerate(AROUND):
        dt, ds = offsets
        valid = jnp.bool_(True)
        if dt:
            valid = (t < TILES - 1) if dt < 0 else (t > 0)
        if ds:
            beside = (s < STEPS - 1) if ds < 0 else (s > 0)
            valid = jnp.logical_and(valid, beside) if dt else beside
        if dt == 0:
            side = 0 if ds < 0 else 1
            taken = jnp.where(valid, edge_in[side].astype(F32), 0.0)
            first = 24 if ds < 0 else 6
            for i, part in enumerate(lane_tiles(taken)):
                for col in (0, 1):
                    grid[i, pl.ds(64 + first + col, 8, stride=32), :] = part[8 * col : 8 * col + 8]
        else:
            slot = d if d < 3 else d - 2
            for r in range(2):
                taken = jnp.where(valid, rows_in[slot, r].astype(F32), 0.0)
                row = (10 + r if dt < 0 else r) * 32
                for i, part in enumerate(lane_tiles(taken)):
                    if ds == 0:
                        grid[i, row + 8 : row + 24, :] = part
                    elif ds < 0:
                        grid[i, row + 24 : row + 32, :] = part[0:8]
                    else:
                        grid[i, row : row + 8, :] = part[8:16]

    def put_blocks(even, odd, index, value):
        even[index] = value.astype(BF16)
        odd[index] = value[8:].astype(BF16)

    for j in range(4):
        value = jnp.concatenate([grid[i, pl.ds(j, 96, stride=4), :] for i in range(2)], axis=1)
        put_blocks(blocks_even, blocks_odd, 1 + j, value)
        if j == 0:
            put_blocks(blocks_even, blocks_odd, 5, pltpu.roll(value, 95, 0))
        if j == 3:
            put_blocks(blocks_even, blocks_odd, 0, pltpu.roll(value, 1, 0))
    pieces = []
    for a in range(3):
        for b in range(3):
            if a == 1:
                window = blocks_odd[b : b + 4, 0:80, :]
            else:
                window = blocks_even[b : b + 4, 8 * a : 8 * a + 80, :]
            pieces.append(window.reshape(320, FEAT))
    pre = dot(jnp.concatenate(pieces, axis=1), enc[...].reshape(9 * FEAT, HID))
    pre_hidden[...] = pre
    hidden = (pre * sigmoid(pre)).astype(BF16)
    hidden = jnp.concatenate([hidden[80 * j : 80 * j + 80] for j in range(4)], axis=1)
    lat_tile[...] = dot(hidden, latw4[...])
    lat_pack[...] = jnp.zeros_like(lat_pack)
    for q in range(4):
        lat_pack[pl.ds(q, 10, stride=4), :] = lat_tile[pl.ds(2 + q, 10, stride=8), :]
    lat_send[...] = lat_pack[...].astype(BF16)

    def lat_copy(k):
        return remote(lat_send, lat_recv.at[k - 1], lat_ss.at[k - 1], lat_rs.at[k - 1], t, (s + k) % STEPS)

    for k in range(1, STEPS):
        lat_copy(k).start()

    inw4_t[...] = jnp.transpose(inw4[...])
    outw4[...] = jnp.transpose(outw4_t[...])
    chosen = time_ref[0]
    angle = ((jnp.full((8, 128), chosen, jnp.int32).astype(F32) + 1.0) / 1000.0 + 0.008) / 1.008 * (math.pi / 2.0)
    cosine = jnp.cos(angle)[0:1, :]
    sine = jnp.sin(angle)[0:1, :]
    l_table.wait()
    onehot = (lax.broadcasted_iota(jnp.int32, (16, table.shape[0]), 1) == chosen).astype(F32).astype(BF16)
    embed[...] = dot(onehot, table[...])[0:8]

    for load in l_midw:
        load.wait()
    for side in (0, 1):
        noise_copies[side].wait()
    noise_rows[576:640, :] = noise_edge_in[0].astype(F32)
    noise_rows[0:64, :] = noise_edge_in[1].astype(F32)

    lat_flat[pl.ds(pl.multiple_of(s * 48, 16), 48), :] = lat_pack[...].astype(BF16).astype(F32)

    for k in range(1, STEPS):
        lat_copy(k).wait()
    for k in range(1, STEPS):
        source = (s - k + STEPS) % STEPS
        lat_flat[pl.ds(pl.multiple_of(source * 48, 16), 48), :] = lat_recv[k - 1].astype(F32)

    def input_rows(pair):
        first = 2 * pair
        latent = [lat_flat[pl.ds((first + r) * 4 + q, 16, stride=48), :] for r in range(2) for q in range(4)]
        noisy = cosine * jnp.concatenate(latent, axis=0) + sine * noise_rows[64 * first : 64 * first + 128, :]
        noisy = noisy.astype(BF16)
        for j in range(4):
            pre = dot(noisy, inw4[:, UNET * j : UNET * j + UNET]) + embed[0:1, :]
            sigma = sigmoid(pre)
            inner = pre * sigma
            slope = slope_of(pre, sigma)
            for r in range(2):
                row = first + r
                own = inner[64 * r : 64 * r + 64]
                if row == 0:
                    own = own * jnp.where(t > 0, 1.0, 0.0)
                if row == 9:
                    own = own * jnp.where(t < TILES - 1, 1.0, 0.0)
                inner_ext[row, 64 + 64 * j : 128 + 64 * j, :] = own.astype(BF16)
                if j == 0:
                    inner_ext[row, 320:384, :] = shift_up(own).astype(BF16)
                if j == 3:
                    inner_ext[row, 0:64, :] = shift_down(own).astype(BF16)
                if 0 < row < 9:
                    inner_slope[row - 1, 64 * j : 64 * j + 64, :] = slope[64 * r : 64 * r + 64]

    def flip_rows(pair):
        for row in (2 * pair, 2 * pair + 1):
            flipped = jnp.transpose(inner_ext[row])
            inner_t[row] = flipped
            inner_tm[row] = flipped[:, 64:320]

    def by_class(value):
        rows = value.shape[0] // 256
        return jnp.concatenate(
            [
                jnp.concatenate([value[256 * r + 64 * j : 256 * r + 64 * j + 64] for j in range(4)], axis=1)
                for r in range(rows)
            ],
            axis=0,
        )

    def by_position(value):
        rows = value.shape[0] // 64
        return jnp.concatenate(
            [value[64 * r : 64 * r + 64, UNET * j : UNET * j + UNET] for r in range(rows) for j in range(4)], axis=0
        )

    def forward_conv(i):
        windows = [
            inner_ext[2 * i + a : 2 * i + a + 2, 64 * b : 64 * b + 256, :].reshape(512, UNET)
            for a in range(3)
            for b in range(3)
        ]
        pre_middle[i % 2] = dot(jnp.concatenate(windows, axis=1), midw[...].reshape(9 * UNET, UNET))

    def forward_after(i):
        r = 2 * i
        pre = pre_middle[i % 2]
        sigma = sigmoid(pre)
        own = inner_ext[r + 1 : r + 3, 64:320, :].reshape(512, UNET)
        mixed = (own.astype(F32) + pre * sigma).astype(BF16)
        prediction = dot(by_class(mixed), outw4[...])
        own_noise = noise_rows[64 + r * 64 : 192 + r * 64, :]
        error = ((prediction - own_noise) * (1.0 / math.sqrt(STEPS))).astype(BF16)
        pulled = by_position(dot(error, outw4_t[...]))
        back_mixed[256 * r : 256 * r + 512, :] = pulled
        back = pulled * slope_of(pre, sigma)
        for row in range(2):
            own = back[256 * row : 256 * row + 256]
            back_ext[r + 1 + row, 64:320, :] = own.astype(BF16)
            back_ext[r + 1 + row, 320:384, :] = shift_up(own[0:64]).astype(BF16)
            back_ext[r + 1 + row, 0:64, :] = shift_down(own[192:256]).astype(BF16)

    halo_copies = []

    def halo_start(side):
        tile, step = near((2 * side - 1, 0))
        src, dst = ((1, 9), (8, 0))[side]
        src, dst = back_ext.at[src, pl.ds(64, 256)], back_ext.at[dst, pl.ds(64, 256)]
        copy = remote(src, dst, halo_ss.at[side], halo_rs.at[side], tile, step)
        copy.start()
        halo_copies.append(copy)

    input_rows(0)
    input_rows(1)
    for i in range(4):
        forward_conv(i)
        if i < 3:
            input_rows(i + 2)
        flip_rows(i)
        if i:
            forward_after(i - 1)
        if i == 1:
            halo_start(0)
    flip_rows(4)
    forward_after(3)
    halo_start(1)

    def s1_copy(a):
        return remote(s1_send.at[a], s1_recv.at[a], s1_ss.at[a], s1_rs.at[a], t, s + 1 - 2 * core)

    def s1_pack(a):
        for n in range(9):
            first = (n // 3) * UNET + n % 3 + 3 * (1 - core)
            block = jnp.concatenate([grad[a * 3 + i, pl.ds(first, 64, stride=6), :] for i in range(3)], axis=1)
            s1_send[a, 64 * n : 64 * n + 64, :] = block.astype(BF16)

    def s1_add(a):
        for n in range(9):
            first = (n // 3) * UNET + n % 3 + 3 * core
            got = s1_recv[a, 64 * n : 64 * n + 64, :].astype(F32)
            for i in range(3):
                own = grad[a * 3 + i, pl.ds(first, 64, stride=6), :]
                sum1[a * 3 + i, 64 * n : 64 * n + 64, :] = own + got[:, 128 * i : 128 * i + 128]

    def axis_peer(axis, k):
        if axis == "z":
            there = (z + k) % 4
            return there, t, there * 4 + s % 4
        if axis == "x":
            there = (x + k) % 4
            return there, y_hi * 4 + there, s
        there = (y + k) % 4
        return there, (there // 2) * 4 + x, z * 4 + (there % 2) * 2 + core

    first_axis, second_axis, third_axis = ("z", "x", "y"), ("x", "z", "z"), ("y", "y", "x")

    def plane_rows(a, b, c, there):
        base = (3 * b + c) * 64
        parts = []
        for i in range(3):
            ref = sum1.at[a * 3 + i]
            if b == 0:
                parts.append(
                    jnp.concatenate([ref[pl.ds(base + 2 * there + low, 8, stride=8), :] for low in (0, 1)], axis=0)
                )
            elif b == 1:
                rows = [pl.ds(pl.multiple_of(base + high * 32 + there * 8, 8), 8) for high in (0, 1)]
                parts.append(jnp.concatenate([ref[row, :] for row in rows], axis=0))
            else:
                parts.append(ref[pl.ds(base + (there // 2) * 32 + there % 2, 16, stride=2), :])
        return jnp.concatenate(parts, axis=1)

    def s2_copy(a, b, k):
        _, tile, step = axis_peer(first_axis[b], k)
        index = (a * 3 + b) * 3 + k - 1
        return remote(s2_send.at[index], s2_recv.at[index], s2_ss.at[index], s2_rs.at[index], tile, step)

    def s2_pack(a):
        for b in range(3):
            for k in range(1, 4):
                there = axis_peer(first_axis[b], k)[0]
                for c in range(3):
                    block = plane_rows(a, b, c, there).astype(BF16)
                    s2_send[(a * 3 + b) * 3 + k - 1, 16 * c : 16 * c + 16, :] = block

    def s2_start(a):
        for k in (2, 1, 3):
            for b in range(3):
                s2_copy(a, b, k).start()

    def s2_wait(a):
        for b in range(3):
            for k in range(1, 4):
                s2_copy(a, b, k).wait()

    def s2_add(a):
        for b in range(3):
            mine = axis_peer(first_axis[b], 0)[0]
            for c in range(3):
                total = plane_rows(a, b, c, mine)
                for k in range(3):
                    total = total + s2_recv[(a * 3 + b) * 3 + k, 16 * c : 16 * c + 16, :].astype(F32)
                row = 16 * (3 * a + c)
                for i, part in enumerate(lane_tiles(total)):
                    sum2[b * 3 + i, row : row + 16, :] = part

    def line_rows(b, there):
        parts = []
        for i in range(3):
            ref = sum2.at[b * 3 + i]
            if b == 1:
                parts.append(
                    jnp.concatenate([ref[pl.ds(2 * there + low, 24, stride=8), :] for low in (0, 1)], axis=0)
                )
            else:
                parts.append(ref[pl.ds(there, 48, stride=4), :])
        return jnp.concatenate(parts, axis=1)

    def s3_copy(b, k):
        _, tile, step = axis_peer(second_axis[b], k)
        index = b * 3 + k - 1
        return remote(s3_send.at[index], s3_recv.at[index], s3_ss.at[index], s3_rs.at[index], tile, step)

    def s3_start():
        for b in range(3):
            for k in range(1, 4):
                s3_send[b * 3 + k - 1] = line_rows(b, axis_peer(second_axis[b], k)[0]).astype(BF16)
        for b in range(3):
            for k in range(1, 4):
                s3_copy(b, k).start()

    def point_rows(b, there):
        if b == 0:
            rows = pl.ds((there % 2) * 2 + there // 2, 16, stride=4)
        elif b == 1:
            rows = pl.ds((there % 2) * 24 + there // 2, 16, stride=2)
        else:
            rows = pl.ds(there, 16, stride=4)
        return jnp.concatenate([sum3[b * 3 + i, rows, :] for i in range(3)], axis=1)

    def s4_copy(b, k):
        _, tile, step = axis_peer(third_axis[b], k)
        index = b * 3 + k - 1
        return remote(s4_send.at[index], s4_recv.at[index], s4_ss.at[index], s4_rs.at[index], tile, step)

    def s4_start():
        for b in range(3):
            for k in range(1, 4):
                s3_copy(b, k).wait()
        for b in range(3):
            total = line_rows(b, axis_peer(second_axis[b], 0)[0])
            for k in range(3):
                total = total + s3_recv[b * 3 + k].astype(F32)
            for i, part in enumerate(lane_tiles(total)):
                sum3[b * 3 + i, 0:48, :] = part
        for b in range(3):
            for k in range(1, 4):
                s4_send[b * 3 + k - 1] = point_rows(b, axis_peer(third_axis[b], k)[0]).astype(BF16)
        for b in range(3):
            for k in range(1, 4):
                s4_copy(b, k).start()

    def finish():
        for b in range(3):
            for k in range(1, 4):
                s4_copy(b, k).wait()
        for b in range(3):
            total = point_rows(b, axis_peer(third_axis[b], 0)[0])
            for k in range(3):
                total = total + s4_recv[b * 3 + k].astype(F32)
            total = total * (1.0 / math.sqrt(64 * 256))
            for a in range(3):
                mgrad_ref[3 * a + b] = total[3 * a : 3 * a + 3]

    def weight_product(a):
        taps = [
            jnp.concatenate([inner_t[r + a, :, 0:256] for r in range(8)], axis=1),
            jnp.concatenate([inner_tm[r + a] for r in range(8)], axis=1),
            jnp.concatenate([inner_t[r + a, :, 128:384] for r in range(8)], axis=1),
        ]
        result = dot(jnp.concatenate(taps, axis=0), back_ext[1:9, 64:320, :].reshape(2048, UNET))
        for i, part in enumerate(lane_tiles(result)):
            grad[a * 3 + i] = part

    sum2[...] = jnp.zeros_like(sum2)
    sum3[...] = jnp.zeros_like(sum3)
    for a in range(3):
        weight_product(a)
        for k in range(3 * a, 3 * a + 3):
            mid_t[k] = jnp.transpose(midw[k])
        s1_pack(a)
        s1_copy(a).start()

    for row, copy in ((9, halo_copies[0]), (0, halo_copies[1])):
        copy.wait()
        back_ext[row, 320:384, :] = shift_up(back_ext[row, 64:128, :].astype(F32)).astype(BF16)
        back_ext[row, 0:64, :] = shift_down(back_ext[row, 256:320, :].astype(F32)).astype(BF16)

    @pl.when(t == 0)
    def _():
        back_ext[0] = jnp.zeros_like(back_ext[0])

    @pl.when(t == TILES - 1)
    def _():
        back_ext[9] = jnp.zeros_like(back_ext[9])

    def backward_conv(i):
        r = 2 * i
        windows = [
            back_ext[r + 2 - a : r + 4 - a, 64 * (2 - b) : 64 * (2 - b) + 256, :].reshape(512, UNET)
            for a in range(3)
            for b in range(3)
        ]
        pre_middle[i % 2] = dot(jnp.concatenate(windows, axis=1), mid_t[...].reshape(9 * UNET, UNET))

    def backward_after(i):
        r = 2 * i
        through = pre_middle[i % 2] + back_mixed[256 * r : 256 * r + 512, :]
        back = (through * inner_slope[r : r + 2].reshape(512, UNET)).astype(BF16)
        back_part[64 * r + 64 : 64 * r + 192, :] = cosine * dot(by_class(back), inw4_t[...])

    def flip_enc(first, last):
        for k in range(first, last):
            enc_t[k] = jnp.transpose(enc[k])

    back_part[640:1024, :] = jnp.zeros((384, 128), F32)
    backward_conv(0)
    flip_enc(0, 4)

    s1_copy(0).wait()
    s1_copy(1).wait()
    backward_conv(3)
    backward_after(0)
    for a in (0, 1):
        s1_add(a)
        s2_pack(a)
    s2_start(0)
    s2_start(1)

    backward_after(3)
    rim_copies = []
    for side, row in ((0, 1), (1, 8)):
        rim_send[side] = back_part[64 * row : 64 * row + 64, :].astype(BF16)
        tile, step = near((2 * side - 1, 0))
        copy = remote(rim_send.at[side], rim_recv.at[side], rim_ss.at[side], rim_rs.at[side], tile, step)
        copy.start()
        rim_copies.append(copy)

    s1_copy(2).wait()
    backward_conv(1)
    s1_add(2)
    s2_pack(2)
    flip_enc(4, 6)
    s2_start(2)
    backward_conv(2)
    backward_after(1)
    flip_enc(6, 9)
    backward_after(2)

    for copy in rim_copies:
        copy.wait()
    back_part[576:640, :] = jnp.where(t < TILES - 1, rim_recv[0].astype(F32), 0.0)
    back_part[0:64, :] = jnp.where(t > 0, rim_recv[1].astype(F32), 0.0)

    lane = lax.broadcasted_iota(jnp.int32, (16, 128), 1)

    def part_of(step):
        beside = jnp.where(
            lane < 64, back_part[pl.ds(step + 1, 16, stride=64), :], back_part[pl.ds(step + 47, 16, stride=64), :]
        )
        return jnp.concatenate([back_part[pl.ds(step, 40, stride=16), :], beside], axis=0)

    def part_copy(k):
        return remote(
            part_send.at[k - 1], part_recv.at[k - 1], part_ss.at[k - 1], part_rs.at[k - 1], t, (s + k) % STEPS
        )

    part_blank = jnp.zeros((8, 128), F32)
    for k in range(1, STEPS):
        block = jnp.concatenate([part_of((s + k) % STEPS), part_blank], axis=0)
        part_send[k - 1] = block.astype(BF16)
    for k in range(1, STEPS):
        part_copy(k).start()

    for a in range(3):
        s2_wait(a)
        s2_add(a)
    s3_start()

    for k in range(1, STEPS):
        part_copy(k).wait()
    total = part_of(s)
    for k in range(1, STEPS):
        total = total + part_recv[k - 1].astype(F32)[0:56]
    part_sum[0:56, :] = total

    s4_start()

    round_grid[...] = jnp.zeros_like(round_grid)
    for q in range(4):
        round_grid[pl.ds(2 + q, 10, stride=8), :] = part_sum[pl.ds(q, 10, stride=4), :]
    beside = part_sum[40:50, :]
    lane = lax.broadcasted_iota(jnp.int32, (10, 128), 1)
    left = jnp.logical_and(s > 0, lane >= 3 * LAT)
    right = jnp.logical_and(s < STEPS - 1, lane < LAT)
    round_grid[pl.ds(1, 10, stride=8), :] = jnp.where(left, beside, 0.0)
    round_grid[pl.ds(6, 10, stride=8), :] = jnp.where(right, beside, 0.0)

    @pl.when(t == 0)
    def _():
        round_grid[0:8, :] = jnp.zeros((8, 128), F32)

    @pl.when(t == TILES - 1)
    def _():
        round_grid[72:80, :] = jnp.zeros((8, 128), F32)

    pulled = dot(round_grid[...].astype(BF16), latw4_t[...])
    for j in range(4):
        pre = pre_hidden[80 * j : 80 * j + 80, :]
        value = pulled[:, HID * j : HID * j + HID] * slope_of(pre, sigmoid(pre))
        put_blocks(hidden_even, hidden_odd, 1 + j, value)
        if j == 0:
            put_blocks(hidden_even, hidden_odd, 5, pltpu.roll(value, 79, 0))
        if j == 3:
            put_blocks(hidden_even, hidden_odd, 0, pltpu.roll(value, 1, 0))
    pieces = []
    for a in range(3):
        for b in range(3):
            if a == 1:
                window = hidden_odd[2 - b : 6 - b, 0:64, :]
            else:
                window = hidden_even[2 - b : 6 - b, 8 * (2 - a) : 8 * (2 - a) + 64, :]
            pieces.append(window.reshape(256, HID))
    result = dot(jnp.concatenate(pieces, axis=1), enc_t[...].reshape(9 * HID, FEAT))
    for j in range(4):
        for i, part in enumerate(lane_tiles(result[64 * j : 64 * j + 64])):
            out_grid[i, pl.ds(j, 64, stride=4), :] = part
    for r in range(8):
        for i in range(2):
            fgrad_ref[r, :, 128 * i : 128 * i + 128] = out_grid[i, r * 32 + 8 : r * 32 + 24, :]

    finish()


def hand_over(fgrad_ref, mgrad_ref, fgrad_out, mgrad_out):
    fgrad_out[...] = fgrad_ref[...]
    mgrad_out[...] = mgrad_ref[...]


def per_device(
    features,
    encoder_weight,
    latent_weight,
    timesteps,
    noise_field,
    time_table,
    input_weight,
    middle_weight,
    output_weight,
):
    hbm = pl.BlockSpec(memory_space=pl.ANY)
    vmem = pl.BlockSpec(memory_space=pltpu.VMEM)
    dma = pltpu.SemaphoreType.DMA
    operands = (
        features,
        encoder_weight,
        latent_weight.T,
        noise_field,
        time_table,
        input_weight,
        middle_weight,
        output_weight.T,
    )
    scratch = [
        pltpu.VMEM((8, 16, FEAT), BF16),
        pltpu.VMEM((9, FEAT, HID), BF16),
        pltpu.VMEM((LAT, HID), BF16),
        pltpu.VMEM(noise_field.shape, BF16),
        pltpu.VMEM(time_table.shape, BF16),
        pltpu.VMEM((LAT, UNET), BF16),
        pltpu.VMEM((9, UNET, UNET), BF16),
        pltpu.VMEM((LAT, UNET), BF16),
        dma((12,)),
        pltpu.VMEM((9, HID, FEAT), BF16),
        pltpu.VMEM((9, UNET, UNET), BF16),
        pltpu.VMEM((4 * HID, 128), BF16),
        pltpu.VMEM((128, 4 * HID), BF16),
        pltpu.VMEM((128, 4 * UNET), BF16),
        pltpu.VMEM((4 * UNET, 128), BF16),
        pltpu.VMEM((4 * UNET, 128), BF16),
        pltpu.VMEM((128, 4 * UNET), BF16),
        pltpu.VMEM((8, UNET), F32),
        pltpu.VMEM((2, 16, FEAT), BF16),
        pltpu.VMEM((2, 16, FEAT), BF16),
        pltpu.VMEM((6, 2, 16, FEAT), BF16),
        pltpu.VMEM((2, 12 * 32, 128), F32),
        pltpu.VMEM((6, 96, FEAT), BF16),
        pltpu.VMEM((6, 88, FEAT), BF16),
        pltpu.VMEM((320, HID), F32),
        pltpu.VMEM((80, 128), F32),
        pltpu.VMEM((48, 128), F32),
        pltpu.VMEM((48, 128), BF16),
        pltpu.VMEM((15, 48, 128), BF16),
        pltpu.VMEM((16 * 48, 128), F32),
        pltpu.VMEM((640, 128), F32),
        pltpu.VMEM((2, 64, 128), BF16),
        pltpu.VMEM((2, 64, 128), BF16),
        pltpu.VMEM((10, 384, UNET), BF16),
        pltpu.VMEM((8, 256, UNET), F32),
        pltpu.VMEM((10, UNET, 384), BF16),
        pltpu.VMEM((10, UNET, 256), BF16),
        pltpu.VMEM((2, 512, UNET), F32),
        pltpu.VMEM((2048, UNET), F32),
        pltpu.VMEM((10, 384, UNET), BF16),
        pltpu.VMEM((1024, 128), F32),
        pltpu.VMEM((15, 64, 128), BF16),
        pltpu.VMEM((15, 64, 128), BF16),
        pltpu.VMEM((2, 64, 128), BF16),
        pltpu.VMEM((2, 64, 128), BF16),
        pltpu.VMEM((64, 128), F32),
        pltpu.VMEM((80, 128), F32),
        pltpu.VMEM((6, 80, HID), BF16),
        pltpu.VMEM((6, 72, HID), BF16),
        pltpu.VMEM((2, 256, 128), F32),
        pltpu.VMEM((9, 3 * UNET, 128), F32),
        pltpu.VMEM((3, 576, UNET), BF16),
        pltpu.VMEM((3, 576, UNET), BF16),
        pltpu.VMEM((9, 576, 128), F32),
        pltpu.VMEM((27, 48, UNET), BF16),
        pltpu.VMEM((27, 48, UNET), BF16),
        pltpu.VMEM((9, 256, 128), F32),
        pltpu.VMEM((9, 48, UNET), BF16),
        pltpu.VMEM((9, 48, UNET), BF16),
        pltpu.VMEM((9, 64, 128), F32),
        pltpu.VMEM((9, 16, UNET), BF16),
        pltpu.VMEM((9, 16, UNET), BF16),
        dma((8,)),
        dma((8,)),
        dma((2,)),
        dma((2,)),
        dma((15,)),
        dma((15,)),
        dma((2,)),
        dma((2,)),
        dma((15,)),
        dma((15,)),
        dma((2,)),
        dma((2,)),
        dma((3,)),
        dma((3,)),
        dma((27,)),
        dma((27,)),
        dma((9,)),
        dma((9,)),
        dma((9,)),
        dma((9,)),
    ]
    shapes = (
        jax.ShapeDtypeStruct((8, 16, FEAT), F32),
        jax.ShapeDtypeStruct((9, 3, UNET), F32),
    )
    results = pl.pallas_call(
        kernel,
        out_shape=shapes,
        in_specs=[pl.BlockSpec(memory_space=pltpu.SMEM)] + [hbm] * 8,
        out_specs=(vmem, vmem),
        scratch_shapes=scratch,
        compiler_params=pltpu.CompilerParams(
            collective_id=0, has_side_effects=True, vmem_limit_bytes=60 * 1024 * 1024
        ),
        cost_estimate=pl.CostEstimate(flops=18_000_000_000, bytes_accessed=8_000_000, transcendentals=3_000_000),
    )(timesteps, *operands)
    feature_grad, middle_grad = pl.pallas_call(
        hand_over,
        out_shape=shapes,
        in_specs=[vmem, vmem],
        out_specs=(vmem, vmem),
    )(*results)
    return feature_grad, jnp.transpose(middle_grad, (1, 0, 2))


def solution(mesh):
    in_specs = (
        P("tile", "step", None),
        P(),
        P(),
        P("step"),
        P("step", "tile", None),
        P(),
        P(),
        P(),
        P(),
    )
    out_specs = (P("tile", "step", None), P(("tile", "step"), None, None))
    return jax.shard_map(per_device, mesh=mesh, in_specs=in_specs, out_specs=out_specs, check_vma=False)
```

```python
import math

import jax
import jax.numpy as jnp
from jax import lax
from jax.experimental import pallas as pl
from jax.experimental.pallas import tpu as pltpu
from jax.sharding import PartitionSpec as P

F32 = jnp.float32
BF16 = jnp.bfloat16
MESH = pl.DeviceIdType.MESH

FEAT, HID, LAT, UNET = 256, 512, 32, 384
TILES, STEPS = 8, 16
AROUND = ((-1, -1), (-1, 0), (-1, 1), (0, -1), (0, 1), (1, -1), (1, 0), (1, 1))


def sigmoid(values):
    return 0.5 * jnp.tanh(0.5 * values) + 0.5


def slope_of(values, sigma):
    return sigma * (1.0 + values * (1.0 - sigma))


def dot(left, right):
    return jnp.dot(left, right, preferred_element_type=F32)


def lane_tiles(value):
    return [value[:, 128 * i : 128 * i + 128] for i in range(value.shape[1] // 128)]


def shift_down(block):
    last = pltpu.roll(block[48:64], 1, 0)
    rows = lax.broadcasted_iota(jnp.int32, last.shape, 0)
    return jnp.concatenate([jnp.where(rows == 0, 0.0, last), block[0:48]], axis=0)


def shift_up(block):
    first = pltpu.roll(block[0:16], 15, 0)
    rows = lax.broadcasted_iota(jnp.int32, first.shape, 0)
    return jnp.concatenate([block[16:64], jnp.where(rows == 15, 0.0, first)], axis=0)


def kernel(
    time_ref,
    feat_hbm,
    enc_hbm,
    latw_hbm,
    noise_hbm,
    table_hbm,
    inw_hbm,
    midw_hbm,
    outw_hbm,
    fgrad_ref,
    mgrad_ref,
    feat,
    enc,
    latw,
    noise,
    table,
    inw,
    midw,
    outw,
    in_sem,
    enc_t,
    mid_t,
    latw4,
    latw4_t,
    inw4,
    inw4_t,
    outw4,
    outw4_t,
    embed,
    edge,
    edge_in,
    rows_in,
    grid,
    blocks_even,
    blocks_odd,
    pre_hidden,
    lat_tile,
    lat_pack,
    lat_send,
    lat_recv,
    lat_flat,
    noise_rows,
    noise_edge,
    noise_edge_in,
    inner_ext,
    inner_slope,
    inner_t,
    inner_tm,
    pre_middle,
    back_mixed,
    back_ext,
    back_part,
    part_send,
    part_recv,
    round_pack,
    round_send,
    round_recv,
    round_grid,
    hidden_even,
    hidden_odd,
    out_grid,
    grad,
    s1_send,
    s1_recv,
    sum1,
    s2_send,
    s2_recv,
    sum2,
    s3_send,
    s3_recv,
    sum3,
    s4_send,
    s4_recv,
    feat_ss,
    feat_rs,
    noise_ss,
    noise_rs,
    lat_ss,
    lat_rs,
    halo_ss,
    halo_rs,
    part_ss,
    part_rs,
    round_ss,
    round_rs,
    s1_ss,
    s1_rs,
    s2_ss,
    s2_rs,
    s3_ss,
    s3_rs,
    s4_ss,
    s4_rs,
):
    t = lax.axis_index("tile")
    s = lax.axis_index("step")
    y_hi, x = t // 4, t % 4
    z, y_lo, core = s // 4, (s // 2) % 2, s % 2
    y = y_hi * 2 + y_lo

    def remote(src, dst, ss, rs, tile, step):
        return pltpu.make_async_remote_copy(
            src_ref=src, dst_ref=dst, send_sem=ss, recv_sem=rs, device_id=(tile, step), device_id_type=MESH
        )

    def near(offsets):
        return (t + offsets[0] + TILES) % TILES, (s + offsets[1] + STEPS) % STEPS

    loads = [
        pltpu.make_async_copy(src, dst, in_sem.at[i])
        for i, (src, dst) in enumerate(
            (
                (feat_hbm, feat),
                (noise_hbm, noise),
                (enc_hbm, enc),
                (latw_hbm, latw),
                (inw_hbm, inw),
                (outw_hbm, outw),
                (table_hbm, table),
                (midw_hbm, midw),
            )
        )
    ]
    for load in loads:
        load.start()
    l_feat, l_noise, l_enc, l_latw, l_inw, l_outw, l_table, l_midw = loads

    barrier = pltpu.get_barrier_semaphore()

    for k in range(1, STEPS):
        pl.semaphore_signal(barrier, inc=1, device_id=(t, (s + k) % STEPS), device_id_type=MESH)
    for k in range(1, TILES):
        pl.semaphore_signal(barrier, inc=1, device_id=((t + k) % TILES, s), device_id_type=MESH)
    for offsets in AROUND:
        if offsets[0] and offsets[1]:
            pl.semaphore_signal(barrier, inc=1, device_id=near(offsets), device_id_type=MESH)

    l_feat.wait()
    grid[...] = jnp.zeros_like(grid)
    for r in range(8):
        for i, part in enumerate(lane_tiles(feat[r].astype(F32))):
            grid[i, (r + 2) * 32 + 8 : (r + 2) * 32 + 24, :] = part
    for side, first in ((0, 8), (1, 22)):
        for i in range(2):
            pair = [grid[i, pl.ds(64 + first + col, 8, stride=32), :] for col in (0, 1)]
            edge[side, :, 128 * i : 128 * i + 128] = jnp.concatenate(pair, axis=0).astype(BF16)

    pl.semaphore_wait(barrier, STEPS - 1 + TILES - 1 + 4)

    feat_copies = []
    for d, offsets in enumerate(AROUND):
        tile, step = near(offsets)
        if offsets[0] == 0:
            side = 0 if offsets[1] < 0 else 1
            src, dst = edge.at[side], edge_in.at[side]
        else:
            slot = d if d < 3 else d - 2
            src, dst = feat.at[pl.ds(0 if offsets[0] < 0 else 6, 2)], rows_in.at[slot]
        copy = remote(src, dst, feat_ss.at[d], feat_rs.at[d], tile, step)
        copy.start()
        feat_copies.append(copy)

    l_noise.wait()
    for q in range(64):
        piece = noise[0, :, 128 * q : 128 * q + 128].astype(F32)
        noise_rows[pl.ds(64 + (q % 4) * 16 + q // 4, 8, stride=64), :] = piece
    noise_edge[0] = noise_rows[64:128, :].astype(BF16)
    noise_edge[1] = noise_rows[512:576, :].astype(BF16)
    noise_copies = []
    for side, offset in ((0, -1), (1, 1)):
        tile, step = near((offset, 0))
        copy = remote(noise_edge.at[side], noise_edge_in.at[side], noise_ss.at[side], noise_rs.at[side], tile, step)
        copy.start()
        noise_copies.append(copy)

    for load, weight, wide, flipped in (
        (l_latw, latw, latw4_t, latw4),
        (l_inw, inw, inw4, inw4_t),
        (l_outw, outw, outw4_t, outw4),
    ):
        load.wait()
        columns = weight.shape[1]
        wide[...] = jnp.zeros_like(wide)
        for j in range(4):
            wide[LAT * j : LAT * j + LAT, columns * j : columns * j + columns] = weight[...]
        if flipped is latw4:
            flipped[...] = jnp.transpose(wide[...])

    l_enc.wait()

    for d, copy in enumerate(feat_copies):
        copy.wait()
    for d, offsets in enumerate(AROUND):
        dt, ds = offsets
        valid = jnp.bool_(True)
        if dt:
            valid = (t < TILES - 1) if dt < 0 else (t > 0)
        if ds:
            beside = (s < STEPS - 1) if ds < 0 else (s > 0)
            valid = jnp.logical_and(valid, beside) if dt else beside
        if dt == 0:
            side = 0 if ds < 0 else 1
            taken = jnp.where(valid, edge_in[side].astype(F32), 0.0)
            first = 24 if ds < 0 else 6
            for i, part in enumerate(lane_tiles(taken)):
                for col in (0, 1):
                    grid[i, pl.ds(64 + first + col, 8, stride=32), :] = part[8 * col : 8 * col + 8]
        else:
            slot = d if d < 3 else d - 2
            for r in range(2):
                taken = jnp.where(valid, rows_in[slot, r].astype(F32), 0.0)
                row = (10 + r if dt < 0 else r) * 32
                for i, part in enumerate(lane_tiles(taken)):
                    if ds == 0:
                        grid[i, row + 8 : row + 24, :] = part
                    elif ds < 0:
                        grid[i, row + 24 : row + 32, :] = part[0:8]
                    else:
                        grid[i, row : row + 8, :] = part[8:16]

    def put_blocks(even, odd, index, value):
        even[index] = value.astype(BF16)
        odd[index] = value[8:].astype(BF16)

    for j in range(4):
        value = jnp.concatenate([grid[i, pl.ds(j, 96, stride=4), :] for i in range(2)], axis=1)
        put_blocks(blocks_even, blocks_odd, 1 + j, value)
        if j == 0:
            put_blocks(blocks_even, blocks_odd, 5, pltpu.roll(value, 95, 0))
        if j == 3:
            put_blocks(blocks_even, blocks_odd, 0, pltpu.roll(value, 1, 0))
    pieces = []
    for a in range(3):
        for b in range(3):
            if a == 1:
                window = blocks_odd[b : b + 4, 0:80, :]
            else:
                window = blocks_even[b : b + 4, 8 * a : 8 * a + 80, :]
            pieces.append(window.reshape(320, FEAT))
    pre = dot(jnp.concatenate(pieces, axis=1), enc[...].reshape(9 * FEAT, HID))
    pre_hidden[...] = pre
    hidden = (pre * sigmoid(pre)).astype(BF16)
    hidden = jnp.concatenate([hidden[80 * j : 80 * j + 80] for j in range(4)], axis=1)
    lat_tile[...] = dot(hidden, latw4[...])
    lat_pack[...] = jnp.zeros_like(lat_pack)
    for q in range(4):
        lat_pack[pl.ds(q, 10, stride=4), :] = lat_tile[pl.ds(2 + q, 10, stride=8), :]
    lat_send[...] = lat_pack[...].astype(BF16)

    def lat_copy(k):
        return remote(lat_send, lat_recv.at[k - 1], lat_ss.at[k - 1], lat_rs.at[k - 1], t, (s + k) % STEPS)

    for k in range(1, STEPS):
        lat_copy(k).start()

    inw4_t[...] = jnp.transpose(inw4[...])
    outw4[...] = jnp.transpose(outw4_t[...])
    chosen = time_ref[0]
    angle = ((jnp.full((8, 128), chosen, jnp.int32).astype(F32) + 1.0) / 1000.0 + 0.008) / 1.008 * (math.pi / 2.0)
    cosine = jnp.cos(angle)[0:1, :]
    sine = jnp.sin(angle)[0:1, :]
    l_table.wait()
    onehot = (lax.broadcasted_iota(jnp.int32, (16, table.shape[0]), 1) == chosen).astype(F32).astype(BF16)
    embed[...] = dot(onehot, table[...])[0:8]

    l_midw.wait()
    for side in (0, 1):
        noise_copies[side].wait()
    noise_rows[576:640, :] = noise_edge_in[0].astype(F32)
    noise_rows[0:64, :] = noise_edge_in[1].astype(F32)

    lat_flat[pl.ds(pl.multiple_of(s * 48, 16), 48), :] = lat_pack[...].astype(BF16).astype(F32)

    for k in range(1, STEPS):
        lat_copy(k).wait()
    for k in range(1, STEPS):
        source = (s - k + STEPS) % STEPS
        lat_flat[pl.ds(pl.multiple_of(source * 48, 16), 48), :] = lat_recv[k - 1].astype(F32)

    def input_rows(pair):
        first = 2 * pair
        latent = [lat_flat[pl.ds((first + r) * 4 + q, 16, stride=48), :] for r in range(2) for q in range(4)]
        noisy = cosine * jnp.concatenate(latent, axis=0) + sine * noise_rows[64 * first : 64 * first + 128, :]
        noisy = noisy.astype(BF16)
        for j in range(4):
            pre = dot(noisy, inw4[:, UNET * j : UNET * j + UNET]) + embed[0:1, :]
            sigma = sigmoid(pre)
            inner = pre * sigma
            slope = slope_of(pre, sigma)
            for r in range(2):
                row = first + r
                own = inner[64 * r : 64 * r + 64]
                if row == 0:
                    own = own * jnp.where(t > 0, 1.0, 0.0)
                if row == 9:
                    own = own * jnp.where(t < TILES - 1, 1.0, 0.0)
                inner_ext[row, 64 + 64 * j : 128 + 64 * j, :] = own.astype(BF16)
                if j == 0:
                    inner_ext[row, 320:384, :] = shift_up(own).astype(BF16)
                if j == 3:
                    inner_ext[row, 0:64, :] = shift_down(own).astype(BF16)
                if 0 < row < 9:
                    inner_slope[row - 1, 64 * j : 64 * j + 64, :] = slope[64 * r : 64 * r + 64]

    def flip_rows(pair):
        for row in (2 * pair, 2 * pair + 1):
            flipped = jnp.transpose(inner_ext[row])
            inner_t[row] = flipped
            inner_tm[row] = flipped[:, 64:320]

    def by_class(value):
        rows = value.shape[0] // 256
        return jnp.concatenate(
            [
                jnp.concatenate([value[256 * r + 64 * j : 256 * r + 64 * j + 64] for j in range(4)], axis=1)
                for r in range(rows)
            ],
            axis=0,
        )

    def by_position(value):
        rows = value.shape[0] // 64
        return jnp.concatenate(
            [value[64 * r : 64 * r + 64, UNET * j : UNET * j + UNET] for r in range(rows) for j in range(4)], axis=0
        )

    def forward_conv(i):
        windows = [
            inner_ext[2 * i + a : 2 * i + a + 2, 64 * b : 64 * b + 256, :].reshape(512, UNET)
            for a in range(3)
            for b in range(3)
        ]
        pre_middle[i % 2] = dot(jnp.concatenate(windows, axis=1), midw[...].reshape(9 * UNET, UNET))

    def forward_after(i):
        r = 2 * i
        pre = pre_middle[i % 2]
        sigma = sigmoid(pre)
        own = inner_ext[r + 1 : r + 3, 64:320, :].reshape(512, UNET)
        mixed = (own.astype(F32) + pre * sigma).astype(BF16)
        prediction = dot(by_class(mixed), outw4[...])
        own_noise = noise_rows[64 + r * 64 : 192 + r * 64, :]
        error = ((prediction - own_noise) * (1.0 / math.sqrt(STEPS))).astype(BF16)
        pulled = by_position(dot(error, outw4_t[...]))
        back_mixed[256 * r : 256 * r + 512, :] = pulled
        back = pulled * slope_of(pre, sigma)
        for row in range(2):
            own = back[256 * row : 256 * row + 256]
            back_ext[r + 1 + row, 64:320, :] = own.astype(BF16)
            back_ext[r + 1 + row, 320:384, :] = shift_up(own[0:64]).astype(BF16)
            back_ext[r + 1 + row, 0:64, :] = shift_down(own[192:256]).astype(BF16)

    halo_copies = []

    def halo_start(side):
        tile, step = near((2 * side - 1, 0))
        src, dst = ((1, 9), (8, 0))[side]
        src, dst = back_ext.at[src, pl.ds(64, 256)], back_ext.at[dst, pl.ds(64, 256)]
        copy = remote(src, dst, halo_ss.at[side], halo_rs.at[side], tile, step)
        copy.start()
        halo_copies.append(copy)

    input_rows(0)
    input_rows(1)
    for i in range(4):
        forward_conv(i)
        if i < 3:
            input_rows(i + 2)
        flip_rows(i)
        if i:
            forward_after(i - 1)
        if i == 1:
            halo_start(0)
    flip_rows(4)
    forward_after(3)
    halo_start(1)

    def s1_copy(a):
        return remote(s1_send.at[a], s1_recv.at[a], s1_ss.at[a], s1_rs.at[a], t, s + 1 - 2 * core)

    def s1_pack(a):
        for n in range(9):
            first = (n // 3) * UNET + n % 3 + 3 * (1 - core)
            block = jnp.concatenate([grad[a * 3 + i, pl.ds(first, 64, stride=6), :] for i in range(3)], axis=1)
            s1_send[a, 64 * n : 64 * n + 64, :] = block.astype(BF16)

    def s1_add(a):
        for n in range(9):
            first = (n // 3) * UNET + n % 3 + 3 * core
            got = s1_recv[a, 64 * n : 64 * n + 64, :].astype(F32)
            for i in range(3):
                own = grad[a * 3 + i, pl.ds(first, 64, stride=6), :]
                sum1[a * 3 + i, 64 * n : 64 * n + 64, :] = own + got[:, 128 * i : 128 * i + 128]

    def axis_peer(axis, k):
        if axis == "z":
            there = (z + k) % 4
            return there, t, there * 4 + s % 4
        if axis == "x":
            there = (x + k) % 4
            return there, y_hi * 4 + there, s
        there = (y + k) % 4
        return there, (there // 2) * 4 + x, z * 4 + (there % 2) * 2 + core

    first_axis, second_axis, third_axis = ("z", "x", "y"), ("x", "z", "z"), ("y", "y", "x")

    def plane_rows(a, b, c, there):
        base = (3 * b + c) * 64
        parts = []
        for i in range(3):
            ref = sum1.at[a * 3 + i]
            if b == 0:
                parts.append(
                    jnp.concatenate([ref[pl.ds(base + 2 * there + low, 8, stride=8), :] for low in (0, 1)], axis=0)
                )
            elif b == 1:
                rows = [pl.ds(pl.multiple_of(base + high * 32 + there * 8, 8), 8) for high in (0, 1)]
                parts.append(jnp.concatenate([ref[row, :] for row in rows], axis=0))
            else:
                parts.append(ref[pl.ds(base + (there // 2) * 32 + there % 2, 16, stride=2), :])
        return jnp.concatenate(parts, axis=1)

    onward = (3, 1)

    def s2_offset(a, slot):
        if a == 2:
            return slot + 1
        return onward[a] if slot else 4 - onward[a]

    def s2_copy(a, b, slot):
        _, tile, step = axis_peer(first_axis[b], s2_offset(a, slot))
        index = (a * 3 + b) * 3 + slot
        return remote(s2_send.at[index], s2_recv.at[index], s2_ss.at[index], s2_rs.at[index], tile, step)

    def s2_pack(a):
        for b in range(3):
            for slot in range(3 if a == 2 else 2):
                away = 2 if a < 2 and slot else s2_offset(a, slot)
                there = axis_peer(first_axis[b], away)[0]
                for c in range(3):
                    block = plane_rows(a, b, c, there).astype(BF16)
                    s2_send[(a * 3 + b) * 3 + slot, 16 * c : 16 * c + 16, :] = block

    def s2_start(a):
        for slot in (1, 0, 2) if a == 2 else (1, 0):
            for b in range(3):
                s2_copy(a, b, slot).start()

    def s2_hand_wait(a):
        for b in range(3):
            s2_copy(a, b, 1).wait()

    def s2_hand_pack(a):
        for b in range(3):
            there = axis_peer(first_axis[b], onward[a])[0]
            index = (a * 3 + b) * 3
            for c in range(3):
                rows = slice(16 * c, 16 * c + 16)
                block = plane_rows(a, b, c, there) + s2_recv[index + 1, rows, :].astype(F32)
                s2_send[index + 2, rows, :] = block.astype(BF16)

    def s2_hand_start(a):
        for b in range(3):
            s2_copy(a, b, 2).start()

    def s2_wait(a):
        for b in range(3):
            for slot in range(3) if a == 2 else (0, 2):
                s2_copy(a, b, slot).wait()

    def s2_add(a):
        for b in range(3):
            mine = axis_peer(first_axis[b], 0)[0]
            for c in range(3):
                total = plane_rows(a, b, c, mine)
                for slot in range(3) if a == 2 else (0, 2):
                    total = total + s2_recv[(a * 3 + b) * 3 + slot, 16 * c : 16 * c + 16, :].astype(F32)
                row = 16 * (3 * a + c)
                for i, part in enumerate(lane_tiles(total)):
                    sum2[b * 3 + i, row : row + 16, :] = part

    def line_rows(b, there):
        parts = []
        for i in range(3):
            ref = sum2.at[b * 3 + i]
            if b == 1:
                parts.append(
                    jnp.concatenate([ref[pl.ds(2 * there + low, 24, stride=8), :] for low in (0, 1)], axis=0)
                )
            else:
                parts.append(ref[pl.ds(there, 48, stride=4), :])
        return jnp.concatenate(parts, axis=1)

    def s3_copy(b, k):
        _, tile, step = axis_peer(second_axis[b], k)
        index = b * 3 + k - 1
        return remote(s3_send.at[index], s3_recv.at[index], s3_ss.at[index], s3_rs.at[index], tile, step)

    def s3_start():
        for b in range(3):
            for k in range(1, 4):
                s3_send[b * 3 + k - 1] = line_rows(b, axis_peer(second_axis[b], k)[0]).astype(BF16)
        for b in range(3):
            for k in range(1, 4):
                s3_copy(b, k).start()

    def point_rows(b, there):
        if b == 0:
            rows = pl.ds((there % 2) * 2 + there // 2, 16, stride=4)
        elif b == 1:
            rows = pl.ds((there % 2) * 24 + there // 2, 16, stride=2)
        else:
            rows = pl.ds(there, 16, stride=4)
        return jnp.concatenate([sum3[b * 3 + i, rows, :] for i in range(3)], axis=1)

    def s4_copy(b, k):
        _, tile, step = axis_peer(third_axis[b], k)
        index = b * 3 + k - 1
        return remote(s4_send.at[index], s4_recv.at[index], s4_ss.at[index], s4_rs.at[index], tile, step)

    def s4_start():
        for b in range(3):
            for k in range(1, 4):
                s3_copy(b, k).wait()
        for b in range(3):
            total = line_rows(b, axis_peer(second_axis[b], 0)[0])
            for k in range(3):
                total = total + s3_recv[b * 3 + k].astype(F32)
            for i, part in enumerate(lane_tiles(total)):
                sum3[b * 3 + i, 0:48, :] = part
        for b in range(3):
            for k in range(1, 4):
                s4_send[b * 3 + k - 1] = point_rows(b, axis_peer(third_axis[b], k)[0]).astype(BF16)
        for b in range(3):
            for k in range(1, 4):
                s4_copy(b, k).start()

    def finish():
        for b in range(3):
            for k in range(1, 4):
                s4_copy(b, k).wait()
        for b in range(3):
            total = point_rows(b, axis_peer(third_axis[b], 0)[0])
            for k in range(3):
                total = total + s4_recv[b * 3 + k].astype(F32)
            total = total * (1.0 / math.sqrt(64 * 256))
            for a in range(3):
                mgrad_ref[3 * a + b] = total[3 * a : 3 * a + 3]

    def weight_product(a):
        taps = [
            jnp.concatenate([inner_t[r + a, :, 0:256] for r in range(8)], axis=1),
            jnp.concatenate([inner_tm[r + a] for r in range(8)], axis=1),
            jnp.concatenate([inner_t[r + a, :, 128:384] for r in range(8)], axis=1),
        ]
        result = dot(jnp.concatenate(taps, axis=0), back_ext[1:9, 64:320, :].reshape(2048, UNET))
        for i, part in enumerate(lane_tiles(result)):
            grad[a * 3 + i] = part

    sum2[...] = jnp.zeros_like(sum2)
    sum3[...] = jnp.zeros_like(sum3)
    for a in range(3):
        weight_product(a)
        for k in range(3 * a, 3 * a + 3):
            mid_t[k] = jnp.transpose(midw[k])
        if a == 2:
            s1_add(0)
            s2_pack(0)
            s2_start(0)
        s1_pack(a)
        s1_copy(a).start()
        if a == 1:
            s1_copy(0).wait()

    for row, copy in ((9, halo_copies[0]), (0, halo_copies[1])):
        copy.wait()
        back_ext[row, 320:384, :] = shift_up(back_ext[row, 64:128, :].astype(F32)).astype(BF16)
        back_ext[row, 0:64, :] = shift_down(back_ext[row, 256:320, :].astype(F32)).astype(BF16)

    @pl.when(t == 0)
    def _():
        back_ext[0] = jnp.zeros_like(back_ext[0])

    @pl.when(t == TILES - 1)
    def _():
        back_ext[9] = jnp.zeros_like(back_ext[9])

    def backward_conv(i):
        r = 2 * i
        windows = [
            back_ext[r + 2 - a : r + 4 - a, 64 * (2 - b) : 64 * (2 - b) + 256, :].reshape(512, UNET)
            for a in range(3)
            for b in range(3)
        ]
        pre_middle[i % 2] = dot(jnp.concatenate(windows, axis=1), mid_t[...].reshape(9 * UNET, UNET))

    def backward_after(i):
        r = 2 * i
        through = pre_middle[i % 2] + back_mixed[256 * r : 256 * r + 512, :]
        back = (through * inner_slope[r : r + 2].reshape(512, UNET)).astype(BF16)
        back_part[64 * r : 64 * r + 128, :] = cosine * dot(by_class(back), inw4_t[...])

    def flip_enc(first, last):
        for k in range(first, last):
            enc_t[k] = jnp.transpose(enc[k])

    s1_copy(1).wait()
    backward_conv(0)
    s1_add(1)
    s2_pack(1)
    flip_enc(0, 3)
    s2_start(1)

    s1_copy(2).wait()
    s2_hand_wait(0)
    backward_conv(1)
    backward_after(0)
    s1_add(2)
    s2_pack(2)
    s2_hand_pack(0)
    flip_enc(3, 6)
    s2_start(2)
    s2_hand_start(0)

    s2_hand_wait(1)
    backward_conv(2)
    backward_after(1)
    s2_hand_pack(1)
    flip_enc(6, 9)
    s2_hand_start(1)

    backward_conv(3)
    backward_after(2)
    backward_after(3)

    def part_copy(k):
        return remote(
            part_send.at[k - 1], part_recv.at[k - 1], part_ss.at[k - 1], part_rs.at[k - 1], t, (s + k) % STEPS
        )

    for k in range(1, STEPS):
        part_send[k - 1] = back_part[pl.ds((s + k) % STEPS, 32, stride=16), :].astype(BF16)
    for k in range(1, STEPS):
        part_copy(k).start()

    for a in range(3):
        s2_wait(a)
        s2_add(a)
    s3_start()

    for k in range(1, STEPS):
        part_copy(k).wait()
    latent_round = back_part[pl.ds(s, 32, stride=16), :]
    for k in range(1, STEPS):
        latent_round = latent_round + part_recv[k - 1].astype(F32)
    round_send[...] = latent_round.astype(BF16)
    round_copies = []
    for d, offsets in enumerate(AROUND):
        tile, step = near(offsets)
        copy = remote(round_send, round_recv.at[d], round_ss.at[d], round_rs.at[d], tile, step)
        copy.start()
        round_copies.append(copy)

    s4_start()

    round_grid[...] = jnp.zeros_like(round_grid)
    round_pack[...] = round_send[...].astype(F32)
    for q in range(4):
        round_grid[pl.ds(10 + q, 8, stride=8), :] = round_pack[pl.ds(q, 8, stride=4), :]
    for d, (dt, ds) in enumerate(AROUND):
        round_copies[d].wait()
        valid = jnp.bool_(True)
        if dt:
            valid = (t < TILES - 1) if dt < 0 else (t > 0)
        if ds:
            beside = (s < STEPS - 1) if ds < 0 else (s > 0)
            valid = jnp.logical_and(valid, beside) if dt else beside
        round_pack[...] = jnp.where(valid, round_recv[d].astype(F32), 0.0)
        if dt == 0:
            q, place = (0, 6) if ds < 0 else (3, 1)
            round_grid[pl.ds(8 + place, 8, stride=8), :] = round_pack[pl.ds(q, 8, stride=4), :]
        else:
            source, row = (0, 72) if dt < 0 else (28, 0)
            if ds == 0:
                round_grid[row + 2 : row + 6, :] = round_pack[source : source + 4, :]
            else:
                q, place = (0, 6) if ds < 0 else (3, 1)
                round_grid[row + place : row + place + 1, :] = round_pack[source + q : source + q + 1, :]
    pulled = dot(round_grid[...].astype(BF16), latw4_t[...])
    for j in range(4):
        pre = pre_hidden[80 * j : 80 * j + 80, :]
        value = pulled[:, HID * j : HID * j + HID] * slope_of(pre, sigmoid(pre))
        put_blocks(hidden_even, hidden_odd, 1 + j, value)
        if j == 0:
            put_blocks(hidden_even, hidden_odd, 5, pltpu.roll(value, 79, 0))
        if j == 3:
            put_blocks(hidden_even, hidden_odd, 0, pltpu.roll(value, 1, 0))
    pieces = []
    for a in range(3):
        for b in range(3):
            if a == 1:
                window = hidden_odd[2 - b : 6 - b, 0:64, :]
            else:
                window = hidden_even[2 - b : 6 - b, 8 * (2 - a) : 8 * (2 - a) + 64, :]
            pieces.append(window.reshape(256, HID))
    result = dot(jnp.concatenate(pieces, axis=1), enc_t[...].reshape(9 * HID, FEAT))
    for j in range(4):
        for i, part in enumerate(lane_tiles(result[64 * j : 64 * j + 64])):
            out_grid[i, pl.ds(j, 64, stride=4), :] = part
    for r in range(8):
        for i in range(2):
            fgrad_ref[r, :, 128 * i : 128 * i + 128] = out_grid[i, r * 32 + 8 : r * 32 + 24, :]

    finish()


def hand_over(fgrad_ref, mgrad_ref, fgrad_out, mgrad_out):
    fgrad_out[...] = fgrad_ref[...]
    mgrad_out[...] = mgrad_ref[...]


def per_device(
    features,
    encoder_weight,
    latent_weight,
    timesteps,
    noise_field,
    time_table,
    input_weight,
    middle_weight,
    output_weight,
):
    hbm = pl.BlockSpec(memory_space=pl.ANY)
    vmem = pl.BlockSpec(memory_space=pltpu.VMEM)
    dma = pltpu.SemaphoreType.DMA
    operands = (
        features,
        encoder_weight,
        latent_weight.T,
        noise_field,
        time_table,
        input_weight,
        middle_weight,
        output_weight.T,
    )
    scratch = [
        pltpu.VMEM((8, 16, FEAT), BF16),
        pltpu.VMEM((9, FEAT, HID), BF16),
        pltpu.VMEM((LAT, HID), BF16),
        pltpu.VMEM(noise_field.shape, BF16),
        pltpu.VMEM(time_table.shape, BF16),
        pltpu.VMEM((LAT, UNET), BF16),
        pltpu.VMEM((9, UNET, UNET), BF16),
        pltpu.VMEM((LAT, UNET), BF16),
        dma((8,)),
        pltpu.VMEM((9, HID, FEAT), BF16),
        pltpu.VMEM((9, UNET, UNET), BF16),
        pltpu.VMEM((4 * HID, 128), BF16),
        pltpu.VMEM((128, 4 * HID), BF16),
        pltpu.VMEM((128, 4 * UNET), BF16),
        pltpu.VMEM((4 * UNET, 128), BF16),
        pltpu.VMEM((4 * UNET, 128), BF16),
        pltpu.VMEM((128, 4 * UNET), BF16),
        pltpu.VMEM((8, UNET), F32),
        pltpu.VMEM((2, 16, FEAT), BF16),
        pltpu.VMEM((2, 16, FEAT), BF16),
        pltpu.VMEM((6, 2, 16, FEAT), BF16),
        pltpu.VMEM((2, 12 * 32, 128), F32),
        pltpu.VMEM((6, 96, FEAT), BF16),
        pltpu.VMEM((6, 88, FEAT), BF16),
        pltpu.VMEM((320, HID), F32),
        pltpu.VMEM((80, 128), F32),
        pltpu.VMEM((48, 128), F32),
        pltpu.VMEM((48, 128), BF16),
        pltpu.VMEM((15, 48, 128), BF16),
        pltpu.VMEM((16 * 48, 128), F32),
        pltpu.VMEM((640, 128), F32),
        pltpu.VMEM((2, 64, 128), BF16),
        pltpu.VMEM((2, 64, 128), BF16),
        pltpu.VMEM((10, 384, UNET), BF16),
        pltpu.VMEM((8, 256, UNET), F32),
        pltpu.VMEM((10, UNET, 384), BF16),
        pltpu.VMEM((10, UNET, 256), BF16),
        pltpu.VMEM((2, 512, UNET), F32),
        pltpu.VMEM((2048, UNET), F32),
        pltpu.VMEM((10, 384, UNET), BF16),
        pltpu.VMEM((512, 128), F32),
        pltpu.VMEM((15, 32, 128), BF16),
        pltpu.VMEM((15, 32, 128), BF16),
        pltpu.VMEM((32, 128), F32),
        pltpu.VMEM((32, 128), BF16),
        pltpu.VMEM((8, 32, 128), BF16),
        pltpu.VMEM((80, 128), F32),
        pltpu.VMEM((6, 80, HID), BF16),
        pltpu.VMEM((6, 72, HID), BF16),
        pltpu.VMEM((2, 256, 128), F32),
        pltpu.VMEM((9, 3 * UNET, 128), F32),
        pltpu.VMEM((3, 576, UNET), BF16),
        pltpu.VMEM((3, 576, UNET), BF16),
        pltpu.VMEM((9, 576, 128), F32),
        pltpu.VMEM((27, 48, UNET), BF16),
        pltpu.VMEM((27, 48, UNET), BF16),
        pltpu.VMEM((9, 256, 128), F32),
        pltpu.VMEM((9, 48, UNET), BF16),
        pltpu.VMEM((9, 48, UNET), BF16),
        pltpu.VMEM((9, 64, 128), F32),
        pltpu.VMEM((9, 16, UNET), BF16),
        pltpu.VMEM((9, 16, UNET), BF16),
        dma((8,)),
        dma((8,)),
        dma((2,)),
        dma((2,)),
        dma((15,)),
        dma((15,)),
        dma((2,)),
        dma((2,)),
        dma((15,)),
        dma((15,)),
        dma((8,)),
        dma((8,)),
        dma((3,)),
        dma((3,)),
        dma((27,)),
        dma((27,)),
        dma((9,)),
        dma((9,)),
        dma((9,)),
        dma((9,)),
    ]
    shapes = (
        jax.ShapeDtypeStruct((8, 16, FEAT), F32),
        jax.ShapeDtypeStruct((9, 3, UNET), F32),
    )
    results = pl.pallas_call(
        kernel,
        out_shape=shapes,
        in_specs=[pl.BlockSpec(memory_space=pltpu.SMEM)] + [hbm] * 8,
        out_specs=(vmem, vmem),
        scratch_shapes=scratch,
        compiler_params=pltpu.CompilerParams(
            collective_id=0, has_side_effects=True, vmem_limit_bytes=60 * 1024 * 1024
        ),
        cost_estimate=pl.CostEstimate(flops=18_000_000_000, bytes_accessed=8_000_000, transcendentals=3_000_000),
    )(timesteps, *operands)
    feature_grad, middle_grad = pl.pallas_call(
        hand_over,
        out_shape=shapes,
        in_specs=[vmem, vmem],
        out_specs=(vmem, vmem),
    )(*results)
    return feature_grad, jnp.transpose(middle_grad, (1, 0, 2))


def solution(mesh):
    in_specs = (
        P("tile", "step", None),
        P(),
        P(),
        P("step"),
        P("step", "tile", None),
        P(),
        P(),
        P(),
        P(),
    )
    out_specs = (P("tile", "step", None), P(("tile", "step"), None, None))
    return jax.shard_map(per_device, mesh=mesh, in_specs=in_specs, out_specs=out_specs, check_vma=False)
```

```python
import math

import jax
import jax.numpy as jnp
from jax import lax
from jax.experimental import pallas as pl
from jax.experimental.pallas import tpu as pltpu
from jax.sharding import PartitionSpec as P

F32 = jnp.float32
BF16 = jnp.bfloat16
MESH = pl.DeviceIdType.MESH

FEAT, HID, LAT, UNET = 256, 512, 32, 384
TILES, STEPS = 8, 16
AROUND = ((-1, -1), (-1, 0), (-1, 1), (0, -1), (0, 1), (1, -1), (1, 0), (1, 1))


def sigmoid(values):
    return 0.5 * jnp.tanh(0.5 * values) + 0.5


def slope_of(values, sigma):
    return sigma * (1.0 + values * (1.0 - sigma))


def dot(left, right):
    return jnp.dot(left, right, preferred_element_type=F32)


def lane_tiles(value):
    return [value[:, 128 * i : 128 * i + 128] for i in range(value.shape[1] // 128)]


def shift_down(block):
    last = pltpu.roll(block[48:64], 1, 0)
    rows = lax.broadcasted_iota(jnp.int32, last.shape, 0)
    return jnp.concatenate([jnp.where(rows == 0, 0.0, last), block[0:48]], axis=0)


def shift_up(block):
    first = pltpu.roll(block[0:16], 15, 0)
    rows = lax.broadcasted_iota(jnp.int32, first.shape, 0)
    return jnp.concatenate([block[16:64], jnp.where(rows == 15, 0.0, first)], axis=0)


def kernel(
    time_ref,
    feat_hbm,
    enc_hbm,
    latw_hbm,
    noise_hbm,
    table_hbm,
    inw_hbm,
    midw_hbm,
    outw_hbm,
    fgrad_ref,
    mgrad_ref,
    feat,
    enc,
    latw,
    noise,
    table,
    inw,
    midw,
    outw,
    in_sem,
    enc_t,
    mid_t,
    latw4,
    latw4_t,
    inw4,
    inw4_t,
    outw4,
    outw4_t,
    embed,
    edge,
    edge_in,
    rows_in,
    grid,
    blocks_even,
    blocks_odd,
    pre_hidden,
    lat_tile,
    lat_pack,
    lat_send,
    lat_recv,
    lat_flat,
    noise_rows,
    noise_edge,
    noise_edge_in,
    inner_ext,
    inner_slope,
    inner_t,
    inner_tm,
    pre_middle,
    back_mixed,
    back_ext,
    back_part,
    part_send,
    part_recv,
    round_pack,
    round_send,
    round_recv,
    round_grid,
    hidden_even,
    hidden_odd,
    out_grid,
    order,
    grad,
    s1_recv,
    s2_send,
    s2_recv,
    sum2,
    s3_send,
    s3_recv,
    sum3,
    s4_send,
    s4_recv,
    feat_ss,
    feat_rs,
    noise_ss,
    noise_rs,
    lat_ss,
    lat_rs,
    halo_ss,
    halo_rs,
    part_ss,
    part_rs,
    round_ss,
    round_rs,
    s1_ss,
    s1_rs,
    s2_ss,
    s2_rs,
    s3_ss,
    s3_rs,
    s4_ss,
    s4_rs,
):
    t = lax.axis_index("tile")
    s = lax.axis_index("step")
    y_hi, x = t // 4, t % 4
    z, y_lo, core = s // 4, (s // 2) % 2, s % 2
    y = y_hi * 2 + y_lo

    def remote(src, dst, ss, rs, tile, step):
        return pltpu.make_async_remote_copy(
            src_ref=src, dst_ref=dst, send_sem=ss, recv_sem=rs, device_id=(tile, step), device_id_type=MESH
        )

    def near(offsets):
        return (t + offsets[0] + TILES) % TILES, (s + offsets[1] + STEPS) % STEPS

    loads = [
        pltpu.make_async_copy(src, dst, in_sem.at[i])
        for i, (src, dst) in enumerate(
            (
                (feat_hbm, feat),
                (noise_hbm, noise),
                (enc_hbm, enc),
                (latw_hbm, latw),
                (inw_hbm, inw),
                (outw_hbm, outw),
                (table_hbm, table),
                (midw_hbm, midw),
            )
        )
    ]
    for load in loads:
        load.start()
    l_feat, l_noise, l_enc, l_latw, l_inw, l_outw, l_table, l_midw = loads

    barrier = pltpu.get_barrier_semaphore()

    for k in range(1, STEPS):
        pl.semaphore_signal(barrier, inc=1, device_id=(t, (s + k) % STEPS), device_id_type=MESH)
    for k in range(1, TILES):
        pl.semaphore_signal(barrier, inc=1, device_id=((t + k) % TILES, s), device_id_type=MESH)
    for offsets in AROUND:
        if offsets[0] and offsets[1]:
            pl.semaphore_signal(barrier, inc=1, device_id=near(offsets), device_id_type=MESH)

    l_feat.wait()
    grid[...] = jnp.zeros_like(grid)
    for r in range(8):
        for i, part in enumerate(lane_tiles(feat[r].astype(F32))):
            grid[i, (r + 2) * 32 + 8 : (r + 2) * 32 + 24, :] = part
    for side, first in ((0, 8), (1, 22)):
        for i in range(2):
            pair = [grid[i, pl.ds(64 + first + col, 8, stride=32), :] for col in (0, 1)]
            edge[side, :, 128 * i : 128 * i + 128] = jnp.concatenate(pair, axis=0).astype(BF16)

    pl.semaphore_wait(barrier, STEPS - 1 + TILES - 1 + 4)

    feat_copies = []
    for d, offsets in enumerate(AROUND):
        tile, step = near(offsets)
        if offsets[0] == 0:
            side = 0 if offsets[1] < 0 else 1
            src, dst = edge.at[side], edge_in.at[side]
        else:
            slot = d if d < 3 else d - 2
            src, dst = feat.at[pl.ds(0 if offsets[0] < 0 else 6, 2)], rows_in.at[slot]
        copy = remote(src, dst, feat_ss.at[d], feat_rs.at[d], tile, step)
        copy.start()
        feat_copies.append(copy)

    l_noise.wait()
    for q in range(64):
        piece = noise[0, :, 128 * q : 128 * q + 128].astype(F32)
        noise_rows[pl.ds(64 + (q % 4) * 16 + q // 4, 8, stride=64), :] = piece
    noise_edge[0] = noise_rows[64:128, :].astype(BF16)
    noise_edge[1] = noise_rows[512:576, :].astype(BF16)
    noise_copies = []
    for side, offset in ((0, -1), (1, 1)):
        tile, step = near((offset, 0))
        copy = remote(noise_edge.at[side], noise_edge_in.at[side], noise_ss.at[side], noise_rs.at[side], tile, step)
        copy.start()
        noise_copies.append(copy)

    for load, weight, wide, flipped in (
        (l_latw, latw, latw4_t, latw4),
        (l_inw, inw, inw4, inw4_t),
        (l_outw, outw, outw4_t, outw4),
    ):
        load.wait()
        columns = weight.shape[1]
        wide[...] = jnp.zeros_like(wide)
        for j in range(4):
            wide[LAT * j : LAT * j + LAT, columns * j : columns * j + columns] = weight[...]
        if flipped is latw4:
            flipped[...] = jnp.transpose(wide[...])

    l_enc.wait()

    for d, copy in enumerate(feat_copies):
        copy.wait()
    for d, offsets in enumerate(AROUND):
        dt, ds = offsets
        valid = jnp.bool_(True)
        if dt:
            valid = (t < TILES - 1) if dt < 0 else (t > 0)
        if ds:
            beside = (s < STEPS - 1) if ds < 0 else (s > 0)
            valid = jnp.logical_and(valid, beside) if dt else beside
        if dt == 0:
            side = 0 if ds < 0 else 1
            taken = jnp.where(valid, edge_in[side].astype(F32), 0.0)
            first = 24 if ds < 0 else 6
            for i, part in enumerate(lane_tiles(taken)):
                for col in (0, 1):
                    grid[i, pl.ds(64 + first + col, 8, stride=32), :] = part[8 * col : 8 * col + 8]
        else:
            slot = d if d < 3 else d - 2
            for r in range(2):
                taken = jnp.where(valid, rows_in[slot, r].astype(F32), 0.0)
                row = (10 + r if dt < 0 else r) * 32
                for i, part in enumerate(lane_tiles(taken)):
                    if ds == 0:
                        grid[i, row + 8 : row + 24, :] = part
                    elif ds < 0:
                        grid[i, row + 24 : row + 32, :] = part[0:8]
                    else:
                        grid[i, row : row + 8, :] = part[8:16]

    def put_blocks(even, odd, index, value):
        even[index] = value.astype(BF16)
        odd[index] = value[8:].astype(BF16)

    for j in range(4):
        value = jnp.concatenate([grid[i, pl.ds(j, 96, stride=4), :] for i in range(2)], axis=1)
        put_blocks(blocks_even, blocks_odd, 1 + j, value)
        if j == 0:
            put_blocks(blocks_even, blocks_odd, 5, pltpu.roll(value, 95, 0))
        if j == 3:
            put_blocks(blocks_even, blocks_odd, 0, pltpu.roll(value, 1, 0))
    pieces = []
    for a in range(3):
        for b in range(3):
            if a == 1:
                window = blocks_odd[b : b + 4, 0:80, :]
            else:
                window = blocks_even[b : b + 4, 8 * a : 8 * a + 80, :]
            pieces.append(window.reshape(320, FEAT))
    pre = dot(jnp.concatenate(pieces, axis=1), enc[...].reshape(9 * FEAT, HID))
    pre_hidden[...] = pre
    hidden = (pre * sigmoid(pre)).astype(BF16)
    hidden = jnp.concatenate([hidden[80 * j : 80 * j + 80] for j in range(4)], axis=1)
    lat_tile[...] = dot(hidden, latw4[...])
    lat_pack[...] = jnp.zeros_like(lat_pack)
    for q in range(4):
        lat_pack[pl.ds(q, 10, stride=4), :] = lat_tile[pl.ds(2 + q, 10, stride=8), :]
    lat_send[...] = lat_pack[...].astype(BF16)

    def lat_copy(k):
        return remote(lat_send, lat_recv.at[k - 1], lat_ss.at[k - 1], lat_rs.at[k - 1], t, (s + k) % STEPS)

    for k in range(1, STEPS):
        lat_copy(k).start()

    place = lax.broadcasted_iota(jnp.int32, (16, UNET), 0)
    channel = lax.broadcasted_iota(jnp.int32, (16, UNET), 1)
    planes = (
        ((place >> 2) & 1) * 64 + (place & 3) * 16 + (place >> 3) * 2,
        (place >> 3) * 64 + ((place >> 1) & 3) * 4 + (place & 1) * 2,
        (place >> 2) * 16 + (place & 3) * 4,
    )
    for b in range(3):
        for block in range(24):
            half, f, c = block // 12, block // 3 % 4, block % 3
            along = (f * 4, f * 16, (f // 2) * 64 + (f % 2) * 2)[b]
            picked = channel == (planes[b] + (along + half)) * 3 + c
            order[b, 16 * block : 16 * block + 16, :] = jnp.where(picked, 1.0, 0.0).astype(BF16)
    inw4_t[...] = jnp.transpose(inw4[...])
    outw4[...] = jnp.transpose(outw4_t[...])
    chosen = time_ref[0]
    angle = ((jnp.full((8, 128), chosen, jnp.int32).astype(F32) + 1.0) / 1000.0 + 0.008) / 1.008 * (math.pi / 2.0)
    cosine = jnp.cos(angle)[0:1, :]
    sine = jnp.sin(angle)[0:1, :]
    l_table.wait()
    onehot = (lax.broadcasted_iota(jnp.int32, (16, table.shape[0]), 1) == chosen).astype(F32).astype(BF16)
    embed[...] = dot(onehot, table[...])[0:8]

    l_midw.wait()
    for side in (0, 1):
        noise_copies[side].wait()
    noise_rows[576:640, :] = noise_edge_in[0].astype(F32)
    noise_rows[0:64, :] = noise_edge_in[1].astype(F32)

    lat_flat[pl.ds(pl.multiple_of(s * 48, 16), 48), :] = lat_pack[...].astype(BF16).astype(F32)

    for k in range(1, STEPS):
        lat_copy(k).wait()
    for k in range(1, STEPS):
        source = (s - k + STEPS) % STEPS
        lat_flat[pl.ds(pl.multiple_of(source * 48, 16), 48), :] = lat_recv[k - 1].astype(F32)

    def input_rows(pair):
        first = 2 * pair
        latent = [lat_flat[pl.ds((first + r) * 4 + q, 16, stride=48), :] for r in range(2) for q in range(4)]
        noisy = cosine * jnp.concatenate(latent, axis=0) + sine * noise_rows[64 * first : 64 * first + 128, :]
        noisy = noisy.astype(BF16)
        for j in range(4):
            pre = dot(noisy, inw4[:, UNET * j : UNET * j + UNET]) + embed[0:1, :]
            sigma = sigmoid(pre)
            inner = pre * sigma
            slope = slope_of(pre, sigma)
            for r in range(2):
                row = first + r
                own = inner[64 * r : 64 * r + 64]
                if row == 0:
                    own = own * jnp.where(t > 0, 1.0, 0.0)
                if row == 9:
                    own = own * jnp.where(t < TILES - 1, 1.0, 0.0)
                inner_ext[row, 64 + 64 * j : 128 + 64 * j, :] = own.astype(BF16)
                if j == 0:
                    inner_ext[row, 320:384, :] = shift_up(own).astype(BF16)
                if j == 3:
                    inner_ext[row, 0:64, :] = shift_down(own).astype(BF16)
                if 0 < row < 9:
                    inner_slope[row - 1, 64 * j : 64 * j + 64, :] = slope[64 * r : 64 * r + 64]

    def flip_rows(pair):
        for row in (2 * pair, 2 * pair + 1):
            flipped = jnp.transpose(inner_ext[row])
            inner_t[row] = flipped
            inner_tm[row] = flipped[:, 64:320]

    def by_class(value):
        rows = value.shape[0] // 256
        return jnp.concatenate(
            [
                jnp.concatenate([value[256 * r + 64 * j : 256 * r + 64 * j + 64] for j in range(4)], axis=1)
                for r in range(rows)
            ],
            axis=0,
        )

    def by_position(value):
        rows = value.shape[0] // 64
        return jnp.concatenate(
            [value[64 * r : 64 * r + 64, UNET * j : UNET * j + UNET] for r in range(rows) for j in range(4)], axis=0
        )

    def forward_conv(i):
        windows = [
            inner_ext[2 * i + a : 2 * i + a + 2, 64 * b : 64 * b + 256, :].reshape(512, UNET)
            for a in range(3)
            for b in range(3)
        ]
        pre_middle[i % 2] = dot(jnp.concatenate(windows, axis=1), midw[...].reshape(9 * UNET, UNET))

    def forward_after(i):
        r = 2 * i
        pre = pre_middle[i % 2]
        sigma = sigmoid(pre)
        own = inner_ext[r + 1 : r + 3, 64:320, :].reshape(512, UNET)
        mixed = (own.astype(F32) + pre * sigma).astype(BF16)
        prediction = dot(by_class(mixed), outw4[...])
        own_noise = noise_rows[64 + r * 64 : 192 + r * 64, :]
        error = ((prediction - own_noise) * (1.0 / math.sqrt(STEPS))).astype(BF16)
        pulled = by_position(dot(error, outw4_t[...]))
        back_mixed[256 * r : 256 * r + 512, :] = pulled
        back = pulled * slope_of(pre, sigma)
        for row in range(2):
            own = back[256 * row : 256 * row + 256]
            back_ext[r + 1 + row, 64:320, :] = own.astype(BF16)
            back_ext[r + 1 + row, 320:384, :] = shift_up(own[0:64]).astype(BF16)
            back_ext[r + 1 + row, 0:64, :] = shift_down(own[192:256]).astype(BF16)

    halo_copies = []

    def halo_start(side):
        tile, step = near((2 * side - 1, 0))
        src, dst = ((1, 9), (8, 0))[side]
        src, dst = back_ext.at[src, pl.ds(64, 256)], back_ext.at[dst, pl.ds(64, 256)]
        copy = remote(src, dst, halo_ss.at[side], halo_rs.at[side], tile, step)
        copy.start()
        halo_copies.append(copy)

    input_rows(0)
    input_rows(1)
    for i in range(4):
        forward_conv(i)
        if i < 3:
            input_rows(i + 2)
        flip_rows(i)
        if i:
            forward_after(i - 1)
        if i == 1:
            halo_start(0)
    flip_rows(4)
    forward_after(3)
    halo_start(1)

    def s1_copy(a):
        return remote(grad.at[a, 1 - core], s1_recv.at[a], s1_ss.at[a], s1_rs.at[a], t, s + 1 - 2 * core)

    def axis_peer(axis, k):
        if axis == "z":
            there = (z + k) % 4
            return there, t, there * 4 + s % 4
        if axis == "x":
            there = (x + k) % 4
            return there, y_hi * 4 + there, s
        there = (y + k) % 4
        return there, (there // 2) * 4 + x, z * 4 + (there % 2) * 2 + core

    first_axis, second_axis, third_axis = ("z", "x", "y"), ("x", "z", "z"), ("y", "y", "x")

    def plane_rows(a, b, there):
        rows = pl.ds(pl.multiple_of(there * 48, 16), 48)
        return grad[a, core, b, rows, :].astype(F32) + s1_recv[a, b, rows, :].astype(F32)

    def s2_copy(a, b, k):
        _, tile, step = axis_peer(first_axis[b], k)
        index = (a * 3 + b) * 3 + k - 1
        return remote(s2_send.at[index], s2_recv.at[index], s2_ss.at[index], s2_rs.at[index], tile, step)

    def s2_pack(a):
        for b in range(3):
            for k in range(1, 4):
                there = axis_peer(first_axis[b], k)[0]
                s2_send[(a * 3 + b) * 3 + k - 1] = plane_rows(a, b, there).astype(BF16)

    def s2_start(a):
        for k in (2, 1, 3):
            for b in range(3):
                s2_copy(a, b, k).start()

    def s2_wait(a):
        for b in range(3):
            for k in range(1, 4):
                s2_copy(a, b, k).wait()

    def s2_add(a):
        for b in range(3):
            mine = axis_peer(first_axis[b], 0)[0]
            total = plane_rows(a, b, mine)
            for k in range(3):
                total = total + s2_recv[(a * 3 + b) * 3 + k].astype(F32)
            for i, part in enumerate(lane_tiles(total)):
                sum2[b * 3 + i, 48 * a : 48 * a + 48, :] = part

    def line_rows(b, there):
        parts = []
        for i in range(3):
            ref = sum2.at[b * 3 + i]
            if b == 1:
                parts.append(
                    jnp.concatenate([ref[pl.ds(2 * there + low, 24, stride=8), :] for low in (0, 1)], axis=0)
                )
            else:
                parts.append(ref[pl.ds(there, 48, stride=4), :])
        return jnp.concatenate(parts, axis=1)

    def s3_copy(b, k):
        _, tile, step = axis_peer(second_axis[b], k)
        index = b * 3 + k - 1
        return remote(s3_send.at[index], s3_recv.at[index], s3_ss.at[index], s3_rs.at[index], tile, step)

    def s3_start():
        for b in range(3):
            for k in range(1, 4):
                s3_send[b * 3 + k - 1] = line_rows(b, axis_peer(second_axis[b], k)[0]).astype(BF16)
        for b in range(3):
            for k in range(1, 4):
                s3_copy(b, k).start()

    def point_rows(b, there):
        if b == 0:
            rows = pl.ds((there % 2) * 2 + there // 2, 16, stride=4)
        elif b == 1:
            rows = pl.ds((there % 2) * 24 + there // 2, 16, stride=2)
        else:
            rows = pl.ds(there, 16, stride=4)
        return jnp.concatenate([sum3[b * 3 + i, rows, :] for i in range(3)], axis=1)

    def s4_copy(b, k):
        _, tile, step = axis_peer(third_axis[b], k)
        index = b * 3 + k - 1
        return remote(s4_send.at[index], s4_recv.at[index], s4_ss.at[index], s4_rs.at[index], tile, step)

    def s4_start():
        for b in range(3):
            for k in range(1, 4):
                s3_copy(b, k).wait()
        for b in range(3):
            total = line_rows(b, axis_peer(second_axis[b], 0)[0])
            for k in range(3):
                total = total + s3_recv[b * 3 + k].astype(F32)
            for i, part in enumerate(lane_tiles(total)):
                sum3[b * 3 + i, 0:48, :] = part
        for b in range(3):
            for k in range(1, 4):
                s4_send[b * 3 + k - 1] = point_rows(b, axis_peer(third_axis[b], k)[0]).astype(BF16)
        for b in range(3):
            for k in range(1, 4):
                s4_copy(b, k).start()

    def finish():
        for b in range(3):
            for k in range(1, 4):
                s4_copy(b, k).wait()
        for b in range(3):
            total = point_rows(b, axis_peer(third_axis[b], 0)[0])
            for k in range(3):
                total = total + s4_recv[b * 3 + k].astype(F32)
            total = total * (1.0 / math.sqrt(64 * 256))
            for a in range(3):
                mgrad_ref[3 * a + b] = total[3 * a : 3 * a + 3]

    def weight_product(a):
        taps = [
            jnp.concatenate([inner_t[r + a, :, 0:256] for r in range(8)], axis=1),
            jnp.concatenate([inner_tm[r + a] for r in range(8)], axis=1),
            jnp.concatenate([inner_t[r + a, :, 128:384] for r in range(8)], axis=1),
        ]
        result = dot(jnp.concatenate(taps, axis=0), back_ext[1:9, 64:320, :].reshape(2048, UNET))
        for b in range(3):
            ordered = dot(order[b], result[UNET * b : UNET * b + UNET].astype(BF16)).astype(BF16)
            grad[a, 0, b] = ordered[0:192]
            grad[a, 1, b] = ordered[192:384]

    sum2[...] = jnp.zeros_like(sum2)
    sum3[...] = jnp.zeros_like(sum3)
    for a in range(3):
        weight_product(a)
        for k in range(3 * a, 3 * a + 3):
            mid_t[k] = jnp.transpose(midw[k])
        s1_copy(a).start()

    for row, copy in ((9, halo_copies[0]), (0, halo_copies[1])):
        copy.wait()
        back_ext[row, 320:384, :] = shift_up(back_ext[row, 64:128, :].astype(F32)).astype(BF16)
        back_ext[row, 0:64, :] = shift_down(back_ext[row, 256:320, :].astype(F32)).astype(BF16)

    @pl.when(t == 0)
    def _():
        back_ext[0] = jnp.zeros_like(back_ext[0])

    @pl.when(t == TILES - 1)
    def _():
        back_ext[9] = jnp.zeros_like(back_ext[9])

    def backward_conv(i):
        r = 2 * i
        windows = [
            back_ext[r + 2 - a : r + 4 - a, 64 * (2 - b) : 64 * (2 - b) + 256, :].reshape(512, UNET)
            for a in range(3)
            for b in range(3)
        ]
        pre_middle[i % 2] = dot(jnp.concatenate(windows, axis=1), mid_t[...].reshape(9 * UNET, UNET))

    def backward_after(i):
        r = 2 * i
        through = pre_middle[i % 2] + back_mixed[256 * r : 256 * r + 512, :]
        back = (through * inner_slope[r : r + 2].reshape(512, UNET)).astype(BF16)
        back_part[64 * r : 64 * r + 128, :] = cosine * dot(by_class(back), inw4_t[...])

    def flip_enc(first, last):
        for k in range(first, last):
            enc_t[k] = jnp.transpose(enc[k])

    s1_copy(0).wait()
    s1_copy(1).wait()
    backward_conv(0)
    s2_pack(0)
    s2_pack(1)
    flip_enc(0, 3)
    s2_start(0)
    s2_start(1)

    s1_copy(2).wait()
    backward_conv(1)
    backward_after(0)
    s2_pack(2)
    flip_enc(3, 6)
    s2_start(2)

    backward_conv(2)
    backward_after(1)
    flip_enc(6, 9)

    s2_wait(0)
    backward_conv(3)
    backward_after(2)
    s2_add(0)
    backward_after(3)

    def part_copy(k):
        return remote(
            part_send.at[k - 1], part_recv.at[k - 1], part_ss.at[k - 1], part_rs.at[k - 1], t, (s + k) % STEPS
        )

    for k in range(1, STEPS):
        part_send[k - 1] = back_part[pl.ds((s + k) % STEPS, 32, stride=16), :].astype(BF16)
    for k in range(1, STEPS):
        part_copy(k).start()

    for a in (1, 2):
        s2_wait(a)
        s2_add(a)
    s3_start()

    for k in range(1, STEPS):
        part_copy(k).wait()
    latent_round = back_part[pl.ds(s, 32, stride=16), :]
    for k in range(1, STEPS):
        latent_round = latent_round + part_recv[k - 1].astype(F32)
    round_send[...] = latent_round.astype(BF16)
    round_copies = []
    for d, offsets in enumerate(AROUND):
        tile, step = near(offsets)
        copy = remote(round_send, round_recv.at[d], round_ss.at[d], round_rs.at[d], tile, step)
        copy.start()
        round_copies.append(copy)

    s4_start()

    round_grid[...] = jnp.zeros_like(round_grid)
    round_pack[...] = round_send[...].astype(F32)
    for q in range(4):
        round_grid[pl.ds(10 + q, 8, stride=8), :] = round_pack[pl.ds(q, 8, stride=4), :]
    for d, (dt, ds) in enumerate(AROUND):
        round_copies[d].wait()
        valid = jnp.bool_(True)
        if dt:
            valid = (t < TILES - 1) if dt < 0 else (t > 0)
        if ds:
            beside = (s < STEPS - 1) if ds < 0 else (s > 0)
            valid = jnp.logical_and(valid, beside) if dt else beside
        round_pack[...] = jnp.where(valid, round_recv[d].astype(F32), 0.0)
        if dt == 0:
            q, place = (0, 6) if ds < 0 else (3, 1)
            round_grid[pl.ds(8 + place, 8, stride=8), :] = round_pack[pl.ds(q, 8, stride=4), :]
        else:
            source, row = (0, 72) if dt < 0 else (28, 0)
            if ds == 0:
                round_grid[row + 2 : row + 6, :] = round_pack[source : source + 4, :]
            else:
                q, place = (0, 6) if ds < 0 else (3, 1)
                round_grid[row + place : row + place + 1, :] = round_pack[source + q : source + q + 1, :]
    pulled = dot(round_grid[...].astype(BF16), latw4_t[...])
    for j in range(4):
        pre = pre_hidden[80 * j : 80 * j + 80, :]
        value = pulled[:, HID * j : HID * j + HID] * slope_of(pre, sigmoid(pre))
        put_blocks(hidden_even, hidden_odd, 1 + j, value)
        if j == 0:
            put_blocks(hidden_even, hidden_odd, 5, pltpu.roll(value, 79, 0))
        if j == 3:
            put_blocks(hidden_even, hidden_odd, 0, pltpu.roll(value, 1, 0))
    pieces = []
    for a in range(3):
        for b in range(3):
            if a == 1:
                window = hidden_odd[2 - b : 6 - b, 0:64, :]
            else:
                window = hidden_even[2 - b : 6 - b, 8 * (2 - a) : 8 * (2 - a) + 64, :]
            pieces.append(window.reshape(256, HID))
    result = dot(jnp.concatenate(pieces, axis=1), enc_t[...].reshape(9 * HID, FEAT))
    for j in range(4):
        for i, part in enumerate(lane_tiles(result[64 * j : 64 * j + 64])):
            out_grid[i, pl.ds(j, 64, stride=4), :] = part
    for r in range(8):
        for i in range(2):
            fgrad_ref[r, :, 128 * i : 128 * i + 128] = out_grid[i, r * 32 + 8 : r * 32 + 24, :]

    finish()


def hand_over(fgrad_ref, mgrad_ref, fgrad_out, mgrad_out):
    fgrad_out[...] = fgrad_ref[...]
    mgrad_out[...] = mgrad_ref[...]


def per_device(
    features,
    encoder_weight,
    latent_weight,
    timesteps,
    noise_field,
    time_table,
    input_weight,
    middle_weight,
    output_weight,
):
    hbm = pl.BlockSpec(memory_space=pl.ANY)
    vmem = pl.BlockSpec(memory_space=pltpu.VMEM)
    dma = pltpu.SemaphoreType.DMA
    operands = (
        features,
        encoder_weight,
        latent_weight.T,
        noise_field,
        time_table,
        input_weight,
        middle_weight,
        output_weight.T,
    )
    scratch = [
        pltpu.VMEM((8, 16, FEAT), BF16),
        pltpu.VMEM((9, FEAT, HID), BF16),
        pltpu.VMEM((LAT, HID), BF16),
        pltpu.VMEM(noise_field.shape, BF16),
        pltpu.VMEM(time_table.shape, BF16),
        pltpu.VMEM((LAT, UNET), BF16),
        pltpu.VMEM((9, UNET, UNET), BF16),
        pltpu.VMEM((LAT, UNET), BF16),
        dma((8,)),
        pltpu.VMEM((9, HID, FEAT), BF16),
        pltpu.VMEM((9, UNET, UNET), BF16),
        pltpu.VMEM((4 * HID, 128), BF16),
        pltpu.VMEM((128, 4 * HID), BF16),
        pltpu.VMEM((128, 4 * UNET), BF16),
        pltpu.VMEM((4 * UNET, 128), BF16),
        pltpu.VMEM((4 * UNET, 128), BF16),
        pltpu.VMEM((128, 4 * UNET), BF16),
        pltpu.VMEM((8, UNET), F32),
        pltpu.VMEM((2, 16, FEAT), BF16),
        pltpu.VMEM((2, 16, FEAT), BF16),
        pltpu.VMEM((6, 2, 16, FEAT), BF16),
        pltpu.VMEM((2, 12 * 32, 128), F32),
        pltpu.VMEM((6, 96, FEAT), BF16),
        pltpu.VMEM((6, 88, FEAT), BF16),
        pltpu.VMEM((320, HID), F32),
        pltpu.VMEM((80, 128), F32),
        pltpu.VMEM((48, 128), F32),
        pltpu.VMEM((48, 128), BF16),
        pltpu.VMEM((15, 48, 128), BF16),
        pltpu.VMEM((16 * 48, 128), F32),
        pltpu.VMEM((640, 128), F32),
        pltpu.VMEM((2, 64, 128), BF16),
        pltpu.VMEM((2, 64, 128), BF16),
        pltpu.VMEM((10, 384, UNET), BF16),
        pltpu.VMEM((8, 256, UNET), F32),
        pltpu.VMEM((10, UNET, 384), BF16),
        pltpu.VMEM((10, UNET, 256), BF16),
        pltpu.VMEM((2, 512, UNET), F32),
        pltpu.VMEM((2048, UNET), F32),
        pltpu.VMEM((10, 384, UNET), BF16),
        pltpu.VMEM((512, 128), F32),
        pltpu.VMEM((15, 32, 128), BF16),
        pltpu.VMEM((15, 32, 128), BF16),
        pltpu.VMEM((32, 128), F32),
        pltpu.VMEM((32, 128), BF16),
        pltpu.VMEM((8, 32, 128), BF16),
        pltpu.VMEM((80, 128), F32),
        pltpu.VMEM((6, 80, HID), BF16),
        pltpu.VMEM((6, 72, HID), BF16),
        pltpu.VMEM((2, 256, 128), F32),
        pltpu.VMEM((3, UNET, UNET), BF16),
        pltpu.VMEM((3, 2, 3, 192, UNET), BF16),
        pltpu.VMEM((3, 3, 192, UNET), BF16),
        pltpu.VMEM((27, 48, UNET), BF16),
        pltpu.VMEM((27, 48, UNET), BF16),
        pltpu.VMEM((9, 256, 128), F32),
        pltpu.VMEM((9, 48, UNET), BF16),
        pltpu.VMEM((9, 48, UNET), BF16),
        pltpu.VMEM((9, 64, 128), F32),
        pltpu.VMEM((9, 16, UNET), BF16),
        pltpu.VMEM((9, 16, UNET), BF16),
        dma((8,)),
        dma((8,)),
        dma((2,)),
        dma((2,)),
        dma((15,)),
        dma((15,)),
        dma((2,)),
        dma((2,)),
        dma((15,)),
        dma((15,)),
        dma((8,)),
        dma((8,)),
        dma((3,)),
        dma((3,)),
        dma((27,)),
        dma((27,)),
        dma((9,)),
        dma((9,)),
        dma((9,)),
        dma((9,)),
    ]
    shapes = (
        jax.ShapeDtypeStruct((8, 16, FEAT), F32),
        jax.ShapeDtypeStruct((9, 3, UNET), F32),
    )
    results = pl.pallas_call(
        kernel,
        out_shape=shapes,
        in_specs=[pl.BlockSpec(memory_space=pltpu.SMEM)] + [hbm] * 8,
        out_specs=(vmem, vmem),
        scratch_shapes=scratch,
        compiler_params=pltpu.CompilerParams(
            collective_id=0, has_side_effects=True, vmem_limit_bytes=60 * 1024 * 1024
        ),
        cost_estimate=pl.CostEstimate(flops=18_000_000_000, bytes_accessed=8_000_000, transcendentals=3_000_000),
    )(timesteps, *operands)
    feature_grad, middle_grad = pl.pallas_call(
        hand_over,
        out_shape=shapes,
        in_specs=[vmem, vmem],
        out_specs=(vmem, vmem),
    )(*results)
    return feature_grad, jnp.transpose(middle_grad, (1, 0, 2))


def solution(mesh):
    in_specs = (
        P("tile", "step", None),
        P(),
        P(),
        P("step"),
        P("step", "tile", None),
        P(),
        P(),
        P(),
        P(),
    )
    out_specs = (P("tile", "step", None), P(("tile", "step"), None, None))
    return jax.shard_map(per_device, mesh=mesh, in_specs=in_specs, out_specs=out_specs, check_vma=False)
```

```python
import math

import jax
import jax.numpy as jnp
from jax import lax
from jax.experimental import pallas as pl
from jax.experimental.pallas import tpu as pltpu
from jax.sharding import PartitionSpec as P

F32 = jnp.float32
BF16 = jnp.bfloat16
MESH = pl.DeviceIdType.MESH

FEAT, HID, LAT, UNET = 256, 512, 32, 384
TILES, STEPS = 8, 16
AROUND = ((-1, -1), (-1, 0), (-1, 1), (0, -1), (0, 1), (1, -1), (1, 0), (1, 1))


def sigmoid(values):
    return 0.5 * jnp.tanh(0.5 * values) + 0.5


def slope_of(values, sigma):
    return sigma * (1.0 + values * (1.0 - sigma))


def dot(left, right):
    return jnp.dot(left, right, preferred_element_type=F32)


def lane_tiles(value):
    return [value[:, 128 * i : 128 * i + 128] for i in range(value.shape[1] // 128)]


def shift_down(block):
    last = pltpu.roll(block[48:64], 1, 0)
    rows = lax.broadcasted_iota(jnp.int32, last.shape, 0)
    return jnp.concatenate([jnp.where(rows == 0, 0.0, last), block[0:48]], axis=0)


def shift_up(block):
    first = pltpu.roll(block[0:16], 15, 0)
    rows = lax.broadcasted_iota(jnp.int32, first.shape, 0)
    return jnp.concatenate([block[16:64], jnp.where(rows == 15, 0.0, first)], axis=0)


def kernel(
    time_ref,
    feat_hbm,
    enc_hbm,
    latw_hbm,
    noise_hbm,
    table_hbm,
    inw_hbm,
    midw_hbm,
    outw_hbm,
    fgrad_ref,
    mgrad_ref,
    feat,
    enc,
    latw,
    noise,
    table,
    inw,
    midw,
    outw,
    in_sem,
    mid_sums,
    latw4,
    latw4_t,
    inw4,
    inw4_t,
    outw4,
    outw4_t,
    embed,
    edge,
    edge_in,
    rows_in,
    grid,
    blocks_even,
    blocks_odd,
    pre_hidden,
    lat_tile,
    lat_pack,
    lat_send,
    lat_recv,
    lat_flat,
    noise_rows,
    noise_edge,
    noise_edge_in,
    inner_ext,
    inner_slope,
    mixes,
    mixes_t,
    mixes_tm,
    back_mixes,
    pre_middle,
    back_mixed,
    back_ext,
    back_part,
    part_send,
    part_recv,
    round_pack,
    round_send,
    round_recv,
    round_grid,
    hidden_even,
    hidden_odd,
    out_grid,
    grad,
    s1_send,
    s1_recv,
    sum1,
    s2_send,
    s2_recv,
    sum2,
    s3_send,
    s3_recv,
    sum3,
    s4_send,
    s4_recv,
    feat_ss,
    feat_rs,
    noise_ss,
    noise_rs,
    lat_ss,
    lat_rs,
    halo_ss,
    halo_rs,
    part_ss,
    part_rs,
    round_ss,
    round_rs,
    s1_ss,
    s1_rs,
    s2_ss,
    s2_rs,
    s3_ss,
    s3_rs,
    s4_ss,
    s4_rs,
):
    t = lax.axis_index("tile")
    s = lax.axis_index("step")
    y_hi, x = t // 4, t % 4
    z, y_lo, core = s // 4, (s // 2) % 2, s % 2
    y = y_hi * 2 + y_lo

    def remote(src, dst, ss, rs, tile, step):
        return pltpu.make_async_remote_copy(
            src_ref=src, dst_ref=dst, send_sem=ss, recv_sem=rs, device_id=(tile, step), device_id_type=MESH
        )

    def near(offsets):
        return (t + offsets[0] + TILES) % TILES, (s + offsets[1] + STEPS) % STEPS

    loads = [
        pltpu.make_async_copy(src, dst, in_sem.at[i])
        for i, (src, dst) in enumerate(
            (
                (feat_hbm, feat),
                (noise_hbm, noise),
                (enc_hbm, enc),
                (latw_hbm, latw),
                (inw_hbm, inw),
                (outw_hbm, outw),
                (table_hbm, table),
                (midw_hbm, midw),
            )
        )
    ]
    for load in loads:
        load.start()
    l_feat, l_noise, l_enc, l_latw, l_inw, l_outw, l_table, l_midw = loads

    barrier = pltpu.get_barrier_semaphore()

    for k in range(1, STEPS):
        pl.semaphore_signal(barrier, inc=1, device_id=(t, (s + k) % STEPS), device_id_type=MESH)
    for k in range(1, TILES):
        pl.semaphore_signal(barrier, inc=1, device_id=((t + k) % TILES, s), device_id_type=MESH)
    for offsets in AROUND:
        if offsets[0] and offsets[1]:
            pl.semaphore_signal(barrier, inc=1, device_id=near(offsets), device_id_type=MESH)

    l_feat.wait()
    grid[...] = jnp.zeros_like(grid)
    for r in range(8):
        for i, part in enumerate(lane_tiles(feat[r].astype(F32))):
            grid[i, (r + 2) * 32 + 8 : (r + 2) * 32 + 24, :] = part
    for side, first in ((0, 8), (1, 22)):
        for i in range(2):
            pair = [grid[i, pl.ds(64 + first + col, 8, stride=32), :] for col in (0, 1)]
            edge[side, :, 128 * i : 128 * i + 128] = jnp.concatenate(pair, axis=0).astype(BF16)

    pl.semaphore_wait(barrier, STEPS - 1 + TILES - 1 + 4)

    feat_copies = []
    for d, offsets in enumerate(AROUND):
        tile, step = near(offsets)
        if offsets[0] == 0:
            side = 0 if offsets[1] < 0 else 1
            src, dst = edge.at[side], edge_in.at[side]
        else:
            slot = d if d < 3 else d - 2
            src, dst = feat.at[pl.ds(0 if offsets[0] < 0 else 6, 2)], rows_in.at[slot]
        copy = remote(src, dst, feat_ss.at[d], feat_rs.at[d], tile, step)
        copy.start()
        feat_copies.append(copy)

    l_noise.wait()
    for q in range(64):
        piece = noise[0, :, 128 * q : 128 * q + 128].astype(F32)
        noise_rows[pl.ds(64 + (q % 4) * 16 + q // 4, 8, stride=64), :] = piece
    noise_edge[0] = noise_rows[64:128, :].astype(BF16)
    noise_edge[1] = noise_rows[512:576, :].astype(BF16)
    noise_copies = []
    for side, offset in ((0, -1), (1, 1)):
        tile, step = near((offset, 0))
        copy = remote(noise_edge.at[side], noise_edge_in.at[side], noise_ss.at[side], noise_rs.at[side], tile, step)
        copy.start()
        noise_copies.append(copy)

    for load, weight, wide, flipped in (
        (l_latw, latw, latw4_t, latw4),
        (l_inw, inw, inw4, inw4_t),
        (l_outw, outw, outw4_t, outw4),
    ):
        load.wait()
        columns = weight.shape[1]
        wide[...] = jnp.zeros_like(wide)
        for j in range(4):
            wide[LAT * j : LAT * j + LAT, columns * j : columns * j + columns] = weight[...]
        if flipped is latw4:
            flipped[...] = jnp.transpose(wide[...])

    l_enc.wait()

    for d, copy in enumerate(feat_copies):
        copy.wait()
    for d, offsets in enumerate(AROUND):
        dt, ds = offsets
        valid = jnp.bool_(True)
        if dt:
            valid = (t < TILES - 1) if dt < 0 else (t > 0)
        if ds:
            beside = (s < STEPS - 1) if ds < 0 else (s > 0)
            valid = jnp.logical_and(valid, beside) if dt else beside
        if dt == 0:
            side = 0 if ds < 0 else 1
            taken = jnp.where(valid, edge_in[side].astype(F32), 0.0)
            first = 24 if ds < 0 else 6
            for i, part in enumerate(lane_tiles(taken)):
                for col in (0, 1):
                    grid[i, pl.ds(64 + first + col, 8, stride=32), :] = part[8 * col : 8 * col + 8]
        else:
            slot = d if d < 3 else d - 2
            for r in range(2):
                taken = jnp.where(valid, rows_in[slot, r].astype(F32), 0.0)
                row = (10 + r if dt < 0 else r) * 32
                for i, part in enumerate(lane_tiles(taken)):
                    if ds == 0:
                        grid[i, row + 8 : row + 24, :] = part
                    elif ds < 0:
                        grid[i, row + 24 : row + 32, :] = part[0:8]
                    else:
                        grid[i, row : row + 8, :] = part[8:16]

    def put_blocks(even, odd, index, value):
        even[index] = value.astype(BF16)
        odd[index] = value[8:].astype(BF16)

    for j in range(4):
        value = jnp.concatenate([grid[i, pl.ds(j, 96, stride=4), :] for i in range(2)], axis=1)
        put_blocks(blocks_even, blocks_odd, 1 + j, value)
        if j == 0:
            put_blocks(blocks_even, blocks_odd, 5, pltpu.roll(value, 95, 0))
        if j == 3:
            put_blocks(blocks_even, blocks_odd, 0, pltpu.roll(value, 1, 0))
    pieces = []
    for a in range(3):
        for b in range(3):
            if a == 1:
                window = blocks_odd[b : b + 4, 0:80, :]
            else:
                window = blocks_even[b : b + 4, 8 * a : 8 * a + 80, :]
            pieces.append(window.reshape(320, FEAT))
    pre = dot(jnp.concatenate(pieces, axis=1), enc[...].reshape(9 * FEAT, HID))
    pre_hidden[...] = pre
    hidden = (pre * sigmoid(pre)).astype(BF16)
    hidden = jnp.concatenate([hidden[80 * j : 80 * j + 80] for j in range(4)], axis=1)
    lat_tile[...] = dot(hidden, latw4[...])
    lat_pack[...] = jnp.zeros_like(lat_pack)
    for q in range(4):
        lat_pack[pl.ds(q, 10, stride=4), :] = lat_tile[pl.ds(2 + q, 10, stride=8), :]
    lat_send[...] = lat_pack[...].astype(BF16)

    def lat_copy(k):
        return remote(lat_send, lat_recv.at[k - 1], lat_ss.at[k - 1], lat_rs.at[k - 1], t, (s + k) % STEPS)

    for k in range(1, STEPS):
        lat_copy(k).start()

    inw4_t[...] = jnp.transpose(inw4[...])
    outw4[...] = jnp.transpose(outw4_t[...])
    chosen = time_ref[0]
    angle = ((jnp.full((8, 128), chosen, jnp.int32).astype(F32) + 1.0) / 1000.0 + 0.008) / 1.008 * (math.pi / 2.0)
    cosine = jnp.cos(angle)[0:1, :]
    sine = jnp.sin(angle)[0:1, :]
    l_table.wait()
    onehot = (lax.broadcasted_iota(jnp.int32, (16, table.shape[0]), 1) == chosen).astype(F32).astype(BF16)
    embed[...] = dot(onehot, table[...])[0:8]

    l_midw.wait()
    for b in range(3):
        ends = midw[b].astype(F32) + midw[6 + b].astype(F32)
        centre = midw[3 + b].astype(F32)
        mid_sums[0, b] = (0.5 * (ends + centre)).astype(BF16)
        mid_sums[1, b] = (0.5 * (ends - centre)).astype(BF16)
    for side in (0, 1):
        noise_copies[side].wait()
    noise_rows[576:640, :] = noise_edge_in[0].astype(F32)
    noise_rows[0:64, :] = noise_edge_in[1].astype(F32)

    lat_flat[pl.ds(pl.multiple_of(s * 48, 16), 48), :] = lat_pack[...].astype(BF16).astype(F32)

    for k in range(1, STEPS):
        lat_copy(k).wait()
    for k in range(1, STEPS):
        source = (s - k + STEPS) % STEPS
        lat_flat[pl.ds(pl.multiple_of(source * 48, 16), 48), :] = lat_recv[k - 1].astype(F32)

    def input_rows(first, count):
        latent = [lat_flat[pl.ds((first + r) * 4 + q, 16, stride=48), :] for r in range(count) for q in range(4)]
        noisy = sine * noise_rows[64 * first : 64 * (first + count), :]
        noisy = (cosine * jnp.concatenate(latent, axis=0) + noisy).astype(BF16)
        for j in range(4):
            pre = dot(noisy, inw4[:, UNET * j : UNET * j + UNET]) + embed[0:1, :]
            sigma = sigmoid(pre)
            inner = pre * sigma
            slope = slope_of(pre, sigma)
            for r in range(count):
                row = first + r
                own = inner[64 * r : 64 * r + 64]
                if row == 0:
                    own = own * jnp.where(t > 0, 1.0, 0.0)
                if row == 9:
                    own = own * jnp.where(t < TILES - 1, 1.0, 0.0)
                inner_ext[row, 64 + 64 * j : 128 + 64 * j, :] = own.astype(BF16)
                if j == 0:
                    inner_ext[row, 320:384, :] = shift_up(own).astype(BF16)
                if j == 3:
                    inner_ext[row, 0:64, :] = shift_down(own).astype(BF16)
                if 0 < row < 9:
                    inner_slope[row - 1, 64 * j : 64 * j + 64, :] = slope[64 * r : 64 * r + 64].astype(BF16)

    def mix_rows(ref, pair):
        d = [ref[2 * pair + r] for r in range(4)]
        mixes[pair, 0] = d[0] - d[2]
        mixes[pair, 1] = d[1] + d[2]
        mixes[pair, 2] = d[2] - d[1]
        mixes[pair, 3] = d[1] - d[3]

    def flip_mixes(pair):
        for k in range(4):
            flipped = jnp.transpose(mixes[pair, k])
            mixes_t[pair, k] = flipped
            mixes_tm[UNET * (4 * pair + k) : UNET * (4 * pair + k + 1), :] = flipped[:, 64:320]

    def mixed_conv(i, weights):
        for k in (1, 2, 0, 3):
            windows = [mixes[2 * i : 2 * i + 2, k, 64 * b : 64 * b + 256, :].reshape(512, UNET) for b in range(3)]
            part = dot(jnp.concatenate(windows, axis=1), weights[k])
            for pair in range(2):
                own = part[256 * pair : 256 * pair + 256]
                even = slice(512 * pair, 512 * pair + 256)
                odd = slice(512 * pair + 256, 512 * pair + 512)
                if k == 1:
                    pre_middle[i, even, :] = own
                    pre_middle[i, odd, :] = own
                elif k == 2:
                    pre_middle[i, even, :] += own
                    pre_middle[i, odd, :] -= own
                elif k == 0:
                    pre_middle[i, even, :] += own
                else:
                    pre_middle[i, odd, :] -= own

    def by_class(value):
        rows = value.shape[0] // 256
        return jnp.concatenate(
            [
                jnp.concatenate([value[256 * r + 64 * j : 256 * r + 64 * j + 64] for j in range(4)], axis=1)
                for r in range(rows)
            ],
            axis=0,
        )

    def by_position(value):
        rows = value.shape[0] // 64
        return jnp.concatenate(
            [value[64 * r : 64 * r + 64, UNET * j : UNET * j + UNET] for r in range(rows) for j in range(4)], axis=0
        )

    def forward_conv(i):
        weights = [midw[0:3], mid_sums[0], mid_sums[1], midw[6:9]]
        mixed_conv(i, [weight.reshape(3 * UNET, UNET) for weight in weights])

    def forward_after(i):
        r = 4 * i
        pre = pre_middle[i]
        sigma = sigmoid(pre)
        own = inner_ext[r + 1 : r + 5, 64:320, :].reshape(1024, UNET)
        mixed = (own.astype(F32) + pre * sigma).astype(BF16)
        prediction = dot(by_class(mixed), outw4[...])
        own_noise = noise_rows[64 + r * 64 : 320 + r * 64, :]
        error = ((prediction - own_noise) * (1.0 / math.sqrt(STEPS))).astype(BF16)
        pulled = by_position(dot(error, outw4_t[...]))
        back_mixed[256 * r : 256 * r + 1024, :] = pulled
        back = pulled * slope_of(pre, sigma)
        for row in range(4):
            own = back[256 * row : 256 * row + 256]
            back_ext[r + 1 + row, 64:320, :] = own.astype(BF16)
            back_ext[r + 1 + row, 320:384, :] = shift_up(own[0:64]).astype(BF16)
            back_ext[r + 1 + row, 0:64, :] = shift_down(own[192:256]).astype(BF16)
        for pair in range(2):
            first, second = back[512 * pair : 512 * pair + 256], back[512 * pair + 256 : 512 * pair + 512]
            back_mixes[2 * i + pair, 0] = (0.5 * (first + second)).astype(BF16)
            back_mixes[2 * i + pair, 1] = (0.5 * (first - second)).astype(BF16)

    halo_copies = []

    def halo_start(side):
        tile, step = near((2 * side - 1, 0))
        src, dst = ((1, 9), (8, 0))[side]
        src, dst = back_ext.at[src, pl.ds(64, 256)], back_ext.at[dst, pl.ds(64, 256)]
        copy = remote(src, dst, halo_ss.at[side], halo_rs.at[side], tile, step)
        copy.start()
        halo_copies.append(copy)

    input_rows(0, 6)
    mix_rows(inner_ext, 0)
    mix_rows(inner_ext, 1)
    forward_conv(0)
    input_rows(6, 4)
    mix_rows(inner_ext, 2)
    mix_rows(inner_ext, 3)
    flip_mixes(0)
    flip_mixes(1)
    forward_conv(1)
    forward_after(0)
    flip_mixes(2)
    flip_mixes(3)
    halo_start(0)
    forward_after(1)
    halo_start(1)

    def s1_copy(a):
        return remote(s1_send.at[a], s1_recv.at[a], s1_ss.at[a], s1_rs.at[a], t, s + 1 - 2 * core)

    def s1_pack(a):
        for n in range(9):
            first = (n // 3) * UNET + n % 3 + 3 * (1 - core)
            block = jnp.concatenate([grad[a * 3 + i, pl.ds(first, 64, stride=6), :] for i in range(3)], axis=1)
            s1_send[a, 64 * n : 64 * n + 64, :] = block.astype(BF16)

    def s1_add(a):
        for n in range(9):
            first = (n // 3) * UNET + n % 3 + 3 * core
            got = s1_recv[a, 64 * n : 64 * n + 64, :].astype(F32)
            for i in range(3):
                own = grad[a * 3 + i, pl.ds(first, 64, stride=6), :]
                sum1[a * 3 + i, 64 * n : 64 * n + 64, :] = own + got[:, 128 * i : 128 * i + 128]

    def axis_peer(axis, k):
        if axis == "z":
            there = (z + k) % 4
            return there, t, there * 4 + s % 4
        if axis == "x":
            there = (x + k) % 4
            return there, y_hi * 4 + there, s
        there = (y + k) % 4
        return there, (there // 2) * 4 + x, z * 4 + (there % 2) * 2 + core

    first_axis, second_axis, third_axis = ("z", "x", "y"), ("x", "z", "z"), ("y", "y", "x")

    def plane_rows(a, b, c, there):
        base = (3 * b + c) * 64
        parts = []
        for i in range(3):
            ref = sum1.at[a * 3 + i]
            if b == 0:
                parts.append(
                    jnp.concatenate([ref[pl.ds(base + 2 * there + low, 8, stride=8), :] for low in (0, 1)], axis=0)
                )
            elif b == 1:
                rows = [pl.ds(pl.multiple_of(base + high * 32 + there * 8, 8), 8) for high in (0, 1)]
                parts.append(jnp.concatenate([ref[row, :] for row in rows], axis=0))
            else:
                parts.append(ref[pl.ds(base + (there // 2) * 32 + there % 2, 16, stride=2), :])
        return jnp.concatenate(parts, axis=1)

    def s2_copy(a, b, k):
        _, tile, step = axis_peer(first_axis[b], k)
        index = (a * 3 + b) * 3 + k - 1
        return remote(s2_send.at[index], s2_recv.at[index], s2_ss.at[index], s2_rs.at[index], tile, step)

    def s2_pack(a):
        for b in range(3):
            for k in range(1, 4):
                there = axis_peer(first_axis[b], k)[0]
                for c in range(3):
                    block = plane_rows(a, b, c, there).astype(BF16)
                    s2_send[(a * 3 + b) * 3 + k - 1, 16 * c : 16 * c + 16, :] = block

    def s2_start(a):
        for k in (2, 1, 3):
            for b in range(3):
                s2_copy(a, b, k).start()

    def s2_wait(a):
        for b in range(3):
            for k in range(1, 4):
                s2_copy(a, b, k).wait()

    def s2_add(a):
        for b in range(3):
            mine = axis_peer(first_axis[b], 0)[0]
            for c in range(3):
                total = plane_rows(a, b, c, mine)
                for k in range(3):
                    total = total + s2_recv[(a * 3 + b) * 3 + k, 16 * c : 16 * c + 16, :].astype(F32)
                row = 16 * (3 * a + c)
                for i, part in enumerate(lane_tiles(total)):
                    sum2[b * 3 + i, row : row + 16, :] = part

    def line_rows(b, there):
        parts = []
        for i in range(3):
            ref = sum2.at[b * 3 + i]
            if b == 1:
                parts.append(
                    jnp.concatenate([ref[pl.ds(2 * there + low, 24, stride=8), :] for low in (0, 1)], axis=0)
                )
            else:
                parts.append(ref[pl.ds(there, 48, stride=4), :])
        return jnp.concatenate(parts, axis=1)

    def s3_copy(b, k):
        _, tile, step = axis_peer(second_axis[b], k)
        index = b * 3 + k - 1
        return remote(s3_send.at[index], s3_recv.at[index], s3_ss.at[index], s3_rs.at[index], tile, step)

    def s3_start():
        for b in range(3):
            for k in range(1, 4):
                s3_send[b * 3 + k - 1] = line_rows(b, axis_peer(second_axis[b], k)[0]).astype(BF16)
        for b in range(3):
            for k in range(1, 4):
                s3_copy(b, k).start()

    def point_rows(b, there):
        if b == 0:
            rows = pl.ds((there % 2) * 2 + there // 2, 16, stride=4)
        elif b == 1:
            rows = pl.ds((there % 2) * 24 + there // 2, 16, stride=2)
        else:
            rows = pl.ds(there, 16, stride=4)
        return jnp.concatenate([sum3[b * 3 + i, rows, :] for i in range(3)], axis=1)

    def s4_copy(b, k):
        _, tile, step = axis_peer(third_axis[b], k)
        index = b * 3 + k - 1
        return remote(s4_send.at[index], s4_recv.at[index], s4_ss.at[index], s4_rs.at[index], tile, step)

    def s4_start():
        for b in range(3):
            for k in range(1, 4):
                s3_copy(b, k).wait()
        for b in range(3):
            total = line_rows(b, axis_peer(second_axis[b], 0)[0])
            for k in range(3):
                total = total + s3_recv[b * 3 + k].astype(F32)
            for i, part in enumerate(lane_tiles(total)):
                sum3[b * 3 + i, 0:48, :] = part
        for b in range(3):
            for k in range(1, 4):
                s4_send[b * 3 + k - 1] = point_rows(b, axis_peer(third_axis[b], k)[0]).astype(BF16)
        for b in range(3):
            for k in range(1, 4):
                s4_copy(b, k).start()

    def finish():
        for b in range(3):
            for k in range(1, 4):
                s4_copy(b, k).wait()
        for b in range(3):
            total = point_rows(b, axis_peer(third_axis[b], 0)[0])
            for k in range(3):
                total = total + s4_recv[b * 3 + k].astype(F32)
            total = total * (1.0 / math.sqrt(64 * 256))
            for a in range(3):
                mgrad_ref[3 * a + b] = total[3 * a : 3 * a + 3]

    def weight_product(k):
        taps = [
            jnp.concatenate([mixes_t[pair, k, :, 0:256] for pair in range(4)], axis=1),
            jnp.concatenate(
                [mixes_tm[UNET * (4 * pair + k) : UNET * (4 * pair + k + 1), :] for pair in range(4)], axis=1
            ),
            jnp.concatenate([mixes_t[pair, k, :, 128:384] for pair in range(4)], axis=1),
        ]
        if k in (0, 3):
            right = [back_ext[1 + 2 * pair + k // 3, 64:320, :] for pair in range(4)]
        else:
            right = [back_mixes[pair, k - 1] for pair in range(4)]
        return lane_tiles(dot(jnp.concatenate(taps, axis=0), jnp.concatenate(right, axis=0)))

    def flip_mid(k):
        for b in range(3):
            source = (midw.at[8 - b], mid_sums.at[0, 2 - b], mid_sums.at[1, 2 - b], midw.at[2 - b])[k]
            inner_ext[3 * k + b] = jnp.transpose(source[...])

    sum2[...] = jnp.zeros_like(sum2)
    sum3[...] = jnp.zeros_like(sum3)
    for i, part in enumerate(weight_product(1)):
        grad[i] = part
        grad[3 + i] = part
        grad[6 + i] = part
    flip_mid(0)
    for i, part in enumerate(weight_product(2)):
        grad[i] += part
        grad[3 + i] -= part
        grad[6 + i] += part
    flip_mid(1)
    s1_pack(1)
    s1_copy(1).start()
    for i, part in enumerate(weight_product(0)):
        grad[i] += part
    flip_mid(2)
    mix_rows(back_ext, 1)
    s1_pack(0)
    s1_copy(0).start()
    for i, part in enumerate(weight_product(3)):
        grad[6 + i] -= part
    flip_mid(3)
    mix_rows(back_ext, 2)
    s1_pack(2)
    s1_copy(2).start()

    for row, copy in ((9, halo_copies[0]), (0, halo_copies[1])):
        copy.wait()
        back_ext[row, 320:384, :] = shift_up(back_ext[row, 64:128, :].astype(F32)).astype(BF16)
        back_ext[row, 0:64, :] = shift_down(back_ext[row, 256:320, :].astype(F32)).astype(BF16)

    @pl.when(t == 0)
    def _():
        back_ext[0] = jnp.zeros_like(back_ext[0])

    @pl.when(t == TILES - 1)
    def _():
        back_ext[9] = jnp.zeros_like(back_ext[9])

    def backward_conv(i):
        mixed_conv(i, [inner_ext[3 * k : 3 * k + 3].reshape(3 * UNET, UNET) for k in range(4)])

    def backward_after(i):
        r = 4 * i
        through = pre_middle[i] + back_mixed[256 * r : 256 * r + 1024, :]
        back = (through * inner_slope[r : r + 4].reshape(1024, UNET).astype(F32)).astype(BF16)
        back_part[64 * r : 64 * r + 256, :] = cosine * dot(by_class(back), inw4_t[...])

    def flip_enc(first, last):
        for k in range(first, last):
            mixes_tm[HID * k : HID * k + HID, :] = jnp.transpose(enc[k])

    mix_rows(back_ext, 0)
    mix_rows(back_ext, 3)
    s1_copy(1).wait()
    s1_copy(0).wait()
    backward_conv(0)
    for a in (1, 0):
        s1_add(a)
        s2_pack(a)
    flip_enc(0, 5)
    s2_start(1)
    s2_start(0)

    s1_copy(2).wait()
    backward_conv(1)
    backward_after(0)
    s1_add(2)
    s2_pack(2)
    flip_enc(5, 9)
    s2_start(2)
    backward_after(1)

    def part_copy(k):
        return remote(
            part_send.at[k - 1], part_recv.at[k - 1], part_ss.at[k - 1], part_rs.at[k - 1], t, (s + k) % STEPS
        )

    for k in range(1, STEPS):
        part_send[k - 1] = back_part[pl.ds((s + k) % STEPS, 32, stride=16), :].astype(BF16)
    for k in range(1, STEPS):
        part_copy(k).start()

    for a in range(3):
        s2_wait(a)
        s2_add(a)
    s3_start()

    for k in range(1, STEPS):
        part_copy(k).wait()
    latent_round = back_part[pl.ds(s, 32, stride=16), :]
    for k in range(1, STEPS):
        latent_round = latent_round + part_recv[k - 1].astype(F32)
    round_send[...] = latent_round.astype(BF16)
    round_copies = []
    for d, offsets in enumerate(AROUND):
        tile, step = near(offsets)
        copy = remote(round_send, round_recv.at[d], round_ss.at[d], round_rs.at[d], tile, step)
        copy.start()
        round_copies.append(copy)

    s4_start()

    round_grid[...] = jnp.zeros_like(round_grid)
    round_pack[...] = round_send[...].astype(F32)
    for q in range(4):
        round_grid[pl.ds(10 + q, 8, stride=8), :] = round_pack[pl.ds(q, 8, stride=4), :]
    for d, (dt, ds) in enumerate(AROUND):
        round_copies[d].wait()
        valid = jnp.bool_(True)
        if dt:
            valid = (t < TILES - 1) if dt < 0 else (t > 0)
        if ds:
            beside = (s < STEPS - 1) if ds < 0 else (s > 0)
            valid = jnp.logical_and(valid, beside) if dt else beside
        round_pack[...] = jnp.where(valid, round_recv[d].astype(F32), 0.0)
        if dt == 0:
            q, place = (0, 6) if ds < 0 else (3, 1)
            round_grid[pl.ds(8 + place, 8, stride=8), :] = round_pack[pl.ds(q, 8, stride=4), :]
        else:
            source, row = (0, 72) if dt < 0 else (28, 0)
            if ds == 0:
                round_grid[row + 2 : row + 6, :] = round_pack[source : source + 4, :]
            else:
                q, place = (0, 6) if ds < 0 else (3, 1)
                round_grid[row + place : row + place + 1, :] = round_pack[source + q : source + q + 1, :]
    pulled = dot(round_grid[...].astype(BF16), latw4_t[...])
    for j in range(4):
        pre = pre_hidden[80 * j : 80 * j + 80, :]
        value = pulled[:, HID * j : HID * j + HID] * slope_of(pre, sigmoid(pre))
        put_blocks(hidden_even, hidden_odd, 1 + j, value)
        if j == 0:
            put_blocks(hidden_even, hidden_odd, 5, pltpu.roll(value, 79, 0))
        if j == 3:
            put_blocks(hidden_even, hidden_odd, 0, pltpu.roll(value, 1, 0))
    pieces = []
    for a in range(3):
        for b in range(3):
            if a == 1:
                window = hidden_odd[2 - b : 6 - b, 0:64, :]
            else:
                window = hidden_even[2 - b : 6 - b, 8 * (2 - a) : 8 * (2 - a) + 64, :]
            pieces.append(window.reshape(256, HID))
    result = dot(jnp.concatenate(pieces, axis=1), mixes_tm[0 : 9 * HID, :])
    for j in range(4):
        for i, part in enumerate(lane_tiles(result[64 * j : 64 * j + 64])):
            out_grid[i, pl.ds(j, 64, stride=4), :] = part
    for r in range(8):
        for i in range(2):
            fgrad_ref[r, :, 128 * i : 128 * i + 128] = out_grid[i, r * 32 + 8 : r * 32 + 24, :]

    finish()


def hand_over(fgrad_ref, mgrad_ref, fgrad_out, mgrad_out):
    fgrad_out[...] = fgrad_ref[...]
    mgrad_out[...] = mgrad_ref[...]


def per_device(
    features,
    encoder_weight,
    latent_weight,
    timesteps,
    noise_field,
    time_table,
    input_weight,
    middle_weight,
    output_weight,
):
    hbm = pl.BlockSpec(memory_space=pl.ANY)
    vmem = pl.BlockSpec(memory_space=pltpu.VMEM)
    dma = pltpu.SemaphoreType.DMA
    operands = (
        features,
        encoder_weight,
        latent_weight.T,
        noise_field,
        time_table,
        input_weight,
        middle_weight,
        output_weight.T,
    )
    scratch = [
        pltpu.VMEM((8, 16, FEAT), BF16),
        pltpu.VMEM((9, FEAT, HID), BF16),
        pltpu.VMEM((LAT, HID), BF16),
        pltpu.VMEM(noise_field.shape, BF16),
        pltpu.VMEM(time_table.shape, BF16),
        pltpu.VMEM((LAT, UNET), BF16),
        pltpu.VMEM((9, UNET, UNET), BF16),
        pltpu.VMEM((LAT, UNET), BF16),
        dma((8,)),
        pltpu.VMEM((2, 3, UNET, UNET), BF16),
        pltpu.VMEM((4 * HID, 128), BF16),
        pltpu.VMEM((128, 4 * HID), BF16),
        pltpu.VMEM((128, 4 * UNET), BF16),
        pltpu.VMEM((4 * UNET, 128), BF16),
        pltpu.VMEM((4 * UNET, 128), BF16),
        pltpu.VMEM((128, 4 * UNET), BF16),
        pltpu.VMEM((8, UNET), F32),
        pltpu.VMEM((2, 16, FEAT), BF16),
        pltpu.VMEM((2, 16, FEAT), BF16),
        pltpu.VMEM((6, 2, 16, FEAT), BF16),
        pltpu.VMEM((2, 12 * 32, 128), F32),
        pltpu.VMEM((6, 96, FEAT), BF16),
        pltpu.VMEM((6, 88, FEAT), BF16),
        pltpu.VMEM((320, HID), F32),
        pltpu.VMEM((80, 128), F32),
        pltpu.VMEM((48, 128), F32),
        pltpu.VMEM((48, 128), BF16),
        pltpu.VMEM((15, 48, 128), BF16),
        pltpu.VMEM((16 * 48, 128), F32),
        pltpu.VMEM((640, 128), F32),
        pltpu.VMEM((2, 64, 128), BF16),
        pltpu.VMEM((2, 64, 128), BF16),
        pltpu.VMEM((12, 384, UNET), BF16),
        pltpu.VMEM((8, 256, UNET), BF16),
        pltpu.VMEM((4, 4, 384, UNET), BF16),
        pltpu.VMEM((4, 4, UNET, 384), BF16),
        pltpu.VMEM((16 * UNET, 256), BF16),
        pltpu.VMEM((4, 2, 256, UNET), BF16),
        pltpu.VMEM((2, 1024, UNET), F32),
        pltpu.VMEM((2048, UNET), F32),
        pltpu.VMEM((10, 384, UNET), BF16),
        pltpu.VMEM((512, 128), F32),
        pltpu.VMEM((15, 32, 128), BF16),
        pltpu.VMEM((15, 32, 128), BF16),
        pltpu.VMEM((32, 128), F32),
        pltpu.VMEM((32, 128), BF16),
        pltpu.VMEM((8, 32, 128), BF16),
        pltpu.VMEM((80, 128), F32),
        pltpu.VMEM((6, 80, HID), BF16),
        pltpu.VMEM((6, 72, HID), BF16),
        pltpu.VMEM((2, 256, 128), F32),
        pltpu.VMEM((9, 3 * UNET, 128), F32),
        pltpu.VMEM((3, 576, UNET), BF16),
        pltpu.VMEM((3, 576, UNET), BF16),
        pltpu.VMEM((9, 576, 128), F32),
        pltpu.VMEM((27, 48, UNET), BF16),
        pltpu.VMEM((27, 48, UNET), BF16),
        pltpu.VMEM((9, 256, 128), F32),
        pltpu.VMEM((9, 48, UNET), BF16),
        pltpu.VMEM((9, 48, UNET), BF16),
        pltpu.VMEM((9, 64, 128), F32),
        pltpu.VMEM((9, 16, UNET), BF16),
        pltpu.VMEM((9, 16, UNET), BF16),
        dma((8,)),
        dma((8,)),
        dma((2,)),
        dma((2,)),
        dma((15,)),
        dma((15,)),
        dma((2,)),
        dma((2,)),
        dma((15,)),
        dma((15,)),
        dma((8,)),
        dma((8,)),
        dma((3,)),
        dma((3,)),
        dma((27,)),
        dma((27,)),
        dma((9,)),
        dma((9,)),
        dma((9,)),
        dma((9,)),
    ]
    shapes = (
        jax.ShapeDtypeStruct((8, 16, FEAT), F32),
        jax.ShapeDtypeStruct((9, 3, UNET), F32),
    )
    results = pl.pallas_call(
        kernel,
        out_shape=shapes,
        in_specs=[pl.BlockSpec(memory_space=pltpu.SMEM)] + [hbm] * 8,
        out_specs=(vmem, vmem),
        scratch_shapes=scratch,
        compiler_params=pltpu.CompilerParams(
            collective_id=0, has_side_effects=True, vmem_limit_bytes=60 * 1024 * 1024
        ),
        cost_estimate=pl.CostEstimate(flops=18_000_000_000, bytes_accessed=8_000_000, transcendentals=3_000_000),
    )(timesteps, *operands)
    feature_grad, middle_grad = pl.pallas_call(
        hand_over,
        out_shape=shapes,
        in_specs=[vmem, vmem],
        out_specs=(vmem, vmem),
    )(*results)
    return feature_grad, jnp.transpose(middle_grad, (1, 0, 2))


def solution(mesh):
    in_specs = (
        P("tile", "step", None),
        P(),
        P(),
        P("step"),
        P("step", "tile", None),
        P(),
        P(),
        P(),
        P(),
    )
    out_specs = (P("tile", "step", None), P(("tile", "step"), None, None))
    return jax.shard_map(per_device, mesh=mesh, in_specs=in_specs, out_specs=out_specs, check_vma=False)
```

```python
import math

import jax
import jax.numpy as jnp
from jax import lax
from jax.experimental import pallas as pl
from jax.experimental.pallas import tpu as pltpu
from jax.sharding import PartitionSpec as P

F32 = jnp.float32
BF16 = jnp.bfloat16
MESH = pl.DeviceIdType.MESH

FEAT, HID, LAT, UNET = 256, 512, 32, 384
TILES, STEPS = 8, 16
AROUND = ((-1, -1), (-1, 0), (-1, 1), (0, -1), (0, 1), (1, -1), (1, 0), (1, 1))


def sigmoid(values):
    return 0.5 * jnp.tanh(0.5 * values) + 0.5


def slope_of(values, sigma):
    return sigma * (1.0 + values * (1.0 - sigma))


def dot(left, right):
    return jnp.dot(left, right, preferred_element_type=F32)


def lane_tiles(value):
    return [value[:, 128 * i : 128 * i + 128] for i in range(value.shape[1] // 128)]


def shift_down(block):
    last = pltpu.roll(block[48:64], 1, 0)
    rows = lax.broadcasted_iota(jnp.int32, last.shape, 0)
    return jnp.concatenate([jnp.where(rows == 0, 0.0, last), block[0:48]], axis=0)


def shift_up(block):
    first = pltpu.roll(block[0:16], 15, 0)
    rows = lax.broadcasted_iota(jnp.int32, first.shape, 0)
    return jnp.concatenate([block[16:64], jnp.where(rows == 15, 0.0, first)], axis=0)


def kernel(
    time_ref,
    feat_hbm,
    enc_hbm,
    latw_hbm,
    noise_hbm,
    table_hbm,
    inw_hbm,
    midw_hbm,
    outw_hbm,
    fgrad_ref,
    mgrad_ref,
    feat,
    enc,
    latw,
    noise,
    table,
    inw,
    midw,
    outw,
    in_sem,
    mid_sums,
    latw4,
    latw4_t,
    inw4,
    inw4_t,
    outw4,
    outw4_t,
    embed,
    edge,
    edge_in,
    rows_in,
    grid,
    blocks_even,
    blocks_odd,
    pre_hidden,
    lat_tile,
    lat_pack,
    lat_send,
    lat_recv,
    lat_flat,
    noise_rows,
    noise_edge,
    noise_edge_in,
    inner_ext,
    inner_slope,
    mixes,
    mixes_t,
    mixes_tm,
    back_mixes,
    pre_middle,
    back_mixed,
    back_ext,
    back_part,
    part_send,
    part_recv,
    round_pack,
    round_send,
    round_recv,
    round_grid,
    hidden_even,
    hidden_odd,
    out_grid,
    grad,
    s1_send,
    s1_recv,
    sum1,
    s2_send,
    s2_recv,
    sum2,
    s3_send,
    s3_recv,
    sum3,
    s4_send,
    s4_recv,
    feat_ss,
    feat_rs,
    noise_ss,
    noise_rs,
    lat_ss,
    lat_rs,
    halo_ss,
    halo_rs,
    part_ss,
    part_rs,
    round_ss,
    round_rs,
    s1_ss,
    s1_rs,
    s2_ss,
    s2_rs,
    s3_ss,
    s3_rs,
    s4_ss,
    s4_rs,
):
    t = lax.axis_index("tile")
    s = lax.axis_index("step")
    y_hi, x = t // 4, t % 4
    z, y_lo, core = s // 4, (s // 2) % 2, s % 2
    y = y_hi * 2 + y_lo

    def remote(src, dst, ss, rs, tile, step):
        return pltpu.make_async_remote_copy(
            src_ref=src, dst_ref=dst, send_sem=ss, recv_sem=rs, device_id=(tile, step), device_id_type=MESH
        )

    def near(offsets):
        return (t + offsets[0] + TILES) % TILES, (s + offsets[1] + STEPS) % STEPS

    loads = [
        pltpu.make_async_copy(src, dst, in_sem.at[i])
        for i, (src, dst) in enumerate(
            (
                (feat_hbm, feat),
                (noise_hbm, noise),
                (enc_hbm, enc),
                (latw_hbm, latw),
                (inw_hbm, inw),
                (outw_hbm, outw),
                (table_hbm, table),
                (midw_hbm, midw),
            )
        )
    ]
    for load in loads:
        load.start()
    l_feat, l_noise, l_enc, l_latw, l_inw, l_outw, l_table, l_midw = loads

    barrier = pltpu.get_barrier_semaphore()

    for k in range(1, STEPS):
        pl.semaphore_signal(barrier, inc=1, device_id=(t, (s + k) % STEPS), device_id_type=MESH)
    for k in range(1, TILES):
        pl.semaphore_signal(barrier, inc=1, device_id=((t + k) % TILES, s), device_id_type=MESH)
    for offsets in AROUND:
        if offsets[0] and offsets[1]:
            pl.semaphore_signal(barrier, inc=1, device_id=near(offsets), device_id_type=MESH)

    l_feat.wait()
    grid[...] = jnp.zeros_like(grid)
    for r in range(8):
        for i, part in enumerate(lane_tiles(feat[r].astype(F32))):
            grid[i, (r + 2) * 32 + 8 : (r + 2) * 32 + 24, :] = part
    for side, first in ((0, 8), (1, 22)):
        for i in range(2):
            pair = [grid[i, pl.ds(64 + first + col, 8, stride=32), :] for col in (0, 1)]
            edge[side, :, 128 * i : 128 * i + 128] = jnp.concatenate(pair, axis=0).astype(BF16)

    pl.semaphore_wait(barrier, STEPS - 1 + TILES - 1 + 4)

    feat_copies = []
    for d, offsets in enumerate(AROUND):
        tile, step = near(offsets)
        if offsets[0] == 0:
            side = 0 if offsets[1] < 0 else 1
            src, dst = edge.at[side], edge_in.at[side]
        else:
            slot = d if d < 3 else d - 2
            src, dst = feat.at[pl.ds(0 if offsets[0] < 0 else 6, 2)], rows_in.at[slot]
        copy = remote(src, dst, feat_ss.at[d], feat_rs.at[d], tile, step)
        copy.start()
        feat_copies.append(copy)

    l_noise.wait()
    for q in range(64):
        piece = noise[0, :, 128 * q : 128 * q + 128].astype(F32)
        noise_rows[pl.ds(64 + (q % 4) * 16 + q // 4, 8, stride=64), :] = piece
    noise_edge[0] = noise_rows[64:128, :].astype(BF16)
    noise_edge[1] = noise_rows[512:576, :].astype(BF16)
    noise_copies = []
    for side, offset in ((0, -1), (1, 1)):
        tile, step = near((offset, 0))
        copy = remote(noise_edge.at[side], noise_edge_in.at[side], noise_ss.at[side], noise_rs.at[side], tile, step)
        copy.start()
        noise_copies.append(copy)

    for load, weight, wide, flipped in (
        (l_latw, latw, latw4_t, latw4),
        (l_inw, inw, inw4, inw4_t),
        (l_outw, outw, outw4_t, outw4),
    ):
        load.wait()
        columns = weight.shape[1]
        wide[...] = jnp.zeros_like(wide)
        for j in range(4):
            wide[LAT * j : LAT * j + LAT, columns * j : columns * j + columns] = weight[...]
        if flipped is latw4:
            flipped[...] = jnp.transpose(wide[...])

    l_enc.wait()

    for d, copy in enumerate(feat_copies):
        copy.wait()
    for d, offsets in enumerate(AROUND):
        dt, ds = offsets
        valid = jnp.bool_(True)
        if dt:
            valid = (t < TILES - 1) if dt < 0 else (t > 0)
        if ds:
            beside = (s < STEPS - 1) if ds < 0 else (s > 0)
            valid = jnp.logical_and(valid, beside) if dt else beside
        if dt == 0:
            side = 0 if ds < 0 else 1
            taken = jnp.where(valid, edge_in[side].astype(F32), 0.0)
            first = 24 if ds < 0 else 6
            for i, part in enumerate(lane_tiles(taken)):
                for col in (0, 1):
                    grid[i, pl.ds(64 + first + col, 8, stride=32), :] = part[8 * col : 8 * col + 8]
        else:
            slot = d if d < 3 else d - 2
            for r in range(2):
                taken = jnp.where(valid, rows_in[slot, r].astype(F32), 0.0)
                row = (10 + r if dt < 0 else r) * 32
                for i, part in enumerate(lane_tiles(taken)):
                    if ds == 0:
                        grid[i, row + 8 : row + 24, :] = part
                    elif ds < 0:
                        grid[i, row + 24 : row + 32, :] = part[0:8]
                    else:
                        grid[i, row : row + 8, :] = part[8:16]

    def put_blocks(even, odd, index, value):
        even[index] = value.astype(BF16)
        odd[index] = value[8:].astype(BF16)

    for j in range(4):
        value = jnp.concatenate([grid[i, pl.ds(j, 96, stride=4), :] for i in range(2)], axis=1)
        put_blocks(blocks_even, blocks_odd, 1 + j, value)
        if j == 0:
            put_blocks(blocks_even, blocks_odd, 5, pltpu.roll(value, 95, 0))
        if j == 3:
            put_blocks(blocks_even, blocks_odd, 0, pltpu.roll(value, 1, 0))
    pieces = []
    for a in range(3):
        for b in range(3):
            if a == 1:
                window = blocks_odd[b : b + 4, 0:80, :]
            else:
                window = blocks_even[b : b + 4, 8 * a : 8 * a + 80, :]
            pieces.append(window.reshape(320, FEAT))
    pre = dot(jnp.concatenate(pieces, axis=1), enc[...].reshape(9 * FEAT, HID))
    pre_hidden[...] = pre
    hidden = (pre * sigmoid(pre)).astype(BF16)
    hidden = jnp.concatenate([hidden[80 * j : 80 * j + 80] for j in range(4)], axis=1)
    lat_tile[...] = dot(hidden, latw4[...])
    lat_pack[...] = jnp.zeros_like(lat_pack)
    for q in range(4):
        lat_pack[pl.ds(q, 10, stride=4), :] = lat_tile[pl.ds(2 + q, 10, stride=8), :]
    lat_send[...] = lat_pack[...].astype(BF16)

    def lat_copy(k):
        return remote(lat_send, lat_recv.at[k - 1], lat_ss.at[k - 1], lat_rs.at[k - 1], t, (s + k) % STEPS)

    for k in range(1, STEPS):
        lat_copy(k).start()

    inw4_t[...] = jnp.transpose(inw4[...])
    outw4[...] = jnp.transpose(outw4_t[...])
    chosen = time_ref[0]
    angle = ((jnp.full((8, 128), chosen, jnp.int32).astype(F32) + 1.0) / 1000.0 + 0.008) / 1.008 * (math.pi / 2.0)
    cosine = jnp.cos(angle)[0:1, :]
    sine = jnp.sin(angle)[0:1, :]
    l_table.wait()
    onehot = (lax.broadcasted_iota(jnp.int32, (16, table.shape[0]), 1) == chosen).astype(F32).astype(BF16)
    embed[...] = dot(onehot, table[...])[0:8]

    l_midw.wait()
    for b in range(3):
        ends = midw[b].astype(F32) + midw[6 + b].astype(F32)
        centre = midw[3 + b].astype(F32)
        mid_sums[0, b] = (0.5 * (ends + centre)).astype(BF16)
        mid_sums[1, b] = (0.5 * (ends - centre)).astype(BF16)
    for side in (0, 1):
        noise_copies[side].wait()
    noise_rows[576:640, :] = noise_edge_in[0].astype(F32)
    noise_rows[0:64, :] = noise_edge_in[1].astype(F32)

    lat_flat[pl.ds(pl.multiple_of(s * 48, 16), 48), :] = lat_pack[...].astype(BF16).astype(F32)

    for k in range(1, STEPS):
        lat_copy(k).wait()
    for k in range(1, STEPS):
        source = (s - k + STEPS) % STEPS
        lat_flat[pl.ds(pl.multiple_of(source * 48, 16), 48), :] = lat_recv[k - 1].astype(F32)

    def input_rows(first, count):
        latent = [lat_flat[pl.ds((first + r) * 4 + q, 16, stride=48), :] for r in range(count) for q in range(4)]
        noisy = sine * noise_rows[64 * first : 64 * (first + count), :]
        noisy = (cosine * jnp.concatenate(latent, axis=0) + noisy).astype(BF16)
        for j in range(4):
            pre = dot(noisy, inw4[:, UNET * j : UNET * j + UNET]) + embed[0:1, :]
            sigma = sigmoid(pre)
            inner = pre * sigma
            slope = slope_of(pre, sigma)
            for r in range(count):
                row = first + r
                own = inner[64 * r : 64 * r + 64]
                if row == 0:
                    own = own * jnp.where(t > 0, 1.0, 0.0)
                if row == 9:
                    own = own * jnp.where(t < TILES - 1, 1.0, 0.0)
                inner_ext[row, 64 + 64 * j : 128 + 64 * j, :] = own.astype(BF16)
                if j == 0:
                    inner_ext[row, 320:384, :] = shift_up(own).astype(BF16)
                if j == 3:
                    inner_ext[row, 0:64, :] = shift_down(own).astype(BF16)
                if 0 < row < 9:
                    inner_slope[row - 1, 64 * j : 64 * j + 64, :] = slope[64 * r : 64 * r + 64].astype(BF16)

    def mix_rows(ref, pair):
        d = [ref[2 * pair + r] for r in range(4)]
        mixes[pair, 0] = d[0] - d[2]
        mixes[pair, 1] = d[1] + d[2]
        mixes[pair, 2] = d[2] - d[1]
        mixes[pair, 3] = d[1] - d[3]

    def flip_mixes(pair):
        for k in range(4):
            flipped = jnp.transpose(mixes[pair, k])
            mixes_t[pair, k] = flipped
            mixes_tm[UNET * (4 * pair + k) : UNET * (4 * pair + k + 1), :] = flipped[:, 64:320]

    def mixed_conv(i, weights):
        for k in (1, 2, 0, 3):
            windows = [mixes[2 * i : 2 * i + 2, k, 64 * b : 64 * b + 256, :].reshape(512, UNET) for b in range(3)]
            part = dot(jnp.concatenate(windows, axis=1), weights[k])
            for pair in range(2):
                own = part[256 * pair : 256 * pair + 256]
                even = slice(512 * pair, 512 * pair + 256)
                odd = slice(512 * pair + 256, 512 * pair + 512)
                if k == 1:
                    pre_middle[i, even, :] = own
                    pre_middle[i, odd, :] = own
                elif k == 2:
                    pre_middle[i, even, :] += own
                    pre_middle[i, odd, :] -= own
                elif k == 0:
                    pre_middle[i, even, :] += own
                else:
                    pre_middle[i, odd, :] -= own

    def by_class(value):
        rows = value.shape[0] // 256
        return jnp.concatenate(
            [
                jnp.concatenate([value[256 * r + 64 * j : 256 * r + 64 * j + 64] for j in range(4)], axis=1)
                for r in range(rows)
            ],
            axis=0,
        )

    def by_position(value):
        rows = value.shape[0] // 64
        return jnp.concatenate(
            [value[64 * r : 64 * r + 64, UNET * j : UNET * j + UNET] for r in range(rows) for j in range(4)], axis=0
        )

    def forward_conv(i):
        weights = [midw[0:3], mid_sums[0], mid_sums[1], midw[6:9]]
        mixed_conv(i, [weight.reshape(3 * UNET, UNET) for weight in weights])

    def forward_after(i):
        r = 4 * i
        pre = pre_middle[i]
        sigma = sigmoid(pre)
        own = inner_ext[r + 1 : r + 5, 64:320, :].reshape(1024, UNET)
        mixed = (own.astype(F32) + pre * sigma).astype(BF16)
        prediction = dot(by_class(mixed), outw4[...])
        own_noise = noise_rows[64 + r * 64 : 320 + r * 64, :]
        error = ((prediction - own_noise) * (1.0 / math.sqrt(STEPS))).astype(BF16)
        pulled = by_position(dot(error, outw4_t[...]))
        back_mixed[256 * r : 256 * r + 1024, :] = pulled
        back = pulled * slope_of(pre, sigma)
        for row in range(4):
            own = back[256 * row : 256 * row + 256]
            back_ext[r + 1 + row, 64:320, :] = own.astype(BF16)
            back_ext[r + 1 + row, 320:384, :] = shift_up(own[0:64]).astype(BF16)
            back_ext[r + 1 + row, 0:64, :] = shift_down(own[192:256]).astype(BF16)
        for pair in range(2):
            first, second = back[512 * pair : 512 * pair + 256], back[512 * pair + 256 : 512 * pair + 512]
            back_mixes[2 * i + pair, 0] = (0.5 * (first + second)).astype(BF16)
            back_mixes[2 * i + pair, 1] = (0.5 * (first - second)).astype(BF16)

    halo_copies = []

    def halo_start(side):
        tile, step = near((2 * side - 1, 0))
        src, dst = ((1, 9), (8, 0))[side]
        src, dst = back_ext.at[src, pl.ds(64, 256)], back_ext.at[dst, pl.ds(64, 256)]
        copy = remote(src, dst, halo_ss.at[side], halo_rs.at[side], tile, step)
        copy.start()
        halo_copies.append(copy)

    def weight_product(k, pairs):
        taps = [
            jnp.concatenate([mixes_t[pair, k, :, 0:256] for pair in pairs], axis=1),
            jnp.concatenate(
                [mixes_tm[UNET * (4 * pair + k) : UNET * (4 * pair + k + 1), :] for pair in pairs], axis=1
            ),
            jnp.concatenate([mixes_t[pair, k, :, 128:384] for pair in pairs], axis=1),
        ]
        if k in (0, 3):
            right = [back_ext[1 + 2 * pair + k // 3, 64:320, :] for pair in pairs]
        else:
            right = [back_mixes[pair, k - 1] for pair in pairs]
        return lane_tiles(dot(jnp.concatenate(taps, axis=0), jnp.concatenate(right, axis=0)))

    input_rows(0, 6)
    mix_rows(inner_ext, 0)
    mix_rows(inner_ext, 1)
    forward_conv(0)
    input_rows(6, 4)
    mix_rows(inner_ext, 2)
    mix_rows(inner_ext, 3)
    flip_mixes(0)
    flip_mixes(1)
    forward_conv(1)
    forward_after(0)
    flip_mixes(2)
    flip_mixes(3)
    halo_start(0)
    for i, part in enumerate(weight_product(0, (0, 1))):
        grad[i] = part
    for i, part in enumerate(weight_product(3, (0, 1))):
        grad[6 + i] = -part
    forward_after(1)
    halo_start(1)

    def s1_copy(a):
        return remote(s1_send.at[a], s1_recv.at[a], s1_ss.at[a], s1_rs.at[a], t, s + 1 - 2 * core)

    def s1_pack(a):
        for n in range(9):
            first = (n // 3) * UNET + n % 3 + 3 * (1 - core)
            block = jnp.concatenate([grad[a * 3 + i, pl.ds(first, 64, stride=6), :] for i in range(3)], axis=1)
            s1_send[a, 64 * n : 64 * n + 64, :] = block.astype(BF16)

    def s1_add(a):
        for n in range(9):
            first = (n // 3) * UNET + n % 3 + 3 * core
            got = s1_recv[a, 64 * n : 64 * n + 64, :].astype(F32)
            for i in range(3):
                own = grad[a * 3 + i, pl.ds(first, 64, stride=6), :]
                sum1[a * 3 + i, 64 * n : 64 * n + 64, :] = own + got[:, 128 * i : 128 * i + 128]

    def axis_peer(axis, k):
        if axis == "z":
            there = (z + k) % 4
            return there, t, there * 4 + s % 4
        if axis == "x":
            there = (x + k) % 4
            return there, y_hi * 4 + there, s
        there = (y + k) % 4
        return there, (there // 2) * 4 + x, z * 4 + (there % 2) * 2 + core

    first_axis, second_axis, third_axis = ("z", "x", "y"), ("x", "z", "z"), ("y", "y", "x")

    def plane_rows(a, b, c, there):
        base = (3 * b + c) * 64
        parts = []
        for i in range(3):
            ref = sum1.at[a * 3 + i]
            if b == 0:
                parts.append(
                    jnp.concatenate([ref[pl.ds(base + 2 * there + low, 8, stride=8), :] for low in (0, 1)], axis=0)
                )
            elif b == 1:
                rows = [pl.ds(pl.multiple_of(base + high * 32 + there * 8, 8), 8) for high in (0, 1)]
                parts.append(jnp.concatenate([ref[row, :] for row in rows], axis=0))
            else:
                parts.append(ref[pl.ds(base + (there // 2) * 32 + there % 2, 16, stride=2), :])
        return jnp.concatenate(parts, axis=1)

    def s2_copy(a, b, k):
        _, tile, step = axis_peer(first_axis[b], k)
        index = (a * 3 + b) * 3 + k - 1
        return remote(s2_send.at[index], s2_recv.at[index], s2_ss.at[index], s2_rs.at[index], tile, step)

    def s2_pack(a):
        for b in range(3):
            for k in range(1, 4):
                there = axis_peer(first_axis[b], k)[0]
                for c in range(3):
                    block = plane_rows(a, b, c, there).astype(BF16)
                    s2_send[(a * 3 + b) * 3 + k - 1, 16 * c : 16 * c + 16, :] = block

    def s2_start(a):
        for k in (2, 1, 3):
            for b in range(3):
                s2_copy(a, b, k).start()

    def s2_wait(a):
        for b in range(3):
            for k in range(1, 4):
                s2_copy(a, b, k).wait()

    def s2_add(a):
        for b in range(3):
            mine = axis_peer(first_axis[b], 0)[0]
            for c in range(3):
                total = plane_rows(a, b, c, mine)
                for k in range(3):
                    total = total + s2_recv[(a * 3 + b) * 3 + k, 16 * c : 16 * c + 16, :].astype(F32)
                row = 16 * (3 * a + c)
                for i, part in enumerate(lane_tiles(total)):
                    sum2[b * 3 + i, row : row + 16, :] = part

    def line_rows(b, there):
        parts = []
        for i in range(3):
            ref = sum2.at[b * 3 + i]
            if b == 1:
                parts.append(
                    jnp.concatenate([ref[pl.ds(2 * there + low, 24, stride=8), :] for low in (0, 1)], axis=0)
                )
            else:
                parts.append(ref[pl.ds(there, 48, stride=4), :])
        return jnp.concatenate(parts, axis=1)

    def s3_copy(b, k):
        _, tile, step = axis_peer(second_axis[b], k)
        index = b * 3 + k - 1
        return remote(s3_send.at[index], s3_recv.at[index], s3_ss.at[index], s3_rs.at[index], tile, step)

    def s3_start():
        for b in range(3):
            for k in range(1, 4):
                s3_send[b * 3 + k - 1] = line_rows(b, axis_peer(second_axis[b], k)[0]).astype(BF16)
        for b in range(3):
            for k in range(1, 4):
                s3_copy(b, k).start()

    def point_rows(b, there):
        if b == 0:
            rows = pl.ds((there % 2) * 2 + there // 2, 16, stride=4)
        elif b == 1:
            rows = pl.ds((there % 2) * 24 + there // 2, 16, stride=2)
        else:
            rows = pl.ds(there, 16, stride=4)
        return jnp.concatenate([sum3[b * 3 + i, rows, :] for i in range(3)], axis=1)

    def s4_copy(b, k):
        _, tile, step = axis_peer(third_axis[b], k)
        index = b * 3 + k - 1
        return remote(s4_send.at[index], s4_recv.at[index], s4_ss.at[index], s4_rs.at[index], tile, step)

    def s4_start():
        for b in range(3):
            for k in range(1, 4):
                s3_copy(b, k).wait()
        for b in range(3):
            total = line_rows(b, axis_peer(second_axis[b], 0)[0])
            for k in range(3):
                total = total + s3_recv[b * 3 + k].astype(F32)
            for i, part in enumerate(lane_tiles(total)):
                sum3[b * 3 + i, 0:48, :] = part
        for b in range(3):
            for k in range(1, 4):
                s4_send[b * 3 + k - 1] = point_rows(b, axis_peer(third_axis[b], k)[0]).astype(BF16)
        for b in range(3):
            for k in range(1, 4):
                s4_copy(b, k).start()

    def finish():
        for b in range(3):
            for k in range(1, 4):
                s4_copy(b, k).wait()
        for b in range(3):
            total = point_rows(b, axis_peer(third_axis[b], 0)[0])
            for k in range(3):
                total = total + s4_recv[b * 3 + k].astype(F32)
            total = total * (1.0 / math.sqrt(64 * 256))
            for a in range(3):
                mgrad_ref[3 * a + b] = total[3 * a : 3 * a + 3]

    def flip_mid(k):
        for b in range(3):
            source = (midw.at[8 - b], mid_sums.at[0, 2 - b], mid_sums.at[1, 2 - b], midw.at[2 - b])[k]
            inner_ext[3 * k + b] = jnp.transpose(source[...])

    sum2[...] = jnp.zeros_like(sum2)
    sum3[...] = jnp.zeros_like(sum3)
    for i, part in enumerate(weight_product(1, range(4))):
        grad[i] += part
        grad[3 + i] = part
        grad[6 + i] += part
    flip_mid(0)
    for i, part in enumerate(weight_product(2, range(4))):
        grad[i] += part
        grad[3 + i] -= part
        grad[6 + i] += part
    flip_mid(1)
    s1_pack(1)
    s1_copy(1).start()
    for i, part in enumerate(weight_product(0, (2, 3))):
        grad[i] += part
    flip_mid(2)
    mix_rows(back_ext, 1)
    s1_pack(0)
    s1_copy(0).start()
    for i, part in enumerate(weight_product(3, (2, 3))):
        grad[6 + i] -= part
    flip_mid(3)
    mix_rows(back_ext, 2)
    s1_pack(2)
    s1_copy(2).start()

    for row, copy in ((9, halo_copies[0]), (0, halo_copies[1])):
        copy.wait()
        back_ext[row, 320:384, :] = shift_up(back_ext[row, 64:128, :].astype(F32)).astype(BF16)
        back_ext[row, 0:64, :] = shift_down(back_ext[row, 256:320, :].astype(F32)).astype(BF16)

    @pl.when(t == 0)
    def _():
        back_ext[0] = jnp.zeros_like(back_ext[0])

    @pl.when(t == TILES - 1)
    def _():
        back_ext[9] = jnp.zeros_like(back_ext[9])

    def backward_conv(i):
        mixed_conv(i, [inner_ext[3 * k : 3 * k + 3].reshape(3 * UNET, UNET) for k in range(4)])

    def backward_after(i):
        r = 4 * i
        through = pre_middle[i] + back_mixed[256 * r : 256 * r + 1024, :]
        back = (through * inner_slope[r : r + 4].reshape(1024, UNET).astype(F32)).astype(BF16)
        back_part[64 * r : 64 * r + 256, :] = cosine * dot(by_class(back), inw4_t[...])

    def flip_enc(first, last):
        for k in range(first, last):
            mixes_tm[HID * k : HID * k + HID, :] = jnp.transpose(enc[k])

    mix_rows(back_ext, 0)
    mix_rows(back_ext, 3)
    s1_copy(1).wait()
    s1_copy(0).wait()
    backward_conv(0)
    for a in (1, 0):
        s1_add(a)
        s2_pack(a)
    flip_enc(0, 5)
    s2_start(1)
    s2_start(0)

    s1_copy(2).wait()
    backward_conv(1)
    backward_after(0)
    s1_add(2)
    s2_pack(2)
    flip_enc(5, 9)
    s2_start(2)
    backward_after(1)

    def part_copy(k):
        return remote(
            part_send.at[k - 1], part_recv.at[k - 1], part_ss.at[k - 1], part_rs.at[k - 1], t, (s + k) % STEPS
        )

    for k in range(1, STEPS):
        part_send[k - 1] = back_part[pl.ds((s + k) % STEPS, 32, stride=16), :].astype(BF16)
    for k in range(1, STEPS):
        part_copy(k).start()

    for a in range(3):
        s2_wait(a)
        s2_add(a)
    s3_start()

    for k in range(1, STEPS):
        part_copy(k).wait()
    latent_round = back_part[pl.ds(s, 32, stride=16), :]
    for k in range(1, STEPS):
        latent_round = latent_round + part_recv[k - 1].astype(F32)
    round_send[...] = latent_round.astype(BF16)
    round_copies = []
    for d, offsets in enumerate(AROUND):
        tile, step = near(offsets)
        copy = remote(round_send, round_recv.at[d], round_ss.at[d], round_rs.at[d], tile, step)
        copy.start()
        round_copies.append(copy)

    s4_start()

    round_grid[...] = jnp.zeros_like(round_grid)
    round_pack[...] = round_send[...].astype(F32)
    for q in range(4):
        round_grid[pl.ds(10 + q, 8, stride=8), :] = round_pack[pl.ds(q, 8, stride=4), :]
    for d, (dt, ds) in enumerate(AROUND):
        round_copies[d].wait()
        valid = jnp.bool_(True)
        if dt:
            valid = (t < TILES - 1) if dt < 0 else (t > 0)
        if ds:
            beside = (s < STEPS - 1) if ds < 0 else (s > 0)
            valid = jnp.logical_and(valid, beside) if dt else beside
        round_pack[...] = jnp.where(valid, round_recv[d].astype(F32), 0.0)
        if dt == 0:
            q, place = (0, 6) if ds < 0 else (3, 1)
            round_grid[pl.ds(8 + place, 8, stride=8), :] = round_pack[pl.ds(q, 8, stride=4), :]
        else:
            source, row = (0, 72) if dt < 0 else (28, 0)
            if ds == 0:
                round_grid[row + 2 : row + 6, :] = round_pack[source : source + 4, :]
            else:
                q, place = (0, 6) if ds < 0 else (3, 1)
                round_grid[row + place : row + place + 1, :] = round_pack[source + q : source + q + 1, :]
    pulled = dot(round_grid[...].astype(BF16), latw4_t[...])
    for j in range(4):
        pre = pre_hidden[80 * j : 80 * j + 80, :]
        value = pulled[:, HID * j : HID * j + HID] * slope_of(pre, sigmoid(pre))
        put_blocks(hidden_even, hidden_odd, 1 + j, value)
        if j == 0:
            put_blocks(hidden_even, hidden_odd, 5, pltpu.roll(value, 79, 0))
        if j == 3:
            put_blocks(hidden_even, hidden_odd, 0, pltpu.roll(value, 1, 0))
    pieces = []
    for a in range(3):
        for b in range(3):
            if a == 1:
                window = hidden_odd[2 - b : 6 - b, 0:64, :]
            else:
                window = hidden_even[2 - b : 6 - b, 8 * (2 - a) : 8 * (2 - a) + 64, :]
            pieces.append(window.reshape(256, HID))
    result = dot(jnp.concatenate(pieces, axis=1), mixes_tm[0 : 9 * HID, :])
    for j in range(4):
        for i, part in enumerate(lane_tiles(result[64 * j : 64 * j + 64])):
            out_grid[i, pl.ds(j, 64, stride=4), :] = part
    for r in range(8):
        for i in range(2):
            fgrad_ref[r, :, 128 * i : 128 * i + 128] = out_grid[i, r * 32 + 8 : r * 32 + 24, :]

    finish()


def hand_over(fgrad_ref, mgrad_ref, fgrad_out, mgrad_out):
    fgrad_out[...] = fgrad_ref[...]
    mgrad_out[...] = mgrad_ref[...]


def per_device(
    features,
    encoder_weight,
    latent_weight,
    timesteps,
    noise_field,
    time_table,
    input_weight,
    middle_weight,
    output_weight,
):
    hbm = pl.BlockSpec(memory_space=pl.ANY)
    vmem = pl.BlockSpec(memory_space=pltpu.VMEM)
    dma = pltpu.SemaphoreType.DMA
    operands = (
        features,
        encoder_weight,
        latent_weight.T,
        noise_field,
        time_table,
        input_weight,
        middle_weight,
        output_weight.T,
    )
    scratch = [
        pltpu.VMEM((8, 16, FEAT), BF16),
        pltpu.VMEM((9, FEAT, HID), BF16),
        pltpu.VMEM((LAT, HID), BF16),
        pltpu.VMEM(noise_field.shape, BF16),
        pltpu.VMEM(time_table.shape, BF16),
        pltpu.VMEM((LAT, UNET), BF16),
        pltpu.VMEM((9, UNET, UNET), BF16),
        pltpu.VMEM((LAT, UNET), BF16),
        dma((8,)),
        pltpu.VMEM((2, 3, UNET, UNET), BF16),
        pltpu.VMEM((4 * HID, 128), BF16),
        pltpu.VMEM((128, 4 * HID), BF16),
        pltpu.VMEM((128, 4 * UNET), BF16),
        pltpu.VMEM((4 * UNET, 128), BF16),
        pltpu.VMEM((4 * UNET, 128), BF16),
        pltpu.VMEM((128, 4 * UNET), BF16),
        pltpu.VMEM((8, UNET), F32),
        pltpu.VMEM((2, 16, FEAT), BF16),
        pltpu.VMEM((2, 16, FEAT), BF16),
        pltpu.VMEM((6, 2, 16, FEAT), BF16),
        pltpu.VMEM((2, 12 * 32, 128), F32),
        pltpu.VMEM((6, 96, FEAT), BF16),
        pltpu.VMEM((6, 88, FEAT), BF16),
        pltpu.VMEM((320, HID), F32),
        pltpu.VMEM((80, 128), F32),
        pltpu.VMEM((48, 128), F32),
        pltpu.VMEM((48, 128), BF16),
        pltpu.VMEM((15, 48, 128), BF16),
        pltpu.VMEM((16 * 48, 128), F32),
        pltpu.VMEM((640, 128), F32),
        pltpu.VMEM((2, 64, 128), BF16),
        pltpu.VMEM((2, 64, 128), BF16),
        pltpu.VMEM((12, 384, UNET), BF16),
        pltpu.VMEM((8, 256, UNET), BF16),
        pltpu.VMEM((4, 4, 384, UNET), BF16),
        pltpu.VMEM((4, 4, UNET, 384), BF16),
        pltpu.VMEM((16 * UNET, 256), BF16),
        pltpu.VMEM((4, 2, 256, UNET), BF16),
        pltpu.VMEM((2, 1024, UNET), F32),
        pltpu.VMEM((2048, UNET), F32),
        pltpu.VMEM((10, 384, UNET), BF16),
        pltpu.VMEM((512, 128), F32),
        pltpu.VMEM((15, 32, 128), BF16),
        pltpu.VMEM((15, 32, 128), BF16),
        pltpu.VMEM((32, 128), F32),
        pltpu.VMEM((32, 128), BF16),
        pltpu.VMEM((8, 32, 128), BF16),
        pltpu.VMEM((80, 128), F32),
        pltpu.VMEM((6, 80, HID), BF16),
        pltpu.VMEM((6, 72, HID), BF16),
        pltpu.VMEM((2, 256, 128), F32),
        pltpu.VMEM((9, 3 * UNET, 128), F32),
        pltpu.VMEM((3, 576, UNET), BF16),
        pltpu.VMEM((3, 576, UNET), BF16),
        pltpu.VMEM((9, 576, 128), F32),
        pltpu.VMEM((27, 48, UNET), BF16),
        pltpu.VMEM((27, 48, UNET), BF16),
        pltpu.VMEM((9, 256, 128), F32),
        pltpu.VMEM((9, 48, UNET), BF16),
        pltpu.VMEM((9, 48, UNET), BF16),
        pltpu.VMEM((9, 64, 128), F32),
        pltpu.VMEM((9, 16, UNET), BF16),
        pltpu.VMEM((9, 16, UNET), BF16),
        dma((8,)),
        dma((8,)),
        dma((2,)),
        dma((2,)),
        dma((15,)),
        dma((15,)),
        dma((2,)),
        dma((2,)),
        dma((15,)),
        dma((15,)),
        dma((8,)),
        dma((8,)),
        dma((3,)),
        dma((3,)),
        dma((27,)),
        dma((27,)),
        dma((9,)),
        dma((9,)),
        dma((9,)),
        dma((9,)),
    ]
    shapes = (
        jax.ShapeDtypeStruct((8, 16, FEAT), F32),
        jax.ShapeDtypeStruct((9, 3, UNET), F32),
    )
    results = pl.pallas_call(
        kernel,
        out_shape=shapes,
        in_specs=[pl.BlockSpec(memory_space=pltpu.SMEM)] + [hbm] * 8,
        out_specs=(vmem, vmem),
        scratch_shapes=scratch,
        compiler_params=pltpu.CompilerParams(
            collective_id=0, has_side_effects=True, vmem_limit_bytes=60 * 1024 * 1024
        ),
        cost_estimate=pl.CostEstimate(flops=18_000_000_000, bytes_accessed=8_000_000, transcendentals=3_000_000),
    )(timesteps, *operands)
    feature_grad, middle_grad = pl.pallas_call(
        hand_over,
        out_shape=shapes,
        in_specs=[vmem, vmem],
        out_specs=(vmem, vmem),
    )(*results)
    return feature_grad, jnp.transpose(middle_grad, (1, 0, 2))


def solution(mesh):
    in_specs = (
        P("tile", "step", None),
        P(),
        P(),
        P("step"),
        P("step", "tile", None),
        P(),
        P(),
        P(),
        P(),
    )
    out_specs = (P("tile", "step", None), P(("tile", "step"), None, None))
    return jax.shard_map(per_device, mesh=mesh, in_specs=in_specs, out_specs=out_specs, check_vma=False)
```
